32 devices in a mesh: fsdp: 8 (over z, x), dp: 4 (over y, core).
Axes of the slice: x: 2, y: 2, z: 4, core: 2. Of those that a mesh axis runs over, the one named last changes fastest.
Arguments:
- features: bfloat16 [512, 256, 1024], P(('fsdp', 'dp')), may hold values from -11 to 11
- half_sides: int32 [512], P(('fsdp', 'dp')), may hold values from 6 to 8
- cotangent: bfloat16 [512, 256, 1024], P(('fsdp', 'dp')), may hold values from -6 to 6
- conv_in: bfloat16 [1024, 256], P('fsdp'), may hold values from -0.1875 to 0.1875
- conv_mid: bfloat16 [2, 9, 128, 256], P(None, None, None, 'fsdp'), may hold values from -0.1875 to 0.1875
- attn_down: bfloat16 [256, 128], P('fsdp'), may hold values from -0.375 to 0.375
- attn_up: bfloat16 [128, 512], P(None, 'fsdp'), may hold values from -0.5 to 0.5
- attn_bias: bfloat16 [512], P('fsdp'), may hold values from -3 to 3
- conv_out: bfloat16 [256, 1024], P(None, 'fsdp'), may hold values from -0.375 to 0.375
- gain_in: bfloat16 [256], P('fsdp'), may hold values from 0.5 to 1.5
- shift_in: bfloat16 [256], P('fsdp'), may hold values from -3 to 3
- gain_mid: bfloat16 [512], P('fsdp'), may hold values from 0.5 to 1.5
- shift_mid: bfloat16 [512], P('fsdp'), may hold values from -3 to 3
- gain_attn: bfloat16 [128], P('fsdp'), may hold values from 0.5 to 1.5
- shift_attn: bfloat16 [128], P('fsdp'), may hold values from -3 to 3
- gain_out: bfloat16 [1024], P('fsdp'), may hold values from 0.5 to 1.5
- shift_out: bfloat16 [1024], P('fsdp'), may hold values from -3 to 3
Outputs:
- block_out: bfloat16 [512, 256, 1024], P(('fsdp', 'dp'))
- grad_features: float32 [512, 256, 1024], P(('fsdp', 'dp'))
- norms: float32 [4], replicated
- grad_conv_in: float32 [1024, 256], P('fsdp')
- grad_conv_mid: float32 [2, 9, 128, 256], P(None, None, None, 'fsdp')
- grad_attn_down: float32 [256, 128], P('fsdp')
- grad_attn_up: float32 [128, 512], P(None, 'fsdp')
- grad_attn_bias: float32 [512], P('fsdp')
- grad_conv_out: float32 [256, 1024], P(None, 'fsdp')
- grad_gain_in: float32 [256], P('fsdp')
- grad_shift_in: float32 [256], P('fsdp')
- grad_gain_mid: float32 [512], P('fsdp')
- grad_shift_mid: float32 [512], P('fsdp')
- grad_gain_attn: float32 [128], P('fsdp')
- grad_shift_attn: float32 [128], P('fsdp')
- grad_gain_out: float32 [1024], P('fsdp')
- grad_shift_out: float32 [1024], P('fsdp')
The draws below stay inside these ranges and needn't reach their ends.
Inputs may be any that keep to these rules, and one draw needn't show every extreme that they name: Half the side of image i's feature map; its valid pixels are the top-left square of side 2 half_sides[i] in its 16 x 16 grid.
All inputs are finite; a program needn't handle non-finite values.
Results may differ from the reference program's by a relative error of at most 0.033.
The reference program's roundings to bfloat16 on the way count: a program that leaves them out, or rounds other values in their place, can miss the bound.
Values may be sent and summed in bfloat16 or wider, within the bound.
No kernel may reach another device: no remote copies, remote signals or barrier semaphores. Data moves between devices by JAX's collectives and lax.ppermute only.
A program may use at most 256 MiB of HBM per device.

```python
import jax
import jax.numpy as jnp
from jax import lax

WIDTH = 1024
BOT = 256
ATT = 128
RADIX = 2
SIDE = 16
PIX = 256
IMAGES = 512


def draw_features(key, part):
    key = jax.random.fold_in(key, 11)
    position = jnp.arange(IMAGES, dtype=jnp.float32) / (IMAGES - 1)
    values = jax.random.truncated_normal(key, -3.5, 3.5, (IMAGES, PIX, WIDTH), jnp.float32)
    rising = jnp.exp(position * 1.0986123)
    return (values * rising[:, None, None]).astype(jnp.bfloat16)


def plant(entries, rng, smallest, high):
    longest = entries.shape.index(max(entries.shape))
    spots = []
    for shift in (0, 1):
        where = [jax.random.randint(jax.random.fold_in(rng, axis), (), 0, length) for axis, length in enumerate(entries.shape)]
        where[longest] = (where[longest] + shift) % entries.shape[longest]
        spots.append(tuple(where))
    return entries.at[spots[0]].set(smallest).at[spots[1]].set(high)


def block_scale(stream_key, shape, cuts, smallest, largest):
    def one(dim, shards_of):
        heights = jax.random.uniform(jax.random.fold_in(jax.random.fold_in(stream_key, 6), dim), (shards_of,), jnp.float32, smallest / len(cuts), largest / len(cuts))
        return jnp.repeat(jnp.exp(heights), shape[dim] // shards_of).reshape((-1,) + (1,) * (len(shape) - dim - 1))

    factor_of = one(*cuts[0])
    for cut in cuts[1:]:
        factor_of = factor_of * one(*cut)
    return factor_of


def gaussian(stream_key, shape, scale, reach, cuts=(), kind=jnp.bfloat16):
    values = jax.random.normal(stream_key, shape, jnp.float32) * scale
    if len(cuts) > 0:
        values = block_scale(stream_key, shape, cuts, -0.22, 0.18) * values
    return jnp.clip(values, min=-reach, max=reach).astype(kind)


def setup_inputs(seed: int = 0) -> dict:
    splits = jax.random.split(jax.random.key(seed), 18)
    return {
        "features": draw_features(jax.random.fold_in(splits[17], 71), 0),
        "half_sides": plant(jax.random.randint(splits[1], (IMAGES,), 6, 9), jax.random.fold_in(splits[1], 1), 6, 8).astype(jnp.int32),
        "cotangent": gaussian(splits[2], (IMAGES, PIX, WIDTH), 1.0, 6.0, ((0, 32),)),
        "conv_in": gaussian(splits[3], (WIDTH, BOT), WIDTH ** -0.5, 0.1875, ((0, 8),)),
        "conv_mid": gaussian(splits[4], (RADIX, 9, BOT // RADIX, BOT), (9 * BOT // RADIX) ** -0.5, 0.1875, ((3, 8),)),
        "attn_down": gaussian(splits[5], (BOT, ATT), BOT ** -0.5, 0.375, ((0, 8),)),
        "attn_up": gaussian(splits[6], (ATT, RADIX * BOT), ATT ** -0.5, 0.5, ((1, 8),)),
        "attn_bias": gaussian(splits[7], (RADIX * BOT,), 0.5, 3.0, ((0, 8),)),
        "conv_out": gaussian(splits[8], (BOT, WIDTH), BOT ** -0.5, 0.375, ((1, 8),)),
        "gain_in": jnp.clip(1.0 + 0.1 * jax.random.normal(splits[9], (BOT,), jnp.float32), 0.5, 1.5).astype(jnp.bfloat16),
        "shift_in": gaussian(splits[10], (BOT,), 0.5, 3.0, ((0, 8),)),
        "gain_mid": jnp.clip(1.0 + 0.1 * jax.random.normal(splits[11], (RADIX * BOT,), jnp.float32), 0.5, 1.5).astype(jnp.bfloat16),
        "shift_mid": gaussian(splits[12], (RADIX * BOT,), 0.5, 3.0, ((0, 8),)),
        "gain_attn": jnp.clip(1.0 + 0.1 * jax.random.normal(splits[13], (ATT,), jnp.float32), 0.5, 1.5).astype(jnp.bfloat16),
        "shift_attn": gaussian(splits[14], (ATT,), 0.5, 3.0, ((0, 8),)),
        "gain_out": jnp.clip(1.0 + 0.1 * jax.random.normal(splits[15], (WIDTH,), jnp.float32), 0.5, 1.5).astype(jnp.bfloat16),
        "shift_out": gaussian(splits[16], (WIDTH,), 0.5, 3.0, ((0, 8),)),
    }


epsilon = 1e-05

@jax.custom_vjp
def low(v):
    return lax.optimization_barrier(v.astype(jnp.bfloat16)).astype(jnp.float32)

@jax.custom_vjp
def low_back(v):
    return v

def low_keep(v):
    return (low(v), None)

def low_pass(kept, grad):
    return (grad,)

def back_keep(v):
    return (v, None)

def back_low(kept, grad):
    return (low(grad),)
low.defvjp(low_keep, low_pass)
low_back.defvjp(back_keep, back_low)

def pixel_mask(half_sides, extent):
    places = jnp.arange(extent * extent, dtype=jnp.int32)
    limits = (2 * half_sides)[:, None]
    inside = ((places // extent)[None, :] < limits) & ((places % extent)[None, :] < limits)
    return inside.astype(jnp.float32)

def patches(planes):
    images, extent = (planes.shape[0], planes.shape[1])
    padded = jnp.pad(planes, ((0, 0), (1, 1), (1, 1), (0, 0)))
    shifted = [padded[:, row_shift:row_shift + extent, col_shift:col_shift + extent, :] for row_shift in range(3) for col_shift in range(3)]
    return jnp.concatenate(shifted, axis=-1).reshape(images * extent * extent, -1)

def batch_norm(values, weight, scales, offsets):
    counted = jnp.sum(weight)
    center = lax.optimization_barrier(jnp.sum(weight * values, axis=0)) / counted
    spread = lax.optimization_barrier(jnp.sum(weight * jnp.square(values - center), axis=0)) / counted
    return scales * ((values - center) * lax.rsqrt(spread + epsilon)) + offsets

def forward(inputs, conv_in, conv_mid, attn_down, attn_up, attn_bias, conv_out, gain_in, shift_in, gain_mid, shift_mid, gain_attn, shift_attn, gain_out, shift_out, inside, per_image):
    highest = lax.Precision.HIGHEST
    rows = inputs.reshape(-1, WIDTH)
    masked = low(rows * inside)
    first = low_back(jnp.dot(masked, low(conv_in), precision=highest))
    act_in = jax.nn.silu(batch_norm(first, inside, gain_in, shift_in)) * inside
    planes = low(act_in).reshape(IMAGES, SIDE, SIDE, BOT)
    kernel = low(conv_mid)
    half_width = BOT // RADIX
    pieces = []
    for branch in range(RADIX):
        columns = patches(planes[..., branch * half_width:(branch + 1) * half_width])
        pieces.append(jnp.dot(columns, kernel[branch].reshape(9 * half_width, BOT), precision=highest))
    second = low_back(jnp.concatenate(pieces, axis=1))
    act_mid = jax.nn.silu(batch_norm(second, inside, gain_mid, shift_mid)) * inside
    split = act_mid.reshape(IMAGES, PIX, RADIX, BOT)
    pooled = lax.optimization_barrier(jnp.sum(lax.optimization_barrier(jnp.sum(split, axis=2)), axis=1)) / per_image[:, None]
    squeeze = low_back(jnp.dot(low(pooled), low(attn_down), precision=highest))
    every_image = jnp.ones((IMAGES, 1), jnp.float32)
    excite = jax.nn.silu(batch_norm(squeeze, every_image, gain_attn, shift_attn))
    logits = low_back(jnp.dot(low(excite), low(attn_up), precision=highest)) + attn_bias
    weights = jax.nn.softmax(logits.reshape(IMAGES, RADIX, BOT), axis=1)
    mixed = lax.optimization_barrier(jnp.sum(weights[:, None, :, :] * split, axis=2)).reshape(-1, BOT)
    third = low_back(jnp.dot(low(mixed), low(conv_out), precision=highest))
    branch_out = batch_norm(third, inside, gain_out, shift_out)
    output = jax.nn.silu(rows + branch_out) * inside
    sums = jnp.stack([jnp.sum(inside * rows * rows), jnp.sum(mixed * mixed), jnp.sum(inside * branch_out * branch_out), jnp.sum(output * output)])
    return (output, sums)

def reference(features, half_sides, cotangent, conv_in, conv_mid, attn_down, attn_up, attn_bias, conv_out, gain_in, shift_in, gain_mid, shift_mid, gain_attn, shift_attn, gain_out, shift_out):
    inside = pixel_mask(half_sides, SIDE).reshape(-1, 1)
    per_image = jnp.square(2.0 * half_sides.astype(jnp.float32))
    params = [features, conv_in, conv_mid, attn_down, attn_up, attn_bias, conv_out, gain_in, shift_in, gain_mid, shift_mid, gain_attn, shift_attn, gain_out, shift_out]
    params = [item.astype(jnp.float32) for item in params]

    def function(*items):
        return forward(*items, inside, per_image)
    output, pullback, sums = jax.vjp(function, *params, has_aux=True)
    grads = pullback(cotangent.astype(jnp.float32).reshape(-1, WIDTH))
    counted = jnp.sum(inside)
    widths = jnp.array([WIDTH, BOT, WIDTH, WIDTH], jnp.float32)
    norms = jnp.sqrt(sums / (counted * widths))
    block_out = output.astype(jnp.bfloat16).reshape(IMAGES, PIX, WIDTH)
    return (block_out, grads[0], norms, grads[1], grads[2], grads[3], grads[4], grads[5], grads[6], grads[7], grads[8], grads[9], grads[10], grads[11], grads[12], grads[13], grads[14])
```

```python
import jax
import jax.numpy as jnp
from jax import lax
from jax.experimental import pallas as pl
from jax.experimental.pallas import tpu as pltpu
from jax.sharding import PartitionSpec as P

RADIX = 2
SIDE = 16
TAPS = 9
STEP = 2

epsilon = 1e-05
AXES = ("fsdp", "dp")
f32 = jnp.float32
bf16 = jnp.bfloat16
HIGH = lax.Precision.HIGHEST


def swap_all(values, axes):
    return lax.all_to_all(values, axes, 0, 0)


def all_sum(values):
    devices = lax.axis_size("fsdp") * lax.axis_size("dp")
    copies = jnp.broadcast_to(values[None], (devices,) + values.shape)
    return jnp.sum(swap_all(copies, AXES), axis=0)


def spread_dp(values):
    count = lax.axis_size("dp")
    return swap_all(jnp.broadcast_to(values[None], (count,) + values.shape), "dp")


def gather_rows(shard):
    pieces = lax.axis_size("fsdp")
    count = lax.axis_size("dp")
    rows, lanes = shard.shape
    odd = lax.rem(lax.axis_index("dp"), 2)
    half = lax.dynamic_slice_in_dim(shard, odd * (rows // 2), rows // 2, 0)
    mine = swap_all(jnp.broadcast_to(half[None], (pieces,) + half.shape), "fsdp")
    other = lax.ppermute(mine, "dp", [(i, i ^ 1) for i in range(count)])
    low = jnp.where(odd == 0, mine, other)
    high = jnp.where(odd == 0, other, mine)
    return jnp.stack([low, high], axis=1).reshape(pieces * rows, lanes)


def scatter_sum(parts):
    summed = jnp.sum(swap_all(parts, AXES).astype(f32), axis=0).astype(bf16)
    return spread_dp(summed)


def sigmoid(values):
    return 0.5 * jnp.tanh(0.5 * values) + 0.5


def fold(values):
    return values[:8] + values[8:]


def wide(mask, lanes):
    return jnp.concatenate([mask] * (lanes // mask.shape[1]), axis=1)


def places():
    return lax.broadcasted_iota(jnp.int32, (SIDE, 128), 0)


def row_mask(place, row, limit):
    return jnp.where((place < limit) & (row < limit), 1.0, 0.0).astype(f32)


def chunk(image, row):
    return pl.ds(pl.multiple_of(image * 256 + row * SIDE, SIDE), SIDE)


def rows_of(carry, body, unroll=2):
    return lax.fori_loop(0, SIDE, body, carry, unroll=unroll)


def contract_lead(left, right):
    return lax.dot_general(left, right, (((0,), (0,)), ((), ())), preferred_element_type=f32)


def contract_last(left, right):
    return lax.dot_general(left, right, (((1,), (1,)), ((), ())), preferred_element_type=f32)


def zeros_at_start(*refs):
    @pl.when(pl.program_id(0) == 0)
    def _():
        for ref in refs:
            ref[...] = jnp.zeros(ref.shape, ref.dtype)


def last_step():
    return pl.program_id(0) == pl.num_programs(0) - 1


def column_total(values):
    return jnp.sum(values, axis=0, keepdims=True)


def first_kernel(sides, x_ref, w_ref, first_ref, stat_ref, acc_ref):
    step = pl.program_id(0)
    zeros_at_start(acc_ref)
    first_ref[...] = jnp.dot(x_ref[...], w_ref[...], preferred_element_type=f32)
    place = places()
    lanes = first_ref.shape[1]
    for image in range(STEP):
        limit = 2 * sides[step * STEP + image]

        def body(row, carry):
            total, square = carry
            here = chunk(image, row)
            values = first_ref[here, :] * wide(row_mask(place, row, limit), lanes)
            first_ref[here, :] = values
            return (total + fold(values), square + fold(values * values))

        total, square = rows_of((acc_ref[0], acc_ref[1]), body)
        acc_ref[0] = total
        acc_ref[1] = square

    @pl.when(last_step())
    def _():
        stat_ref[...] = jnp.zeros(stat_ref.shape, f32)
        stat_ref[0:1, :] = column_total(acc_ref[0])
        stat_ref[1:2, :] = column_total(acc_ref[1])


def cross_kernel(sides, x_ref, first_ref, cross_ref, square_ref, ones_ref):
    step = pl.program_id(0)
    zeros_at_start(cross_ref, square_ref, ones_ref)
    cross_ref[...] += contract_lead(first_ref[...].astype(bf16), x_ref[...])
    place = places()
    lanes = x_ref.shape[1]
    for image in range(STEP):
        limit = 2 * sides[step * STEP + image]

        def body(row, carry):
            square, total = carry
            values = x_ref[chunk(image, row), :].astype(f32) * wide(
                row_mask(place, row, limit), lanes
            )
            return (square + fold(values * values), total + fold(values))

        square, total = rows_of((square_ref[...], ones_ref[...]), body)
        square_ref[...] = square
        ones_ref[...] = total


def write_patches(patch_ref, image, row, low, place):
    values = low.astype(f32)
    lanes = values.shape[1]
    inner = wide(place, lanes)
    left = jnp.where(inner == 0, 0.0, pltpu.roll(values, 1, 0)).astype(bf16)
    right = jnp.where(inner == SIDE - 1, 0.0, pltpu.roll(values, SIDE - 1, 0)).astype(bf16)
    half = lanes // RADIX
    for tap in range(TAPS):
        up, side = tap // 3, tap % 3
        source = (left, low, right)[side]
        here = pl.ds(pl.multiple_of((row + 2 - up) * SIDE, SIDE), SIDE)
        for group in range(RADIX):
            at = group * TAPS * half + tap * half
            patch_ref[image, here, at : at + half] = source[:, group * half : (group + 1) * half]


def second_kernel(sides, first_ref, ab_ref, w_ref, act_ref, second_ref, stat_ref, patch_ref, acc_ref):
    step = pl.program_id(0)
    zeros_at_start(acc_ref, patch_ref)
    place = places()
    lanes = first_ref.shape[1]
    columns = TAPS * lanes // RADIX
    for image in range(STEP):
        limit = 2 * sides[step * STEP + image]

        def body(row, carry):
            here = chunk(image, row)
            pre = first_ref[here, :] * ab_ref[0:1, :] + ab_ref[1:2, :]
            act = pre * (sigmoid(pre) * wide(row_mask(place, row, limit), lanes))
            low = act.astype(bf16)
            act_ref[here, :] = low
            write_patches(patch_ref, image, row, low, place)
            return carry

        rows_of(0, body)
    for image in range(STEP):
        for group in range(RADIX):
            second_ref[image * 256 : image * 256 + 256, group * lanes : (group + 1) * lanes] = (
                contract_last(
                    patch_ref[image, SIDE : SIDE + 256, group * columns : (group + 1) * columns],
                    w_ref[:, group * columns : (group + 1) * columns],
                )
            )
    for image in range(STEP):
        limit = 2 * sides[step * STEP + image]

        def body(row, carry):
            total, square = carry
            values = second_ref[chunk(image, row), :]
            values = values * wide(row_mask(place, row, limit), values.shape[1])
            return (total + fold(values), square + fold(values * values))

        total, square = rows_of((acc_ref[0], acc_ref[1]), body)
        acc_ref[0] = total
        acc_ref[1] = square

    @pl.when(last_step())
    def _():
        stat_ref[...] = jnp.zeros(stat_ref.shape, f32)
        stat_ref[0:1, :] = column_total(acc_ref[0])
        stat_ref[1:2, :] = column_total(acc_ref[1])


def pool_kernel(sides, second_ref, ab_ref, down_ref, pooled_ref, squeeze_ref, stat_ref, pool_ref):
    step = pl.program_id(0)
    place = places()
    lanes = second_ref.shape[1]
    for image in range(STEP):
        limit = 2 * sides[step * STEP + image]

        def body(row, total):
            pre = second_ref[chunk(image, row), :] * ab_ref[0:1, :] + ab_ref[1:2, :]
            act = pre * (sigmoid(pre) * wide(row_mask(place, row, limit), lanes))
            return total + fold(act)

        total = column_total(rows_of(jnp.zeros((8, lanes), f32), body))
        both = total[:, : lanes // 2] + total[:, lanes // 2 :]
        area = jnp.full(both.shape, limit * limit, jnp.int32).astype(f32)
        pool_ref[pl.ds(step * STEP + image, 1), :] = both / area

    @pl.when(last_step())
    def _():
        low = pool_ref[...].astype(bf16)
        pooled_ref[...] = low
        squeeze = jnp.dot(low, down_ref[...], preferred_element_type=f32)
        squeeze_ref[...] = squeeze
        stat_ref[...] = jnp.zeros(stat_ref.shape, f32)
        stat_ref[0:1, :] = column_total(squeeze)
        stat_ref[1:2, :] = column_total(squeeze * squeeze)


def mix_kernel(
    sides,
    second_ref,
    ab_ref,
    squeeze_ref,
    gate_ref,
    up_ref,
    bias_ref,
    out_ref,
    mixed_ref,
    weights_ref,
    excite_ref,
    gram_ref,
    gw_ref,
    stat_ref,
    colsum_ref,
    power_ref,
    acc_ref,
):
    step = pl.program_id(0)
    zeros_at_start(acc_ref, gram_ref)
    place = places()
    lanes = second_ref.shape[1]
    half = lanes // 2

    @pl.when(step == 0)
    def _():
        pre = squeeze_ref[...] * gate_ref[0:1, :] + gate_ref[1:2, :]
        excite = (pre * sigmoid(pre)).astype(bf16)
        excite_ref[...] = excite
        logits = contract_last(excite, up_ref[...]) + bias_ref[0:1, :]
        one, two = logits[:, :half], logits[:, half:]
        top = jnp.maximum(one, two)
        one, two = jnp.exp(one - top), jnp.exp(two - top)
        weights_ref[:, :half] = one / (one + two)
        weights_ref[:, half:] = two / (one + two)

    for image in range(STEP):
        limit = 2 * sides[step * STEP + image]
        weights = weights_ref[pl.ds(step * STEP + image, 1), :]

        def body(row, carry):
            total, square = carry
            here = chunk(image, row)
            pre = second_ref[here, :] * ab_ref[0:1, :] + ab_ref[1:2, :]
            act = pre * (sigmoid(pre) * wide(row_mask(place, row, limit), lanes))
            act = act * weights
            mixed = act[:, :half] + act[:, half:]
            low = mixed.astype(bf16)
            mixed_ref[here, :] = low
            return (total + fold(low.astype(f32)), square + fold(mixed * mixed))

        total, square = rows_of((acc_ref[0], acc_ref[1]), body)
        acc_ref[0] = total
        acc_ref[1] = square
    gram_ref[...] += contract_lead(mixed_ref[...], mixed_ref[...])

    @pl.when(last_step())
    def _():
        whole = out_ref[...].astype(f32)
        total = column_total(acc_ref[0])
        colsum_ref[...] = jnp.broadcast_to(total, colsum_ref.shape)
        power_ref[...] = acc_ref[1]
        gw = jnp.dot(gram_ref[...], whole, precision=HIGH, preferred_element_type=f32)
        gw_ref[...] = gw
        stat_ref[...] = jnp.zeros(stat_ref.shape, f32)
        sums = jnp.dot(
            jnp.broadcast_to(total, (8, half)), whole, precision=HIGH, preferred_element_type=f32
        )
        stat_ref[0:1, :] = sums[0:1, :]
        stat_ref[1:2, :] = column_total(gw * whole)


def out_kernel(
    sides,
    mixed_ref,
    x_ref,
    cot_ref,
    ab_ref,
    w_ref,
    wt_ref,
    block_ref,
    slope_ref,
    back_ref,
    grad_ref,
    stat_ref,
    power_ref,
    third_ref,
    acc_ref,
    square_ref,
):
    step = pl.program_id(0)
    zeros_at_start(acc_ref, square_ref, grad_ref)
    place = places()
    lanes = x_ref.shape[1]
    part = 512 if lanes % 512 == 0 else lanes
    third_ref[...] = jnp.dot(mixed_ref[...], w_ref[...], preferred_element_type=f32)
    for image in range(STEP):
        limit = 2 * sides[step * STEP + image]

        def body(row, square):
            here = chunk(image, row)
            mask = wide(row_mask(place, row, limit), part)
            for at in range(0, lanes, part):
                cut = slice(at, at + part)
                total = (
                    x_ref[here, cut].astype(f32)
                    + third_ref[here, cut] * ab_ref[0:1, cut]
                    + ab_ref[1:2, cut]
                )
                plain = sigmoid(total)
                gate = plain * mask
                output = total * gate
                block_ref[here, cut] = output.astype(bf16)
                slope = gate + output * (1.0 - plain)
                grad = cot_ref[here, cut].astype(f32) * (slope * ab_ref[0:1, cut])
                slope_ref[here, cut] = grad.astype(bf16)
                acc_ref[:, cut] += fold(grad)
                power = fold(output * output)
                for lane in range(0, part, 128):
                    square = square + power[:, lane : lane + 128]
            return square

        square_ref[...] = rows_of(square_ref[...], body, 1)
    back_ref[...] = jnp.dot(slope_ref[...], wt_ref[...], preferred_element_type=f32)
    grad_ref[...] += contract_lead(mixed_ref[...], slope_ref[...])

    @pl.when(last_step())
    def _():
        stat_ref[...] = jnp.zeros(stat_ref.shape, f32)
        stat_ref[0:1, :] = column_total(acc_ref[...])
        stat_ref[1:2, :] = column_total(grad_ref[...] * w_ref[...].astype(f32))
        power_ref[...] = square_ref[...]


def mid_terms(second_ref, ab_ref, here, mask):
    pre = second_ref[here, :] * ab_ref[0:1, :] + ab_ref[1:2, :]
    plain = sigmoid(pre)
    gate = plain * mask
    act = pre * gate
    return pre, act, gate + act * (1.0 - plain)


def gate_kernel(
    sides,
    second_ref,
    ab_ref,
    back_ref,
    mixed_ref,
    turn_ref,
    row_ref,
    weights_ref,
    excite_ref,
    squeeze_ref,
    gate_ref,
    up_ref,
    dmixed_ref,
    sums_ref,
    dup_ref,
    dbias_ref,
    dq_ref,
    stat_ref,
):
    step = pl.program_id(0)
    place = places()
    lanes = second_ref.shape[1]
    half = lanes // 2
    dmixed_ref[...] = back_ref[...] - jnp.dot(
        mixed_ref[...], turn_ref[...], preferred_element_type=f32
    )
    for image in range(STEP):
        limit = 2 * sides[step * STEP + image]

        def body(row, carry):
            here = chunk(image, row)
            mask = row_mask(place, row, limit)
            dmixed = (dmixed_ref[here, :] - row_ref[0:1, :]) * wide(mask, half)
            dmixed_ref[here, :] = dmixed
            both = jnp.concatenate([dmixed, dmixed], axis=1)
            pre, act, slope = mid_terms(second_ref, ab_ref, here, wide(mask, lanes))
            along = slope * both
            terms = (act * both, along, along * pre, slope, slope * pre)
            return tuple(old + fold(new) for old, new in zip(carry, terms))

        start = tuple(jnp.zeros((8, lanes), f32) for _ in range(5))
        totals = rows_of(start, body, 1)
        for index in range(5):
            sums_ref[index, pl.ds(step * STEP + image, 1), :] = column_total(totals[index])

    @pl.when(last_step())
    def _():
        weights = weights_ref[...]
        grads = sums_ref[0]
        mean = weights * grads
        mean = mean[:, :half] + mean[:, half:]
        dlogits = weights * (grads - jnp.concatenate([mean, mean], axis=1))
        dbias_ref[...] = jnp.broadcast_to(column_total(dlogits), dbias_ref.shape)
        low = dlogits.astype(bf16)
        dup_ref[...] = contract_lead(low, excite_ref[...])
        dexcite = jnp.dot(low, up_ref[...], preferred_element_type=f32)
        squeeze = squeeze_ref[...]
        pre = squeeze * gate_ref[0:1, :] + gate_ref[1:2, :]
        normed = squeeze * gate_ref[2:3, :] + gate_ref[3:4, :]
        plain = sigmoid(pre)
        dq = dexcite * (plain * (1.0 + pre * (1.0 - plain)))
        dq_ref[...] = dq
        stat_ref[...] = jnp.zeros(stat_ref.shape, f32)
        stat_ref[0:1, :] = column_total(dq)
        stat_ref[1:2, :] = column_total(dq * normed)


def squeeze_kernel(
    dq_ref,
    squeeze_ref,
    gate_ref,
    grads_ref,
    pooled_ref,
    down_ref,
    area_ref,
    weights_ref,
    sums_ref,
    ddown_ref,
    dpool_ref,
    stat_ref,
):
    normed = squeeze_ref[...] * gate_ref[2:3, :] + gate_ref[3:4, :]
    dsqueeze = gate_ref[0:1, :] * (
        dq_ref[...] - (grads_ref[0:1, :] + normed * grads_ref[1:2, :])
    )
    low = dsqueeze.astype(bf16)
    ddown_ref[...] = contract_lead(pooled_ref[...], low)
    dpool = contract_last(low, down_ref[...]) / area_ref[...]
    dpool_ref[...] = dpool
    both = jnp.concatenate([dpool, dpool], axis=1)
    weights = weights_ref[...]
    stat_ref[...] = jnp.zeros(stat_ref.shape, f32)
    stat_ref[0:1, :] = column_total(weights * sums_ref[1] + both * sums_ref[3])
    stat_ref[1:2, :] = column_total(weights * sums_ref[2] + both * sums_ref[4])


def conv_back_kernel(
    sides,
    second_ref,
    ab_ref,
    dmixed_ref,
    weights_ref,
    dpool_ref,
    first_ref,
    ab_in_ref,
    w_ref,
    dsecond_ref,
    dfirst_ref,
    stat_ref,
    column_ref,
    acc_ref,
):
    step = pl.program_id(0)
    zeros_at_start(acc_ref, column_ref)
    place = places()
    lanes = second_ref.shape[1]
    half = lanes // 2
    quarter = half // RADIX
    columns = TAPS * quarter
    for image in range(STEP):
        limit = 2 * sides[step * STEP + image]
        weights = weights_ref[pl.ds(step * STEP + image, 1), :]
        dpool = dpool_ref[pl.ds(step * STEP + image, 1), :]
        dpool = jnp.concatenate([dpool, dpool], axis=1)

        def body(row, carry):
            here = chunk(image, row)
            mask = wide(row_mask(place, row, limit), lanes)
            dmixed = dmixed_ref[here, :]
            both = jnp.concatenate([dmixed, dmixed], axis=1)
            pre, _, slope = mid_terms(second_ref, ab_ref, here, mask)
            grad = slope * (weights * both + dpool) * ab_ref[0:1, :]
            grad = grad - mask * (pre * ab_ref[2:3, :] + ab_ref[3:4, :])
            dsecond_ref[here, :] = grad.astype(bf16)
            return carry

        rows_of(0, body)
    for image in range(STEP):
        for group in range(RADIX):
            column_ref[image, SIDE : SIDE + 256, group * columns : (group + 1) * columns] = jnp.dot(
                dsecond_ref[image * 256 : image * 256 + 256, group * half : (group + 1) * half],
                w_ref[:, group * columns : (group + 1) * columns],
                preferred_element_type=f32,
            )
    for image in range(STEP):
        limit = 2 * sides[step * STEP + image]

        def body(row, carry):
            total, product = carry
            here = chunk(image, row)
            mask = row_mask(place, row, limit)
            parts = []
            for group in range(RADIX):
                sides_sum = []
                for side in range(3):
                    summed = None
                    for up in range(3):
                        at = group * columns + (up * 3 + side) * quarter
                        rows = pl.ds(pl.multiple_of((row + 2 - up) * SIDE, SIDE), SIDE)
                        piece = column_ref[image, rows, at : at + quarter]
                        summed = piece if summed is None else summed + piece
                    sides_sum.append(summed)
                inner = wide(place, quarter)
                low = jnp.where(inner == SIDE - 1, 0.0, pltpu.roll(sides_sum[0], SIDE - 1, 0))
                high = jnp.where(inner == 0, 0.0, pltpu.roll(sides_sum[2], 1, 0))
                parts.append(sides_sum[1] + low + high)
            dact = jnp.concatenate(parts, axis=1)
            first = first_ref[here, :]
            pre = first * ab_in_ref[0:1, :] + ab_in_ref[1:2, :]
            normed = first * ab_in_ref[2:3, :] + ab_in_ref[3:4, :]
            plain = sigmoid(pre)
            grad = dact * (plain * (1.0 + pre * (1.0 - plain)) * wide(mask, half))
            dfirst_ref[here, :] = grad
            return (total + fold(grad), product + fold(grad * normed))

        total, product = rows_of((acc_ref[0], acc_ref[1]), body, 1)
        acc_ref[0] = total
        acc_ref[1] = product

    @pl.when(last_step())
    def _():
        stat_ref[...] = jnp.zeros(stat_ref.shape, f32)
        stat_ref[0:1, :] = column_total(acc_ref[0])
        stat_ref[1:2, :] = column_total(acc_ref[1])


def conv_grad_kernel(act_ref, dsecond_ref, x_ref, dfirst_ref, conv_ref, in_ref, patch_ref):
    zeros_at_start(conv_ref, in_ref, patch_ref)
    place = places()
    lanes = act_ref.shape[1]
    columns = TAPS * lanes // RADIX
    for image in range(STEP):

        def body(row, carry):
            write_patches(patch_ref, image, row, act_ref[chunk(image, row), :], place)
            return carry

        rows_of(0, body)
    for image in range(STEP):
        for group in range(RADIX):
            conv_ref[:, group * columns : (group + 1) * columns] += contract_lead(
                dsecond_ref[image * 256 : image * 256 + 256, group * lanes : (group + 1) * lanes],
                patch_ref[image, SIDE : SIDE + 256, group * columns : (group + 1) * columns],
            )
    in_ref[...] += contract_lead(dfirst_ref[...].astype(bf16), x_ref[...])


def last_kernel(sides, dfirst_ref, first_ref, ab_ref, w_ref, slope_ref, scale_ref, out_ref, low_ref):
    step = pl.program_id(0)
    place = places()
    lanes = first_ref.shape[1]
    width = out_ref.shape[1]
    part = 512 if width % 512 == 0 else width
    for image in range(STEP):
        limit = 2 * sides[step * STEP + image]

        def body(row, carry):
            here = chunk(image, row)
            mask = wide(row_mask(place, row, limit), lanes)
            grad = dfirst_ref[here, :] * ab_ref[0:1, :]
            grad = grad - mask * (first_ref[here, :] * ab_ref[1:2, :] + ab_ref[2:3, :])
            low_ref[here, :] = grad.astype(bf16)
            return carry

        rows_of(0, body)
    out_ref[...] = contract_last(low_ref[...], w_ref[...])
    for image in range(STEP):

        def body(row, carry):
            here = chunk(image, row)
            for at in range(0, width, part):
                cut = slice(at, at + part)
                out_ref[here, cut] += slope_ref[here, cut].astype(f32) * scale_ref[0:1, cut]
            return carry

        rows_of(0, body)


def tiles(lanes):
    return pl.BlockSpec((STEP * 256, lanes), lambda i: (i, 0))


def held(*shape):
    return pl.BlockSpec(shape, lambda i: (0,) * len(shape))


def scalars():
    return pl.BlockSpec(memory_space=pltpu.SMEM)


def shaped(shape, dtype=f32):
    return jax.ShapeDtypeStruct(shape, dtype)


def call(kernel, steps, ins, outs, out_shapes, scratch=(), limit=48, name=None):
    return pl.pallas_call(
        kernel,
        grid=(steps,),
        in_specs=ins,
        out_specs=outs,
        out_shape=out_shapes,
        scratch_shapes=scratch,
        compiler_params=pltpu.CompilerParams(
            dimension_semantics=("arbitrary",), vmem_limit_bytes=limit * 1024 * 1024
        ),
        name=name,
    )


def rows8(*vectors):
    stacked = jnp.stack(vectors, axis=0)
    return jnp.pad(stacked, ((0, 8 - len(vectors)), (0, 0)))


def norm_terms(sums, squares, counted, gain, shift):
    center = sums / counted
    spread = squares / counted - center * center
    inv = lax.rsqrt(spread + epsilon)
    scale = gain * inv
    return center, spread, inv, scale, shift - center * scale


def local(
    features,
    half_sides,
    cotangent,
    conv_in,
    conv_mid,
    attn_down,
    attn_up,
    attn_bias,
    conv_out,
    gain_in,
    shift_in,
    gain_mid,
    shift_mid,
    gain_attn,
    shift_attn,
    gain_out,
    shift_out,
):
    images, pixels, width = features.shape
    rows = images * pixels
    steps = images // STEP
    pieces = lax.axis_size("fsdp")
    groups = lax.axis_size("dp")
    devices = pieces * groups
    bottleneck = conv_in.shape[1]
    att = attn_down.shape[1]
    mid = RADIX * bottleneck
    columns = RADIX * TAPS * conv_mid.shape[2]

    whole_in = gather_rows(conv_in)
    small = [gain_in, shift_in, gain_mid, shift_mid, gain_attn, shift_attn, gain_out, shift_out, attn_bias]
    lengths = [item.shape[0] for item in small]
    flat = jnp.concatenate(small)
    vector_rows = -(-flat.shape[0] // (4 * 128)) * 4
    flat = jnp.pad(flat, (0, vector_rows * 128 - flat.shape[0])).reshape(vector_rows, 128)
    out_cut = conv_out.T.reshape(-1, 128)
    packed = jnp.concatenate([out_cut, attn_down, attn_up.T, flat], axis=0)
    marks = [out_cut.shape[0], attn_down.shape[0], attn_up.shape[1]]
    packed = gather_rows(packed).reshape(pieces, -1, 128)
    whole_mid = gather_rows(conv_mid.transpose(3, 0, 1, 2).reshape(conv_mid.shape[3], columns))
    whole_out_t = packed[:, : marks[0]].reshape(width, bottleneck)
    whole_out = whole_out_t.T
    whole_down = packed[:, marks[0] : marks[0] + marks[1]].reshape(bottleneck, att)
    whole_up = packed[:, marks[0] + marks[1] : sum(marks)].reshape(mid, att)
    vectors = packed[:, sum(marks) :].reshape(pieces, -1)
    found = []
    at = 0
    for length in lengths:
        found.append(vectors[:, at : at + length].reshape(-1).astype(f32))
        at += length
    g_in, s_in, g_mid, s_mid, g_attn, s_attn, g_out, s_out, bias = found

    x = features.reshape(rows, width)
    cot = cotangent.reshape(rows, width)
    sides_float = 2.0 * half_sides.astype(f32)
    areas = sides_float * sides_float

    first, stat = call(
        first_kernel,
        steps,
        [scalars(), tiles(width), held(width, bottleneck)],
        [tiles(bottleneck), held(8, bottleneck)],
        [shaped((rows, bottleneck)), shaped((8, bottleneck))],
        [pltpu.VMEM((2, 8, bottleneck), f32)],
        name="first",
    )(half_sides, x, whole_in)
    stat = jnp.concatenate([stat[:2], jnp.full((1, bottleneck), jnp.sum(areas))], axis=0)
    stat = all_sum(stat)
    counted = stat[2, 0]
    c_in, _, i_in, a_in, b_in = norm_terms(stat[0], stat[1], counted, g_in, s_in)
    cross, x_square, x_sum = call(
        cross_kernel,
        steps,
        [scalars(), tiles(width), tiles(bottleneck)],
        [held(bottleneck, width), held(8, width), held(8, width)],
        [shaped((bottleneck, width)), shaped((8, width)), shaped((8, width))],
        name="cross",
    )(half_sides, x, first)

    act_low, second, stat = call(
        second_kernel,
        steps,
        [scalars(), tiles(bottleneck), held(8, bottleneck), held(bottleneck, columns)],
        [tiles(bottleneck), tiles(mid), held(8, mid)],
        [shaped((rows, bottleneck), bf16), shaped((rows, mid)), shaped((8, mid))],
        [pltpu.VMEM((STEP, 256 + 2 * SIDE, columns), bf16), pltpu.VMEM((2, 8, mid), f32)],
        name="second",
    )(half_sides, first, rows8(a_in, b_in), whole_mid)
    stat = all_sum(stat[:2])
    c_mid, _, i_mid, a_mid, b_mid = norm_terms(stat[0], stat[1], counted, g_mid, s_mid)
    ab_mid = rows8(a_mid, b_mid)

    pooled, squeeze, stat = call(
        pool_kernel,
        steps,
        [scalars(), tiles(mid), held(8, mid), held(bottleneck, att)],
        [held(images, bottleneck), held(images, att), held(8, att)],
        [shaped((images, bottleneck), bf16), shaped((images, att)), shaped((8, att))],
        [pltpu.VMEM((images, bottleneck), f32)],
        name="pool",
    )(half_sides, second, ab_mid, whole_down)
    stat = all_sum(stat[:2])
    counted_attn = jnp.float32(images * devices)
    c_attn, _, i_attn, a_attn, b_attn = norm_terms(stat[0], stat[1], counted_attn, g_attn, s_attn)
    gate = rows8(a_attn, b_attn, i_attn, -c_attn * i_attn)

    mixed, weights, excite, gram, gram_out, stat, colsum, power = call(
        mix_kernel,
        steps,
        [
            scalars(),
            tiles(mid),
            held(8, mid),
            held(images, att),
            held(8, att),
            held(mid, att),
            held(8, mid),
            held(bottleneck, width),
        ],
        [
            tiles(bottleneck),
            held(images, mid),
            held(images, att),
            held(bottleneck, bottleneck),
            held(bottleneck, width),
            held(8, width),
            held(8, bottleneck),
            held(8, bottleneck),
        ],
        [
            shaped((rows, bottleneck), bf16),
            shaped((images, mid)),
            shaped((images, att), bf16),
            shaped((bottleneck, bottleneck)),
            shaped((bottleneck, width)),
            shaped((8, width)),
            shaped((8, bottleneck)),
            shaped((8, bottleneck)),
        ],
        [pltpu.VMEM((2, 8, bottleneck), f32)],
        name="mix",
    )(half_sides, second, ab_mid, squeeze, gate, whole_up, rows8(bias), whole_out)
    sums_x = jnp.sum(x_square)
    sums_mixed = jnp.sum(power)
    lane = lax.broadcasted_iota(jnp.int32, (1, width), 1)
    extra = jnp.where(lane == 0, sums_x, jnp.where(lane == 1, sums_mixed, 0.0))
    stat = all_sum(jnp.concatenate([stat[:2], extra, column_total(x_sum)], axis=0))
    x_sum_all = stat[3]
    power_x, power_mixed = stat[2, 0], stat[2, 1]
    c_out, v_out, i_out, a_out, b_out = norm_terms(stat[0], stat[1], counted, g_out, s_out)
    power_branch = counted * jnp.sum(g_out * g_out * v_out * i_out * i_out + s_out * s_out)

    block, slope, back, grad_out, stat, power = call(
        out_kernel,
        steps,
        [
            scalars(),
            tiles(bottleneck),
            tiles(width),
            tiles(width),
            held(8, width),
            held(bottleneck, width),
            held(width, bottleneck),
        ],
        [
            tiles(width),
            tiles(width),
            tiles(bottleneck),
            held(bottleneck, width),
            held(8, width),
            held(8, 128),
        ],
        [
            shaped((rows, width), bf16),
            shaped((rows, width), bf16),
            shaped((rows, bottleneck)),
            shaped((bottleneck, width)),
            shaped((8, width)),
            shaped((8, 128)),
        ],
        [
            pltpu.VMEM((STEP * 256, width), f32),
            pltpu.VMEM((8, width), f32),
            pltpu.VMEM((8, 128), f32),
        ],
        name="output",
    )(half_sides, mixed, x, cot, rows8(a_out, b_out), whole_out, whole_out_t)
    extra = jnp.full((1, width), jnp.sum(power))
    stat = all_sum(jnp.concatenate([stat[:2], extra], axis=0))
    power_output = stat[2, 0]
    shift_out_grad = stat[0] / a_out
    gain_out_grad = (stat[1] - c_out * stat[0]) / g_out
    slant = a_out * i_out * gain_out_grad / counted
    level = stat[0] / counted - c_out * slant
    global_sums = jnp.stack([power_x, power_mixed, power_branch, power_output])
    widths = jnp.array([width, bottleneck, width, width], f32)
    norms = jnp.sqrt(global_sums / (counted * widths))
    out_float = whole_out.astype(f32)
    turn = jnp.dot((out_float * slant).astype(bf16), whole_out_t, preferred_element_type=f32)
    row = jnp.sum(out_float * level, axis=1)
    grad_conv_out = grad_out - colsum[0][:, None] * level - gram_out * slant

    dmixed, sums, dup, dbias, dq, stat = call(
        gate_kernel,
        steps,
        [
            scalars(),
            tiles(mid),
            held(8, mid),
            tiles(bottleneck),
            tiles(bottleneck),
            held(bottleneck, bottleneck),
            held(8, bottleneck),
            held(images, mid),
            held(images, att),
            held(images, att),
            held(8, att),
            held(mid, att),
        ],
        [
            tiles(bottleneck),
            held(5, images, mid),
            held(mid, att),
            held(8, mid),
            held(images, att),
            held(8, att),
        ],
        [
            shaped((rows, bottleneck)),
            shaped((5, images, mid)),
            shaped((mid, att)),
            shaped((8, mid)),
            shaped((images, att)),
            shaped((8, att)),
        ],
        name="gate",
    )(
        half_sides,
        second,
        ab_mid,
        back,
        mixed,
        turn.astype(bf16),
        rows8(row),
        weights,
        excite,
        squeeze,
        gate,
        whole_up,
    )
    stat = all_sum(stat[:2])
    shift_attn_grad, gain_attn_grad = stat[0], stat[1]
    ddown, dpool, stat = call(
        squeeze_kernel,
        1,
        [
            held(images, att),
            held(images, att),
            held(8, att),
            held(8, att),
            held(images, bottleneck),
            held(bottleneck, att),
            held(images, bottleneck),
            held(images, mid),
            held(5, images, mid),
        ],
        [held(bottleneck, att), held(images, bottleneck), held(8, mid)],
        [shaped((bottleneck, att)), shaped((images, bottleneck)), shaped((8, mid))],
        name="squeeze",
    )(
        dq,
        squeeze,
        gate,
        rows8(shift_attn_grad / counted_attn, gain_attn_grad / counted_attn),
        pooled,
        whole_down,
        jnp.broadcast_to(areas[:, None], (images, bottleneck)),
        weights,
        sums,
    )
    stat = all_sum(stat[:2])
    shift_mid_grad = stat[0]
    gain_mid_grad = (stat[1] - s_mid * stat[0]) / g_mid
    slant = a_mid * gain_mid_grad / (counted * g_mid)
    level = a_mid * shift_mid_grad / counted - s_mid * slant

    dsecond, dfirst, stat = call(
        conv_back_kernel,
        steps,
        [
            scalars(),
            tiles(mid),
            held(8, mid),
            tiles(bottleneck),
            held(images, mid),
            held(images, bottleneck),
            tiles(bottleneck),
            held(8, bottleneck),
            held(bottleneck, columns),
        ],
        [tiles(mid), tiles(bottleneck), held(8, bottleneck)],
        [shaped((rows, mid), bf16), shaped((rows, bottleneck)), shaped((8, bottleneck))],
        [pltpu.VMEM((STEP, 256 + 2 * SIDE, columns), f32), pltpu.VMEM((2, 8, bottleneck), f32)],
        name="conv_back",
    )(
        half_sides,
        second,
        rows8(a_mid, b_mid, slant, level),
        dmixed,
        weights,
        dpool,
        first,
        rows8(a_in, b_in, i_in, -c_in * i_in),
        whole_mid,
    )
    stat = all_sum(stat[:2])
    shift_in_grad, gain_in_grad = stat[0], stat[1]
    slant = a_in * i_in * gain_in_grad / counted
    level = a_in * shift_in_grad / counted - c_in * slant
    conv_grad, in_grad = call(
        conv_grad_kernel,
        steps,
        [tiles(bottleneck), tiles(mid), tiles(width), tiles(bottleneck)],
        [held(bottleneck, columns), held(bottleneck, width)],
        [shaped((bottleneck, columns)), shaped((bottleneck, width))],
        [pltpu.VMEM((STEP, 256 + 2 * SIDE, columns), bf16)],
        name="conv_grad",
    )(act_low, dsecond, x, dfirst)
    grad_features = call(
        last_kernel,
        steps,
        [
            scalars(),
            tiles(bottleneck),
            tiles(bottleneck),
            held(8, bottleneck),
            held(width, bottleneck),
            tiles(width),
            held(8, width),
        ],
        tiles(width),
        shaped((rows, width)),
        [pltpu.VMEM((STEP * 256, bottleneck), bf16)],
        name="last",
    )(half_sides, dfirst, first, rows8(a_in, slant, level), whole_in, slope, rows8(1.0 / a_out))

    def lanes_out(grad):
        cut = grad.astype(bf16).reshape(bottleneck, pieces, -1).transpose(1, 0, 2)
        cut = cut.reshape(devices, bottleneck // groups, -1)
        return scatter_sum(cut).reshape(bottleneck, -1).astype(f32)

    shard_out = lanes_out(grad_conv_out)
    shard_in = lanes_out(
        in_grad * a_in[:, None]
        - cross * slant[:, None]
        - column_total(x_sum) * level[:, None]
    ).T
    shard_mid = scatter_sum(conv_grad.astype(bf16).reshape(devices, -1, columns))
    shard_mid = shard_mid.reshape(-1, columns).astype(f32).T.reshape(RADIX, TAPS, -1, conv_mid.shape[3])
    up_rows = mid // pieces
    down_rows = bottleneck // pieces
    bias_rows = jnp.pad(
        dbias[0].reshape(pieces, 1, up_rows), ((0, 0), (0, groups - 1), (0, att - up_rows))
    )
    gates = jnp.concatenate(
        [dup.reshape(pieces, up_rows, att), ddown.reshape(pieces, down_rows, att), bias_rows], axis=1
    )
    gates = scatter_sum(gates.astype(bf16).reshape(devices, -1, att))
    gates = gates.reshape(-1, att).astype(f32)
    shard_up = gates[:up_rows].T
    shard_down = gates[up_rows : up_rows + down_rows]
    shard_bias = gates[up_rows + down_rows, :up_rows]

    def own_part(whole):
        length = whole.shape[0] // pieces
        return lax.dynamic_slice_in_dim(whole, lax.axis_index("fsdp") * length, length, 0)

    return (
        block.reshape(images, pixels, width),
        grad_features.reshape(images, pixels, width),
        norms,
        shard_in,
        shard_mid,
        shard_down,
        shard_up,
        shard_bias,
        shard_out,
        own_part(gain_in_grad),
        own_part(shift_in_grad),
        own_part(gain_mid_grad),
        own_part(shift_mid_grad),
        own_part(gain_attn_grad),
        own_part(shift_attn_grad),
        own_part(gain_out_grad),
        own_part(shift_out_grad),
    )


def solution(mesh):
    return jax.shard_map(
        local,
        mesh=mesh,
        in_specs=(
            P(("fsdp", "dp"), None, None),
            P(("fsdp", "dp")),
            P(("fsdp", "dp"), None, None),
            P("fsdp", None),
            P(None, None, None, "fsdp"),
            P("fsdp", None),
            P(None, "fsdp"),
            P("fsdp"),
            P(None, "fsdp"),
            P("fsdp"),
            P("fsdp"),
            P("fsdp"),
            P("fsdp"),
            P("fsdp"),
            P("fsdp"),
            P("fsdp"),
            P("fsdp"),
        ),
        out_specs=(
            P(("fsdp", "dp"), None, None),
            P(("fsdp", "dp"), None, None),
            P(),
            P("fsdp", None),
            P(None, None, None, "fsdp"),
            P("fsdp", None),
            P(None, "fsdp"),
            P("fsdp"),
            P(None, "fsdp"),
            P("fsdp"),
            P("fsdp"),
            P("fsdp"),
            P("fsdp"),
            P("fsdp"),
            P("fsdp"),
            P("fsdp"),
            P("fsdp"),
        ),
        check_vma=False,
    )
```

```python
import functools

import jax
import jax.numpy as jnp
from jax import lax
from jax.experimental import pallas as pl
from jax.experimental.pallas import tpu as pltpu
from jax.sharding import PartitionSpec as P

RADIX = 2
SIDE = 16
TAPS = 9
STEP = 2

epsilon = 1e-05
AXES = ("fsdp", "dp")
f32 = jnp.float32
bf16 = jnp.bfloat16
HIGH = lax.Precision.HIGHEST


def swap_all(values, axes):
    return lax.all_to_all(values, axes, 0, 0)


def gather_all(shard):
    pieces = lax.axis_size("fsdp")
    return swap_all(jnp.broadcast_to(shard[None], (pieces,) + shard.shape), "fsdp")


def neighbour(values):
    return lax.ppermute(values, "dp", [(i, i ^ 1) for i in range(lax.axis_size("dp"))])


def half_of(shard, axis):
    odd = lax.rem(lax.axis_index("dp"), 2)
    return lax.dynamic_slice_in_dim(shard, odd * (shard.shape[axis] // 2), shard.shape[axis] // 2, axis)


def sigmoid(values):
    return 0.5 * jnp.tanh(0.5 * values) + 0.5


def fold(values):
    return values[:8] + values[8:]


def wide(mask, lanes):
    return jnp.concatenate([mask] * (lanes // mask.shape[1]), axis=1)


def places():
    return lax.broadcasted_iota(jnp.int32, (SIDE, 128), 0)


def row_mask(place, row, limit):
    return jnp.where((place < limit) & (row < limit), 1.0, 0.0).astype(f32)


def chunk(image, row):
    return pl.ds(pl.multiple_of(image * 256 + row * SIDE, SIDE), SIDE)


def rows_of(carry, body, unroll=8):
    return lax.fori_loop(0, SIDE, body, carry, unroll=unroll)


def contract_lead(left, right):
    return lax.dot_general(left, right, (((0,), (0,)), ((), ())), preferred_element_type=f32)


def contract_last(left, right):
    return lax.dot_general(left, right, (((1,), (1,)), ((), ())), preferred_element_type=f32)


def zeros_at_start(*refs):
    @pl.when(pl.program_id(0) == 0)
    def _():
        for ref in refs:
            ref[...] = jnp.zeros(ref.shape, ref.dtype)


def last_step():
    return pl.program_id(0) == pl.num_programs(0) - 1


def column_total(values):
    return jnp.sum(values, axis=0, keepdims=True)


def take(recv_ref, tile_ref):
    tile_ref[...] = lax.fori_loop(
        1,
        recv_ref.shape[0],
        lambda j, total: total + recv_ref[j].astype(f32),
        recv_ref[0].astype(f32),
        unroll=True if recv_ref.shape[0] <= 32 else 1,
    )


def row_at(tile_ref, start, lanes):
    return jnp.concatenate(
        [tile_ref[start + q : start + q + 1, :] for q in range(lanes // 128)], axis=1
    )


def put(tile_ref, start, row):
    for q in range(row.shape[1] // 128):
        tile_ref[start + q : start + q + 1, :] = row[:, q * 128 : (q + 1) * 128]


def send(send_ref, tile_ref):
    tile = tile_ref[...].astype(send_ref.dtype)

    def body(j, carry):
        send_ref[j] = tile
        return carry

    lax.fori_loop(0, send_ref.shape[0], body, 0, unroll=True if send_ref.shape[0] <= 32 else 1)


def norm_rows(sums, squares, counted, gain, shift):
    center = sums / counted
    spread = squares / counted - center * center
    inv = lax.rsqrt(spread + epsilon)
    scale = gain * inv
    return center, spread, inv, scale, shift - center * scale


def fill_half(whole_ref, mine_ref, other_ref, odd_ref):
    half = whole_ref.shape[1] // 2

    @pl.when(odd_ref[0] == 0)
    def _():
        whole_ref[:, :half] = mine_ref[...]
        whole_ref[:, half:] = other_ref[...]

    @pl.when(odd_ref[0] != 0)
    def _():
        whole_ref[:, :half] = other_ref[...]
        whole_ref[:, half:] = mine_ref[...]


def at_start(body):
    pl.when(pl.program_id(0) == 0)(body)


def at_end(body):
    pl.when(pl.program_id(0) == pl.num_programs(0) - 1)(body)


def lane_parts(values):
    total = values[:, :128]
    for at in range(128, values.shape[1], 128):
        total = total + values[:, at : at + 128]
    return total


def lane_sum(row):
    return jnp.broadcast_to(jnp.sum(row, axis=1, keepdims=True), (1, 128))


def first_kernel(
    sides, odd, x_ref, mine_ref, other_ref, first_ref, w_ref, send_ref, acc_ref, tile_ref
):
    step = pl.program_id(0)
    zeros_at_start(acc_ref)
    at_start(lambda: fill_half(w_ref, mine_ref, other_ref, odd))
    first_ref[...] = jnp.dot(x_ref[...], w_ref[...], preferred_element_type=f32)
    place = places()
    lanes = first_ref.shape[1]
    for image in range(STEP):
        limit = 2 * sides[step * STEP + image]

        def body(row, carry):
            total, square = carry
            here = chunk(image, row)
            values = first_ref[here, :] * wide(row_mask(place, row, limit), lanes)
            first_ref[here, :] = values
            return (total + fold(values), square + fold(values * values))

        total, square = rows_of((acc_ref[0], acc_ref[1]), body)
        acc_ref[0] = total
        acc_ref[1] = square

    @at_end
    def _():
        count = jnp.int32(0)
        for image in range(sides.shape[0]):
            count = count + 4 * sides[image] * sides[image]
        tile_ref[...] = jnp.zeros(tile_ref.shape, f32)
        put(tile_ref, 0, column_total(acc_ref[0]))
        put(tile_ref, lanes // 128, column_total(acc_ref[1]))
        put(tile_ref, 2 * lanes // 128, jnp.full((1, 128), count, jnp.int32).astype(f32))
        send(send_ref, tile_ref)


def cross_kernel(
    sides, x_ref, first_ref, part_ref, cross_ref, ones_ref, power_ref, copies_ref, square_ref
):
    step = pl.program_id(0)
    zeros_at_start(cross_ref, square_ref, ones_ref)
    cross_ref[...] += contract_lead(first_ref[...].astype(bf16), x_ref[...])
    place = places()
    lanes = x_ref.shape[1]
    for image in range(STEP):
        limit = 2 * sides[step * STEP + image]

        def body(row, carry):
            square, total = carry
            values = x_ref[chunk(image, row), :].astype(f32) * wide(
                row_mask(place, row, limit), lanes
            )
            return (square + fold(values * values), total + fold(values))

        square, total = rows_of((square_ref[...], ones_ref[...]), body)
        square_ref[...] = square
        ones_ref[...] = total

    @at_end
    def _():
        power_ref[...] = lane_parts(square_ref[...])
        for j in range(copies_ref.shape[0]):
            copies_ref[j] = part_ref[...]


def write_patches(patch_ref, image, row, low, place):
    values = low.astype(f32)
    lanes = values.shape[1]
    inner = wide(place, lanes)
    left = jnp.where(inner == 0, 0.0, pltpu.roll(values, 1, 0)).astype(bf16)
    right = jnp.where(inner == SIDE - 1, 0.0, pltpu.roll(values, SIDE - 1, 0)).astype(bf16)
    for tap in range(TAPS):
        up, side = tap // 3, tap % 3
        source = (left, low, right)[side]
        here = pl.ds(pl.multiple_of((row + 2 - up) * SIDE, SIDE), SIDE)
        for group in range(lanes // 128):
            at = (group * TAPS + tap) * 128
            patch_ref[image, here, at : at + 128] = source[:, group * 128 : (group + 1) * 128]


def second_kernel(
    sides,
    odd,
    first_ref,
    recv_ref,
    param_ref,
    mine_ref,
    other_ref,
    _,
    act_ref,
    second_ref,
    terms_ref,
    count_ref,
    w_ref,
    send_ref,
    patch_ref,
    acc_ref,
    tile_ref,
):
    step = pl.program_id(0)
    zeros_at_start(acc_ref, patch_ref)
    place = places()
    lanes = first_ref.shape[1]
    columns = TAPS * lanes // RADIX

    @at_start
    def _():
        fill_half(w_ref, mine_ref, other_ref, odd)
        take(recv_ref, tile_ref)
        count = tile_ref[2 * lanes // 128 : 2 * lanes // 128 + 1, :]
        count_ref[...] = jnp.broadcast_to(count, count_ref.shape)
        center, _, inv, scale, offset = norm_rows(
            row_at(tile_ref, 0, lanes),
            row_at(tile_ref, lanes // 128, lanes),
            wide(count, lanes),
            param_ref[0:1, :],
            param_ref[1:2, :],
        )
        terms_ref[0:1, :] = scale
        terms_ref[1:2, :] = offset
        terms_ref[2:3, :] = inv
        terms_ref[3:4, :] = -center * inv
        terms_ref[4:5, :] = center

    for image in range(STEP):
        limit = 2 * sides[step * STEP + image]

        def body(row, carry):
            here = chunk(image, row)
            pre = first_ref[here, :] * terms_ref[0:1, :] + terms_ref[1:2, :]
            act = pre * (sigmoid(pre) * wide(row_mask(place, row, limit), lanes))
            low = act.astype(bf16)
            act_ref[here, :] = low
            write_patches(patch_ref, image, row, low, place)
            return carry

        rows_of(0, body)
    for image in range(STEP):
        for group in range(RADIX):
            second_ref[image * 256 : image * 256 + 256, group * lanes : (group + 1) * lanes] = (
                contract_last(
                    patch_ref[image, SIDE : SIDE + 256, group * columns : (group + 1) * columns],
                    w_ref[:, group * columns : (group + 1) * columns],
                )
            )
    for image in range(STEP):
        limit = 2 * sides[step * STEP + image]

        def body(row, carry):
            total, square = carry
            values = second_ref[chunk(image, row), :]
            values = values * wide(row_mask(place, row, limit), values.shape[1])
            return (total + fold(values), square + fold(values * values))

        total, square = rows_of((acc_ref[0], acc_ref[1]), body)
        acc_ref[0] = total
        acc_ref[1] = square

    @at_end
    def _():
        tile_ref[...] = jnp.zeros(tile_ref.shape, f32)
        put(tile_ref, 0, column_total(acc_ref[0]))
        put(tile_ref, RADIX * lanes // 128, column_total(acc_ref[1]))
        send(send_ref, tile_ref)


def pool_kernel(
    sides,
    second_ref,
    recv_ref,
    param_ref,
    count_ref,
    down_ref,
    power_ref,
    _,
    pooled_ref,
    squeeze_ref,
    terms_ref,
    send_ref,
    pool_ref,
    tile_ref,
):
    step = pl.program_id(0)
    place = places()
    lanes = second_ref.shape[1]

    @at_start
    def _():
        take(recv_ref, tile_ref)
        _, _, _, scale, offset = norm_rows(
            row_at(tile_ref, 0, lanes),
            row_at(tile_ref, lanes // 128, lanes),
            wide(count_ref[0:1, :], lanes),
            param_ref[0:1, :],
            param_ref[1:2, :],
        )
        terms_ref[0:1, :] = scale
        terms_ref[1:2, :] = offset

    for image in range(STEP):
        limit = 2 * sides[step * STEP + image]

        def body(row, total):
            pre = second_ref[chunk(image, row), :] * terms_ref[0:1, :] + terms_ref[1:2, :]
            act = pre * (sigmoid(pre) * wide(row_mask(place, row, limit), lanes))
            return total + fold(act)

        total = column_total(rows_of(jnp.zeros((8, lanes), f32), body))
        both = total[:, : lanes // 2] + total[:, lanes // 2 :]
        area = jnp.full(both.shape, limit * limit, jnp.int32).astype(f32)
        pool_ref[pl.ds(step * STEP + image, 1), :] = both / area

    @at_end
    def _():
        low = pool_ref[...].astype(bf16)
        pooled_ref[...] = low
        squeeze = jnp.dot(low, down_ref[...], preferred_element_type=f32)
        squeeze_ref[...] = squeeze
        tile_ref[...] = jnp.zeros(tile_ref.shape, f32)
        tile_ref[0:1, :] = column_total(squeeze)
        tile_ref[1:2, :] = column_total(squeeze * squeeze)
        tile_ref[2:3, :] = column_total(power_ref[...])
        send(send_ref, tile_ref)


def mix_kernel(
    images_all,
    sides,
    second_ref,
    ab_ref,
    squeeze_ref,
    recv_ref,
    param_ref,
    up_ref,
    bias_ref,
    out_ref,
    mixed_ref,
    weights_ref,
    excite_ref,
    gate_ref,
    gw_ref,
    colsum_ref,
    power_ref,
    send_ref,
    gram_ref,
    acc_ref,
    tile_ref,
):
    step = pl.program_id(0)
    zeros_at_start(acc_ref, gram_ref)
    place = places()
    lanes = second_ref.shape[1]
    half = lanes // 2

    @at_start
    def _():
        tile_ref[0:8, :] = recv_ref[0]
        for j in range(1, recv_ref.shape[0]):
            tile_ref[0:8, :] += recv_ref[j]
        center, _, inv, scale, offset = norm_rows(
            tile_ref[0:1, :],
            tile_ref[1:2, :],
            jnp.float32(images_all),
            param_ref[0:1, :],
            param_ref[1:2, :],
        )
        gate_ref[0:1, :] = scale
        gate_ref[1:2, :] = offset
        gate_ref[2:3, :] = inv
        gate_ref[3:4, :] = -center * inv
        gate_ref[4:5, :] = tile_ref[2:3, :]
        pre = squeeze_ref[...] * scale + offset
        excite = (pre * sigmoid(pre)).astype(bf16)
        excite_ref[...] = excite
        logits = contract_last(excite, up_ref[...]) + bias_ref[0:1, :]
        one, two = logits[:, :half], logits[:, half:]
        top = jnp.maximum(one, two)
        one, two = jnp.exp(one - top), jnp.exp(two - top)
        weights_ref[:, :half] = one / (one + two)
        weights_ref[:, half:] = two / (one + two)

    for image in range(STEP):
        limit = 2 * sides[step * STEP + image]
        weights = weights_ref[pl.ds(step * STEP + image, 1), :]

        def body(row, carry):
            total, square = carry
            here = chunk(image, row)
            pre = second_ref[here, :] * ab_ref[0:1, :] + ab_ref[1:2, :]
            act = pre * (sigmoid(pre) * wide(row_mask(place, row, limit), lanes))
            act = act * weights
            mixed = act[:, :half] + act[:, half:]
            low = mixed.astype(bf16)
            mixed_ref[here, :] = low
            return (total + fold(low.astype(f32)), square + fold(mixed * mixed))

        total, square = rows_of((acc_ref[0], acc_ref[1]), body)
        acc_ref[0] = total
        acc_ref[1] = square
    gram_ref[...] += contract_lead(mixed_ref[...], mixed_ref[...])

    @at_end
    def _():
        whole = out_ref[...].astype(f32)
        total = column_total(acc_ref[0])
        colsum_ref[...] = jnp.broadcast_to(total, colsum_ref.shape)
        power_ref[...] = lane_parts(acc_ref[1])
        gw = jnp.dot(gram_ref[...], whole, precision=HIGH, preferred_element_type=f32)
        gw_ref[...] = gw
        sums = jnp.dot(
            jnp.broadcast_to(total, (8, half)), whole, precision=HIGH, preferred_element_type=f32
        )
        put(tile_ref, 0, sums[0:1, :])
        put(tile_ref, whole.shape[1] // 128, column_total(gw * whole))
        send(send_ref, tile_ref)


def out_kernel(
    sides,
    mixed_ref,
    x_ref,
    cot_ref,
    recv_ref,
    param_ref,
    count_ref,
    w_ref,
    wt_ref,
    block_ref,
    slope_ref,
    back_ref,
    grad_ref,
    terms_ref,
    power_ref,
    send_ref,
    third_ref,
    acc_ref,
    square_ref,
    tile_ref,
):
    step = pl.program_id(0)
    zeros_at_start(acc_ref, square_ref, grad_ref)
    place = places()
    lanes = x_ref.shape[1]
    part = 512 if lanes % 512 == 0 else lanes

    @at_start
    def _():
        take(recv_ref, tile_ref)
        count = count_ref[0:1, :]
        gain, shift = param_ref[0:1, :], param_ref[1:2, :]
        center, spread, inv, scale, offset = norm_rows(
            row_at(tile_ref, 0, lanes),
            row_at(tile_ref, lanes // 128, lanes),
            wide(count, lanes),
            gain,
            shift,
        )
        branch = gain * gain * spread * inv * inv + shift * shift
        terms_ref[0:1, :] = scale
        terms_ref[1:2, :] = offset
        terms_ref[2:3, :] = center
        terms_ref[3:4, :] = inv
        terms_ref[4:5, :] = 1.0 / scale
        terms_ref[5:6, :] = wide(lane_sum(branch), lanes)

    third_ref[...] = jnp.dot(mixed_ref[...], w_ref[...], preferred_element_type=f32)
    for image in range(STEP):
        limit = 2 * sides[step * STEP + image]

        def body(row, square):
            here = chunk(image, row)
            mask = wide(row_mask(place, row, limit), part)
            for at in range(0, lanes, part):
                cut = slice(at, at + part)
                total = (
                    x_ref[here, cut].astype(f32)
                    + third_ref[here, cut] * terms_ref[0:1, cut]
                    + terms_ref[1:2, cut]
                )
                plain = sigmoid(total)
                gate = plain * mask
                output = total * gate
                block_ref[here, cut] = output.astype(bf16)
                slope = gate + output * (1.0 - plain)
                grad = cot_ref[here, cut].astype(f32) * (slope * terms_ref[0:1, cut])
                slope_ref[here, cut] = grad.astype(bf16)
                acc_ref[:, cut] += fold(grad)
                square = square + lane_parts(fold(output * output))
            return square

        square_ref[...] = rows_of(square_ref[...], body, 4)
    back_ref[...] = jnp.dot(slope_ref[...], wt_ref[...], preferred_element_type=f32)
    grad_ref[...] += contract_lead(mixed_ref[...], slope_ref[...])

    @at_end
    def _():
        power_ref[...] = square_ref[...]
        total = column_total(acc_ref[...])
        put(tile_ref, 0, total)
        turned = column_total(grad_ref[...] * w_ref[...].astype(f32))
        put(tile_ref, lanes // 128, turned - terms_ref[2:3, :] * total)
        send(send_ref, tile_ref)


def mid_terms(second_ref, ab_ref, here, mask):
    pre = second_ref[here, :] * ab_ref[0:1, :] + ab_ref[1:2, :]
    plain = sigmoid(pre)
    gate = plain * mask
    act = pre * gate
    return pre, act, gate + act * (1.0 - plain)


def gate_kernel(
    sides,
    second_ref,
    ab_ref,
    back_ref,
    mixed_ref,
    recv_ref,
    terms_ref,
    param_ref,
    count_ref,
    w_ref,
    wt_ref,
    weights_ref,
    excite_ref,
    squeeze_ref,
    gate_ref,
    up_ref,
    power_out_ref,
    power_mix_ref,
    dmixed_ref,
    sums_ref,
    dup_ref,
    dbias_ref,
    dq_ref,
    grads_ref,
    send_ref,
    turn_ref,
    row_ref,
    tile_ref,
):
    step = pl.program_id(0)
    place = places()
    lanes = second_ref.shape[1]
    half = lanes // 2
    width = w_ref.shape[1]

    @at_start
    def _():
        take(recv_ref, tile_ref)
        count = wide(count_ref[0:1, :], width)
        total = row_at(tile_ref, 0, width)
        scale, center, inv = terms_ref[0:1, :], terms_ref[2:3, :], terms_ref[3:4, :]
        gain_grad = row_at(tile_ref, width // 128, width) / param_ref[0:1, :]
        slant = scale * inv * gain_grad / count
        level = total / count - center * slant
        grads_ref[0:1, :] = total * terms_ref[4:5, :]
        grads_ref[1:2, :] = gain_grad
        grads_ref[2:3, :] = slant
        grads_ref[3:4, :] = level
        whole = w_ref[...].astype(f32)
        turn_ref[...] = jnp.dot(
            (whole * slant).astype(bf16), wt_ref[...], preferred_element_type=f32
        ).astype(bf16)
        row_ref[...] = jnp.dot(
            jnp.broadcast_to(level, (8, width)),
            wt_ref[...].astype(f32),
            precision=HIGH,
            preferred_element_type=f32,
        )

    dmixed_ref[...] = back_ref[...] - jnp.dot(
        mixed_ref[...], turn_ref[...], preferred_element_type=f32
    )
    for image in range(STEP):
        limit = 2 * sides[step * STEP + image]

        def body(row, carry):
            here = chunk(image, row)
            mask = row_mask(place, row, limit)
            dmixed = (dmixed_ref[here, :] - row_ref[0:1, :]) * wide(mask, half)
            dmixed_ref[here, :] = dmixed
            both = jnp.concatenate([dmixed, dmixed], axis=1)
            pre, act, slope = mid_terms(second_ref, ab_ref, here, wide(mask, lanes))
            along = slope * both
            terms = (act * both, along, along * pre, slope, slope * pre)
            return tuple(old + fold(new) for old, new in zip(carry, terms))

        start = tuple(jnp.zeros((8, lanes), f32) for _ in range(5))
        totals = rows_of(start, body, 4)
        for index in range(5):
            sums_ref[index, pl.ds(step * STEP + image, 1), :] = column_total(totals[index])

    @at_end
    def _():
        weights = weights_ref[...]
        grads = sums_ref[0]
        mean = weights * grads
        mean = mean[:, :half] + mean[:, half:]
        dlogits = weights * (grads - jnp.concatenate([mean, mean], axis=1))
        dbias_ref[...] = jnp.broadcast_to(column_total(dlogits), dbias_ref.shape)
        low = dlogits.astype(bf16)
        dup_ref[...] = contract_lead(low, excite_ref[...])
        dexcite = jnp.dot(low, up_ref[...], preferred_element_type=f32)
        squeeze = squeeze_ref[...]
        pre = squeeze * gate_ref[0:1, :] + gate_ref[1:2, :]
        normed = squeeze * gate_ref[2:3, :] + gate_ref[3:4, :]
        plain = sigmoid(pre)
        dq = dexcite * (plain * (1.0 + pre * (1.0 - plain)))
        dq_ref[...] = dq
        tile_ref[0:1, :] = column_total(dq)
        tile_ref[1:2, :] = column_total(dq * normed)
        tile_ref[2:3, :] = column_total(power_out_ref[...])
        tile_ref[3:4, :] = column_total(power_mix_ref[...])
        tile_ref[4:8, :] = jnp.zeros((4, 128), f32)
        tile = tile_ref[0:8, :]
        for j in range(send_ref.shape[0]):
            send_ref[j] = tile


def squeeze_kernel(
    images_all,
    width,
    sides,
    dq_ref,
    squeeze_ref,
    gate_ref,
    recv_ref,
    pooled_ref,
    down_ref,
    weights_ref,
    sums_ref,
    param_ref,
    count_ref,
    terms_ref,
    ddown_ref,
    dpool_ref,
    grads_ref,
    send_ref,
    tile_ref,
    area_ref,
):
    take(recv_ref, tile_ref)
    shift, gain = tile_ref[0:1, :], tile_ref[1:2, :]
    grads_ref[0:1, :] = shift
    grads_ref[1:2, :] = gain
    bottleneck = pooled_ref.shape[1]
    count = count_ref[0:1, :]
    powers = (
        lane_sum(gate_ref[4:5, :]) / (count * width),
        lane_sum(tile_ref[3:4, :]) / (count * bottleneck),
        terms_ref[5:6, :128] / width,
        lane_sum(tile_ref[2:3, :]) / (count * width),
    )
    place = lax.broadcasted_iota(jnp.int32, (1, 128), 1)
    norms = powers[3]
    for index in range(3):
        norms = jnp.where(place == index, powers[index], norms)
    grads_ref[2:3, :] = jnp.sqrt(norms)
    normed = squeeze_ref[...] * gate_ref[2:3, :] + gate_ref[3:4, :]
    dsqueeze = gate_ref[0:1, :] * (
        dq_ref[...] - (shift + normed * gain) / jnp.float32(images_all)
    )
    low = dsqueeze.astype(bf16)
    ddown_ref[...] = contract_lead(pooled_ref[...], low)
    for image in range(area_ref.shape[0]):
        area = 4 * sides[image] * sides[image]
        area_ref[image : image + 1, :] = jnp.full((1, bottleneck), area, jnp.int32).astype(f32)
    dpool = contract_last(low, down_ref[...]) / area_ref[...]
    dpool_ref[...] = dpool
    both = jnp.concatenate([dpool, dpool], axis=1)
    weights = weights_ref[...]
    total = column_total(weights * sums_ref[1] + both * sums_ref[3])
    product = column_total(weights * sums_ref[2] + both * sums_ref[4])
    lanes = weights.shape[1]
    put(tile_ref, 0, total)
    put(tile_ref, lanes // 128, (product - param_ref[1:2, :] * total) / param_ref[0:1, :])
    send(send_ref, tile_ref)


def conv_back_kernel(
    sides,
    second_ref,
    ab_ref,
    recv_ref,
    param_ref,
    count_ref,
    dmixed_ref,
    weights_ref,
    dpool_ref,
    first_ref,
    ab_in_ref,
    w_ref,
    dsecond_ref,
    dfirst_ref,
    grads_ref,
    stat_ref,
    column_ref,
    acc_ref,
    tile_ref,
):
    step = pl.program_id(0)
    zeros_at_start(acc_ref, column_ref)
    place = places()
    lanes = second_ref.shape[1]
    half = lanes // 2
    quarter = half // RADIX
    columns = TAPS * quarter

    @at_start
    def _():
        take(recv_ref, tile_ref)
        total = row_at(tile_ref, 0, lanes)
        product = row_at(tile_ref, lanes // 128, lanes)
        count = wide(count_ref[0:1, :], lanes)
        slant = ab_ref[0:1, :] * product / (count * param_ref[0:1, :])
        grads_ref[0:1, :] = total
        grads_ref[1:2, :] = product
        grads_ref[2:3, :] = slant
        grads_ref[3:4, :] = ab_ref[0:1, :] * total / count - param_ref[1:2, :] * slant

    for image in range(STEP):
        limit = 2 * sides[step * STEP + image]
        weights = weights_ref[pl.ds(step * STEP + image, 1), :] * ab_ref[0:1, :]
        dpool = dpool_ref[pl.ds(step * STEP + image, 1), :]
        dpool = jnp.concatenate([dpool, dpool], axis=1) * ab_ref[0:1, :]

        def body(row, carry):
            here = chunk(image, row)
            mask = wide(row_mask(place, row, limit), lanes)
            dmixed = dmixed_ref[here, :]
            both = jnp.concatenate([dmixed, dmixed], axis=1)
            pre = second_ref[here, :] * ab_ref[0:1, :] + ab_ref[1:2, :]
            plain = sigmoid(pre)
            slope = plain + pre * plain * (1.0 - plain)
            grad = slope * (weights * both + dpool)
            grad = mask * (grad - (pre * grads_ref[2:3, :] + grads_ref[3:4, :]))
            dsecond_ref[here, :] = grad.astype(bf16)
            return carry

        rows_of(0, body)
    for image in range(STEP):
        for group in range(RADIX):
            column_ref[image, SIDE : SIDE + 256, group * columns : (group + 1) * columns] = jnp.dot(
                dsecond_ref[image * 256 : image * 256 + 256, group * half : (group + 1) * half],
                w_ref[:, group * columns : (group + 1) * columns],
                preferred_element_type=f32,
            )
    for image in range(STEP):
        limit = 2 * sides[step * STEP + image]

        def body(row, carry):
            total, product = carry
            here = chunk(image, row)
            mask = row_mask(place, row, limit)
            parts = []
            for group in range(RADIX):
                sides_sum = []
                for side in range(3):
                    summed = None
                    for up in range(3):
                        at = group * columns + (up * 3 + side) * quarter
                        rows = pl.ds(pl.multiple_of((row + 2 - up) * SIDE, SIDE), SIDE)
                        piece = column_ref[image, rows, at : at + quarter]
                        summed = piece if summed is None else summed + piece
                    sides_sum.append(summed)
                inner = wide(place, quarter)
                low = jnp.where(inner == SIDE - 1, 0.0, pltpu.roll(sides_sum[0], SIDE - 1, 0))
                high = jnp.where(inner == 0, 0.0, pltpu.roll(sides_sum[2], 1, 0))
                parts.append(sides_sum[1] + low + high)
            dact = jnp.concatenate(parts, axis=1)
            first = first_ref[here, :]
            pre = first * ab_in_ref[0:1, :] + ab_in_ref[1:2, :]
            normed = first * ab_in_ref[2:3, :] + ab_in_ref[3:4, :]
            plain = sigmoid(pre)
            grad = dact * (plain * (1.0 + pre * (1.0 - plain)) * wide(mask, half))
            dfirst_ref[here, :] = grad
            return (total + fold(grad), product + fold(grad * normed))

        total, product = rows_of((acc_ref[0], acc_ref[1]), body, 4)
        acc_ref[0] = total
        acc_ref[1] = product

    @at_end
    def _():
        stat_ref[...] = jnp.zeros(stat_ref.shape, f32)
        put(stat_ref, 0, column_total(acc_ref[0]))
        put(stat_ref, half // 128, column_total(acc_ref[1]))


def conv_grad_kernel(act_ref, dsecond_ref, x_ref, dfirst_ref, part_ref, in_ref, conv_ref, patch_ref):
    zeros_at_start(conv_ref, in_ref, patch_ref)
    place = places()
    lanes = act_ref.shape[1]
    columns = TAPS * lanes // RADIX
    for image in range(STEP):

        def body(row, carry):
            write_patches(patch_ref, image, row, act_ref[chunk(image, row), :], place)
            return carry

        rows_of(0, body)
    for image in range(STEP):
        for group in range(RADIX):
            conv_ref[:, group * columns : (group + 1) * columns] += contract_lead(
                dsecond_ref[image * 256 : image * 256 + 256, group * lanes : (group + 1) * lanes],
                patch_ref[image, SIDE : SIDE + 256, group * columns : (group + 1) * columns],
            )
    in_ref[...] += contract_lead(dfirst_ref[...].astype(bf16), x_ref[...])

    @at_end
    def _():
        rows = conv_ref.shape[0] // part_ref.shape[0]
        if rows % 8:
            for tap in range(RADIX * TAPS):
                tile = conv_ref[:, tap * 128 : (tap + 1) * 128]
                part_ref[:, tap * rows : (tap + 1) * rows, :] = tile.reshape(-1, rows, 128)
            return
        for piece in range(part_ref.shape[0]):
            for tap in range(RADIX * TAPS):
                part_ref[piece, tap * rows : (tap + 1) * rows, :] = conv_ref[
                    piece * rows : (piece + 1) * rows, tap * 128 : (tap + 1) * 128
                ]


def in_kernel(recv_ref, terms_ref, count_ref, grads_ref, tile_ref):
    take(recv_ref, tile_ref)
    lanes = terms_ref.shape[1]
    total = row_at(tile_ref, 0, lanes)
    product = row_at(tile_ref, lanes // 128, lanes)
    count = wide(count_ref[0:1, :], lanes)
    slant = terms_ref[0:1, :] * terms_ref[2:3, :] * product / count
    grads_ref[0:1, :] = total
    grads_ref[1:2, :] = product
    grads_ref[2:3, :] = slant
    grads_ref[3:4, :] = terms_ref[0:1, :] * total / count - terms_ref[4:5, :] * slant
    grads_ref[4:5, :] = terms_ref[0:1, :]


def last_kernel(
    sides, dfirst_ref, first_ref, grads_ref, w_ref, slope_ref, terms_ref, out_ref, done_ref, low_ref
):
    step = pl.program_id(0)
    place = places()
    lanes = first_ref.shape[1]
    width = out_ref.shape[1]
    part = 512 if width % 512 == 0 else width
    for image in range(STEP):
        limit = 2 * sides[step * STEP + image]

        def body(row, carry):
            here = chunk(image, row)
            mask = wide(row_mask(place, row, limit), lanes)
            grad = dfirst_ref[here, :] * grads_ref[4:5, :]
            grad = grad - mask * (first_ref[here, :] * grads_ref[2:3, :] + grads_ref[3:4, :])
            low_ref[here, :] = grad.astype(bf16)
            return carry

        rows_of(0, body)
    out_ref[...] = contract_last(low_ref[...], w_ref[...])
    for image in range(STEP):

        def body(row, carry):
            here = chunk(image, row)
            for at in range(0, width, part):
                cut = slice(at, at + part)
                out_ref[here, cut] += slope_ref[here, cut].astype(f32) * terms_ref[4:5, cut]
            return carry

        rows_of(0, body)

    @at_end
    def _():
        done_ref[...] = jnp.zeros(done_ref.shape, f32)


def total_of(ref):
    total = ref[0].astype(f32)
    for j in range(1, ref.shape[0]):
        total = total + ref[j].astype(f32)
    return total.astype(bf16)


def total_kernel(part_ref, tile_ref, sum_ref, send_ref):
    sum_ref[...] = total_of(part_ref)
    send(send_ref, tile_ref)


def spread_kernel(one_ref, part_ref, _, send_ref):
    cut = one_ref.shape[0]
    one = one_ref[...]
    total = total_of(part_ref)
    for j in range(send_ref.shape[0]):
        send_ref[j, :cut, :] = one
        send_ref[j, cut:, :] = total


def tiles(lanes, block=0):
    return pl.BlockSpec((STEP * 256, lanes), lambda i: (i, block))


def held(*shape):
    return pl.BlockSpec(shape, lambda i: (0,) * len(shape))


def token():
    return pl.BlockSpec(memory_space=pl.ANY)


def scalars():
    return pl.BlockSpec(memory_space=pltpu.SMEM)


def shaped(shape, dtype=f32):
    return jax.ShapeDtypeStruct(shape, dtype)


def call(kernel, steps, ins, outs, scratch=(), cost=5, limit=56, name=None):
    return pl.pallas_call(
        kernel,
        grid=(steps,),
        in_specs=ins,
        out_specs=[spec for spec, _ in outs],
        out_shape=[shape for _, shape in outs],
        scratch_shapes=[pltpu.VMEM(shape, dtype) for shape, dtype in scratch],
        compiler_params=pltpu.CompilerParams(
            dimension_semantics=("arbitrary",), vmem_limit_bytes=limit * 1024 * 1024
        ),
        cost_estimate=pl.CostEstimate(
            flops=int(cost * 1e9), bytes_accessed=int(cost * 3e6), transcendentals=0
        ),
        name=name,
    )


def whole_out(shape, dtype=f32):
    return held(*shape), shaped(shape, dtype)


def rows8(*vectors):
    stacked = jnp.stack(vectors, axis=0)
    return jnp.pad(stacked, ((0, 8 - len(vectors)), (0, 0)))


def local(
    features,
    half_sides,
    cotangent,
    conv_in,
    conv_mid,
    attn_down,
    attn_up,
    attn_bias,
    conv_out,
    gain_in,
    shift_in,
    gain_mid,
    shift_mid,
    gain_attn,
    shift_attn,
    gain_out,
    shift_out,
):
    images, pixels, width = features.shape
    rows = images * pixels
    steps = images // STEP
    pieces = lax.axis_size("fsdp")
    groups = lax.axis_size("dp")
    devices = pieces * groups
    images_all = images * devices
    bottleneck = conv_in.shape[1]
    att = attn_down.shape[1]
    mid = RADIX * bottleneck
    columns = TAPS * conv_mid.shape[2]
    odd = lax.rem(lax.axis_index("dp"), 2).reshape(1)

    in_mine = gather_all(half_of(conv_in, 1)).reshape(width, bottleneck // 2)
    in_other = neighbour(in_mine)
    down_rows, up_rows = attn_down.shape[0], attn_up.shape[1]
    own_columns = conv_mid.shape[3]
    small = [gain_in, shift_in, gain_mid, shift_mid, gain_attn, shift_attn, gain_out, shift_out, attn_bias]
    lengths = [item.shape[0] for item in small]
    vectors = jnp.stack([jnp.pad(item, (0, 128 - item.shape[0])) for item in small])
    vectors = jnp.pad(vectors, ((0, 16 - len(small)), (0, 0)))
    mid_cut = half_of(conv_mid, 0)[0].transpose(0, 2, 1).reshape(TAPS * own_columns, 128)
    packed = gather_all(jnp.concatenate([mid_cut, attn_down, attn_up.T, vectors], axis=0))
    at = TAPS * own_columns
    mid_mine = packed[:, :at].reshape(pieces, TAPS, own_columns, 128).transpose(0, 2, 1, 3)
    mid_mine = mid_mine.reshape(bottleneck, columns)
    mid_other = neighbour(mid_mine)
    whole_down = packed[:, at : at + down_rows].reshape(bottleneck, att)
    at += down_rows
    whole_up = packed[:, at : at + up_rows].reshape(mid, att)
    at += up_rows
    found = [
        packed[:, at + k, :length].reshape(-1).astype(f32) for k, length in enumerate(lengths)
    ]
    p_in, p_mid, p_attn, p_out = [rows8(found[2 * k], found[2 * k + 1]) for k in range(4)]
    p_bias = rows8(found[8])

    x = features.reshape(rows, width)
    cot = cotangent.reshape(rows, width)

    def tiled(lanes, dtype=f32):
        return tiles(lanes), shaped((rows, lanes), dtype)

    def sending(count, dtype=f32):
        return whole_out((devices, count, 128), dtype)

    def received(count):
        return held(devices, count, 128)

    first, whole_in, out = call(
        first_kernel,
        steps,
        [scalars(), scalars(), tiles(width), held(width, bottleneck // 2), held(width, bottleneck // 2)],
        [tiled(bottleneck), whole_out((width, bottleneck), bf16), sending(8)],
        [((2, 8, bottleneck), f32), ((8, 128), f32)],
        8,
        name="first",
    )(half_sides, odd, x, in_mine, in_other)
    got = swap_all(out, AXES)
    out_half = half_of(conv_out, 0).T
    cross, x_sum, power_x, out_copies = call(
        cross_kernel,
        steps,
        [scalars(), tiles(width), tiles(bottleneck), held(*out_half.shape)],
        [
            whole_out((bottleneck, width)),
            whole_out((8, width)),
            whole_out((8, 128)),
            whole_out((pieces,) + out_half.shape, bf16),
        ],
        [((8, width), f32)],
        10,
        name="cross",
    )(half_sides, x, first, out_half)
    out_mine = swap_all(out_copies, "fsdp").reshape(width, bottleneck // 2)
    out_other = neighbour(out_mine)
    whole_out_t = jnp.where(
        odd[0] == 0,
        jnp.concatenate([out_mine, out_other], axis=1),
        jnp.concatenate([out_other, out_mine], axis=1),
    )
    whole_w_out = whole_out_t.T

    act_low, second, terms_in, count, whole_mid, out = call(
        second_kernel,
        steps,
        [
            scalars(),
            scalars(),
            tiles(bottleneck),
            received(8),
            held(8, bottleneck),
            held(bottleneck, columns),
            held(bottleneck, columns),
            token(),
        ],
        [
            tiled(bottleneck, bf16),
            tiled(mid),
            whole_out((8, bottleneck)),
            whole_out((8, 128)),
            whole_out((bottleneck, RADIX * columns), bf16),
            sending(8),
        ],
        [
            ((STEP, 256 + 2 * SIDE, RADIX * columns), bf16),
            ((2, 8, mid), f32),
            ((8, 128), f32),
        ],
        15,
        name="second",
    )(half_sides, odd, first, got, p_in, mid_mine, mid_other, power_x)
    got = swap_all(out, AXES)

    pooled, squeeze, terms_mid, out = call(
        pool_kernel,
        steps,
        [
            scalars(),
            tiles(mid),
            received(8),
            held(8, mid),
            held(8, 128),
            held(bottleneck, att),
            held(8, 128),
            token(),
        ],
        [
            whole_out((images, bottleneck), bf16),
            whole_out((images, att)),
            whole_out((8, mid)),
            sending(8),
        ],
        [((images, bottleneck), f32), ((8, 128), f32)],
        7,
        name="pool",
    )(half_sides, second, got, p_mid, count, whole_down, power_x, out_other)
    got = swap_all(out, AXES)

    wide_rows = 2 * width // 128
    mixed, weights, excite, gate, gram_out, colsum, power_mix, out = call(
        functools.partial(mix_kernel, images_all),
        steps,
        [
            scalars(),
            tiles(mid),
            held(8, mid),
            held(images, att),
            received(8),
            held(8, att),
            held(mid, att),
            held(8, mid),
            held(bottleneck, width),
        ],
        [
            tiled(bottleneck, bf16),
            whole_out((images, mid)),
            whole_out((images, att), bf16),
            whole_out((8, att)),
            whole_out((bottleneck, width)),
            whole_out((8, bottleneck)),
            whole_out((8, 128)),
            sending(wide_rows),
        ],
        [((bottleneck, bottleneck), f32), ((2, 8, bottleneck), f32), ((wide_rows, 128), f32)],
        11,
        name="mix",
    )(half_sides, second, terms_mid, squeeze, got, p_attn, whole_up, p_bias, whole_w_out)
    got = swap_all(out, AXES)

    block, slope, back, grad_out, terms_out, power_out, out = call(
        out_kernel,
        steps,
        [
            scalars(),
            tiles(bottleneck),
            tiles(width),
            tiles(width),
            received(wide_rows),
            held(8, width),
            held(8, 128),
            held(bottleneck, width),
            held(width, bottleneck),
        ],
        [
            tiled(width, bf16),
            tiled(width, bf16),
            tiled(bottleneck),
            whole_out((bottleneck, width)),
            whole_out((8, width)),
            whole_out((8, 128)),
            sending(wide_rows, bf16),
        ],
        [
            ((STEP * 256, width), f32),
            ((8, width), f32),
            ((8, 128), f32),
            ((wide_rows, 128), f32),
        ],
        25,
        name="output",
    )(half_sides, mixed, x, cot, got, p_out, count, whole_w_out, whole_out_t)
    got = swap_all(out, AXES)

    dmixed, sums, dup, dbias, dq, grads_out, out = call(
        gate_kernel,
        steps,
        [
            scalars(),
            tiles(mid),
            held(8, mid),
            tiles(bottleneck),
            tiles(bottleneck),
            received(wide_rows),
            held(8, width),
            held(8, width),
            held(8, 128),
            held(bottleneck, width),
            held(width, bottleneck),
            held(images, mid),
            held(images, att),
            held(images, att),
            held(8, att),
            held(mid, att),
            held(8, 128),
            held(8, 128),
        ],
        [
            tiled(bottleneck),
            whole_out((5, images, mid)),
            whole_out((mid, att)),
            whole_out((8, mid)),
            whole_out((images, att)),
            whole_out((8, width)),
            sending(8),
        ],
        [
            ((bottleneck, bottleneck), bf16),
            ((8, bottleneck), f32),
            ((wide_rows, 128), f32),
        ],
        13,
        name="gate",
    )(
        half_sides,
        second,
        terms_mid,
        back,
        mixed,
        got,
        terms_out,
        p_out,
        count,
        whole_w_out,
        whole_out_t,
        weights,
        excite,
        squeeze,
        gate,
        whole_up,
        power_out,
        power_mix,
    )
    got = swap_all(out, AXES)
    grad_conv_out = grad_out - colsum[0][:, None] * grads_out[3] - gram_out * grads_out[2]

    ddown, dpool, grads_attn, out = call(
        functools.partial(squeeze_kernel, images_all, width),
        1,
        [
            scalars(),
            held(images, att),
            held(images, att),
            held(8, att),
            received(8),
            held(images, bottleneck),
            held(bottleneck, att),
            held(images, mid),
            held(5, images, mid),
            held(8, mid),
            held(8, 128),
            held(8, width),
        ],
        [
            whole_out((bottleneck, att)),
            whole_out((images, bottleneck)),
            whole_out((8, att)),
            sending(8),
        ],
        [((8, 128), f32), ((images, bottleneck), f32)],
        1,
        name="squeeze",
    )(
        half_sides,
        dq,
        squeeze,
        gate,
        got,
        pooled,
        whole_down,
        weights,
        sums,
        p_mid,
        count,
        terms_out,
    )
    got = swap_all(out, AXES)

    out_cut = grad_conv_out.astype(bf16).reshape(bottleneck, pieces, -1).transpose(1, 0, 2)
    out_cut = out_cut.reshape(devices, -1, 128)
    bias_rows = jnp.pad(dbias[0].reshape(pieces, 1, up_rows), ((0, 0), (0, 0), (0, att - up_rows)))
    gates = jnp.concatenate(
        [
            dup.reshape(devices, -1, att),
            ddown.reshape(devices, -1, att),
            jnp.repeat(bias_rows, groups, axis=0),
        ],
        axis=1,
    ).astype(bf16)
    marks = [out_cut.shape[1], up_rows // groups, down_rows // groups]
    gates = jnp.concatenate([out_cut, gates], axis=1)
    gates = jnp.pad(gates, ((0, 0), (0, -gates.shape[1] % 16), (0, 0)))

    gates = swap_all(gates, AXES)
    dsecond, dfirst, grads_mid, stat = call(
        conv_back_kernel,
        steps,
        [
            scalars(),
            tiles(mid),
            held(8, mid),
            received(8),
            held(8, mid),
            held(8, 128),
            tiles(bottleneck),
            held(images, mid),
            held(images, bottleneck),
            tiles(bottleneck),
            held(8, bottleneck),
            held(bottleneck, RADIX * columns),
        ],
        [tiled(mid, bf16), tiled(bottleneck), whole_out((8, mid)), whole_out((8, 128))],
        [
            ((STEP, 256 + 2 * SIDE, RADIX * columns), f32),
            ((2, 8, bottleneck), f32),
            ((8, 128), f32),
        ],
        20,
        name="conv_back",
    )(
        half_sides,
        second,
        terms_mid,
        got,
        p_mid,
        count,
        dmixed,
        weights,
        dpool,
        first,
        terms_in,
        whole_mid,
    )
    gates, out = call(
        total_kernel,
        1,
        [held(*gates.shape), held(8, 128)],
        [whole_out(gates.shape[1:], bf16), sending(8)],
        (),
        2,
        name="last_gates",
    )(gates, stat)
    got = swap_all(out, AXES)

    conv_parts, in_grad = call(
        conv_grad_kernel,
        steps,
        [tiles(bottleneck), tiles(mid), tiles(width), tiles(bottleneck)],
        [
            whole_out((devices, bottleneck // devices * RADIX * TAPS, 128)),
            whole_out((bottleneck, width)),
        ],
        [
            ((bottleneck, RADIX * columns), f32),
            ((STEP, 256 + 2 * SIDE, RADIX * columns), bf16),
        ],
        15,
        name="conv_grad",
    )(act_low, dsecond, x, dfirst)
    (grads_in,) = call(
        in_kernel,
        1,
        [received(8), held(8, bottleneck), held(8, 128)],
        [whole_out((8, bottleneck))],
        [((8, 128), f32)],
        1,
        name="last_terms",
    )(got, terms_in, count)
    grad_features, done = call(
        last_kernel,
        steps,
        [
            scalars(),
            tiles(bottleneck),
            tiles(bottleneck),
            held(8, bottleneck),
            held(width, bottleneck),
            tiles(width),
            held(8, width),
        ],
        [tiled(width), whole_out((8, 128))],
        [((STEP * 256, bottleneck), bf16)],
        15,
        name="last",
    )(half_sides, dfirst, first, grads_in, whole_in, slope, terms_out)

    grad_conv_in = (
        in_grad * grads_in[4][:, None]
        - cross * grads_in[2][:, None]
        - column_total(x_sum) * grads_in[3][:, None]
    )
    in_cut = grad_conv_in.astype(bf16).reshape(bottleneck, pieces, -1).transpose(1, 0, 2)
    in_cut = in_cut.reshape(devices, -1, 128)
    mid_rows = bottleneck // devices
    marks += [in_cut.shape[1], conv_parts.shape[1]]
    late = jnp.concatenate([in_cut, conv_parts.astype(bf16)], axis=1)
    late = jnp.pad(late, ((0, 0), (0, -late.shape[1] % 16), (0, 0)))
    late = late.reshape(devices // 2, 2, -1, 128)
    mine = lax.dynamic_index_in_dim(late, odd[0], 1, False)
    other = lax.dynamic_index_in_dim(late, 1 - odd[0], 1, False)
    late = (mine.astype(f32) + neighbour(other).astype(f32)).astype(bf16)
    sides_of = [[2 * i + side for i in range(devices // 2)] for side in range(2)]
    late = lax.all_to_all(late, AXES, 0, 0, axis_index_groups=sides_of)
    (summed,) = call(
        spread_kernel,
        1,
        [held(*gates.shape), held(*late.shape), token()],
        [whole_out((groups, gates.shape[0] + late.shape[1], 128), bf16)],
        (),
        2,
        name="last_total",
    )(gates, late, done)
    summed = swap_all(summed, "dp").astype(f32)
    shard_out = summed[:, : marks[0]].reshape(bottleneck, -1)
    at = marks[0]
    shard_up = summed[:, at : at + marks[1]].reshape(up_rows, att).T
    at += marks[1]
    shard_down = summed[:, at : at + marks[2]].reshape(down_rows, att)
    at += marks[2]
    shard_bias = summed[0, at, :up_rows]
    at = gates.shape[0]
    shard_in = summed[:, at : at + marks[3]].reshape(bottleneck, -1).T
    at += marks[3]
    shard_mid = summed[:, at : at + marks[4]].reshape(groups, RADIX, TAPS, mid_rows, 128)
    shard_mid = shard_mid.transpose(1, 2, 4, 0, 3).reshape(RADIX, TAPS, 128, own_columns)

    def own_part(row):
        length = row.shape[0] // pieces
        return lax.dynamic_slice_in_dim(row, lax.axis_index("fsdp") * length, length, 0)

    return (
        block.reshape(images, pixels, width),
        grad_features.reshape(images, pixels, width),
        grads_attn[2, :4],
        shard_in,
        shard_mid,
        shard_down,
        shard_up,
        shard_bias,
        shard_out,
        own_part(grads_in[1]),
        own_part(grads_in[0]),
        own_part(grads_mid[1]),
        own_part(grads_mid[0]),
        own_part(grads_attn[1]),
        own_part(grads_attn[0]),
        own_part(grads_out[1]),
        own_part(grads_out[0]),
    )


def solution(mesh):
    return jax.shard_map(
        local,
        mesh=mesh,
        in_specs=(
            P(("fsdp", "dp"), None, None),
            P(("fsdp", "dp")),
            P(("fsdp", "dp"), None, None),
            P("fsdp", None),
            P(None, None, None, "fsdp"),
            P("fsdp", None),
            P(None, "fsdp"),
            P("fsdp"),
            P(None, "fsdp"),
            P("fsdp"),
            P("fsdp"),
            P("fsdp"),
            P("fsdp"),
            P("fsdp"),
            P("fsdp"),
            P("fsdp"),
            P("fsdp"),
        ),
        out_specs=(
            P(("fsdp", "dp"), None, None),
            P(("fsdp", "dp"), None, None),
            P(),
            P("fsdp", None),
            P(None, None, None, "fsdp"),
            P("fsdp", None),
            P(None, "fsdp"),
            P("fsdp"),
            P(None, "fsdp"),
            P("fsdp"),
            P("fsdp"),
            P("fsdp"),
            P("fsdp"),
            P("fsdp"),
            P("fsdp"),
            P("fsdp"),
            P("fsdp"),
        ),
        check_vma=False,
    )
```

```python
import functools

import jax
import jax.numpy as jnp
from jax import lax
from jax.experimental import pallas as pl
from jax.experimental.pallas import tpu as pltpu
from jax.sharding import PartitionSpec as P

RADIX = 2
SIDE = 16
TAPS = 9
STEP = 4

epsilon = 1e-05
AXES = ("fsdp", "dp")
f32 = jnp.float32
bf16 = jnp.bfloat16
HIGH = lax.Precision.HIGHEST


def swap_all(values, axes):
    return lax.all_to_all(values, axes, 0, 0)


def gather_all(shard):
    pieces = lax.axis_size("fsdp")
    return swap_all(jnp.broadcast_to(shard[None], (pieces,) + shard.shape), "fsdp")


def neighbour(values):
    return lax.ppermute(values, "dp", [(i, i ^ 1) for i in range(lax.axis_size("dp"))])


ORDER = (0, 4, 2, 6, 1, 5, 3, 7)


def partner(values, k):
    pieces = lax.axis_size("fsdp")
    return lax.ppermute(values, "fsdp", [(i, i ^ k) for i in range(pieces)])


def half_of(shard, axis):
    odd = lax.rem(lax.axis_index("dp"), 2)
    return lax.dynamic_slice_in_dim(shard, odd * (shard.shape[axis] // 2), shard.shape[axis] // 2, axis)


def sigmoid(values):
    return 0.5 * jnp.tanh(0.5 * values) + 0.5


def fold(values):
    return values[:8] + values[8:]


def wide(mask, lanes):
    return jnp.concatenate([mask] * (lanes // mask.shape[1]), axis=1)


def places():
    return lax.broadcasted_iota(jnp.int32, (SIDE, 128), 0)


def row_mask(place, row, limit):
    return jnp.where((place < limit) & (row < limit), 1.0, 0.0).astype(f32)


def chunk(image, row):
    return pl.ds(pl.multiple_of(image * 256 + row * SIDE, SIDE), SIDE)


def rows_of(carry, body, unroll=8):
    return lax.fori_loop(0, SIDE, body, carry, unroll=unroll)


def contract_lead(left, right):
    return lax.dot_general(left, right, (((0,), (0,)), ((), ())), preferred_element_type=f32)


def contract_last(left, right):
    return lax.dot_general(left, right, (((1,), (1,)), ((), ())), preferred_element_type=f32)


def zeros_at_start(*refs):
    @pl.when(pl.program_id(0) == 0)
    def _():
        for ref in refs:
            ref[...] = jnp.zeros(ref.shape, ref.dtype)


def last_step():
    return pl.program_id(0) == pl.num_programs(0) - 1


def column_total(values):
    return jnp.sum(values, axis=0, keepdims=True)


def take(recv_ref, tile_ref):
    tile_ref[...] = lax.fori_loop(
        1,
        recv_ref.shape[0],
        lambda j, total: total + recv_ref[j].astype(f32),
        recv_ref[0].astype(f32),
        unroll=True if recv_ref.shape[0] <= 32 else 1,
    )


def row_at(tile_ref, start, lanes):
    return jnp.concatenate(
        [tile_ref[start + q : start + q + 1, :] for q in range(lanes // 128)], axis=1
    )


def put(tile_ref, start, row):
    for q in range(row.shape[1] // 128):
        tile_ref[start + q : start + q + 1, :] = row[:, q * 128 : (q + 1) * 128]


def send(send_ref, tile_ref):
    tile = tile_ref[...].astype(send_ref.dtype)

    def body(j, carry):
        send_ref[j] = tile
        return carry

    lax.fori_loop(0, send_ref.shape[0], body, 0, unroll=True if send_ref.shape[0] <= 32 else 1)


def norm_rows(sums, squares, counted, gain, shift):
    center = sums / counted
    spread = squares / counted - center * center
    inv = lax.rsqrt(spread + epsilon)
    scale = gain * inv
    return center, spread, inv, scale, shift - center * scale


def fill_half(whole_ref, mine_ref, other_ref, odd_ref):
    half = whole_ref.shape[1] // 2

    @pl.when(odd_ref[0] == 0)
    def _():
        whole_ref[:, :half] = mine_ref[...]
        whole_ref[:, half:] = other_ref[...]

    @pl.when(odd_ref[0] != 0)
    def _():
        whole_ref[:, :half] = other_ref[...]
        whole_ref[:, half:] = mine_ref[...]


def at_start(body):
    pl.when(pl.program_id(0) == 0)(body)


def at_end(body):
    pl.when(pl.program_id(0) == pl.num_programs(0) - 1)(body)


def lane_parts(values):
    total = values[:, :128]
    for at in range(128, values.shape[1], 128):
        total = total + values[:, at : at + 128]
    return total


def lane_sum(row):
    return jnp.broadcast_to(jnp.sum(row, axis=1, keepdims=True), (1, 128))


def prepare_kernel(odd, in_ref, mid_ref, down_ref, up_ref, out_ref, *refs):
    *vector_refs, in_send, most_send, rows_ref = refs
    rows_ref[...] = jnp.zeros(rows_ref.shape, f32)
    for k, ref in enumerate(vector_refs):
        rows_ref[k : k + 1, : ref.shape[1]] = ref[...].astype(f32)
    at = mid_ref.shape[1] + 128
    for ref in (down_ref, up_ref):
        most_send[at : at + ref.shape[0], :] = ref[...]
        at += ref.shape[0]
    most_send[at : at + 16, :] = rows_ref[...].astype(bf16)
    for side in range(2):

        @pl.when(odd[0] == side)
        def _():
            for j in range(in_send.shape[0]):
                in_send[j] = in_ref[:, side * 128 : side * 128 + 128]
            at = mid_ref.shape[1]
            most_send[:at, :] = mid_ref[side]
            most_send[at : at + 128, :] = jnp.transpose(out_ref[side * 128 : side * 128 + 128, :])


def first_kernel(
    sides, odd, x_ref, mine_ref, other_ref, first_ref, w_ref, send_ref, acc_ref, tile_ref
):
    step = pl.program_id(0)
    zeros_at_start(acc_ref)
    at_start(lambda: fill_half(w_ref, mine_ref, other_ref, odd))
    first_ref[...] = jnp.dot(x_ref[...], w_ref[...], preferred_element_type=f32)
    place = places()
    lanes = first_ref.shape[1]
    for image in range(STEP):
        limit = 2 * sides[step * STEP + image]

        def body(row, carry):
            total, square = carry
            here = chunk(image, row)
            values = first_ref[here, :] * wide(row_mask(place, row, limit), lanes)
            first_ref[here, :] = values
            return (total + fold(values), square + fold(values * values))

        total, square = rows_of((acc_ref[0], acc_ref[1]), body)
        acc_ref[0] = total
        acc_ref[1] = square

    @at_end
    def _():
        count = jnp.int32(0)
        for image in range(sides.shape[0]):
            count = count + 4 * sides[image] * sides[image]
        tile_ref[...] = jnp.zeros(tile_ref.shape, f32)
        put(tile_ref, 0, column_total(acc_ref[0]))
        put(tile_ref, lanes // 128, column_total(acc_ref[1]))
        put(tile_ref, 2 * lanes // 128, jnp.full((1, 128), count, jnp.int32).astype(f32))
        send(send_ref, tile_ref)


def cross_kernel(
    sides, x_ref, first_ref, cross_ref, ones_ref, power_ref, square_ref
):
    step = pl.program_id(0)
    zeros_at_start(cross_ref, square_ref, ones_ref)
    cross_ref[...] += contract_lead(first_ref[...].astype(bf16), x_ref[...])
    place = places()
    lanes = x_ref.shape[1]
    for image in range(STEP):
        limit = 2 * sides[step * STEP + image]

        def body(row, carry):
            square, total = carry
            values = x_ref[chunk(image, row), :].astype(f32) * wide(
                row_mask(place, row, limit), lanes
            )
            return (square + fold(values * values), total + fold(values))

        square, total = rows_of((square_ref[...], ones_ref[...]), body)
        square_ref[...] = square
        ones_ref[...] = total

    @at_end
    def _():
        power_ref[...] = lane_parts(square_ref[...])


def write_patches(patch_ref, image, row, low, place):
    values = low.astype(f32)
    lanes = values.shape[1]
    inner = wide(place, lanes)
    left = jnp.where(inner == 0, 0.0, pltpu.roll(values, 1, 0)).astype(bf16)
    right = jnp.where(inner == SIDE - 1, 0.0, pltpu.roll(values, SIDE - 1, 0)).astype(bf16)
    for tap in range(TAPS):
        up, side = tap // 3, tap % 3
        source = (left, low, right)[side]
        here = pl.ds(pl.multiple_of((row + 2 - up) * SIDE, SIDE), SIDE)
        for group in range(lanes // 128):
            at = (group * TAPS + tap) * 128
            patch_ref[image, here, at : at + 128] = source[:, group * 128 : (group + 1) * 128]


def second_kernel(lengths, sides, first_ref, recv_ref, _, *refs):
    if lengths:
        member, odd, *refs = refs
        shard_refs, refs = refs[:4], refs[4:]
        act_ref, second_ref, terms_ref, count_ref, send_ref, w_ref, down_ref, up_ref, *refs = refs
        *param_refs, patch_ref, acc_ref, tile_ref, param_ref = refs
    else:
        w_ref, param_ref, act_ref, second_ref, terms_ref, count_ref, send_ref, *refs = refs
        patch_ref, acc_ref, tile_ref = refs
    step = pl.program_id(0)
    zeros_at_start(acc_ref, patch_ref)
    place = places()
    lanes = first_ref.shape[1]
    columns = TAPS * lanes // RADIX

    @at_start
    def _():
        if lengths:
            own = w_ref.shape[0] // len(ORDER)
            downs, ups = down_ref.shape[0] // len(ORDER), up_ref.shape[0] // len(ORDER)
            wholes = [jnp.zeros((16, length * len(ORDER)), f32) for length in lengths]
            lane = lax.broadcasted_iota(jnp.int32, (16, 128), 1)
            for index, k in enumerate(ORDER):
                piece = member[0] ^ k
                ref = shard_refs[index // 4]
                index = index % 4
                at = TAPS * own + 128
                down_ref[pl.ds(pl.multiple_of(piece * downs, downs), downs), :] = ref[
                    index, at : at + downs, :
                ]
                at += downs
                up_ref[pl.ds(pl.multiple_of(piece * ups, ups), ups), :] = ref[
                    index, at : at + ups, :
                ]
                at += ups
                rows = ref[index, at : at + 16, :].astype(f32)
                for length in sorted(set(lengths)):
                    part = jnp.where(lane < length, rows, 0.0)
                    spare = (length * len(ORDER) - 128) // 128
                    part = jnp.concatenate([part] + [jnp.zeros((16, 128), f32)] * spare, axis=1)
                    part = pltpu.roll(part, piece * length, 1)
                    wholes = [
                        whole + part if whole.shape == part.shape else whole for whole in wholes
                    ]
            for side in range(2):

                @pl.when(odd[0] == side)
                def _():
                    for index, k in enumerate(ORDER):
                        here = pl.ds(pl.multiple_of((member[0] ^ k) * own, own), own)
                        for refs, group in ((shard_refs[:2], side), (shard_refs[2:], 1 - side)):
                            for tap in range(TAPS):
                                at = (group * TAPS + tap) * 128
                                w_ref[here, at : at + 128] = refs[index // 4][
                                    index % 4, tap * own : (tap + 1) * own, :
                                ]

            for k, whole in enumerate(wholes):
                ref = ([param_ref] + param_refs)[k // 2]
                ref[k % 2 : k % 2 + 1, :] = whole[k : k + 1, :]
        take(recv_ref, tile_ref)
        count = tile_ref[2 * lanes // 128 : 2 * lanes // 128 + 1, :]
        count_ref[...] = jnp.broadcast_to(count, count_ref.shape)
        center, _, inv, scale, offset = norm_rows(
            row_at(tile_ref, 0, lanes),
            row_at(tile_ref, lanes // 128, lanes),
            wide(count, lanes),
            param_ref[0:1, :],
            param_ref[1:2, :],
        )
        terms_ref[0:1, :] = scale
        terms_ref[1:2, :] = offset
        terms_ref[2:3, :] = inv
        terms_ref[3:4, :] = -center * inv
        terms_ref[4:5, :] = center

    for image in range(STEP):
        limit = 2 * sides[step * STEP + image]

        def body(row, carry):
            here = chunk(image, row)
            pre = first_ref[here, :] * terms_ref[0:1, :] + terms_ref[1:2, :]
            act = pre * (sigmoid(pre) * wide(row_mask(place, row, limit), lanes))
            low = act.astype(bf16)
            act_ref[here, :] = low
            write_patches(patch_ref, image, row, low, place)
            return carry

        rows_of(0, body)
    for image in range(STEP):
        for group in range(RADIX):
            second_ref[image * 256 : image * 256 + 256, group * lanes : (group + 1) * lanes] = (
                contract_last(
                    patch_ref[image, SIDE : SIDE + 256, group * columns : (group + 1) * columns],
                    w_ref[:, group * columns : (group + 1) * columns],
                )
            )
    for image in range(STEP):
        limit = 2 * sides[step * STEP + image]

        def body(row, carry):
            total, square = carry
            values = second_ref[chunk(image, row), :]
            values = values * wide(row_mask(place, row, limit), values.shape[1])
            return (total + fold(values), square + fold(values * values))

        total, square = rows_of((acc_ref[0], acc_ref[1]), body)
        acc_ref[0] = total
        acc_ref[1] = square

    @at_end
    def _():
        tile_ref[...] = jnp.zeros(tile_ref.shape, f32)
        put(tile_ref, 0, column_total(acc_ref[0]))
        put(tile_ref, RADIX * lanes // 128, column_total(acc_ref[1]))
        send(send_ref, tile_ref)


def pool_kernel(
    sides,
    second_ref,
    recv_ref,
    param_ref,
    count_ref,
    down_ref,
    power_ref,
    pooled_ref,
    squeeze_ref,
    terms_ref,
    send_ref,
    pool_ref,
    tile_ref,
):
    step = pl.program_id(0)
    place = places()
    lanes = second_ref.shape[1]

    @at_start
    def _():
        take(recv_ref, tile_ref)
        _, _, _, scale, offset = norm_rows(
            row_at(tile_ref, 0, lanes),
            row_at(tile_ref, lanes // 128, lanes),
            wide(count_ref[0:1, :], lanes),
            param_ref[0:1, :],
            param_ref[1:2, :],
        )
        terms_ref[0:1, :] = scale
        terms_ref[1:2, :] = offset

    for image in range(STEP):
        limit = 2 * sides[step * STEP + image]

        def body(row, total):
            pre = second_ref[chunk(image, row), :] * terms_ref[0:1, :] + terms_ref[1:2, :]
            act = pre * (sigmoid(pre) * wide(row_mask(place, row, limit), lanes))
            return total + fold(act)

        total = column_total(rows_of(jnp.zeros((8, lanes), f32), body))
        both = total[:, : lanes // 2] + total[:, lanes // 2 :]
        area = jnp.full(both.shape, limit * limit, jnp.int32).astype(f32)
        pool_ref[pl.ds(step * STEP + image, 1), :] = both / area

    @at_end
    def _():
        low = pool_ref[...].astype(bf16)
        pooled_ref[...] = low
        squeeze = jnp.dot(low, down_ref[...], preferred_element_type=f32)
        squeeze_ref[...] = squeeze
        tile_ref[...] = jnp.zeros(tile_ref.shape, f32)
        tile_ref[0:1, :] = column_total(squeeze)
        tile_ref[1:2, :] = column_total(squeeze * squeeze)
        tile_ref[2:3, :] = column_total(power_ref[...])
        send(send_ref, tile_ref)


def out_weights_kernel(start, place, odd, _, *refs):
    *shard_refs, w_ref, wt_ref = refs
    for side in range(2):

        @pl.when(odd[0] == side)
        def _():
            for index, k in enumerate(ORDER):
                here = pl.ds(pl.multiple_of((place[0] ^ k) * 128, 128), 128)
                for refs, half in ((shard_refs[:2], side), (shard_refs[2:], 1 - side)):
                    wt_ref[here, half * 128 : half * 128 + 128] = refs[index // 4][
                        index % 4, start : start + 128, :
                    ]

    w_ref[...] = jnp.transpose(wt_ref[...])


def mix_kernel(
    images_all,
    sides,
    second_ref,
    ab_ref,
    squeeze_ref,
    recv_ref,
    param_ref,
    up_ref,
    bias_ref,
    out_ref,
    mixed_ref,
    weights_ref,
    excite_ref,
    gate_ref,
    gw_ref,
    colsum_ref,
    power_ref,
    send_ref,
    gram_ref,
    acc_ref,
    tile_ref,
):
    step = pl.program_id(0)
    zeros_at_start(acc_ref, gram_ref)
    place = places()
    lanes = second_ref.shape[1]
    half = lanes // 2

    @at_start
    def _():
        tile_ref[0:8, :] = recv_ref[0]
        for j in range(1, recv_ref.shape[0]):
            tile_ref[0:8, :] += recv_ref[j]
        center, _, inv, scale, offset = norm_rows(
            tile_ref[0:1, :],
            tile_ref[1:2, :],
            jnp.float32(images_all),
            param_ref[0:1, :],
            param_ref[1:2, :],
        )
        gate_ref[0:1, :] = scale
        gate_ref[1:2, :] = offset
        gate_ref[2:3, :] = inv
        gate_ref[3:4, :] = -center * inv
        gate_ref[4:5, :] = tile_ref[2:3, :]
        pre = squeeze_ref[...] * scale + offset
        excite = (pre * sigmoid(pre)).astype(bf16)
        excite_ref[...] = excite
        logits = contract_last(excite, up_ref[...]) + bias_ref[0:1, :]
        one, two = logits[:, :half], logits[:, half:]
        top = jnp.maximum(one, two)
        one, two = jnp.exp(one - top), jnp.exp(two - top)
        weights_ref[:, :half] = one / (one + two)
        weights_ref[:, half:] = two / (one + two)

    for image in range(STEP):
        limit = 2 * sides[step * STEP + image]
        weights = weights_ref[pl.ds(step * STEP + image, 1), :]

        def body(row, carry):
            total, square = carry
            here = chunk(image, row)
            pre = second_ref[here, :] * ab_ref[0:1, :] + ab_ref[1:2, :]
            act = pre * (sigmoid(pre) * wide(row_mask(place, row, limit), lanes))
            act = act * weights
            mixed = act[:, :half] + act[:, half:]
            low = mixed.astype(bf16)
            mixed_ref[here, :] = low
            return (total + fold(low.astype(f32)), square + fold(mixed * mixed))

        total, square = rows_of((acc_ref[0], acc_ref[1]), body)
        acc_ref[0] = total
        acc_ref[1] = square
    gram_ref[...] += contract_lead(mixed_ref[...], mixed_ref[...])

    @at_end
    def _():
        whole = out_ref[...].astype(f32)
        total = column_total(acc_ref[0])
        colsum_ref[...] = jnp.broadcast_to(total, colsum_ref.shape)
        power_ref[...] = lane_parts(acc_ref[1])
        gw = jnp.dot(gram_ref[...], whole, precision=HIGH, preferred_element_type=f32)
        gw_ref[...] = gw
        sums = jnp.dot(
            jnp.broadcast_to(total, (8, half)), whole, precision=HIGH, preferred_element_type=f32
        )
        put(tile_ref, 0, sums[0:1, :])
        put(tile_ref, whole.shape[1] // 128, column_total(gw * whole))
        send(send_ref, tile_ref)


def out_kernel(
    sides,
    mixed_ref,
    x_ref,
    cot_ref,
    recv_ref,
    param_ref,
    count_ref,
    w_ref,
    wt_ref,
    block_ref,
    slope_ref,
    back_ref,
    grad_ref,
    terms_ref,
    power_ref,
    send_ref,
    third_ref,
    acc_ref,
    square_ref,
    tile_ref,
):
    step = pl.program_id(0)
    zeros_at_start(acc_ref, square_ref, grad_ref)
    place = places()
    lanes = x_ref.shape[1]
    part = 512 if lanes % 512 == 0 else lanes

    @at_start
    def _():
        take(recv_ref, tile_ref)
        count = count_ref[0:1, :]
        gain, shift = param_ref[0:1, :], param_ref[1:2, :]
        center, spread, inv, scale, offset = norm_rows(
            row_at(tile_ref, 0, lanes),
            row_at(tile_ref, lanes // 128, lanes),
            wide(count, lanes),
            gain,
            shift,
        )
        branch = gain * gain * spread * inv * inv + shift * shift
        terms_ref[0:1, :] = scale
        terms_ref[1:2, :] = offset
        terms_ref[2:3, :] = center
        terms_ref[3:4, :] = inv
        terms_ref[4:5, :] = 1.0 / scale
        terms_ref[5:6, :] = wide(lane_sum(branch), lanes)

    third_ref[...] = jnp.dot(mixed_ref[...], w_ref[...], preferred_element_type=f32)
    for image in range(STEP):
        limit = 2 * sides[step * STEP + image]

        def body(row, square):
            here = chunk(image, row)
            mask = wide(row_mask(place, row, limit), part)
            for at in range(0, lanes, part):
                cut = slice(at, at + part)
                total = (
                    x_ref[here, cut].astype(f32)
                    + third_ref[here, cut] * terms_ref[0:1, cut]
                    + terms_ref[1:2, cut]
                )
                plain = sigmoid(total)
                gate = plain * mask
                output = total * gate
                block_ref[here, cut] = output.astype(bf16)
                slope = gate + output * (1.0 - plain)
                grad = cot_ref[here, cut].astype(f32) * (slope * terms_ref[0:1, cut])
                slope_ref[here, cut] = grad.astype(bf16)
                acc_ref[:, cut] += fold(grad)
                square = square + lane_parts(fold(output * output))
            return square

        square_ref[...] = rows_of(square_ref[...], body, 4)
    back_ref[...] = jnp.dot(slope_ref[...], wt_ref[...], preferred_element_type=f32)
    grad_ref[...] += contract_lead(mixed_ref[...], slope_ref[...])

    @at_end
    def _():
        power_ref[...] = square_ref[...]
        total = column_total(acc_ref[...])
        put(tile_ref, 0, total)
        turned = column_total(grad_ref[...] * w_ref[...].astype(f32))
        put(tile_ref, lanes // 128, turned - terms_ref[2:3, :] * total)
        send(send_ref, tile_ref)


def mid_terms(second_ref, ab_ref, here, mask):
    pre = second_ref[here, :] * ab_ref[0:1, :] + ab_ref[1:2, :]
    plain = sigmoid(pre)
    gate = plain * mask
    act = pre * gate
    return pre, act, gate + act * (1.0 - plain)


def gate_kernel(
    sides,
    second_ref,
    ab_ref,
    back_ref,
    mixed_ref,
    recv_ref,
    terms_ref,
    param_ref,
    count_ref,
    w_ref,
    wt_ref,
    weights_ref,
    excite_ref,
    squeeze_ref,
    gate_ref,
    up_ref,
    power_out_ref,
    power_mix_ref,
    dmixed_ref,
    sums_ref,
    dup_ref,
    dbias_ref,
    dq_ref,
    grads_ref,
    send_ref,
    turn_ref,
    row_ref,
    tile_ref,
):
    step = pl.program_id(0)
    place = places()
    lanes = second_ref.shape[1]
    half = lanes // 2
    width = w_ref.shape[1]

    @at_start
    def _():
        take(recv_ref, tile_ref)
        count = wide(count_ref[0:1, :], width)
        total = row_at(tile_ref, 0, width)
        scale, center, inv = terms_ref[0:1, :], terms_ref[2:3, :], terms_ref[3:4, :]
        gain_grad = row_at(tile_ref, width // 128, width) / param_ref[0:1, :]
        slant = scale * inv * gain_grad / count
        level = total / count - center * slant
        grads_ref[0:1, :] = total * terms_ref[4:5, :]
        grads_ref[1:2, :] = gain_grad
        grads_ref[2:3, :] = slant
        grads_ref[3:4, :] = level
        whole = w_ref[...].astype(f32)
        turn_ref[...] = jnp.dot(
            (whole * slant).astype(bf16), wt_ref[...], preferred_element_type=f32
        ).astype(bf16)
        row_ref[...] = jnp.dot(
            jnp.broadcast_to(level, (8, width)),
            wt_ref[...].astype(f32),
            precision=HIGH,
            preferred_element_type=f32,
        )

    dmixed_ref[...] = back_ref[...] - jnp.dot(
        mixed_ref[...], turn_ref[...], preferred_element_type=f32
    )
    for image in range(STEP):
        limit = 2 * sides[step * STEP + image]

        def body(row, carry):
            here = chunk(image, row)
            mask = row_mask(place, row, limit)
            dmixed = (dmixed_ref[here, :] - row_ref[0:1, :]) * wide(mask, half)
            dmixed_ref[here, :] = dmixed
            both = jnp.concatenate([dmixed, dmixed], axis=1)
            pre, act, slope = mid_terms(second_ref, ab_ref, here, wide(mask, lanes))
            along = slope * both
            terms = (act * both, along, along * pre, slope, slope * pre)
            return tuple(old + fold(new) for old, new in zip(carry, terms))

        start = tuple(jnp.zeros((8, lanes), f32) for _ in range(5))
        totals = rows_of(start, body, 4)
        for index in range(5):
            sums_ref[index, pl.ds(step * STEP + image, 1), :] = column_total(totals[index])

    @at_end
    def _():
        weights = weights_ref[...]
        grads = sums_ref[0]
        mean = weights * grads
        mean = mean[:, :half] + mean[:, half:]
        dlogits = weights * (grads - jnp.concatenate([mean, mean], axis=1))
        dbias_ref[...] = jnp.broadcast_to(column_total(dlogits), dbias_ref.shape)
        low = dlogits.astype(bf16)
        dup_ref[...] = contract_lead(low, excite_ref[...])
        dexcite = jnp.dot(low, up_ref[...], preferred_element_type=f32)
        squeeze = squeeze_ref[...]
        pre = squeeze * gate_ref[0:1, :] + gate_ref[1:2, :]
        normed = squeeze * gate_ref[2:3, :] + gate_ref[3:4, :]
        plain = sigmoid(pre)
        dq = dexcite * (plain * (1.0 + pre * (1.0 - plain)))
        dq_ref[...] = dq
        tile_ref[0:1, :] = column_total(dq)
        tile_ref[1:2, :] = column_total(dq * normed)
        tile_ref[2:3, :] = column_total(power_out_ref[...])
        tile_ref[3:4, :] = column_total(power_mix_ref[...])
        tile_ref[4:8, :] = jnp.zeros((4, 128), f32)
        tile = tile_ref[0:8, :]
        for j in range(send_ref.shape[0]):
            send_ref[j] = tile


def squeeze_kernel(
    images_all,
    width,
    sides,
    dq_ref,
    squeeze_ref,
    gate_ref,
    recv_ref,
    pooled_ref,
    down_ref,
    weights_ref,
    sums_ref,
    param_ref,
    count_ref,
    terms_ref,
    ddown_ref,
    dpool_ref,
    grads_ref,
    send_ref,
    tile_ref,
    area_ref,
):
    take(recv_ref, tile_ref)
    shift, gain = tile_ref[0:1, :], tile_ref[1:2, :]
    grads_ref[0:1, :] = shift
    grads_ref[1:2, :] = gain
    bottleneck = pooled_ref.shape[1]
    count = count_ref[0:1, :]
    powers = (
        lane_sum(gate_ref[4:5, :]) / (count * width),
        lane_sum(tile_ref[3:4, :]) / (count * bottleneck),
        terms_ref[5:6, :128] / width,
        lane_sum(tile_ref[2:3, :]) / (count * width),
    )
    place = lax.broadcasted_iota(jnp.int32, (1, 128), 1)
    norms = powers[3]
    for index in range(3):
        norms = jnp.where(place == index, powers[index], norms)
    grads_ref[2:3, :] = jnp.sqrt(norms)
    normed = squeeze_ref[...] * gate_ref[2:3, :] + gate_ref[3:4, :]
    dsqueeze = gate_ref[0:1, :] * (
        dq_ref[...] - (shift + normed * gain) / jnp.float32(images_all)
    )
    low = dsqueeze.astype(bf16)
    ddown_ref[...] = contract_lead(pooled_ref[...], low)
    for image in range(area_ref.shape[0]):
        area = 4 * sides[image] * sides[image]
        area_ref[image : image + 1, :] = jnp.full((1, bottleneck), area, jnp.int32).astype(f32)
    dpool = contract_last(low, down_ref[...]) / area_ref[...]
    dpool_ref[...] = dpool
    both = jnp.concatenate([dpool, dpool], axis=1)
    weights = weights_ref[...]
    total = column_total(weights * sums_ref[1] + both * sums_ref[3])
    product = column_total(weights * sums_ref[2] + both * sums_ref[4])
    lanes = weights.shape[1]
    put(tile_ref, 0, total)
    put(tile_ref, lanes // 128, (product - param_ref[1:2, :] * total) / param_ref[0:1, :])
    send(send_ref, tile_ref)


def conv_back_kernel(
    sides,
    second_ref,
    ab_ref,
    recv_ref,
    param_ref,
    count_ref,
    dmixed_ref,
    weights_ref,
    dpool_ref,
    first_ref,
    ab_in_ref,
    w_ref,
    dsecond_ref,
    dfirst_ref,
    grads_ref,
    stat_ref,
    column_ref,
    acc_ref,
    tile_ref,
):
    step = pl.program_id(0)
    zeros_at_start(acc_ref, column_ref)
    place = places()
    lanes = second_ref.shape[1]
    half = lanes // 2
    quarter = half // RADIX
    columns = TAPS * quarter

    @at_start
    def _():
        take(recv_ref, tile_ref)
        total = row_at(tile_ref, 0, lanes)
        product = row_at(tile_ref, lanes // 128, lanes)
        count = wide(count_ref[0:1, :], lanes)
        slant = ab_ref[0:1, :] * product / (count * param_ref[0:1, :])
        grads_ref[0:1, :] = total
        grads_ref[1:2, :] = product
        grads_ref[2:3, :] = slant
        grads_ref[3:4, :] = ab_ref[0:1, :] * total / count - param_ref[1:2, :] * slant

    for image in range(STEP):
        limit = 2 * sides[step * STEP + image]
        weights = weights_ref[pl.ds(step * STEP + image, 1), :] * ab_ref[0:1, :]
        dpool = dpool_ref[pl.ds(step * STEP + image, 1), :]
        dpool = jnp.concatenate([dpool, dpool], axis=1) * ab_ref[0:1, :]

        def body(row, carry):
            here = chunk(image, row)
            mask = wide(row_mask(place, row, limit), lanes)
            dmixed = dmixed_ref[here, :]
            both = jnp.concatenate([dmixed, dmixed], axis=1)
            pre = second_ref[here, :] * ab_ref[0:1, :] + ab_ref[1:2, :]
            plain = sigmoid(pre)
            slope = plain + pre * plain * (1.0 - plain)
            grad = slope * (weights * both + dpool)
            grad = mask * (grad - (pre * grads_ref[2:3, :] + grads_ref[3:4, :]))
            dsecond_ref[here, :] = grad.astype(bf16)
            return carry

        rows_of(0, body)
    for image in range(STEP):
        for group in range(RADIX):
            column_ref[image, SIDE : SIDE + 256, group * columns : (group + 1) * columns] = jnp.dot(
                dsecond_ref[image * 256 : image * 256 + 256, group * half : (group + 1) * half],
                w_ref[:, group * columns : (group + 1) * columns],
                preferred_element_type=f32,
            )
    for image in range(STEP):
        limit = 2 * sides[step * STEP + image]

        def body(row, carry):
            total, product = carry
            here = chunk(image, row)
            mask = row_mask(place, row, limit)
            parts = []
            for group in range(RADIX):
                sides_sum = []
                for side in range(3):
                    summed = None
                    for up in range(3):
                        at = group * columns + (up * 3 + side) * quarter
                        rows = pl.ds(pl.multiple_of((row + 2 - up) * SIDE, SIDE), SIDE)
                        piece = column_ref[image, rows, at : at + quarter]
                        summed = piece if summed is None else summed + piece
                    sides_sum.append(summed)
                inner = wide(place, quarter)
                low = jnp.where(inner == SIDE - 1, 0.0, pltpu.roll(sides_sum[0], SIDE - 1, 0))
                high = jnp.where(inner == 0, 0.0, pltpu.roll(sides_sum[2], 1, 0))
                parts.append(sides_sum[1] + low + high)
            dact = jnp.concatenate(parts, axis=1)
            first = first_ref[here, :]
            pre = first * ab_in_ref[0:1, :] + ab_in_ref[1:2, :]
            normed = first * ab_in_ref[2:3, :] + ab_in_ref[3:4, :]
            plain = sigmoid(pre)
            grad = dact * (plain * (1.0 + pre * (1.0 - plain)) * wide(mask, half))
            dfirst_ref[here, :] = grad
            return (total + fold(grad), product + fold(grad * normed))

        total, product = rows_of((acc_ref[0], acc_ref[1]), body, 4)
        acc_ref[0] = total
        acc_ref[1] = product

    @at_end
    def _():
        stat_ref[...] = jnp.zeros(stat_ref.shape, f32)
        put(stat_ref, 0, column_total(acc_ref[0]))
        put(stat_ref, half // 128, column_total(acc_ref[1]))


def conv_grad_kernel(aligned, odd, act_ref, dsecond_ref, x_ref, dfirst_ref, _, in_ref, *refs):
    if aligned:
        mine_ref, other_ref, conv_ref, patch_ref = refs
    else:
        conv_ref, patch_ref = refs
    zeros_at_start(conv_ref, in_ref, patch_ref)
    place = places()
    lanes = act_ref.shape[1]
    columns = TAPS * lanes // RADIX
    for image in range(STEP):

        def body(row, carry):
            write_patches(patch_ref, image, row, act_ref[chunk(image, row), :], place)
            return carry

        rows_of(0, body)
    for image in range(STEP):
        for group in range(RADIX):
            conv_ref[:, group * columns : (group + 1) * columns] += contract_lead(
                dsecond_ref[image * 256 : image * 256 + 256, group * lanes : (group + 1) * lanes],
                patch_ref[image, SIDE : SIDE + 256, group * columns : (group + 1) * columns],
            )
    in_ref[...] += contract_lead(dfirst_ref[...].astype(bf16), x_ref[...])

    if aligned:

        @at_end
        def _():
            for piece in range(mine_ref.shape[0]):
                for ref, side in ((mine_ref, odd[0]), (other_ref, 1 - odd[0])):
                    here = pl.ds(pl.multiple_of((2 * piece + side) * 8, 8), 8)
                    for pair in range(RADIX * TAPS // 2):
                        two = [
                            conv_ref[here, (2 * pair + k) * 128 : (2 * pair + k + 1) * 128]
                            for k in range(2)
                        ]
                        ref[piece, pair * 16 : pair * 16 + 16, :] = jnp.concatenate(
                            two, axis=0
                        ).astype(bf16)


def late_kernel(
    aligned, odd, recv_ref, terms_ref, count_ref, in_ref, cross_ref, ones_ref, grads_ref, *refs
):
    tile_ref = refs[-1]
    take(recv_ref, tile_ref)
    lanes = terms_ref.shape[1]
    total = row_at(tile_ref, 0, lanes)
    product = row_at(tile_ref, lanes // 128, lanes)
    count = wide(count_ref[0:1, :], lanes)
    slant = terms_ref[0:1, :] * terms_ref[2:3, :] * product / count
    level = terms_ref[0:1, :] * total / count - terms_ref[4:5, :] * slant
    grads_ref[0:1, :] = total
    grads_ref[1:2, :] = product
    grads_ref[2:3, :] = slant
    grads_ref[3:4, :] = level
    grads_ref[4:5, :] = terms_ref[0:1, :]
    grads_ref[5:8, :] = jnp.zeros((3, lanes), f32)
    if not aligned:
        return
    mine_ref, other_ref, full_ref, _ = refs
    columns = jnp.transpose(grads_ref[...])
    ones = column_total(ones_ref[...])
    full_ref[...] = (
        in_ref[...] * columns[:, 4:5]
        - cross_ref[...] * columns[:, 2:3]
        - ones * columns[:, 3:4]
    )
    rows = mine_ref.shape[1]
    groups = lanes // rows
    for piece in range(mine_ref.shape[0]):
        owner, pair = 2 * piece // groups, piece % (groups // 2)
        for ref, side in ((mine_ref, odd[0]), (other_ref, 1 - odd[0])):
            here = pl.ds(pl.multiple_of((2 * pair + side) * rows, rows), rows)
            ref[piece] = full_ref[here, owner * 128 : (owner + 1) * 128].astype(bf16)


def merge_kernel(mid_ref, mid_got_ref, in_ref, in_got_ref, out_ref):
    cut = in_ref.shape[1]
    for piece in range(out_ref.shape[0]):
        out_ref[piece, :cut, :] = (
            in_ref[piece].astype(f32) + in_got_ref[piece].astype(f32)
        ).astype(bf16)
        out_ref[piece, cut:, :] = (
            mid_ref[piece].astype(f32) + mid_got_ref[piece].astype(f32)
        ).astype(bf16)


def last_kernel(
    sides, dfirst_ref, first_ref, grads_ref, w_ref, slope_ref, terms_ref, out_ref, done_ref, low_ref
):
    step = pl.program_id(0)
    place = places()
    lanes = first_ref.shape[1]
    width = out_ref.shape[1]
    part = 512 if width % 512 == 0 else width
    for image in range(STEP):
        limit = 2 * sides[step * STEP + image]

        def body(row, carry):
            here = chunk(image, row)
            mask = wide(row_mask(place, row, limit), lanes)
            grad = dfirst_ref[here, :] * grads_ref[4:5, :]
            grad = grad - mask * (first_ref[here, :] * grads_ref[2:3, :] + grads_ref[3:4, :])
            low_ref[here, :] = grad.astype(bf16)
            return carry

        rows_of(0, body)
    out_ref[...] = contract_last(low_ref[...], w_ref[...])
    for image in range(STEP):

        def body(row, carry):
            here = chunk(image, row)
            for at in range(0, width, part):
                cut = slice(at, at + part)
                out_ref[here, cut] += slope_ref[here, cut].astype(f32) * terms_ref[4:5, cut]
            return carry

        rows_of(0, body)

    @at_end
    def _():
        done_ref[...] = jnp.zeros(done_ref.shape, f32)


def total_of(ref):
    total = ref[0].astype(f32)
    for j in range(1, ref.shape[0]):
        total = total + ref[j].astype(f32)
    return total.astype(bf16)


def total_kernel(part_ref, tile_ref, sum_ref, send_ref):
    sum_ref[...] = total_of(part_ref)
    send(send_ref, tile_ref)


def total_last_kernel(one_ref, part_ref, _, sum_ref):
    cut = one_ref.shape[0]
    sum_ref[:cut, :] = one_ref[...]
    sum_ref[cut:, :] = total_of(part_ref)


def shards_kernel(
    marks, place, *refs
):
    groups = len(refs) - 7
    out_ref, up_ref, down_ref, bias_ref, in_ref, mid_ref, all_ref = refs[groups:]
    for k in range(groups):
        all_ref[place[0] ^ k] = refs[k][...].astype(f32)

    def rows_from(start, count):
        return jnp.concatenate([all_ref[k, start : start + count, :] for k in range(groups)], axis=0)

    at = 0
    out_ref[...] = rows_from(at, marks[0])
    at += marks[0]
    up_ref[...] = rows_from(at, marks[1])
    at += marks[1]
    down_ref[...] = rows_from(at, marks[2])
    at += marks[2]
    bias_ref[...] = all_ref[0, at : at + 8, :]
    at = marks[3]
    in_ref[...] = jnp.transpose(rows_from(at, marks[4]))
    at += marks[4]
    for tap in range(RADIX * TAPS):
        mid_ref[tap] = rows_from(at + tap * 8, 8)


def tiles(lanes, block=0):
    return pl.BlockSpec((STEP * 256, lanes), lambda i: (i, block))


def held(*shape):
    return pl.BlockSpec(shape, lambda i: (0,) * len(shape))


def token():
    return pl.BlockSpec(memory_space=pl.ANY)


def scalars():
    return pl.BlockSpec(memory_space=pltpu.SMEM)


def shaped(shape, dtype=f32):
    return jax.ShapeDtypeStruct(shape, dtype)


def call(kernel, steps, ins, outs, scratch=(), cost=5, limit=56, name=None):
    return pl.pallas_call(
        kernel,
        grid=(steps,),
        in_specs=ins,
        out_specs=[spec for spec, _ in outs],
        out_shape=[shape for _, shape in outs],
        scratch_shapes=[pltpu.VMEM(shape, dtype) for shape, dtype in scratch],
        compiler_params=pltpu.CompilerParams(
            dimension_semantics=("arbitrary",), vmem_limit_bytes=limit * 1024 * 1024
        ),
        cost_estimate=pl.CostEstimate(
            flops=int(cost * 1e9), bytes_accessed=int(cost * 3e6), transcendentals=0
        ),
        name=name,
    )


def whole_out(shape, dtype=f32):
    return held(*shape), shaped(shape, dtype)


def rows8(*vectors):
    stacked = jnp.stack(vectors, axis=0)
    return jnp.pad(stacked, ((0, 8 - len(vectors)), (0, 0)))


def local(
    features,
    half_sides,
    cotangent,
    conv_in,
    conv_mid,
    attn_down,
    attn_up,
    attn_bias,
    conv_out,
    gain_in,
    shift_in,
    gain_mid,
    shift_mid,
    gain_attn,
    shift_attn,
    gain_out,
    shift_out,
):
    images, pixels, width = features.shape
    rows = images * pixels
    steps = images // STEP
    pieces = lax.axis_size("fsdp")
    groups = lax.axis_size("dp")
    devices = pieces * groups
    images_all = images * devices
    bottleneck = conv_in.shape[1]
    att = attn_down.shape[1]
    mid = RADIX * bottleneck
    columns = TAPS * conv_mid.shape[2]
    odd = lax.rem(lax.axis_index("dp"), 2).reshape(1)

    down_rows, up_rows = attn_down.shape[0], attn_up.shape[1]
    own_columns = conv_mid.shape[3]
    small = [gain_in, shift_in, gain_mid, shift_mid, gain_attn, shift_attn, gain_out, shift_out, attn_bias]
    lengths = [item.shape[0] for item in small]
    aligned = (
        own_columns % 16 == 0
        and width == 128 * pieces
        and bottleneck == 8 * devices
        and groups == 4
        and pieces == len(ORDER)
    )
    mid_cut = conv_mid.transpose(0, 1, 3, 2)
    if aligned:
        place = lax.axis_index("fsdp").reshape(1)
        at = TAPS * own_columns
        cut = (at + 128 + down_rows + up_rows + 16, 128)
        in_send, most = call(
            prepare_kernel,
            1,
            [
                scalars(),
                held(*conv_in.shape),
                held(RADIX, at, 128),
                held(*attn_down.shape),
                held(up_rows, att),
                held(*conv_out.shape),
            ]
            + [held(1, length) for length in lengths],
            [
                whole_out((pieces, conv_in.shape[0], 128), bf16),
                whole_out(cut, bf16),
            ],
            [((16, 128), f32)],
            2,
            name="last_prepare",
        )(
            odd,
            conv_in,
            mid_cut.reshape(RADIX, at, 128),
            attn_down,
            attn_up.T,
            conv_out,
            *[item.reshape(1, -1) for item in small],
        )
        in_mine = swap_all(in_send, "fsdp").reshape(width, bottleneck // 2)
        in_other = neighbour(in_mine)

        most = most[None]
        most = jnp.concatenate([most, partner(most, 4)], axis=0)
        most = jnp.concatenate([most, partner(most, 2)], axis=0)
        shards = [most, partner(most, 1)]
        shards += [neighbour(item) for item in shards]
    else:
        in_send = jnp.broadcast_to(half_of(conv_in, 1)[None], (pieces, conv_in.shape[0], 128))
        vectors = jnp.stack([jnp.pad(item, (0, 128 - item.shape[0])) for item in small])
        most = jnp.concatenate([mid_cut.reshape(-1, 128), attn_down, attn_up.T, vectors], axis=0)
        most = lax.all_gather(most, "fsdp")
        at = RADIX * TAPS * own_columns
        in_mine = swap_all(in_send, "fsdp").reshape(width, bottleneck // 2)
        in_other = neighbour(in_mine)
        whole_down = most[:, at : at + down_rows].reshape(bottleneck, att)
        whole_up = most[:, at + down_rows : at + down_rows + up_rows].reshape(mid, att)

    x = features.reshape(rows, width)
    cot = cotangent.reshape(rows, width)

    def tiled(lanes, dtype=f32):
        return tiles(lanes), shaped((rows, lanes), dtype)

    def sending(count, dtype=f32):
        return whole_out((devices, count, 128), dtype)

    def received(count):
        return held(devices, count, 128)

    first, whole_in, out = call(
        first_kernel,
        steps,
        [scalars(), scalars(), tiles(width), held(width, bottleneck // 2), held(width, bottleneck // 2)],
        [tiled(bottleneck), whole_out((width, bottleneck), bf16), sending(8)],
        [((2, 8, bottleneck), f32), ((8, 128), f32)],
        8,
        name="first",
    )(half_sides, odd, x, in_mine, in_other)
    got = swap_all(out, AXES)
    cross, x_sum, power_x = call(
        cross_kernel,
        steps,
        [scalars(), tiles(width), tiles(bottleneck)],
        [
            whole_out((bottleneck, width)),
            whole_out((8, width)),
            whole_out((8, 128)),
        ],
        [((8, width), f32)],
        10,
        name="cross",
    )(half_sides, x, first)

    ins = [scalars(), tiles(bottleneck), received(8), token()]
    args = (half_sides, first, got, power_x)
    outs = [
        tiled(bottleneck, bf16),
        tiled(mid),
        whole_out((8, bottleneck)),
        whole_out((8, 128)),
        sending(8),
    ]
    scratch = [
        ((STEP, 256 + 2 * SIDE, RADIX * columns), bf16),
        ((2, 8, mid), f32),
        ((8, 128), f32),
    ]
    if aligned:
        ins += [scalars(), scalars()] + [held(*item.shape) for item in shards]
        args += (place, odd) + tuple(shards)
        outs += [whole_out((bottleneck, RADIX * columns), bf16)]
        outs += [whole_out((bottleneck, att), bf16), whole_out((mid, att), bf16)]
        outs += [whole_out((8, lanes)) for lanes in (mid, att, width, mid)]
        scratch += [((8, bottleneck), f32)]
    else:
        whole_mid = most[:, :at].reshape(pieces, RADIX * TAPS, own_columns, 128)
        whole_mid = whole_mid.transpose(0, 2, 1, 3).reshape(bottleneck, RADIX * columns)
        at += down_rows + up_rows
        found = [
            most[:, at + k, :length].reshape(-1).astype(f32) for k, length in enumerate(lengths)
        ]
        p_in, p_mid, p_attn, p_out = [rows8(found[2 * k], found[2 * k + 1]) for k in range(4)]
        p_bias = rows8(found[8])
        ins += [held(bottleneck, RADIX * columns), held(8, bottleneck)]
        args += (whole_mid, p_in)
    act_low, second, terms_in, count, out, *rest = call(
        functools.partial(second_kernel, lengths if aligned else None),
        steps,
        ins,
        outs,
        scratch,
        15,
        name="second",
    )(*args)
    if aligned:
        whole_mid, whole_down, whole_up, p_mid, p_attn, p_out, p_bias = rest
    got = swap_all(out, AXES)

    pooled, squeeze, terms_mid, out = call(
        pool_kernel,
        steps,
        [
            scalars(),
            tiles(mid),
            received(8),
            held(8, mid),
            held(8, 128),
            held(bottleneck, att),
            held(8, 128),
        ],
        [
            whole_out((images, bottleneck), bf16),
            whole_out((images, att)),
            whole_out((8, mid)),
            sending(8),
        ],
        [((images, bottleneck), f32), ((8, 128), f32)],
        7,
        name="pool",
    )(half_sides, second, got, p_mid, count, whole_down, power_x)
    got = swap_all(out, AXES)

    if aligned:
        whole_w_out, whole_out_t = call(
            functools.partial(out_weights_kernel, TAPS * own_columns),
            1,
            [scalars(), scalars(), token()] + [held(*item.shape) for item in shards],
            [whole_out((bottleneck, width), bf16), whole_out((width, bottleneck), bf16)],
            (),
            1,
            name="last_weights",
        )(place, odd, pooled, *shards)
    else:
        whole_w_out = lax.all_gather(conv_out, "fsdp", axis=1, tiled=True)
        whole_out_t = whole_w_out.T
    wide_rows = 2 * width // 128
    mixed, weights, excite, gate, gram_out, colsum, power_mix, out = call(
        functools.partial(mix_kernel, images_all),
        steps,
        [
            scalars(),
            tiles(mid),
            held(8, mid),
            held(images, att),
            received(8),
            held(8, att),
            held(mid, att),
            held(8, mid),
            held(bottleneck, width),
        ],
        [
            tiled(bottleneck, bf16),
            whole_out((images, mid)),
            whole_out((images, att), bf16),
            whole_out((8, att)),
            whole_out((bottleneck, width)),
            whole_out((8, bottleneck)),
            whole_out((8, 128)),
            sending(wide_rows),
        ],
        [((bottleneck, bottleneck), f32), ((2, 8, bottleneck), f32), ((wide_rows, 128), f32)],
        11,
        name="mix",
    )(half_sides, second, terms_mid, squeeze, got, p_attn, whole_up, p_bias, whole_w_out)
    got = swap_all(out, AXES)

    block, slope, back, grad_out, terms_out, power_out, out = call(
        out_kernel,
        steps,
        [
            scalars(),
            tiles(bottleneck),
            tiles(width),
            tiles(width),
            received(wide_rows),
            held(8, width),
            held(8, 128),
            held(bottleneck, width),
            held(width, bottleneck),
        ],
        [
            tiled(width, bf16),
            tiled(width, bf16),
            tiled(bottleneck),
            whole_out((bottleneck, width)),
            whole_out((8, width)),
            whole_out((8, 128)),
            sending(wide_rows, bf16),
        ],
        [
            ((STEP * 256, width), f32),
            ((8, width), f32),
            ((8, 128), f32),
            ((wide_rows, 128), f32),
        ],
        25,
        name="output",
    )(half_sides, mixed, x, cot, got, p_out, count, whole_w_out, whole_out_t)
    got = swap_all(out, AXES)

    dmixed, sums, dup, dbias, dq, grads_out, out = call(
        gate_kernel,
        steps,
        [
            scalars(),
            tiles(mid),
            held(8, mid),
            tiles(bottleneck),
            tiles(bottleneck),
            received(wide_rows),
            held(8, width),
            held(8, width),
            held(8, 128),
            held(bottleneck, width),
            held(width, bottleneck),
            held(images, mid),
            held(images, att),
            held(images, att),
            held(8, att),
            held(mid, att),
            held(8, 128),
            held(8, 128),
        ],
        [
            tiled(bottleneck),
            whole_out((5, images, mid)),
            whole_out((mid, att)),
            whole_out((8, mid)),
            whole_out((images, att)),
            whole_out((8, width)),
            sending(8),
        ],
        [
            ((bottleneck, bottleneck), bf16),
            ((8, bottleneck), f32),
            ((wide_rows, 128), f32),
        ],
        13,
        name="gate",
    )(
        half_sides,
        second,
        terms_mid,
        back,
        mixed,
        got,
        terms_out,
        p_out,
        count,
        whole_w_out,
        whole_out_t,
        weights,
        excite,
        squeeze,
        gate,
        whole_up,
        power_out,
        power_mix,
    )
    got = swap_all(out, AXES)
    grad_conv_out = grad_out - colsum[0][:, None] * grads_out[3] - gram_out * grads_out[2]

    ddown, dpool, grads_attn, out = call(
        functools.partial(squeeze_kernel, images_all, width),
        1,
        [
            scalars(),
            held(images, att),
            held(images, att),
            held(8, att),
            received(8),
            held(images, bottleneck),
            held(bottleneck, att),
            held(images, mid),
            held(5, images, mid),
            held(8, mid),
            held(8, 128),
            held(8, width),
        ],
        [
            whole_out((bottleneck, att)),
            whole_out((images, bottleneck)),
            whole_out((8, att)),
            sending(8),
        ],
        [((8, 128), f32), ((images, bottleneck), f32)],
        1,
        name="squeeze",
    )(
        half_sides,
        dq,
        squeeze,
        gate,
        got,
        pooled,
        whole_down,
        weights,
        sums,
        p_mid,
        count,
        terms_out,
    )
    got = swap_all(out, AXES)

    out_cut = grad_conv_out.astype(bf16).reshape(bottleneck, pieces, -1).transpose(1, 0, 2)
    out_cut = out_cut.reshape(devices, -1, 128)
    bias_rows = jnp.pad(dbias[0].reshape(pieces, 1, up_rows), ((0, 0), (0, 0), (0, att - up_rows)))
    gates = jnp.concatenate(
        [
            dup.reshape(devices, -1, att),
            ddown.reshape(devices, -1, att),
            jnp.repeat(bias_rows, groups, axis=0),
        ],
        axis=1,
    ).astype(bf16)
    marks = [out_cut.shape[1], up_rows // groups, down_rows // groups]
    gates = jnp.concatenate([out_cut, gates], axis=1)
    gates = jnp.pad(gates, ((0, 0), (0, -gates.shape[1] % 16), (0, 0)))

    gates = swap_all(gates, AXES)
    dsecond, dfirst, grads_mid, stat = call(
        conv_back_kernel,
        steps,
        [
            scalars(),
            tiles(mid),
            held(8, mid),
            received(8),
            held(8, mid),
            held(8, 128),
            tiles(bottleneck),
            held(images, mid),
            held(images, bottleneck),
            tiles(bottleneck),
            held(8, bottleneck),
            held(bottleneck, RADIX * columns),
        ],
        [tiled(mid, bf16), tiled(bottleneck), whole_out((8, mid)), whole_out((8, 128))],
        [
            ((STEP, 256 + 2 * SIDE, RADIX * columns), f32),
            ((2, 8, bottleneck), f32),
            ((8, 128), f32),
        ],
        20,
        name="conv_back",
    )(
        half_sides,
        second,
        terms_mid,
        got,
        p_mid,
        count,
        dmixed,
        weights,
        dpool,
        first,
        terms_in,
        whole_mid,
    )
    gates, out = call(
        total_kernel,
        1,
        [held(*gates.shape), held(8, 128)],
        [whole_out(gates.shape[1:], bf16), sending(8)],
        (),
        2,
        name="last_gates",
    )(gates, stat)
    got = swap_all(out, AXES)

    outs = [whole_out((bottleneck, width))]
    scratch = [((STEP, 256 + 2 * SIDE, RADIX * columns), bf16)]
    mid_rows = bottleneck // devices * RADIX * TAPS
    if aligned:
        outs += [whole_out((devices // 2, mid_rows, 128), bf16)] * 2
        scratch = [((bottleneck, RADIX * columns), f32)] + scratch
    else:
        outs += [whole_out((bottleneck, RADIX * columns))]
    in_grad, *conv_parts = call(
        functools.partial(conv_grad_kernel, aligned),
        steps,
        [scalars(), tiles(bottleneck), tiles(mid), tiles(width), tiles(bottleneck), token()],
        outs,
        scratch,
        15,
        name="conv_grad",
    )(odd, act_low, dsecond, x, dfirst, gates)
    outs = [whole_out((8, bottleneck))]
    scratch = [((8, 128), f32)]
    in_rows = bottleneck // groups * (width // pieces) // 128
    if aligned:
        outs += [whole_out((devices // 2, in_rows, 128), bf16)] * 2
        scratch = [((bottleneck, width), f32)] + scratch
    grads_in, *in_parts = call(
        functools.partial(late_kernel, aligned),
        1,
        [
            scalars(),
            received(8),
            held(8, bottleneck),
            held(8, 128),
            held(bottleneck, width),
            held(bottleneck, width),
            held(8, width),
        ],
        outs,
        scratch,
        2,
        name="last_terms",
    )(odd, got, terms_in, count, in_grad, cross, x_sum)
    grad_features, done = call(
        last_kernel,
        steps,
        [
            scalars(),
            tiles(bottleneck),
            tiles(bottleneck),
            held(8, bottleneck),
            held(width, bottleneck),
            tiles(width),
            held(8, width),
        ],
        [tiled(width), whole_out((8, 128))],
        [((STEP * 256, bottleneck), bf16)],
        15,
        name="last",
    )(half_sides, dfirst, first, grads_in, whole_in, slope, terms_out)

    if aligned:
        mid_got, in_got = neighbour(conv_parts[1]), neighbour(in_parts[1])
        (late,) = call(
            merge_kernel,
            1,
            [held(*mid_got.shape)] * 2 + [held(*in_got.shape)] * 2,
            [whole_out((devices // 2, in_rows + mid_rows, 128), bf16)],
            (),
            2,
            name="last_merge",
        )(conv_parts[0], mid_got, in_parts[0], in_got)
    else:
        grad_conv_in = (
            in_grad * grads_in[4][:, None]
            - cross * grads_in[2][:, None]
            - column_total(x_sum) * grads_in[3][:, None]
        )
        in_cut = grad_conv_in.astype(bf16).reshape(bottleneck, pieces, -1).transpose(1, 0, 2)
        mid_cut = conv_parts[0].astype(bf16).reshape(devices, -1, RADIX * TAPS, 128)
        mid_cut = mid_cut.transpose(0, 2, 1, 3).reshape(devices, -1, 128)
        late = jnp.concatenate([in_cut.reshape(devices, -1, 128), mid_cut], axis=1)
        late = jnp.pad(late, ((0, 0), (0, -late.shape[1] % 16), (0, 0)))
        late = late.reshape(devices // 2, 2, -1, 128)
        mine = lax.dynamic_index_in_dim(late, odd[0], 1, False)
        other = lax.dynamic_index_in_dim(late, 1 - odd[0], 1, False)
        late = (mine.astype(f32) + neighbour(other).astype(f32)).astype(bf16)
    sides_of = [[2 * i + side for i in range(devices // 2)] for side in range(2)]
    late = lax.all_to_all(late, AXES, 0, 0, axis_index_groups=sides_of)
    (summed,) = call(
        total_last_kernel,
        1,
        [held(*gates.shape), held(*late.shape), token()],
        [whole_out((gates.shape[0] + late.shape[1], 128), bf16)],
        (),
        2,
        name="last_total",
    )(gates, late, done)
    marks += [gates.shape[0], in_rows]
    own_width = width // pieces
    if aligned:
        members = [summed] + [
            lax.ppermute(summed, "dp", [(i, i ^ k) for i in range(groups)])
            for k in range(1, groups)
        ]
        shard_out, shard_up, shard_down, shard_bias, shard_in, shard_mid = call(
            functools.partial(shards_kernel, marks),
            1,
            [scalars()] + [held(*summed.shape)] * groups,
            [
                whole_out((bottleneck, own_width)),
                whole_out((up_rows, att)),
                whole_out((down_rows, att)),
                whole_out((8, 128)),
                whole_out((own_width, bottleneck)),
                whole_out((RADIX * TAPS, own_columns, 128)),
            ],
            [((groups,) + summed.shape, f32)],
            2,
            name="last_shards",
        )(lax.axis_index("dp").reshape(1), *members)
        shard_bias = shard_bias[0, :up_rows]
        shard_up = shard_up.T
        shard_mid = shard_mid.reshape(RADIX, TAPS, own_columns, 128).transpose(0, 1, 3, 2)
    else:
        summed = swap_all(jnp.broadcast_to(summed[None], (groups,) + summed.shape), "dp")
        summed = summed.astype(f32)
        shard_out = summed[:, : marks[0]].reshape(bottleneck, -1)
        at = marks[0]
        shard_up = summed[:, at : at + marks[1]].reshape(up_rows, att).T
        at += marks[1]
        shard_down = summed[:, at : at + marks[2]].reshape(down_rows, att)
        at += marks[2]
        shard_bias = summed[0, at, :up_rows]
        at = marks[3]
        shard_in = summed[:, at : at + in_rows].reshape(bottleneck, -1).T
        at += in_rows
        shard_mid = summed[:, at : at + mid_rows].reshape(groups, RADIX, TAPS, -1, 128)
        shard_mid = shard_mid.transpose(1, 2, 4, 0, 3).reshape(RADIX, TAPS, 128, own_columns)

    def own_part(row):
        length = row.shape[0] // pieces
        return lax.dynamic_slice_in_dim(row, lax.axis_index("fsdp") * length, length, 0)

    return (
        block.reshape(images, pixels, width),
        grad_features.reshape(images, pixels, width),
        grads_attn[2, :4],
        shard_in,
        shard_mid,
        shard_down,
        shard_up,
        shard_bias,
        shard_out,
        own_part(grads_in[1]),
        own_part(grads_in[0]),
        own_part(grads_mid[1]),
        own_part(grads_mid[0]),
        own_part(grads_attn[1]),
        own_part(grads_attn[0]),
        own_part(grads_out[1]),
        own_part(grads_out[0]),
    )


def solution(mesh):
    return jax.shard_map(
        local,
        mesh=mesh,
        in_specs=(
            P(("fsdp", "dp"), None, None),
            P(("fsdp", "dp")),
            P(("fsdp", "dp"), None, None),
            P("fsdp", None),
            P(None, None, None, "fsdp"),
            P("fsdp", None),
            P(None, "fsdp"),
            P("fsdp"),
            P(None, "fsdp"),
            P("fsdp"),
            P("fsdp"),
            P("fsdp"),
            P("fsdp"),
            P("fsdp"),
            P("fsdp"),
            P("fsdp"),
            P("fsdp"),
        ),
        out_specs=(
            P(("fsdp", "dp"), None, None),
            P(("fsdp", "dp"), None, None),
            P(),
            P("fsdp", None),
            P(None, None, None, "fsdp"),
            P("fsdp", None),
            P(None, "fsdp"),
            P("fsdp"),
            P(None, "fsdp"),
            P("fsdp"),
            P("fsdp"),
            P("fsdp"),
            P("fsdp"),
            P("fsdp"),
            P("fsdp"),
            P("fsdp"),
            P("fsdp"),
        ),
        check_vma=False,
    )
```

```python
import functools

import jax
import jax.numpy as jnp
from jax import lax
from jax.experimental import pallas as pl
from jax.experimental.pallas import tpu as pltpu
from jax.sharding import PartitionSpec as P

RADIX = 2
SIDE = 16
TAPS = 9
STEP = 4

epsilon = 1e-05
AXES = ("fsdp", "dp")
f32 = jnp.float32
bf16 = jnp.bfloat16
HIGH = lax.Precision.HIGHEST


def swap_all(values, axes):
    return lax.all_to_all(values, axes, 0, 0)


def gather_all(shard):
    pieces = lax.axis_size("fsdp")
    return swap_all(jnp.broadcast_to(shard[None], (pieces,) + shard.shape), "fsdp")


def neighbour(values):
    return lax.ppermute(values, "dp", [(i, i ^ 1) for i in range(lax.axis_size("dp"))])


ORDER = (0, 4, 2, 6, 1, 5, 3, 7)


def partner(values, k):
    pieces = lax.axis_size("fsdp")
    return lax.ppermute(values, "fsdp", [(i, i ^ k) for i in range(pieces)])


def half_of(shard, axis):
    odd = lax.rem(lax.axis_index("dp"), 2)
    return lax.dynamic_slice_in_dim(shard, odd * (shard.shape[axis] // 2), shard.shape[axis] // 2, axis)


def sigmoid(values):
    return 0.5 * jnp.tanh(0.5 * values) + 0.5


def fold(values):
    return values[:8] + values[8:]


def wide(mask, lanes):
    return jnp.concatenate([mask] * (lanes // mask.shape[1]), axis=1)


def places():
    return lax.broadcasted_iota(jnp.int32, (SIDE, 128), 0)


def row_mask(place, row, limit):
    return jnp.where((place < limit) & (row < limit), 1.0, 0.0).astype(f32)


def chunk(image, row):
    return pl.ds(pl.multiple_of(image * 256 + row * SIDE, SIDE), SIDE)


def of_image(image):
    return slice(image * 256, image * 256 + 256)


def of_row(image, row):
    return slice(image * 256 + row * SIDE, image * 256 + row * SIDE + SIDE)


def stages(*parts):
    for stage in range(STEP + len(parts) - 1):
        for late, part in reversed(list(enumerate(parts))):
            if 0 <= stage - late < STEP:
                part(stage - late)


def rows_of(carry, body, unroll=8):
    return lax.fori_loop(0, SIDE, body, carry, unroll=unroll)


def contract_lead(left, right):
    return lax.dot_general(left, right, (((0,), (0,)), ((), ())), preferred_element_type=f32)


def contract_last(left, right):
    return lax.dot_general(left, right, (((1,), (1,)), ((), ())), preferred_element_type=f32)


def zeros_at_start(*refs):
    @pl.when(pl.program_id(0) == 0)
    def _():
        for ref in refs:
            ref[...] = jnp.zeros(ref.shape, ref.dtype)


def last_step():
    return pl.program_id(0) == pl.num_programs(0) - 1


def column_total(values):
    return jnp.sum(values, axis=0, keepdims=True)


def take(recv_ref, tile_ref):
    tile_ref[...] = lax.fori_loop(
        1,
        recv_ref.shape[0],
        lambda j, total: total + recv_ref[j].astype(f32),
        recv_ref[0].astype(f32),
        unroll=True if recv_ref.shape[0] <= 32 else 1,
    )


def row_at(tile_ref, start, lanes):
    return jnp.concatenate(
        [tile_ref[start + q : start + q + 1, :] for q in range(lanes // 128)], axis=1
    )


def put(tile_ref, start, row):
    for q in range(row.shape[1] // 128):
        tile_ref[start + q : start + q + 1, :] = row[:, q * 128 : (q + 1) * 128]


def send(send_ref, tile_ref):
    tile = tile_ref[...].astype(send_ref.dtype)

    def body(j, carry):
        send_ref[j] = tile
        return carry

    lax.fori_loop(0, send_ref.shape[0], body, 0, unroll=True if send_ref.shape[0] <= 32 else 1)


def norm_rows(sums, squares, counted, gain, shift):
    center = sums / counted
    spread = squares / counted - center * center
    inv = lax.rsqrt(spread + epsilon)
    scale = gain * inv
    return center, spread, inv, scale, shift - center * scale


def fill_half(whole_ref, mine_ref, other_ref, odd_ref):
    half = whole_ref.shape[1] // 2

    @pl.when(odd_ref[0] == 0)
    def _():
        whole_ref[:, :half] = mine_ref[...]
        whole_ref[:, half:] = other_ref[...]

    @pl.when(odd_ref[0] != 0)
    def _():
        whole_ref[:, :half] = other_ref[...]
        whole_ref[:, half:] = mine_ref[...]


def at_start(body):
    pl.when(pl.program_id(0) == 0)(body)


def at_end(body):
    pl.when(pl.program_id(0) == pl.num_programs(0) - 1)(body)


def lane_parts(values):
    total = values[:, :128]
    for at in range(128, values.shape[1], 128):
        total = total + values[:, at : at + 128]
    return total


def lane_sum(row):
    return jnp.broadcast_to(jnp.sum(row, axis=1, keepdims=True), (1, 128))


def prepare_kernel(odd, in_ref, mid_ref, down_ref, up_ref, out_ref, *refs):
    *vector_refs, in_send, most_send, rows_ref = refs
    rows_ref[...] = jnp.zeros(rows_ref.shape, f32)
    for k, ref in enumerate(vector_refs):
        rows_ref[k : k + 1, : ref.shape[1]] = ref[...].astype(f32)
    at = mid_ref.shape[1] + 128
    for ref in (down_ref, up_ref):
        most_send[at : at + ref.shape[0], :] = ref[...]
        at += ref.shape[0]
    most_send[at : at + 16, :] = rows_ref[...].astype(bf16)
    for side in range(2):

        @pl.when(odd[0] == side)
        def _():
            for j in range(in_send.shape[0]):
                in_send[j] = in_ref[:, side * 128 : side * 128 + 128]
            at = mid_ref.shape[1]
            most_send[:at, :] = mid_ref[side]
            most_send[at : at + 128, :] = jnp.transpose(out_ref[side * 128 : side * 128 + 128, :])


def first_kernel(
    sides, odd, x_ref, mine_ref, other_ref, first_ref, w_ref, send_ref, acc_ref, tile_ref
):
    step = pl.program_id(0)
    zeros_at_start(acc_ref)
    at_start(lambda: fill_half(w_ref, mine_ref, other_ref, odd))
    place = places()
    lanes = first_ref.shape[1]
    sums = [acc_ref[0], acc_ref[1]]

    def multiply(image):
        first_ref[of_image(image), :] = jnp.dot(
            x_ref[of_image(image), :], w_ref[...], preferred_element_type=f32
        )

    def finish(image):
        limit = 2 * sides[step * STEP + image]
        for row in range(SIDE):
            here = of_row(image, row)
            values = first_ref[here, :] * wide(row_mask(place, row, limit), lanes)
            first_ref[here, :] = values
            sums[0] = sums[0] + fold(values)
            sums[1] = sums[1] + fold(values * values)

    stages(multiply, finish)
    acc_ref[0], acc_ref[1] = sums

    @at_end
    def _():
        count = jnp.int32(0)
        for image in range(sides.shape[0]):
            count = count + 4 * sides[image] * sides[image]
        tile_ref[...] = jnp.zeros(tile_ref.shape, f32)
        put(tile_ref, 0, column_total(acc_ref[0]))
        put(tile_ref, lanes // 128, column_total(acc_ref[1]))
        put(tile_ref, 2 * lanes // 128, jnp.full((1, 128), count, jnp.int32).astype(f32))
        send(send_ref, tile_ref)


def cross_kernel(
    sides, x_ref, first_ref, cross_ref, ones_ref, power_ref, square_ref
):
    step = pl.program_id(0)
    zeros_at_start(cross_ref, square_ref, ones_ref)
    cross_ref[...] += contract_lead(first_ref[...].astype(bf16), x_ref[...])
    place = places()
    lanes = x_ref.shape[1]
    for image in range(STEP):
        limit = 2 * sides[step * STEP + image]

        def body(row, carry):
            square, total = carry
            values = x_ref[chunk(image, row), :].astype(f32) * wide(
                row_mask(place, row, limit), lanes
            )
            return (square + fold(values * values), total + fold(values))

        square, total = rows_of((square_ref[...], ones_ref[...]), body)
        square_ref[...] = square
        ones_ref[...] = total

    @at_end
    def _():
        power_ref[...] = lane_parts(square_ref[...])


def write_patches(patch_ref, image, row, low, place):
    values = low.astype(f32)
    lanes = values.shape[1]
    inner = wide(place, lanes)
    left = jnp.where(inner == 0, 0.0, pltpu.roll(values, 1, 0)).astype(bf16)
    right = jnp.where(inner == SIDE - 1, 0.0, pltpu.roll(values, SIDE - 1, 0)).astype(bf16)
    for tap in range(TAPS):
        up, side = tap // 3, tap % 3
        source = (left, low, right)[side]
        here = (row + 2 - up) * SIDE
        if isinstance(row, int):
            here = slice(here, here + SIDE)
        else:
            here = pl.ds(pl.multiple_of(here, SIDE), SIDE)
        for group in range(lanes // 128):
            at = (group * TAPS + tap) * 128
            patch_ref[image, here, at : at + 128] = source[:, group * 128 : (group + 1) * 128]


def second_kernel(lengths, sides, first_ref, recv_ref, _, *refs):
    if lengths:
        member, odd, *refs = refs
        shard_refs, refs = refs[:4], refs[4:]
        act_ref, second_ref, terms_ref, count_ref, send_ref, w_ref, down_ref, up_ref, *refs = refs
        *param_refs, patch_ref, acc_ref, tile_ref, param_ref = refs
    else:
        w_ref, param_ref, act_ref, second_ref, terms_ref, count_ref, send_ref, *refs = refs
        patch_ref, acc_ref, tile_ref = refs
    step = pl.program_id(0)
    zeros_at_start(acc_ref, patch_ref)
    place = places()
    lanes = first_ref.shape[1]
    columns = TAPS * lanes // RADIX

    @at_start
    def _():
        if lengths:
            own = w_ref.shape[0] // len(ORDER)
            downs, ups = down_ref.shape[0] // len(ORDER), up_ref.shape[0] // len(ORDER)
            wholes = [jnp.zeros((16, length * len(ORDER)), f32) for length in lengths]
            lane = lax.broadcasted_iota(jnp.int32, (16, 128), 1)
            for index, k in enumerate(ORDER):
                piece = member[0] ^ k
                ref = shard_refs[index // 4]
                index = index % 4
                at = TAPS * own + 128
                down_ref[pl.ds(pl.multiple_of(piece * downs, downs), downs), :] = ref[
                    index, at : at + downs, :
                ]
                at += downs
                up_ref[pl.ds(pl.multiple_of(piece * ups, ups), ups), :] = ref[
                    index, at : at + ups, :
                ]
                at += ups
                rows = ref[index, at : at + 16, :].astype(f32)
                for length in sorted(set(lengths)):
                    part = jnp.where(lane < length, rows, 0.0)
                    spare = (length * len(ORDER) - 128) // 128
                    part = jnp.concatenate([part] + [jnp.zeros((16, 128), f32)] * spare, axis=1)
                    part = pltpu.roll(part, piece * length, 1)
                    wholes = [
                        whole + part if whole.shape == part.shape else whole for whole in wholes
                    ]
            for side in range(2):

                @pl.when(odd[0] == side)
                def _():
                    for index, k in enumerate(ORDER):
                        here = pl.ds(pl.multiple_of((member[0] ^ k) * own, own), own)
                        for refs, group in ((shard_refs[:2], side), (shard_refs[2:], 1 - side)):
                            for tap in range(TAPS):
                                at = (group * TAPS + tap) * 128
                                w_ref[here, at : at + 128] = refs[index // 4][
                                    index % 4, tap * own : (tap + 1) * own, :
                                ]

            for k, whole in enumerate(wholes):
                ref = ([param_ref] + param_refs)[k // 2]
                ref[k % 2 : k % 2 + 1, :] = whole[k : k + 1, :]
        take(recv_ref, tile_ref)
        count = tile_ref[2 * lanes // 128 : 2 * lanes // 128 + 1, :]
        count_ref[...] = jnp.broadcast_to(count, count_ref.shape)
        center, _, inv, scale, offset = norm_rows(
            row_at(tile_ref, 0, lanes),
            row_at(tile_ref, lanes // 128, lanes),
            wide(count, lanes),
            param_ref[0:1, :],
            param_ref[1:2, :],
        )
        terms_ref[0:1, :] = scale
        terms_ref[1:2, :] = offset
        terms_ref[2:3, :] = inv
        terms_ref[3:4, :] = -center * inv
        terms_ref[4:5, :] = center

    def start_image(image):
        limit = 2 * sides[step * STEP + image]
        for row in range(SIDE):
            here = slice(image * 256 + row * SIDE, image * 256 + row * SIDE + SIDE)
            pre = first_ref[here, :] * terms_ref[0:1, :] + terms_ref[1:2, :]
            act = pre * (sigmoid(pre) * wide(row_mask(place, row, limit), lanes))
            low = act.astype(bf16)
            act_ref[here, :] = low
            write_patches(patch_ref, image, row, low, place)

    def multiply_image(image):
        for group in range(RADIX):
            second_ref[image * 256 : image * 256 + 256, group * lanes : (group + 1) * lanes] = (
                contract_last(
                    patch_ref[image, SIDE : SIDE + 256, group * columns : (group + 1) * columns],
                    w_ref[:, group * columns : (group + 1) * columns],
                )
            )

    def sum_image(image, carry):
        limit = 2 * sides[step * STEP + image]
        total, square = carry
        for row in range(SIDE):
            values = second_ref[image * 256 + row * SIDE : image * 256 + row * SIDE + SIDE, :]
            values = values * wide(row_mask(place, row, limit), values.shape[1])
            total, square = total + fold(values), square + fold(values * values)
        return total, square

    carry = (acc_ref[0], acc_ref[1])
    for stage in range(STEP + 2):
        if 0 <= stage - 1 < STEP:
            multiply_image(stage - 1)
        if stage < STEP:
            start_image(stage)
        if stage >= 2:
            carry = sum_image(stage - 2, carry)
    acc_ref[0], acc_ref[1] = carry

    @at_end
    def _():
        tile_ref[...] = jnp.zeros(tile_ref.shape, f32)
        put(tile_ref, 0, column_total(acc_ref[0]))
        put(tile_ref, RADIX * lanes // 128, column_total(acc_ref[1]))
        send(send_ref, tile_ref)


def pool_kernel(
    sides,
    second_ref,
    recv_ref,
    param_ref,
    count_ref,
    down_ref,
    power_ref,
    pooled_ref,
    squeeze_ref,
    terms_ref,
    send_ref,
    pool_ref,
    tile_ref,
):
    step = pl.program_id(0)
    place = places()
    lanes = second_ref.shape[1]

    @at_start
    def _():
        take(recv_ref, tile_ref)
        _, _, _, scale, offset = norm_rows(
            row_at(tile_ref, 0, lanes),
            row_at(tile_ref, lanes // 128, lanes),
            wide(count_ref[0:1, :], lanes),
            param_ref[0:1, :],
            param_ref[1:2, :],
        )
        terms_ref[0:1, :] = scale
        terms_ref[1:2, :] = offset

    for image in range(STEP):
        limit = 2 * sides[step * STEP + image]

        def body(row, total):
            pre = second_ref[chunk(image, row), :] * terms_ref[0:1, :] + terms_ref[1:2, :]
            act = pre * (sigmoid(pre) * wide(row_mask(place, row, limit), lanes))
            return total + fold(act)

        total = column_total(rows_of(jnp.zeros((8, lanes), f32), body))
        both = total[:, : lanes // 2] + total[:, lanes // 2 :]
        area = jnp.full(both.shape, limit * limit, jnp.int32).astype(f32)
        pool_ref[pl.ds(step * STEP + image, 1), :] = both / area

    @at_end
    def _():
        low = pool_ref[...].astype(bf16)
        pooled_ref[...] = low
        squeeze = jnp.dot(low, down_ref[...], preferred_element_type=f32)
        squeeze_ref[...] = squeeze
        tile_ref[...] = jnp.zeros(tile_ref.shape, f32)
        tile_ref[0:1, :] = column_total(squeeze)
        tile_ref[1:2, :] = column_total(squeeze * squeeze)
        tile_ref[2:3, :] = column_total(power_ref[...])
        send(send_ref, tile_ref)


def out_weights_kernel(start, place, odd, _, *refs):
    *shard_refs, w_ref, wt_ref = refs
    for side in range(2):

        @pl.when(odd[0] == side)
        def _():
            for index, k in enumerate(ORDER):
                here = pl.ds(pl.multiple_of((place[0] ^ k) * 128, 128), 128)
                for refs, half in ((shard_refs[:2], side), (shard_refs[2:], 1 - side)):
                    wt_ref[here, half * 128 : half * 128 + 128] = refs[index // 4][
                        index % 4, start : start + 128, :
                    ]

    w_ref[...] = jnp.transpose(wt_ref[...])


def mix_kernel(
    images_all,
    sides,
    second_ref,
    ab_ref,
    squeeze_ref,
    recv_ref,
    param_ref,
    up_ref,
    bias_ref,
    out_ref,
    mixed_ref,
    weights_ref,
    excite_ref,
    gate_ref,
    gw_ref,
    colsum_ref,
    power_ref,
    send_ref,
    gram_ref,
    acc_ref,
    tile_ref,
):
    step = pl.program_id(0)
    zeros_at_start(acc_ref, gram_ref)
    place = places()
    lanes = second_ref.shape[1]
    half = lanes // 2

    @at_start
    def _():
        tile_ref[0:8, :] = recv_ref[0]
        for j in range(1, recv_ref.shape[0]):
            tile_ref[0:8, :] += recv_ref[j]
        center, _, inv, scale, offset = norm_rows(
            tile_ref[0:1, :],
            tile_ref[1:2, :],
            jnp.float32(images_all),
            param_ref[0:1, :],
            param_ref[1:2, :],
        )
        gate_ref[0:1, :] = scale
        gate_ref[1:2, :] = offset
        gate_ref[2:3, :] = inv
        gate_ref[3:4, :] = -center * inv
        gate_ref[4:5, :] = tile_ref[2:3, :]
        pre = squeeze_ref[...] * scale + offset
        excite = (pre * sigmoid(pre)).astype(bf16)
        excite_ref[...] = excite
        logits = contract_last(excite, up_ref[...]) + bias_ref[0:1, :]
        one, two = logits[:, :half], logits[:, half:]
        top = jnp.maximum(one, two)
        one, two = jnp.exp(one - top), jnp.exp(two - top)
        weights_ref[:, :half] = one / (one + two)
        weights_ref[:, half:] = two / (one + two)

    sums = [acc_ref[0], acc_ref[1]]

    def mix(image):
        limit = 2 * sides[step * STEP + image]
        weights = weights_ref[pl.ds(step * STEP + image, 1), :]
        for row in range(SIDE):
            here = of_row(image, row)
            pre = second_ref[here, :] * ab_ref[0:1, :] + ab_ref[1:2, :]
            act = pre * (sigmoid(pre) * wide(row_mask(place, row, limit), lanes))
            act = act * weights
            mixed = act[:, :half] + act[:, half:]
            low = mixed.astype(bf16)
            mixed_ref[here, :] = low
            sums[0] = sums[0] + fold(low.astype(f32))
            sums[1] = sums[1] + fold(mixed * mixed)

    def square(image):
        values = mixed_ref[of_image(image), :]
        gram_ref[...] += contract_lead(values, values)

    stages(mix, square)
    acc_ref[0], acc_ref[1] = sums

    @at_end
    def _():
        whole = out_ref[...].astype(f32)
        total = column_total(acc_ref[0])
        colsum_ref[...] = jnp.broadcast_to(total, colsum_ref.shape)
        power_ref[...] = lane_parts(acc_ref[1])
        gw = jnp.dot(gram_ref[...], whole, precision=HIGH, preferred_element_type=f32)
        gw_ref[...] = gw
        sums = jnp.dot(
            jnp.broadcast_to(total, (8, half)), whole, precision=HIGH, preferred_element_type=f32
        )
        put(tile_ref, 0, sums[0:1, :])
        put(tile_ref, whole.shape[1] // 128, column_total(gw * whole))
        send(send_ref, tile_ref)


def out_kernel(
    sides,
    mixed_ref,
    x_ref,
    cot_ref,
    recv_ref,
    param_ref,
    count_ref,
    w_ref,
    wt_ref,
    block_ref,
    slope_ref,
    back_ref,
    grad_ref,
    terms_ref,
    power_ref,
    send_ref,
    third_ref,
    acc_ref,
    square_ref,
    tile_ref,
    half_ref,
):
    step = pl.program_id(0)
    zeros_at_start(acc_ref, square_ref, grad_ref)
    place = places()
    lanes = x_ref.shape[1]
    part = 512 if lanes % 512 == 0 else lanes

    @at_start
    def _():
        take(recv_ref, tile_ref)
        count = count_ref[0:1, :]
        gain, shift = param_ref[0:1, :], param_ref[1:2, :]
        center, spread, inv, scale, offset = norm_rows(
            row_at(tile_ref, 0, lanes),
            row_at(tile_ref, lanes // 128, lanes),
            wide(count, lanes),
            gain,
            shift,
        )
        branch = gain * gain * spread * inv * inv + shift * shift
        terms_ref[0:1, :] = scale
        terms_ref[1:2, :] = offset
        terms_ref[2:3, :] = center
        terms_ref[3:4, :] = inv
        terms_ref[4:5, :] = 1.0 / scale
        terms_ref[5:6, :] = wide(lane_sum(branch), lanes)
        half_ref[0:1, :] = 0.5 * scale
        half_ref[1:2, :] = 0.5 * offset

    squares = [square_ref[...]]

    def expand(image):
        third_ref[of_image(image), :] = jnp.dot(
            mixed_ref[of_image(image), :], w_ref[...], preferred_element_type=f32
        )

    def finish(image):
        limit = 2 * sides[step * STEP + image]
        for row in range(SIDE):
            here = of_row(image, row)
            mask = wide(row_mask(place, row, limit), part)
            for at in range(0, lanes, part):
                cut = slice(at, at + part)
                half = (
                    (x_ref[here, cut] * bf16(0.5)).astype(f32)
                    + third_ref[here, cut] * half_ref[0:1, cut]
                    + half_ref[1:2, cut]
                )
                turned = jnp.tanh(half)
                gate = (1.0 + turned) * mask
                output = half * gate
                block_ref[here, cut] = output.astype(bf16)
                slope = gate + output * (1.0 - turned)
                grad = cot_ref[here, cut].astype(f32) * (slope * half_ref[0:1, cut])
                slope_ref[here, cut] = grad.astype(bf16)
                acc_ref[:, cut] += fold(grad)
                squares[0] = squares[0] + lane_parts(fold(output * output))

    def contract(image):
        here = of_image(image)
        back_ref[here, :] = jnp.dot(slope_ref[here, :], wt_ref[...], preferred_element_type=f32)
        grad_ref[...] += contract_lead(mixed_ref[here, :], slope_ref[here, :])

    stages(expand, finish, contract)
    square_ref[...] = squares[0]

    @at_end
    def _():
        power_ref[...] = square_ref[...]
        total = column_total(acc_ref[...])
        put(tile_ref, 0, total)
        turned = column_total(grad_ref[...] * w_ref[...].astype(f32))
        put(tile_ref, lanes // 128, turned - terms_ref[2:3, :] * total)
        send(send_ref, tile_ref)


def mid_terms(second_ref, ab_ref, here, mask):
    pre = second_ref[here, :] * ab_ref[0:1, :] + ab_ref[1:2, :]
    plain = sigmoid(pre)
    gate = plain * mask
    act = pre * gate
    return pre, act, gate + act * (1.0 - plain)


def gate_kernel(
    sides,
    second_ref,
    ab_ref,
    back_ref,
    mixed_ref,
    recv_ref,
    terms_ref,
    param_ref,
    count_ref,
    w_ref,
    wt_ref,
    weights_ref,
    excite_ref,
    squeeze_ref,
    gate_ref,
    up_ref,
    power_out_ref,
    power_mix_ref,
    dmixed_ref,
    sums_ref,
    dup_ref,
    dbias_ref,
    dq_ref,
    grads_ref,
    send_ref,
    turn_ref,
    row_ref,
    tile_ref,
):
    step = pl.program_id(0)
    place = places()
    lanes = second_ref.shape[1]
    half = lanes // 2
    width = w_ref.shape[1]

    @at_start
    def _():
        take(recv_ref, tile_ref)
        count = wide(count_ref[0:1, :], width)
        total = row_at(tile_ref, 0, width)
        scale, center, inv = terms_ref[0:1, :], terms_ref[2:3, :], terms_ref[3:4, :]
        gain_grad = row_at(tile_ref, width // 128, width) / param_ref[0:1, :]
        slant = scale * inv * gain_grad / count
        level = total / count - center * slant
        grads_ref[0:1, :] = total * terms_ref[4:5, :]
        grads_ref[1:2, :] = gain_grad
        grads_ref[2:3, :] = slant
        grads_ref[3:4, :] = level
        whole = w_ref[...].astype(f32)
        turn_ref[...] = jnp.dot(
            (whole * slant).astype(bf16), wt_ref[...], preferred_element_type=f32
        ).astype(bf16)
        row_ref[...] = jnp.dot(
            jnp.broadcast_to(level, (8, width)),
            wt_ref[...].astype(f32),
            precision=HIGH,
            preferred_element_type=f32,
        )

    def turn(image):
        here = of_image(image)
        dmixed_ref[here, :] = back_ref[here, :] - jnp.dot(
            mixed_ref[here, :], turn_ref[...], preferred_element_type=f32
        )

    def add_up(image):
        limit = 2 * sides[step * STEP + image]
        totals = [jnp.zeros((8, lanes), f32) for _ in range(5)]
        for row in range(SIDE):
            here = of_row(image, row)
            mask = row_mask(place, row, limit)
            dmixed = (dmixed_ref[here, :] - row_ref[0:1, :]) * wide(mask, half)
            dmixed_ref[here, :] = dmixed
            both = jnp.concatenate([dmixed, dmixed], axis=1)
            pre, act, slope = mid_terms(second_ref, ab_ref, here, wide(mask, lanes))
            along = slope * both
            terms = (act * both, along, along * pre, slope, slope * pre)
            totals = [old + fold(new) for old, new in zip(totals, terms)]
        for index in range(5):
            sums_ref[index, pl.ds(step * STEP + image, 1), :] = column_total(totals[index])

    stages(turn, add_up)

    @at_end
    def _():
        weights = weights_ref[...]
        grads = sums_ref[0]
        mean = weights * grads
        mean = mean[:, :half] + mean[:, half:]
        dlogits = weights * (grads - jnp.concatenate([mean, mean], axis=1))
        dbias_ref[...] = jnp.broadcast_to(column_total(dlogits), dbias_ref.shape)
        low = dlogits.astype(bf16)
        dup_ref[...] = contract_lead(low, excite_ref[...])
        dexcite = jnp.dot(low, up_ref[...], preferred_element_type=f32)
        squeeze = squeeze_ref[...]
        pre = squeeze * gate_ref[0:1, :] + gate_ref[1:2, :]
        normed = squeeze * gate_ref[2:3, :] + gate_ref[3:4, :]
        plain = sigmoid(pre)
        dq = dexcite * (plain * (1.0 + pre * (1.0 - plain)))
        dq_ref[...] = dq
        tile_ref[0:1, :] = column_total(dq)
        tile_ref[1:2, :] = column_total(dq * normed)
        tile_ref[2:3, :] = column_total(power_out_ref[...])
        tile_ref[3:4, :] = column_total(power_mix_ref[...])
        tile_ref[4:8, :] = jnp.zeros((4, 128), f32)
        tile = tile_ref[0:8, :]
        for j in range(send_ref.shape[0]):
            send_ref[j] = tile


def squeeze_kernel(
    images_all,
    width,
    sides,
    dq_ref,
    squeeze_ref,
    gate_ref,
    recv_ref,
    pooled_ref,
    down_ref,
    weights_ref,
    sums_ref,
    param_ref,
    count_ref,
    terms_ref,
    ddown_ref,
    dpool_ref,
    grads_ref,
    send_ref,
    tile_ref,
    area_ref,
):
    take(recv_ref, tile_ref)
    shift, gain = tile_ref[0:1, :], tile_ref[1:2, :]
    grads_ref[0:1, :] = shift
    grads_ref[1:2, :] = gain
    bottleneck = pooled_ref.shape[1]
    count = count_ref[0:1, :]
    powers = (
        lane_sum(gate_ref[4:5, :]) / (count * width),
        lane_sum(tile_ref[3:4, :]) / (count * bottleneck),
        terms_ref[5:6, :128] / width,
        lane_sum(tile_ref[2:3, :]) / (count * width),
    )
    place = lax.broadcasted_iota(jnp.int32, (1, 128), 1)
    norms = powers[3]
    for index in range(3):
        norms = jnp.where(place == index, powers[index], norms)
    grads_ref[2:3, :] = jnp.sqrt(norms)
    normed = squeeze_ref[...] * gate_ref[2:3, :] + gate_ref[3:4, :]
    dsqueeze = gate_ref[0:1, :] * (
        dq_ref[...] - (shift + normed * gain) / jnp.float32(images_all)
    )
    low = dsqueeze.astype(bf16)
    ddown_ref[...] = contract_lead(pooled_ref[...], low)
    for image in range(area_ref.shape[0]):
        area = 4 * sides[image] * sides[image]
        area_ref[image : image + 1, :] = jnp.full((1, bottleneck), area, jnp.int32).astype(f32)
    dpool = contract_last(low, down_ref[...]) / area_ref[...]
    dpool_ref[...] = dpool
    both = jnp.concatenate([dpool, dpool], axis=1)
    weights = weights_ref[...]
    total = column_total(weights * sums_ref[1] + both * sums_ref[3])
    product = column_total(weights * sums_ref[2] + both * sums_ref[4])
    lanes = weights.shape[1]
    put(tile_ref, 0, total)
    put(tile_ref, lanes // 128, (product - param_ref[1:2, :] * total) / param_ref[0:1, :])
    send(send_ref, tile_ref)


def conv_back_kernel(
    sides,
    second_ref,
    ab_ref,
    recv_ref,
    param_ref,
    count_ref,
    dmixed_ref,
    weights_ref,
    dpool_ref,
    first_ref,
    ab_in_ref,
    w_ref,
    dsecond_ref,
    dfirst_ref,
    grads_ref,
    stat_ref,
    column_ref,
    acc_ref,
    tile_ref,
):
    step = pl.program_id(0)
    zeros_at_start(acc_ref, column_ref)
    place = places()
    lanes = second_ref.shape[1]
    half = lanes // 2
    quarter = half // RADIX
    columns = TAPS * quarter

    @at_start
    def _():
        take(recv_ref, tile_ref)
        total = row_at(tile_ref, 0, lanes)
        product = row_at(tile_ref, lanes // 128, lanes)
        count = wide(count_ref[0:1, :], lanes)
        slant = ab_ref[0:1, :] * product / (count * param_ref[0:1, :])
        grads_ref[0:1, :] = total
        grads_ref[1:2, :] = product
        grads_ref[2:3, :] = slant
        grads_ref[3:4, :] = ab_ref[0:1, :] * total / count - param_ref[1:2, :] * slant

    def start(image):
        limit = 2 * sides[step * STEP + image]
        weights = weights_ref[pl.ds(step * STEP + image, 1), :] * ab_ref[0:1, :]
        dpool = dpool_ref[pl.ds(step * STEP + image, 1), :]
        dpool = jnp.concatenate([dpool, dpool], axis=1) * ab_ref[0:1, :]
        for row in range(SIDE):
            here = of_row(image, row)
            mask = wide(row_mask(place, row, limit), lanes)
            dmixed = dmixed_ref[here, :]
            both = jnp.concatenate([dmixed, dmixed], axis=1)
            pre = second_ref[here, :] * ab_ref[0:1, :] + ab_ref[1:2, :]
            plain = sigmoid(pre)
            slope = plain + pre * plain * (1.0 - plain)
            grad = slope * (weights * both + dpool)
            grad = mask * (grad - (pre * grads_ref[2:3, :] + grads_ref[3:4, :]))
            dsecond_ref[here, :] = grad.astype(bf16)

    def multiply(image):
        for group in range(RADIX):
            column_ref[image, SIDE : SIDE + 256, group * columns : (group + 1) * columns] = jnp.dot(
                dsecond_ref[of_image(image), group * half : (group + 1) * half],
                w_ref[:, group * columns : (group + 1) * columns],
                preferred_element_type=f32,
            )

    sums = [acc_ref[0], acc_ref[1]]
    inner = wide(place, quarter)

    def finish(image):
        limit = 2 * sides[step * STEP + image]
        for row in range(SIDE):
            here = of_row(image, row)
            mask = row_mask(place, row, limit)
            parts = []
            for group in range(RADIX):
                summed = []
                for side in range(3):
                    pieces = []
                    for up in range(3):
                        at = group * columns + (up * 3 + side) * quarter
                        start_row = (row + 2 - up) * SIDE
                        pieces.append(
                            column_ref[image, start_row : start_row + SIDE, at : at + quarter]
                        )
                    summed.append(pieces[0] + pieces[1] + pieces[2])
                low = jnp.where(inner == SIDE - 1, 0.0, pltpu.roll(summed[0], SIDE - 1, 0))
                high = jnp.where(inner == 0, 0.0, pltpu.roll(summed[2], 1, 0))
                parts.append(summed[1] + low + high)
            dact = jnp.concatenate(parts, axis=1)
            first = first_ref[here, :]
            pre = first * ab_in_ref[0:1, :] + ab_in_ref[1:2, :]
            normed = first * ab_in_ref[2:3, :] + ab_in_ref[3:4, :]
            plain = sigmoid(pre)
            grad = dact * (plain * (1.0 + pre * (1.0 - plain)) * wide(mask, half))
            dfirst_ref[here, :] = grad
            sums[0] = sums[0] + fold(grad)
            sums[1] = sums[1] + fold(grad * normed)

    stages(start, multiply, finish)
    acc_ref[0], acc_ref[1] = sums

    @at_end
    def _():
        stat_ref[...] = jnp.zeros(stat_ref.shape, f32)
        put(stat_ref, 0, column_total(acc_ref[0]))
        put(stat_ref, half // 128, column_total(acc_ref[1]))


def conv_grad_kernel(aligned, odd, act_ref, dsecond_ref, x_ref, dfirst_ref, _, in_ref, *refs):
    if aligned:
        mine_ref, other_ref, conv_ref, patch_ref = refs
    else:
        conv_ref, patch_ref = refs
    zeros_at_start(conv_ref, in_ref, patch_ref)
    place = places()
    lanes = act_ref.shape[1]
    columns = TAPS * lanes // RADIX
    def start(image):
        for row in range(SIDE):
            write_patches(patch_ref, image, row, act_ref[of_row(image, row), :], place)

    def multiply(image):
        here = of_image(image)
        for group in range(RADIX):
            conv_ref[:, group * columns : (group + 1) * columns] += contract_lead(
                dsecond_ref[here, group * lanes : (group + 1) * lanes],
                patch_ref[image, SIDE : SIDE + 256, group * columns : (group + 1) * columns],
            )

    stages(start, multiply)
    in_ref[...] += contract_lead(dfirst_ref[...].astype(bf16), x_ref[...])

    if aligned:

        @at_end
        def _():
            for piece in range(mine_ref.shape[0]):
                for ref, side in ((mine_ref, odd[0]), (other_ref, 1 - odd[0])):
                    here = pl.ds(pl.multiple_of((2 * piece + side) * 8, 8), 8)
                    for pair in range(RADIX * TAPS // 2):
                        two = [
                            conv_ref[here, (2 * pair + k) * 128 : (2 * pair + k + 1) * 128]
                            for k in range(2)
                        ]
                        ref[piece, pair * 16 : pair * 16 + 16, :] = jnp.concatenate(
                            two, axis=0
                        ).astype(bf16)


def late_kernel(
    aligned, odd, recv_ref, terms_ref, count_ref, in_ref, cross_ref, ones_ref, grads_ref, *refs
):
    tile_ref = refs[-1]
    take(recv_ref, tile_ref)
    lanes = terms_ref.shape[1]
    total = row_at(tile_ref, 0, lanes)
    product = row_at(tile_ref, lanes // 128, lanes)
    count = wide(count_ref[0:1, :], lanes)
    slant = terms_ref[0:1, :] * terms_ref[2:3, :] * product / count
    level = terms_ref[0:1, :] * total / count - terms_ref[4:5, :] * slant
    grads_ref[0:1, :] = total
    grads_ref[1:2, :] = product
    grads_ref[2:3, :] = slant
    grads_ref[3:4, :] = level
    grads_ref[4:5, :] = terms_ref[0:1, :]
    grads_ref[5:8, :] = jnp.zeros((3, lanes), f32)
    if not aligned:
        return
    mine_ref, other_ref, full_ref, _ = refs
    columns = jnp.transpose(grads_ref[...])
    ones = column_total(ones_ref[...])
    full_ref[...] = (
        in_ref[...] * columns[:, 4:5]
        - cross_ref[...] * columns[:, 2:3]
        - ones * columns[:, 3:4]
    )
    rows = mine_ref.shape[1]
    groups = lanes // rows
    for piece in range(mine_ref.shape[0]):
        owner, pair = 2 * piece // groups, piece % (groups // 2)
        for ref, side in ((mine_ref, odd[0]), (other_ref, 1 - odd[0])):
            here = pl.ds(pl.multiple_of((2 * pair + side) * rows, rows), rows)
            ref[piece] = full_ref[here, owner * 128 : (owner + 1) * 128].astype(bf16)


def merge_kernel(mid_ref, mid_got_ref, in_ref, in_got_ref, out_ref):
    cut = in_ref.shape[1]
    for piece in range(out_ref.shape[0]):
        out_ref[piece, :cut, :] = (
            in_ref[piece].astype(f32) + in_got_ref[piece].astype(f32)
        ).astype(bf16)
        out_ref[piece, cut:, :] = (
            mid_ref[piece].astype(f32) + mid_got_ref[piece].astype(f32)
        ).astype(bf16)


def last_kernel(
    sides, dfirst_ref, first_ref, grads_ref, w_ref, slope_ref, terms_ref, out_ref, done_ref, low_ref
):
    step = pl.program_id(0)
    place = places()
    lanes = first_ref.shape[1]
    width = out_ref.shape[1]
    part = 512 if width % 512 == 0 else width
    def start(image):
        limit = 2 * sides[step * STEP + image]
        for row in range(SIDE):
            here = of_row(image, row)
            mask = wide(row_mask(place, row, limit), lanes)
            grad = dfirst_ref[here, :] * grads_ref[4:5, :]
            grad = grad - mask * (first_ref[here, :] * grads_ref[2:3, :] + grads_ref[3:4, :])
            low_ref[here, :] = grad.astype(bf16)

    def multiply(image):
        here = of_image(image)
        out_ref[here, :] = contract_last(low_ref[here, :], w_ref[...])

    def finish(image):
        for row in range(SIDE):
            here = of_row(image, row)
            for at in range(0, width, part):
                cut = slice(at, at + part)
                out_ref[here, cut] += slope_ref[here, cut].astype(f32) * terms_ref[4:5, cut]

    stages(start, multiply, finish)

    @at_end
    def _():
        done_ref[...] = jnp.zeros(done_ref.shape, f32)


def total_of(ref):
    total = ref[0].astype(f32)
    for j in range(1, ref.shape[0]):
        total = total + ref[j].astype(f32)
    return total.astype(bf16)


def total_kernel(part_ref, tile_ref, sum_ref, send_ref):
    sum_ref[...] = total_of(part_ref)
    send(send_ref, tile_ref)


def total_last_kernel(one_ref, part_ref, _, sum_ref):
    cut = one_ref.shape[0]
    sum_ref[:cut, :] = one_ref[...]
    sum_ref[cut:, :] = total_of(part_ref)


def shards_kernel(
    marks, place, *refs
):
    groups = len(refs) - 7
    out_ref, up_ref, down_ref, bias_ref, in_ref, mid_ref, all_ref = refs[groups:]
    for k in range(groups):
        all_ref[place[0] ^ k] = refs[k][...].astype(f32)

    def rows_from(start, count):
        return jnp.concatenate([all_ref[k, start : start + count, :] for k in range(groups)], axis=0)

    at = 0
    out_ref[...] = rows_from(at, marks[0])
    at += marks[0]
    up_ref[...] = rows_from(at, marks[1])
    at += marks[1]
    down_ref[...] = rows_from(at, marks[2])
    at += marks[2]
    bias_ref[...] = all_ref[0, at : at + 8, :]
    at = marks[3]
    in_ref[...] = jnp.transpose(rows_from(at, marks[4]))
    at += marks[4]
    for tap in range(RADIX * TAPS):
        mid_ref[tap] = rows_from(at + tap * 8, 8)


def tiles(lanes, block=0):
    return pl.BlockSpec((STEP * 256, lanes), lambda i: (i, block))


def held(*shape):
    return pl.BlockSpec(shape, lambda i: (0,) * len(shape))


def token():
    return pl.BlockSpec(memory_space=pl.ANY)


def scalars():
    return pl.BlockSpec(memory_space=pltpu.SMEM)


def shaped(shape, dtype=f32):
    return jax.ShapeDtypeStruct(shape, dtype)


def call(kernel, steps, ins, outs, scratch=(), cost=5, limit=56, name=None):
    return pl.pallas_call(
        kernel,
        grid=(steps,),
        in_specs=ins,
        out_specs=[spec for spec, _ in outs],
        out_shape=[shape for _, shape in outs],
        scratch_shapes=[pltpu.VMEM(shape, dtype) for shape, dtype in scratch],
        compiler_params=pltpu.CompilerParams(
            dimension_semantics=("arbitrary",), vmem_limit_bytes=limit * 1024 * 1024
        ),
        cost_estimate=pl.CostEstimate(
            flops=int(cost * 1e9), bytes_accessed=int(cost * 3e6), transcendentals=0
        ),
        name=name,
    )


def whole_out(shape, dtype=f32):
    return held(*shape), shaped(shape, dtype)


def rows8(*vectors):
    stacked = jnp.stack(vectors, axis=0)
    return jnp.pad(stacked, ((0, 8 - len(vectors)), (0, 0)))


def local(
    features,
    half_sides,
    cotangent,
    conv_in,
    conv_mid,
    attn_down,
    attn_up,
    attn_bias,
    conv_out,
    gain_in,
    shift_in,
    gain_mid,
    shift_mid,
    gain_attn,
    shift_attn,
    gain_out,
    shift_out,
):
    images, pixels, width = features.shape
    rows = images * pixels
    steps = images // STEP
    pieces = lax.axis_size("fsdp")
    groups = lax.axis_size("dp")
    devices = pieces * groups
    images_all = images * devices
    bottleneck = conv_in.shape[1]
    att = attn_down.shape[1]
    mid = RADIX * bottleneck
    columns = TAPS * conv_mid.shape[2]
    odd = lax.rem(lax.axis_index("dp"), 2).reshape(1)

    down_rows, up_rows = attn_down.shape[0], attn_up.shape[1]
    own_columns = conv_mid.shape[3]
    small = [gain_in, shift_in, gain_mid, shift_mid, gain_attn, shift_attn, gain_out, shift_out, attn_bias]
    lengths = [item.shape[0] for item in small]
    aligned = (
        own_columns % 16 == 0
        and width == 128 * pieces
        and bottleneck == 8 * devices
        and groups == 4
        and pieces == len(ORDER)
    )
    mid_cut = conv_mid.transpose(0, 1, 3, 2)
    if aligned:
        place = lax.axis_index("fsdp").reshape(1)
        at = TAPS * own_columns
        cut = (at + 128 + down_rows + up_rows + 16, 128)
        in_send, most = call(
            prepare_kernel,
            1,
            [
                scalars(),
                held(*conv_in.shape),
                held(RADIX, at, 128),
                held(*attn_down.shape),
                held(up_rows, att),
                held(*conv_out.shape),
            ]
            + [held(1, length) for length in lengths],
            [
                whole_out((pieces, conv_in.shape[0], 128), bf16),
                whole_out(cut, bf16),
            ],
            [((16, 128), f32)],
            2,
            name="last_prepare",
        )(
            odd,
            conv_in,
            mid_cut.reshape(RADIX, at, 128),
            attn_down,
            attn_up.T,
            conv_out,
            *[item.reshape(1, -1) for item in small],
        )
        in_mine = swap_all(in_send, "fsdp").reshape(width, bottleneck // 2)
        in_other = neighbour(in_mine)

        most = most[None]
        most = jnp.concatenate([most, partner(most, 4)], axis=0)
        most = jnp.concatenate([most, partner(most, 2)], axis=0)
        shards = [most, partner(most, 1)]
        shards += [neighbour(item) for item in shards]
    else:
        in_send = jnp.broadcast_to(half_of(conv_in, 1)[None], (pieces, conv_in.shape[0], 128))
        vectors = jnp.stack([jnp.pad(item, (0, 128 - item.shape[0])) for item in small])
        most = jnp.concatenate([mid_cut.reshape(-1, 128), attn_down, attn_up.T, vectors], axis=0)
        most = lax.all_gather(most, "fsdp")
        at = RADIX * TAPS * own_columns
        in_mine = swap_all(in_send, "fsdp").reshape(width, bottleneck // 2)
        in_other = neighbour(in_mine)
        whole_down = most[:, at : at + down_rows].reshape(bottleneck, att)
        whole_up = most[:, at + down_rows : at + down_rows + up_rows].reshape(mid, att)

    x = features.reshape(rows, width)
    cot = cotangent.reshape(rows, width)

    def tiled(lanes, dtype=f32):
        return tiles(lanes), shaped((rows, lanes), dtype)

    def sending(count, dtype=f32):
        return whole_out((devices, count, 128), dtype)

    def received(count):
        return held(devices, count, 128)

    first, whole_in, out = call(
        first_kernel,
        steps,
        [scalars(), scalars(), tiles(width), held(width, bottleneck // 2), held(width, bottleneck // 2)],
        [tiled(bottleneck), whole_out((width, bottleneck), bf16), sending(8)],
        [((2, 8, bottleneck), f32), ((8, 128), f32)],
        8,
        name="first",
    )(half_sides, odd, x, in_mine, in_other)
    got = swap_all(out, AXES)
    cross, x_sum, power_x = call(
        cross_kernel,
        steps,
        [scalars(), tiles(width), tiles(bottleneck)],
        [
            whole_out((bottleneck, width)),
            whole_out((8, width)),
            whole_out((8, 128)),
        ],
        [((8, width), f32)],
        10,
        name="cross",
    )(half_sides, x, first)

    ins = [scalars(), tiles(bottleneck), received(8), token()]
    args = (half_sides, first, got, power_x)
    outs = [
        tiled(bottleneck, bf16),
        tiled(mid),
        whole_out((8, bottleneck)),
        whole_out((8, 128)),
        sending(8),
    ]
    scratch = [
        ((STEP, 256 + 2 * SIDE, RADIX * columns), bf16),
        ((2, 8, mid), f32),
        ((8, 128), f32),
    ]
    if aligned:
        ins += [scalars(), scalars()] + [held(*item.shape) for item in shards]
        args += (place, odd) + tuple(shards)
        outs += [whole_out((bottleneck, RADIX * columns), bf16)]
        outs += [whole_out((bottleneck, att), bf16), whole_out((mid, att), bf16)]
        outs += [whole_out((8, lanes)) for lanes in (mid, att, width, mid)]
        scratch += [((8, bottleneck), f32)]
    else:
        whole_mid = most[:, :at].reshape(pieces, RADIX * TAPS, own_columns, 128)
        whole_mid = whole_mid.transpose(0, 2, 1, 3).reshape(bottleneck, RADIX * columns)
        at += down_rows + up_rows
        found = [
            most[:, at + k, :length].reshape(-1).astype(f32) for k, length in enumerate(lengths)
        ]
        p_in, p_mid, p_attn, p_out = [rows8(found[2 * k], found[2 * k + 1]) for k in range(4)]
        p_bias = rows8(found[8])
        ins += [held(bottleneck, RADIX * columns), held(8, bottleneck)]
        args += (whole_mid, p_in)
    act_low, second, terms_in, count, out, *rest = call(
        functools.partial(second_kernel, lengths if aligned else None),
        steps,
        ins,
        outs,
        scratch,
        15,
        name="second",
    )(*args)
    if aligned:
        whole_mid, whole_down, whole_up, p_mid, p_attn, p_out, p_bias = rest
    got = swap_all(out, AXES)

    pooled, squeeze, terms_mid, out = call(
        pool_kernel,
        steps,
        [
            scalars(),
            tiles(mid),
            received(8),
            held(8, mid),
            held(8, 128),
            held(bottleneck, att),
            held(8, 128),
        ],
        [
            whole_out((images, bottleneck), bf16),
            whole_out((images, att)),
            whole_out((8, mid)),
            sending(8),
        ],
        [((images, bottleneck), f32), ((8, 128), f32)],
        7,
        name="pool",
    )(half_sides, second, got, p_mid, count, whole_down, power_x)
    got = swap_all(out, AXES)

    if aligned:
        whole_w_out, whole_out_t = call(
            functools.partial(out_weights_kernel, TAPS * own_columns),
            1,
            [scalars(), scalars(), token()] + [held(*item.shape) for item in shards],
            [whole_out((bottleneck, width), bf16), whole_out((width, bottleneck), bf16)],
            (),
            1,
            name="last_weights",
        )(place, odd, pooled, *shards)
    else:
        whole_w_out = lax.all_gather(conv_out, "fsdp", axis=1, tiled=True)
        whole_out_t = whole_w_out.T
    wide_rows = 2 * width // 128
    mixed, weights, excite, gate, gram_out, colsum, power_mix, out = call(
        functools.partial(mix_kernel, images_all),
        steps,
        [
            scalars(),
            tiles(mid),
            held(8, mid),
            held(images, att),
            received(8),
            held(8, att),
            held(mid, att),
            held(8, mid),
            held(bottleneck, width),
        ],
        [
            tiled(bottleneck, bf16),
            whole_out((images, mid)),
            whole_out((images, att), bf16),
            whole_out((8, att)),
            whole_out((bottleneck, width)),
            whole_out((8, bottleneck)),
            whole_out((8, 128)),
            sending(wide_rows),
        ],
        [((bottleneck, bottleneck), f32), ((2, 8, bottleneck), f32), ((wide_rows, 128), f32)],
        11,
        name="mix",
    )(half_sides, second, terms_mid, squeeze, got, p_attn, whole_up, p_bias, whole_w_out)
    got = swap_all(out, AXES)

    block, slope, back, grad_out, terms_out, power_out, out = call(
        out_kernel,
        steps,
        [
            scalars(),
            tiles(bottleneck),
            tiles(width),
            tiles(width),
            received(wide_rows),
            held(8, width),
            held(8, 128),
            held(bottleneck, width),
            held(width, bottleneck),
        ],
        [
            tiled(width, bf16),
            tiled(width, bf16),
            tiled(bottleneck),
            whole_out((bottleneck, width)),
            whole_out((8, width)),
            whole_out((8, 128)),
            sending(wide_rows, bf16),
        ],
        [
            ((STEP * 256, width), f32),
            ((8, width), f32),
            ((8, 128), f32),
            ((wide_rows, 128), f32),
            ((8, width), f32),
        ],
        25,
        name="output",
    )(half_sides, mixed, x, cot, got, p_out, count, whole_w_out, whole_out_t)
    got = swap_all(out, AXES)

    dmixed, sums, dup, dbias, dq, grads_out, out = call(
        gate_kernel,
        steps,
        [
            scalars(),
            tiles(mid),
            held(8, mid),
            tiles(bottleneck),
            tiles(bottleneck),
            received(wide_rows),
            held(8, width),
            held(8, width),
            held(8, 128),
            held(bottleneck, width),
            held(width, bottleneck),
            held(images, mid),
            held(images, att),
            held(images, att),
            held(8, att),
            held(mid, att),
            held(8, 128),
            held(8, 128),
        ],
        [
            tiled(bottleneck),
            whole_out((5, images, mid)),
            whole_out((mid, att)),
            whole_out((8, mid)),
            whole_out((images, att)),
            whole_out((8, width)),
            sending(8),
        ],
        [
            ((bottleneck, bottleneck), bf16),
            ((8, bottleneck), f32),
            ((wide_rows, 128), f32),
        ],
        13,
        name="gate",
    )(
        half_sides,
        second,
        terms_mid,
        back,
        mixed,
        got,
        terms_out,
        p_out,
        count,
        whole_w_out,
        whole_out_t,
        weights,
        excite,
        squeeze,
        gate,
        whole_up,
        power_out,
        power_mix,
    )
    got = swap_all(out, AXES)
    grad_conv_out = grad_out - colsum[0][:, None] * grads_out[3] - gram_out * grads_out[2]

    ddown, dpool, grads_attn, out = call(
        functools.partial(squeeze_kernel, images_all, width),
        1,
        [
            scalars(),
            held(images, att),
            held(images, att),
            held(8, att),
            received(8),
            held(images, bottleneck),
            held(bottleneck, att),
            held(images, mid),
            held(5, images, mid),
            held(8, mid),
            held(8, 128),
            held(8, width),
        ],
        [
            whole_out((bottleneck, att)),
            whole_out((images, bottleneck)),
            whole_out((8, att)),
            sending(8),
        ],
        [((8, 128), f32), ((images, bottleneck), f32)],
        1,
        name="squeeze",
    )(
        half_sides,
        dq,
        squeeze,
        gate,
        got,
        pooled,
        whole_down,
        weights,
        sums,
        p_mid,
        count,
        terms_out,
    )
    got = swap_all(out, AXES)

    out_cut = grad_conv_out.astype(bf16).reshape(bottleneck, pieces, -1).transpose(1, 0, 2)
    out_cut = out_cut.reshape(devices, -1, 128)
    bias_rows = jnp.pad(dbias[0].reshape(pieces, 1, up_rows), ((0, 0), (0, 0), (0, att - up_rows)))
    gates = jnp.concatenate(
        [
            dup.reshape(devices, -1, att),
            ddown.reshape(devices, -1, att),
            jnp.repeat(bias_rows, groups, axis=0),
        ],
        axis=1,
    ).astype(bf16)
    marks = [out_cut.shape[1], up_rows // groups, down_rows // groups]
    gates = jnp.concatenate([out_cut, gates], axis=1)
    gates = jnp.pad(gates, ((0, 0), (0, -gates.shape[1] % 16), (0, 0)))

    gates = swap_all(gates, AXES)
    dsecond, dfirst, grads_mid, stat = call(
        conv_back_kernel,
        steps,
        [
            scalars(),
            tiles(mid),
            held(8, mid),
            received(8),
            held(8, mid),
            held(8, 128),
            tiles(bottleneck),
            held(images, mid),
            held(images, bottleneck),
            tiles(bottleneck),
            held(8, bottleneck),
            held(bottleneck, RADIX * columns),
        ],
        [tiled(mid, bf16), tiled(bottleneck), whole_out((8, mid)), whole_out((8, 128))],
        [
            ((STEP, 256 + 2 * SIDE, RADIX * columns), f32),
            ((2, 8, bottleneck), f32),
            ((8, 128), f32),
        ],
        20,
        name="conv_back",
    )(
        half_sides,
        second,
        terms_mid,
        got,
        p_mid,
        count,
        dmixed,
        weights,
        dpool,
        first,
        terms_in,
        whole_mid,
    )
    gates, out = call(
        total_kernel,
        1,
        [held(*gates.shape), held(8, 128)],
        [whole_out(gates.shape[1:], bf16), sending(8)],
        (),
        2,
        name="last_gates",
    )(gates, stat)
    got = swap_all(out, AXES)

    outs = [whole_out((bottleneck, width))]
    scratch = [((STEP, 256 + 2 * SIDE, RADIX * columns), bf16)]
    mid_rows = bottleneck // devices * RADIX * TAPS
    if aligned:
        outs += [whole_out((devices // 2, mid_rows, 128), bf16)] * 2
        scratch = [((bottleneck, RADIX * columns), f32)] + scratch
    else:
        outs += [whole_out((bottleneck, RADIX * columns))]
    in_grad, *conv_parts = call(
        functools.partial(conv_grad_kernel, aligned),
        steps,
        [scalars(), tiles(bottleneck), tiles(mid), tiles(width), tiles(bottleneck), token()],
        outs,
        scratch,
        15,
        name="conv_grad",
    )(odd, act_low, dsecond, x, dfirst, gates)
    outs = [whole_out((8, bottleneck))]
    scratch = [((8, 128), f32)]
    in_rows = bottleneck // groups * (width // pieces) // 128
    if aligned:
        outs += [whole_out((devices // 2, in_rows, 128), bf16)] * 2
        scratch = [((bottleneck, width), f32)] + scratch
    grads_in, *in_parts = call(
        functools.partial(late_kernel, aligned),
        1,
        [
            scalars(),
            received(8),
            held(8, bottleneck),
            held(8, 128),
            held(bottleneck, width),
            held(bottleneck, width),
            held(8, width),
        ],
        outs,
        scratch,
        2,
        name="last_terms",
    )(odd, got, terms_in, count, in_grad, cross, x_sum)
    grad_features, done = call(
        last_kernel,
        steps,
        [
            scalars(),
            tiles(bottleneck),
            tiles(bottleneck),
            held(8, bottleneck),
            held(width, bottleneck),
            tiles(width),
            held(8, width),
        ],
        [tiled(width), whole_out((8, 128))],
        [((STEP * 256, bottleneck), bf16)],
        15,
        name="last",
    )(half_sides, dfirst, first, grads_in, whole_in, slope, terms_out)

    if aligned:
        mid_got, in_got = neighbour(conv_parts[1]), neighbour(in_parts[1])
        (late,) = call(
            merge_kernel,
            1,
            [held(*mid_got.shape)] * 2 + [held(*in_got.shape)] * 2,
            [whole_out((devices // 2, in_rows + mid_rows, 128), bf16)],
            (),
            2,
            name="last_merge",
        )(conv_parts[0], mid_got, in_parts[0], in_got)
    else:
        grad_conv_in = (
            in_grad * grads_in[4][:, None]
            - cross * grads_in[2][:, None]
            - column_total(x_sum) * grads_in[3][:, None]
        )
        in_cut = grad_conv_in.astype(bf16).reshape(bottleneck, pieces, -1).transpose(1, 0, 2)
        mid_cut = conv_parts[0].astype(bf16).reshape(devices, -1, RADIX * TAPS, 128)
        mid_cut = mid_cut.transpose(0, 2, 1, 3).reshape(devices, -1, 128)
        late = jnp.concatenate([in_cut.reshape(devices, -1, 128), mid_cut], axis=1)
        late = jnp.pad(late, ((0, 0), (0, -late.shape[1] % 16), (0, 0)))
        late = late.reshape(devices // 2, 2, -1, 128)
        mine = lax.dynamic_index_in_dim(late, odd[0], 1, False)
        other = lax.dynamic_index_in_dim(late, 1 - odd[0], 1, False)
        late = (mine.astype(f32) + neighbour(other).astype(f32)).astype(bf16)
    sides_of = [[2 * i + side for i in range(devices // 2)] for side in range(2)]
    late = lax.all_to_all(late, AXES, 0, 0, axis_index_groups=sides_of)
    (summed,) = call(
        total_last_kernel,
        1,
        [held(*gates.shape), held(*late.shape), token()],
        [whole_out((gates.shape[0] + late.shape[1], 128), bf16)],
        (),
        2,
        name="last_total",
    )(gates, late, done)
    marks += [gates.shape[0], in_rows]
    own_width = width // pieces
    if aligned:
        members = [summed] + [
            lax.ppermute(summed, "dp", [(i, i ^ k) for i in range(groups)])
            for k in range(1, groups)
        ]
        shard_out, shard_up, shard_down, shard_bias, shard_in, shard_mid = call(
            functools.partial(shards_kernel, marks),
            1,
            [scalars()] + [held(*summed.shape)] * groups,
            [
                whole_out((bottleneck, own_width)),
                whole_out((up_rows, att)),
                whole_out((down_rows, att)),
                whole_out((8, 128)),
                whole_out((own_width, bottleneck)),
                whole_out((RADIX * TAPS, own_columns, 128)),
            ],
            [((groups,) + summed.shape, f32)],
            2,
            name="last_shards",
        )(lax.axis_index("dp").reshape(1), *members)
        shard_bias = shard_bias[0, :up_rows]
        shard_up = shard_up.T
        shard_mid = shard_mid.reshape(RADIX, TAPS, own_columns, 128).transpose(0, 1, 3, 2)
    else:
        summed = swap_all(jnp.broadcast_to(summed[None], (groups,) + summed.shape), "dp")
        summed = summed.astype(f32)
        shard_out = summed[:, : marks[0]].reshape(bottleneck, -1)
        at = marks[0]
        shard_up = summed[:, at : at + marks[1]].reshape(up_rows, att).T
        at += marks[1]
        shard_down = summed[:, at : at + marks[2]].reshape(down_rows, att)
        at += marks[2]
        shard_bias = summed[0, at, :up_rows]
        at = marks[3]
        shard_in = summed[:, at : at + in_rows].reshape(bottleneck, -1).T
        at += in_rows
        shard_mid = summed[:, at : at + mid_rows].reshape(groups, RADIX, TAPS, -1, 128)
        shard_mid = shard_mid.transpose(1, 2, 4, 0, 3).reshape(RADIX, TAPS, 128, own_columns)

    def own_part(row):
        length = row.shape[0] // pieces
        return lax.dynamic_slice_in_dim(row, lax.axis_index("fsdp") * length, length, 0)

    return (
        block.reshape(images, pixels, width),
        grad_features.reshape(images, pixels, width),
        grads_attn[2, :4],
        shard_in,
        shard_mid,
        shard_down,
        shard_up,
        shard_bias,
        shard_out,
        own_part(grads_in[1]),
        own_part(grads_in[0]),
        own_part(grads_mid[1]),
        own_part(grads_mid[0]),
        own_part(grads_attn[1]),
        own_part(grads_attn[0]),
        own_part(grads_out[1]),
        own_part(grads_out[0]),
    )


def solution(mesh):
    return jax.shard_map(
        local,
        mesh=mesh,
        in_specs=(
            P(("fsdp", "dp"), None, None),
            P(("fsdp", "dp")),
            P(("fsdp", "dp"), None, None),
            P("fsdp", None),
            P(None, None, None, "fsdp"),
            P("fsdp", None),
            P(None, "fsdp"),
            P("fsdp"),
            P(None, "fsdp"),
            P("fsdp"),
            P("fsdp"),
            P("fsdp"),
            P("fsdp"),
            P("fsdp"),
            P("fsdp"),
            P("fsdp"),
            P("fsdp"),
        ),
        out_specs=(
            P(("fsdp", "dp"), None, None),
            P(("fsdp", "dp"), None, None),
            P(),
            P("fsdp", None),
            P(None, None, None, "fsdp"),
            P("fsdp", None),
            P(None, "fsdp"),
            P("fsdp"),
            P(None, "fsdp"),
            P("fsdp"),
            P("fsdp"),
            P("fsdp"),
            P("fsdp"),
            P("fsdp"),
            P("fsdp"),
            P("fsdp"),
            P("fsdp"),
        ),
        check_vma=False,
    )
```

```python
import functools

import jax
import jax.numpy as jnp
from jax import lax
from jax.experimental import pallas as pl
from jax.experimental.pallas import tpu as pltpu
from jax.sharding import PartitionSpec as P

RADIX = 2
SIDE = 16
TAPS = 9
STEP = 4

epsilon = 1e-05
AXES = ("fsdp", "dp")
f32 = jnp.float32
bf16 = jnp.bfloat16
HIGH = lax.Precision.HIGHEST


def swap_all(values, axes):
    return lax.all_to_all(values, axes, 0, 0)


def gather_all(shard):
    pieces = lax.axis_size("fsdp")
    return swap_all(jnp.broadcast_to(shard[None], (pieces,) + shard.shape), "fsdp")


def neighbour(values):
    return lax.ppermute(values, "dp", [(i, i ^ 1) for i in range(lax.axis_size("dp"))])


ORDER = (0, 4, 2, 6, 1, 5, 3, 7)


def partner(values, k):
    pieces = lax.axis_size("fsdp")
    return lax.ppermute(values, "fsdp", [(i, i ^ k) for i in range(pieces)])


def on_own_side(parts):
    odd = lax.rem(lax.axis_index("dp"), 2)
    parts = parts.reshape((parts.shape[0] // 2, 2) + parts.shape[1:])
    mine = lax.dynamic_index_in_dim(parts, odd, 1, False)
    other = lax.dynamic_index_in_dim(parts, 1 - odd, 1, False)
    return (mine.astype(f32) + neighbour(other).astype(f32)).astype(bf16)


def across_sides(parts):
    count = parts.shape[0]
    sides = [[2 * i + side for i in range(count)] for side in range(2)]
    return lax.all_to_all(parts, AXES, 0, 0, axis_index_groups=sides)


def to_owners(parts):
    return across_sides(on_own_side(parts))


def half_of(shard, axis):
    odd = lax.rem(lax.axis_index("dp"), 2)
    return lax.dynamic_slice_in_dim(shard, odd * (shard.shape[axis] // 2), shard.shape[axis] // 2, axis)


def sigmoid(values):
    return 0.5 * jnp.tanh(0.5 * values) + 0.5


def fold(values):
    return values[:8] + values[8:]


def wide(mask, lanes):
    return jnp.concatenate([mask] * (lanes // mask.shape[1]), axis=1)


def places():
    return lax.broadcasted_iota(jnp.int32, (SIDE, 128), 0)


def row_mask(place, row, limit):
    return jnp.where((place < limit) & (row < limit), 1.0, 0.0).astype(f32)


def chunk(image, row):
    return pl.ds(pl.multiple_of(image * 256 + row * SIDE, SIDE), SIDE)


def of_image(image):
    return slice(image * 256, image * 256 + 256)


def of_row(image, row):
    return slice(image * 256 + row * SIDE, image * 256 + row * SIDE + SIDE)


def stages(*parts):
    for stage in range(STEP + len(parts) - 1):
        for late, part in reversed(list(enumerate(parts))):
            if 0 <= stage - late < STEP:
                part(stage - late)


def rows_of(carry, body, unroll=8):
    return lax.fori_loop(0, SIDE, body, carry, unroll=unroll)


def contract_lead(left, right):
    return lax.dot_general(left, right, (((0,), (0,)), ((), ())), preferred_element_type=f32)


def contract_last(left, right):
    return lax.dot_general(left, right, (((1,), (1,)), ((), ())), preferred_element_type=f32)


def three_parts(values):
    high = values.astype(bf16)
    rest = values - high.astype(f32)
    middle = rest.astype(bf16)
    low = (rest - middle.astype(f32)).astype(bf16)
    return jnp.concatenate([high, middle, low], axis=0)


def exact_dot(values, right):
    rows = values.shape[0]
    parts = jnp.dot(three_parts(values), right, preferred_element_type=f32)
    return parts[:rows] + (parts[rows : 2 * rows] + parts[2 * rows :])


def zeros_at_start(*refs):
    @pl.when(pl.program_id(0) == 0)
    def _():
        for ref in refs:
            ref[...] = jnp.zeros(ref.shape, ref.dtype)


def last_step():
    return pl.program_id(0) == pl.num_programs(0) - 1


def column_total(values):
    return jnp.sum(values, axis=0, keepdims=True)


def take(recv_ref, tile_ref):
    tile_ref[...] = lax.fori_loop(
        1,
        recv_ref.shape[0],
        lambda j, total: total + recv_ref[j].astype(f32),
        recv_ref[0].astype(f32),
        unroll=True if recv_ref.shape[0] <= 32 else 1,
    )


def row_at(tile_ref, start, lanes):
    return jnp.concatenate(
        [tile_ref[start + q : start + q + 1, :] for q in range(lanes // 128)], axis=1
    )


def put(tile_ref, start, row):
    for q in range(row.shape[1] // 128):
        tile_ref[start + q : start + q + 1, :] = row[:, q * 128 : (q + 1) * 128]


def send(send_ref, tile_ref):
    tile = tile_ref[...].astype(send_ref.dtype)

    def body(j, carry):
        send_ref[j] = tile
        return carry

    lax.fori_loop(0, send_ref.shape[0], body, 0, unroll=True if send_ref.shape[0] <= 32 else 1)


def norm_rows(sums, squares, counted, gain, shift):
    center = sums / counted
    spread = squares / counted - center * center
    inv = lax.rsqrt(spread + epsilon)
    scale = gain * inv
    return center, spread, inv, scale, shift - center * scale


def fill_half(whole_ref, mine_ref, other_ref, odd_ref):
    half = whole_ref.shape[1] // 2

    @pl.when(odd_ref[0] == 0)
    def _():
        whole_ref[:, :half] = mine_ref[...]
        whole_ref[:, half:] = other_ref[...]

    @pl.when(odd_ref[0] != 0)
    def _():
        whole_ref[:, :half] = other_ref[...]
        whole_ref[:, half:] = mine_ref[...]


def at_start(body):
    pl.when(pl.program_id(0) == 0)(body)


def at_end(body):
    pl.when(pl.program_id(0) == pl.num_programs(0) - 1)(body)


def lane_parts(values):
    total = values[:, :128]
    for at in range(128, values.shape[1], 128):
        total = total + values[:, at : at + 128]
    return total


def lane_sum(row):
    return jnp.broadcast_to(jnp.sum(row, axis=1, keepdims=True), (1, 128))


def prepare_kernel(odd, in_ref, mid_ref, down_ref, up_ref, out_ref, *refs):
    *vector_refs, in_send, most_send, rows_ref = refs
    rows_ref[...] = jnp.zeros(rows_ref.shape, f32)
    for k, ref in enumerate(vector_refs):
        rows_ref[k : k + 1, : ref.shape[1]] = ref[...].astype(f32)
    at = mid_ref.shape[1] + 128
    for ref in (down_ref, up_ref):
        most_send[at : at + ref.shape[0], :] = ref[...]
        at += ref.shape[0]
    most_send[at : at + 16, :] = rows_ref[...].astype(bf16)
    for side in range(2):

        @pl.when(odd[0] == side)
        def _():
            for j in range(in_send.shape[0]):
                in_send[j] = in_ref[:, side * 128 : side * 128 + 128]
            at = mid_ref.shape[1]
            most_send[:at, :] = mid_ref[side]
            most_send[at : at + 128, :] = jnp.transpose(out_ref[side * 128 : side * 128 + 128, :])


def first_kernel(
    sides, odd, x_ref, mine_ref, other_ref, first_ref, w_ref, send_ref, acc_ref, tile_ref
):
    step = pl.program_id(0)
    zeros_at_start(acc_ref)
    at_start(lambda: fill_half(w_ref, mine_ref, other_ref, odd))
    place = places()
    lanes = first_ref.shape[1]
    sums = [acc_ref[0], acc_ref[1]]

    def multiply(image):
        first_ref[of_image(image), :] = jnp.dot(
            x_ref[of_image(image), :], w_ref[...], preferred_element_type=f32
        )

    def finish(image):
        limit = 2 * sides[step * STEP + image]
        for row in range(SIDE):
            here = of_row(image, row)
            values = first_ref[here, :] * wide(row_mask(place, row, limit), lanes)
            first_ref[here, :] = values
            sums[0] = sums[0] + fold(values)
            sums[1] = sums[1] + fold(values * values)

    stages(multiply, finish)
    acc_ref[0], acc_ref[1] = sums

    @at_end
    def _():
        count = jnp.int32(0)
        for image in range(sides.shape[0]):
            count = count + 4 * sides[image] * sides[image]
        tile_ref[...] = jnp.zeros(tile_ref.shape, f32)
        put(tile_ref, 0, column_total(acc_ref[0]))
        put(tile_ref, lanes // 128, column_total(acc_ref[1]))
        put(tile_ref, 2 * lanes // 128, jnp.full((1, 128), count, jnp.int32).astype(f32))
        send(send_ref, tile_ref)


def cross_kernel(
    sides, x_ref, first_ref, cross_ref, ones_ref, power_ref, square_ref
):
    step = pl.program_id(0)
    zeros_at_start(cross_ref, square_ref, ones_ref)
    cross_ref[...] += contract_lead(first_ref[...].astype(bf16), x_ref[...])
    place = places()
    lanes = x_ref.shape[1]
    for image in range(STEP):
        limit = 2 * sides[step * STEP + image]

        def body(row, carry):
            square, total = carry
            values = x_ref[chunk(image, row), :].astype(f32) * wide(
                row_mask(place, row, limit), lanes
            )
            return (square + fold(values * values), total + fold(values))

        square, total = rows_of((square_ref[...], ones_ref[...]), body)
        square_ref[...] = square
        ones_ref[...] = total

    @at_end
    def _():
        power_ref[...] = lane_parts(square_ref[...])


def write_patches(patch_ref, image, row, low, place):
    values = low.astype(f32)
    lanes = values.shape[1]
    inner = wide(place, lanes)
    left = jnp.where(inner == 0, 0.0, pltpu.roll(values, 1, 0)).astype(bf16)
    right = jnp.where(inner == SIDE - 1, 0.0, pltpu.roll(values, SIDE - 1, 0)).astype(bf16)
    for tap in range(TAPS):
        up, side = tap // 3, tap % 3
        source = (left, low, right)[side]
        here = (row + 2 - up) * SIDE
        if isinstance(row, int):
            here = slice(here, here + SIDE)
        else:
            here = pl.ds(pl.multiple_of(here, SIDE), SIDE)
        for group in range(lanes // 128):
            at = (group * TAPS + tap) * 128
            patch_ref[image, here, at : at + 128] = source[:, group * 128 : (group + 1) * 128]


def second_kernel(lengths, sides, first_ref, recv_ref, _, *refs):
    if lengths:
        member, odd, *refs = refs
        shard_refs, refs = refs[:4], refs[4:]
        act_ref, second_ref, terms_ref, count_ref, send_ref, w_ref, down_ref, up_ref, *refs = refs
        *param_refs, patch_ref, acc_ref, tile_ref, param_ref = refs
    else:
        w_ref, param_ref, act_ref, second_ref, terms_ref, count_ref, send_ref, *refs = refs
        patch_ref, acc_ref, tile_ref = refs
    step = pl.program_id(0)
    zeros_at_start(acc_ref, patch_ref)
    place = places()
    lanes = first_ref.shape[1]
    columns = TAPS * lanes // RADIX

    @at_start
    def _():
        if lengths:
            own = w_ref.shape[0] // len(ORDER)
            downs, ups = down_ref.shape[0] // len(ORDER), up_ref.shape[0] // len(ORDER)
            wholes = [jnp.zeros((16, length * len(ORDER)), f32) for length in lengths]
            lane = lax.broadcasted_iota(jnp.int32, (16, 128), 1)
            for index, k in enumerate(ORDER):
                piece = member[0] ^ k
                ref = shard_refs[index // 4]
                index = index % 4
                at = TAPS * own + 128
                down_ref[pl.ds(pl.multiple_of(piece * downs, downs), downs), :] = ref[
                    index, at : at + downs, :
                ]
                at += downs
                up_ref[pl.ds(pl.multiple_of(piece * ups, ups), ups), :] = ref[
                    index, at : at + ups, :
                ]
                at += ups
                rows = ref[index, at : at + 16, :].astype(f32)
                for length in sorted(set(lengths)):
                    part = jnp.where(lane < length, rows, 0.0)
                    spare = (length * len(ORDER) - 128) // 128
                    part = jnp.concatenate([part] + [jnp.zeros((16, 128), f32)] * spare, axis=1)
                    part = pltpu.roll(part, piece * length, 1)
                    wholes = [
                        whole + part if whole.shape == part.shape else whole for whole in wholes
                    ]
            for side in range(2):

                @pl.when(odd[0] == side)
                def _():
                    for index, k in enumerate(ORDER):
                        here = pl.ds(pl.multiple_of((member[0] ^ k) * own, own), own)
                        for refs, group in ((shard_refs[:2], side), (shard_refs[2:], 1 - side)):
                            for tap in range(TAPS):
                                at = (group * TAPS + tap) * 128
                                w_ref[here, at : at + 128] = refs[index // 4][
                                    index % 4, tap * own : (tap + 1) * own, :
                                ]

            for k, whole in enumerate(wholes):
                ref = ([param_ref] + param_refs)[k // 2]
                ref[k % 2 : k % 2 + 1, :] = whole[k : k + 1, :]
        take(recv_ref, tile_ref)
        count = tile_ref[2 * lanes // 128 : 2 * lanes // 128 + 1, :]
        count_ref[...] = jnp.broadcast_to(count, count_ref.shape)
        center, _, inv, scale, offset = norm_rows(
            row_at(tile_ref, 0, lanes),
            row_at(tile_ref, lanes // 128, lanes),
            wide(count, lanes),
            param_ref[0:1, :],
            param_ref[1:2, :],
        )
        terms_ref[0:1, :] = scale
        terms_ref[1:2, :] = offset
        terms_ref[2:3, :] = inv
        terms_ref[3:4, :] = -center * inv
        terms_ref[4:5, :] = center

    def start_image(image):
        limit = 2 * sides[step * STEP + image]
        for row in range(SIDE):
            here = slice(image * 256 + row * SIDE, image * 256 + row * SIDE + SIDE)
            pre = first_ref[here, :] * terms_ref[0:1, :] + terms_ref[1:2, :]
            act = pre * (sigmoid(pre) * wide(row_mask(place, row, limit), lanes))
            low = act.astype(bf16)
            act_ref[here, :] = low
            write_patches(patch_ref, image, row, low, place)

    def multiply_image(image):
        for group in range(RADIX):
            second_ref[image * 256 : image * 256 + 256, group * lanes : (group + 1) * lanes] = (
                contract_last(
                    patch_ref[image, SIDE : SIDE + 256, group * columns : (group + 1) * columns],
                    w_ref[:, group * columns : (group + 1) * columns],
                )
            )

    def sum_image(image, carry):
        limit = 2 * sides[step * STEP + image]
        total, square = carry
        for row in range(SIDE):
            values = second_ref[image * 256 + row * SIDE : image * 256 + row * SIDE + SIDE, :]
            values = values * wide(row_mask(place, row, limit), values.shape[1])
            total, square = total + fold(values), square + fold(values * values)
        return total, square

    carry = (acc_ref[0], acc_ref[1])
    for stage in range(STEP + 2):
        if 0 <= stage - 1 < STEP:
            multiply_image(stage - 1)
        if stage < STEP:
            start_image(stage)
        if stage >= 2:
            carry = sum_image(stage - 2, carry)
    acc_ref[0], acc_ref[1] = carry

    @at_end
    def _():
        tile_ref[...] = jnp.zeros(tile_ref.shape, f32)
        put(tile_ref, 0, column_total(acc_ref[0]))
        put(tile_ref, RADIX * lanes // 128, column_total(acc_ref[1]))
        send(send_ref, tile_ref)


def pool_kernel(
    sides,
    second_ref,
    recv_ref,
    param_ref,
    count_ref,
    down_ref,
    power_ref,
    pooled_ref,
    squeeze_ref,
    terms_ref,
    send_ref,
    pool_ref,
    tile_ref,
):
    step = pl.program_id(0)
    place = places()
    lanes = second_ref.shape[1]

    @at_start
    def _():
        take(recv_ref, tile_ref)
        _, _, _, scale, offset = norm_rows(
            row_at(tile_ref, 0, lanes),
            row_at(tile_ref, lanes // 128, lanes),
            wide(count_ref[0:1, :], lanes),
            param_ref[0:1, :],
            param_ref[1:2, :],
        )
        terms_ref[0:1, :] = scale
        terms_ref[1:2, :] = offset

    for image in range(STEP):
        limit = 2 * sides[step * STEP + image]

        def body(row, total):
            pre = second_ref[chunk(image, row), :] * terms_ref[0:1, :] + terms_ref[1:2, :]
            act = pre * (sigmoid(pre) * wide(row_mask(place, row, limit), lanes))
            return total + fold(act)

        total = column_total(rows_of(jnp.zeros((8, lanes), f32), body))
        both = total[:, : lanes // 2] + total[:, lanes // 2 :]
        area = jnp.full(both.shape, limit * limit, jnp.int32).astype(f32)
        pool_ref[pl.ds(step * STEP + image, 1), :] = both / area

    @at_end
    def _():
        low = pool_ref[...].astype(bf16)
        pooled_ref[...] = low
        squeeze = jnp.dot(low, down_ref[...], preferred_element_type=f32)
        squeeze_ref[...] = squeeze
        tile_ref[...] = jnp.zeros(tile_ref.shape, f32)
        tile_ref[0:1, :] = column_total(squeeze)
        tile_ref[1:2, :] = column_total(squeeze * squeeze)
        tile_ref[2:3, :] = column_total(power_ref[...])
        send(send_ref, tile_ref)


def out_weights_kernel(start, place, odd, _, *refs):
    *shard_refs, w_ref, wt_ref = refs
    for side in range(2):

        @pl.when(odd[0] == side)
        def _():
            for index, k in enumerate(ORDER):
                here = pl.ds(pl.multiple_of((place[0] ^ k) * 128, 128), 128)
                for refs, half in ((shard_refs[:2], side), (shard_refs[2:], 1 - side)):
                    wt_ref[here, half * 128 : half * 128 + 128] = refs[index // 4][
                        index % 4, start : start + 128, :
                    ]

    w_ref[...] = jnp.transpose(wt_ref[...])


def mix_kernel(
    images_all,
    sides,
    second_ref,
    ab_ref,
    squeeze_ref,
    recv_ref,
    param_ref,
    up_ref,
    bias_ref,
    out_ref,
    mixed_ref,
    weights_ref,
    excite_ref,
    gate_ref,
    gw_ref,
    colsum_ref,
    power_ref,
    send_ref,
    gram_ref,
    acc_ref,
    tile_ref,
):
    step = pl.program_id(0)
    zeros_at_start(acc_ref, gram_ref)
    place = places()
    lanes = second_ref.shape[1]
    half = lanes // 2

    @at_start
    def _():
        tile_ref[0:8, :] = recv_ref[0]
        for j in range(1, recv_ref.shape[0]):
            tile_ref[0:8, :] += recv_ref[j]
        center, _, inv, scale, offset = norm_rows(
            tile_ref[0:1, :],
            tile_ref[1:2, :],
            jnp.float32(images_all),
            param_ref[0:1, :],
            param_ref[1:2, :],
        )
        gate_ref[0:1, :] = scale
        gate_ref[1:2, :] = offset
        gate_ref[2:3, :] = inv
        gate_ref[3:4, :] = -center * inv
        gate_ref[4:5, :] = tile_ref[2:3, :]
        pre = squeeze_ref[...] * scale + offset
        excite = (pre * sigmoid(pre)).astype(bf16)
        excite_ref[...] = excite
        logits = contract_last(excite, up_ref[...]) + bias_ref[0:1, :]
        one, two = logits[:, :half], logits[:, half:]
        top = jnp.maximum(one, two)
        one, two = jnp.exp(one - top), jnp.exp(two - top)
        weights_ref[:, :half] = one / (one + two)
        weights_ref[:, half:] = two / (one + two)

    sums = [acc_ref[0], acc_ref[1]]

    def mix(image):
        limit = 2 * sides[step * STEP + image]
        weights = weights_ref[pl.ds(step * STEP + image, 1), :]
        for row in range(SIDE):
            here = of_row(image, row)
            pre = second_ref[here, :] * ab_ref[0:1, :] + ab_ref[1:2, :]
            act = pre * (sigmoid(pre) * wide(row_mask(place, row, limit), lanes))
            act = act * weights
            mixed = act[:, :half] + act[:, half:]
            low = mixed.astype(bf16)
            mixed_ref[here, :] = low
            sums[0] = sums[0] + fold(low.astype(f32))
            sums[1] = sums[1] + fold(mixed * mixed)

    def square(image):
        values = mixed_ref[of_image(image), :]
        gram_ref[...] += contract_lead(values, values)

    stages(mix, square)
    acc_ref[0], acc_ref[1] = sums

    @at_end
    def _():
        whole = out_ref[...].astype(f32)
        total = column_total(acc_ref[0])
        colsum_ref[...] = jnp.broadcast_to(total, colsum_ref.shape)
        power_ref[...] = lane_parts(acc_ref[1])
        both = jnp.concatenate([gram_ref[...], jnp.broadcast_to(total, (16, half))], axis=0)
        both = exact_dot(both, out_ref[...])
        gw = both[:half]
        gw_ref[...] = gw
        sums = both[half:]
        put(tile_ref, 0, sums[0:1, :])
        put(tile_ref, whole.shape[1] // 128, column_total(gw * whole))
        send(send_ref, tile_ref)


def out_kernel(
    sides,
    mixed_ref,
    x_ref,
    cot_ref,
    recv_ref,
    param_ref,
    count_ref,
    w_ref,
    wt_ref,
    block_ref,
    slope_ref,
    back_ref,
    grad_ref,
    terms_ref,
    power_ref,
    send_ref,
    third_ref,
    acc_ref,
    square_ref,
    tile_ref,
    half_ref,
):
    step = pl.program_id(0)
    zeros_at_start(acc_ref, square_ref, grad_ref)
    place = places()
    lanes = x_ref.shape[1]
    part = 512 if lanes % 512 == 0 else lanes

    @at_start
    def _():
        take(recv_ref, tile_ref)
        count = count_ref[0:1, :]
        gain, shift = param_ref[0:1, :], param_ref[1:2, :]
        center, spread, inv, scale, offset = norm_rows(
            row_at(tile_ref, 0, lanes),
            row_at(tile_ref, lanes // 128, lanes),
            wide(count, lanes),
            gain,
            shift,
        )
        branch = gain * gain * spread * inv * inv + shift * shift
        terms_ref[0:1, :] = scale
        terms_ref[1:2, :] = offset
        terms_ref[2:3, :] = center
        terms_ref[3:4, :] = inv
        terms_ref[4:5, :] = 1.0 / scale
        terms_ref[5:6, :] = wide(lane_sum(branch), lanes)
        half_ref[0:1, :] = 0.5 * scale
        half_ref[1:2, :] = 0.5 * offset

    squares = [square_ref[...]]
    sums = {at: acc_ref[:, at : at + part] for at in range(0, lanes, part)}

    def expand(image):
        third_ref[of_image(image), :] = jnp.dot(
            mixed_ref[of_image(image), :], w_ref[...], preferred_element_type=f32
        )

    def finish(image):
        limit = 2 * sides[step * STEP + image]
        for row in range(SIDE):
            here = of_row(image, row)
            mask = wide(row_mask(place, row, limit), part)
            for at in range(0, lanes, part):
                cut = slice(at, at + part)
                half = (
                    (x_ref[here, cut] * bf16(0.5)).astype(f32)
                    + third_ref[here, cut] * half_ref[0:1, cut]
                    + half_ref[1:2, cut]
                )
                turned = jnp.tanh(half)
                gate = (1.0 + turned) * mask
                output = half * gate
                block_ref[here, cut] = output.astype(bf16)
                slope = gate + output * (1.0 - turned)
                grad = cot_ref[here, cut].astype(f32) * (slope * half_ref[0:1, cut])
                slope_ref[here, cut] = grad.astype(bf16)
                sums[at] = sums[at] + fold(grad)
                squares[0] = squares[0] + lane_parts(fold(output * output))

    def contract(image):
        here = of_image(image)
        back_ref[here, :] = jnp.dot(slope_ref[here, :], wt_ref[...], preferred_element_type=f32)
        grad_ref[...] += contract_lead(mixed_ref[here, :], slope_ref[here, :])

    stages(expand, finish, contract)
    square_ref[...] = squares[0]
    for at, total in sums.items():
        acc_ref[:, at : at + part] = total

    @at_end
    def _():
        power_ref[...] = square_ref[...]
        total = column_total(acc_ref[...])
        put(tile_ref, 0, total)
        turned = column_total(grad_ref[...] * w_ref[...].astype(f32))
        put(tile_ref, lanes // 128, turned - terms_ref[2:3, :] * total)
        send(send_ref, tile_ref)


def mid_terms(second_ref, ab_ref, here, mask):
    pre = second_ref[here, :] * ab_ref[0:1, :] + ab_ref[1:2, :]
    plain = sigmoid(pre)
    gate = plain * mask
    act = pre * gate
    return pre, act, gate + act * (1.0 - plain)


def gate_kernel(
    sides,
    second_ref,
    ab_ref,
    back_ref,
    mixed_ref,
    recv_ref,
    terms_ref,
    param_ref,
    count_ref,
    w_ref,
    wt_ref,
    weights_ref,
    excite_ref,
    squeeze_ref,
    gate_ref,
    up_ref,
    power_out_ref,
    power_mix_ref,
    dmixed_ref,
    sums_ref,
    dup_ref,
    dbias_ref,
    dq_ref,
    grads_ref,
    send_ref,
    turn_ref,
    row_ref,
    tile_ref,
):
    step = pl.program_id(0)
    place = places()
    lanes = second_ref.shape[1]
    half = lanes // 2
    width = w_ref.shape[1]

    @at_start
    def _():
        take(recv_ref, tile_ref)
        count = wide(count_ref[0:1, :], width)
        total = row_at(tile_ref, 0, width)
        scale, center, inv = terms_ref[0:1, :], terms_ref[2:3, :], terms_ref[3:4, :]
        gain_grad = row_at(tile_ref, width // 128, width) / param_ref[0:1, :]
        slant = scale * inv * gain_grad / count
        level = total / count - center * slant
        grads_ref[0:1, :] = total * terms_ref[4:5, :]
        grads_ref[1:2, :] = gain_grad
        grads_ref[2:3, :] = slant
        grads_ref[3:4, :] = level
        whole = w_ref[...].astype(f32)
        turn_ref[...] = jnp.dot(
            (whole * slant).astype(bf16), wt_ref[...], preferred_element_type=f32
        ).astype(bf16)
        row_ref[...] = exact_dot(jnp.broadcast_to(level, (16, width)), wt_ref[...])[:8]

    def turn(image):
        here = of_image(image)
        dmixed_ref[here, :] = back_ref[here, :] - jnp.dot(
            mixed_ref[here, :], turn_ref[...], preferred_element_type=f32
        )

    def add_up(image):
        limit = 2 * sides[step * STEP + image]
        totals = [jnp.zeros((8, lanes), f32) for _ in range(5)]
        for row in range(SIDE):
            here = of_row(image, row)
            mask = row_mask(place, row, limit)
            dmixed = (dmixed_ref[here, :] - row_ref[0:1, :]) * wide(mask, half)
            dmixed_ref[here, :] = dmixed
            both = jnp.concatenate([dmixed, dmixed], axis=1)
            pre, act, slope = mid_terms(second_ref, ab_ref, here, wide(mask, lanes))
            along = slope * both
            terms = (act * both, along, along * pre, slope, slope * pre)
            totals = [old + fold(new) for old, new in zip(totals, terms)]
        for index in range(5):
            sums_ref[index, pl.ds(step * STEP + image, 1), :] = column_total(totals[index])

    stages(turn, add_up)

    @at_end
    def _():
        weights = weights_ref[...]
        grads = sums_ref[0]
        mean = weights * grads
        mean = mean[:, :half] + mean[:, half:]
        dlogits = weights * (grads - jnp.concatenate([mean, mean], axis=1))
        dbias_ref[...] = jnp.broadcast_to(column_total(dlogits), dbias_ref.shape)
        low = dlogits.astype(bf16)
        dup_ref[...] = contract_lead(low, excite_ref[...])
        dexcite = jnp.dot(low, up_ref[...], preferred_element_type=f32)
        squeeze = squeeze_ref[...]
        pre = squeeze * gate_ref[0:1, :] + gate_ref[1:2, :]
        normed = squeeze * gate_ref[2:3, :] + gate_ref[3:4, :]
        plain = sigmoid(pre)
        dq = dexcite * (plain * (1.0 + pre * (1.0 - plain)))
        dq_ref[...] = dq
        tile_ref[0:1, :] = column_total(dq)
        tile_ref[1:2, :] = column_total(dq * normed)
        tile_ref[2:3, :] = column_total(power_out_ref[...])
        tile_ref[3:4, :] = column_total(power_mix_ref[...])
        tile_ref[4:8, :] = jnp.zeros((4, 128), f32)
        tile = tile_ref[0:8, :]
        for j in range(send_ref.shape[0]):
            send_ref[j] = tile


def squeeze_kernel(
    images_all,
    width,
    sides,
    dq_ref,
    squeeze_ref,
    gate_ref,
    recv_ref,
    pooled_ref,
    down_ref,
    weights_ref,
    sums_ref,
    param_ref,
    count_ref,
    terms_ref,
    ddown_ref,
    dpool_ref,
    grads_ref,
    send_ref,
    tile_ref,
    area_ref,
):
    take(recv_ref, tile_ref)
    shift, gain = tile_ref[0:1, :], tile_ref[1:2, :]
    grads_ref[0:1, :] = shift
    grads_ref[1:2, :] = gain
    bottleneck = pooled_ref.shape[1]
    count = count_ref[0:1, :]
    powers = (
        lane_sum(gate_ref[4:5, :]) / (count * width),
        lane_sum(tile_ref[3:4, :]) / (count * bottleneck),
        terms_ref[5:6, :128] / width,
        lane_sum(tile_ref[2:3, :]) / (count * width),
    )
    place = lax.broadcasted_iota(jnp.int32, (1, 128), 1)
    norms = powers[3]
    for index in range(3):
        norms = jnp.where(place == index, powers[index], norms)
    grads_ref[2:3, :] = jnp.sqrt(norms)
    normed = squeeze_ref[...] * gate_ref[2:3, :] + gate_ref[3:4, :]
    dsqueeze = gate_ref[0:1, :] * (
        dq_ref[...] - (shift + normed * gain) / jnp.float32(images_all)
    )
    low = dsqueeze.astype(bf16)
    ddown_ref[...] = contract_lead(pooled_ref[...], low)
    for image in range(area_ref.shape[0]):
        area = 4 * sides[image] * sides[image]
        area_ref[image : image + 1, :] = jnp.full((1, bottleneck), area, jnp.int32).astype(f32)
    dpool = contract_last(low, down_ref[...]) / area_ref[...]
    dpool_ref[...] = dpool
    both = jnp.concatenate([dpool, dpool], axis=1)
    weights = weights_ref[...]
    total = column_total(weights * sums_ref[1] + both * sums_ref[3])
    product = column_total(weights * sums_ref[2] + both * sums_ref[4])
    lanes = weights.shape[1]
    put(tile_ref, 0, total)
    put(tile_ref, lanes // 128, (product - param_ref[1:2, :] * total) / param_ref[0:1, :])
    send(send_ref, tile_ref)


def conv_back_kernel(
    sides,
    second_ref,
    ab_ref,
    recv_ref,
    param_ref,
    count_ref,
    dmixed_ref,
    weights_ref,
    dpool_ref,
    first_ref,
    ab_in_ref,
    w_ref,
    x_ref,
    dsecond_ref,
    dfirst_ref,
    in_ref,
    grads_ref,
    stat_ref,
    column_ref,
    acc_ref,
    tile_ref,
):
    step = pl.program_id(0)
    zeros_at_start(acc_ref, column_ref, in_ref)
    place = places()
    lanes = second_ref.shape[1]
    half = lanes // 2
    quarter = half // RADIX
    columns = TAPS * quarter

    @at_start
    def _():
        take(recv_ref, tile_ref)
        total = row_at(tile_ref, 0, lanes)
        product = row_at(tile_ref, lanes // 128, lanes)
        count = wide(count_ref[0:1, :], lanes)
        slant = ab_ref[0:1, :] * product / (count * param_ref[0:1, :])
        grads_ref[0:1, :] = total
        grads_ref[1:2, :] = product
        grads_ref[2:3, :] = slant
        grads_ref[3:4, :] = ab_ref[0:1, :] * total / count - param_ref[1:2, :] * slant

    def start(image):
        limit = 2 * sides[step * STEP + image]
        weights = weights_ref[pl.ds(step * STEP + image, 1), :] * ab_ref[0:1, :]
        dpool = dpool_ref[pl.ds(step * STEP + image, 1), :]
        dpool = jnp.concatenate([dpool, dpool], axis=1) * ab_ref[0:1, :]
        for row in range(SIDE):
            here = of_row(image, row)
            mask = wide(row_mask(place, row, limit), lanes)
            dmixed = dmixed_ref[here, :]
            both = jnp.concatenate([dmixed, dmixed], axis=1)
            pre = second_ref[here, :] * ab_ref[0:1, :] + ab_ref[1:2, :]
            plain = sigmoid(pre)
            slope = plain + pre * plain * (1.0 - plain)
            grad = slope * (weights * both + dpool)
            grad = mask * (grad - (pre * grads_ref[2:3, :] + grads_ref[3:4, :]))
            dsecond_ref[here, :] = grad.astype(bf16)

    def multiply(image):
        for group in range(RADIX):
            column_ref[image, SIDE : SIDE + 256, group * columns : (group + 1) * columns] = jnp.dot(
                dsecond_ref[of_image(image), group * half : (group + 1) * half],
                w_ref[:, group * columns : (group + 1) * columns],
                preferred_element_type=f32,
            )

    sums = [acc_ref[0], acc_ref[1]]
    inner = wide(place, quarter)

    def finish(image):
        limit = 2 * sides[step * STEP + image]
        for row in range(SIDE):
            here = of_row(image, row)
            mask = row_mask(place, row, limit)
            parts = []
            for group in range(RADIX):
                summed = []
                for side in range(3):
                    pieces = []
                    for up in range(3):
                        at = group * columns + (up * 3 + side) * quarter
                        start_row = (row + 2 - up) * SIDE
                        pieces.append(
                            column_ref[image, start_row : start_row + SIDE, at : at + quarter]
                        )
                    summed.append(pieces[0] + pieces[1] + pieces[2])
                low = jnp.where(inner == SIDE - 1, 0.0, pltpu.roll(summed[0], SIDE - 1, 0))
                high = jnp.where(inner == 0, 0.0, pltpu.roll(summed[2], 1, 0))
                parts.append(summed[1] + low + high)
            dact = jnp.concatenate(parts, axis=1)
            first = first_ref[here, :]
            pre = first * ab_in_ref[0:1, :] + ab_in_ref[1:2, :]
            normed = first * ab_in_ref[2:3, :] + ab_in_ref[3:4, :]
            plain = sigmoid(pre)
            grad = dact * (plain * (1.0 + pre * (1.0 - plain)) * wide(mask, half))
            dfirst_ref[here, :] = grad
            sums[0] = sums[0] + fold(grad)
            sums[1] = sums[1] + fold(grad * normed)

    def cross(image):
        here = of_image(image)
        in_ref[...] += contract_lead(dfirst_ref[here, :].astype(bf16), x_ref[here, :])

    stages(start, multiply, finish, cross)
    acc_ref[0], acc_ref[1] = sums

    @at_end
    def _():
        stat_ref[...] = jnp.zeros(stat_ref.shape, f32)
        put(stat_ref, 0, column_total(acc_ref[0]))
        put(stat_ref, half // 128, column_total(acc_ref[1]))


def conv_grad_kernel(aligned, odd, act_ref, dsecond_ref, _, *refs):
    if aligned:
        mine_ref, other_ref, conv_ref, patch_ref = refs
    else:
        conv_ref, patch_ref = refs
    zeros_at_start(conv_ref, patch_ref)
    place = places()
    lanes = act_ref.shape[1]
    columns = TAPS * lanes // RADIX
    def start(image):
        for row in range(SIDE):
            write_patches(patch_ref, image, row, act_ref[of_row(image, row), :], place)

    def multiply(image):
        here = of_image(image)
        for group in range(RADIX):
            conv_ref[:, group * columns : (group + 1) * columns] += contract_lead(
                dsecond_ref[here, group * lanes : (group + 1) * lanes],
                patch_ref[image, SIDE : SIDE + 256, group * columns : (group + 1) * columns],
            )

    stages(start, multiply)

    if aligned:

        @at_end
        def _():
            for piece in range(mine_ref.shape[0]):
                for ref, side in ((mine_ref, odd[0]), (other_ref, 1 - odd[0])):
                    here = pl.ds(pl.multiple_of((2 * piece + side) * 8, 8), 8)
                    for pair in range(RADIX * TAPS // 2):
                        two = [
                            conv_ref[here, (2 * pair + k) * 128 : (2 * pair + k + 1) * 128]
                            for k in range(2)
                        ]
                        ref[piece, pair * 16 : pair * 16 + 16, :] = jnp.concatenate(
                            two, axis=0
                        ).astype(bf16)


def late_kernel(
    aligned, odd, recv_ref, terms_ref, count_ref, in_ref, cross_ref, ones_ref, grads_ref, *refs
):
    tile_ref = refs[-1]
    take(recv_ref, tile_ref)
    lanes = terms_ref.shape[1]
    total = row_at(tile_ref, 0, lanes)
    product = row_at(tile_ref, lanes // 128, lanes)
    count = wide(count_ref[0:1, :], lanes)
    slant = terms_ref[0:1, :] * terms_ref[2:3, :] * product / count
    level = terms_ref[0:1, :] * total / count - terms_ref[4:5, :] * slant
    grads_ref[0:1, :] = total
    grads_ref[1:2, :] = product
    grads_ref[2:3, :] = slant
    grads_ref[3:4, :] = level
    grads_ref[4:5, :] = terms_ref[0:1, :]
    grads_ref[5:8, :] = jnp.zeros((3, lanes), f32)
    if not aligned:
        return
    mine_ref, other_ref, full_ref, _ = refs
    columns = jnp.transpose(grads_ref[...])
    ones = column_total(ones_ref[...])
    full_ref[...] = (
        in_ref[...] * columns[:, 4:5]
        - cross_ref[...] * columns[:, 2:3]
        - ones * columns[:, 3:4]
    )
    rows = mine_ref.shape[1]
    groups = lanes // rows
    for piece in range(mine_ref.shape[0]):
        owner, pair = 2 * piece // groups, piece % (groups // 2)
        for ref, side in ((mine_ref, odd[0]), (other_ref, 1 - odd[0])):
            here = pl.ds(pl.multiple_of((2 * pair + side) * rows, rows), rows)
            ref[piece] = full_ref[here, owner * 128 : (owner + 1) * 128].astype(bf16)


def merge_kernel(mid_ref, mid_got_ref, in_ref, in_got_ref, out_ref):
    cut = in_ref.shape[1]
    for piece in range(out_ref.shape[0]):
        out_ref[piece, :cut, :] = (
            in_ref[piece].astype(f32) + in_got_ref[piece].astype(f32)
        ).astype(bf16)
        out_ref[piece, cut:, :] = (
            mid_ref[piece].astype(f32) + mid_got_ref[piece].astype(f32)
        ).astype(bf16)


def last_kernel(
    sides, dfirst_ref, first_ref, grads_ref, w_ref, slope_ref, terms_ref, out_ref, done_ref, low_ref
):
    step = pl.program_id(0)
    place = places()
    lanes = first_ref.shape[1]
    width = out_ref.shape[1]
    part = 512 if width % 512 == 0 else width
    def start(image):
        limit = 2 * sides[step * STEP + image]
        for row in range(SIDE):
            here = of_row(image, row)
            mask = wide(row_mask(place, row, limit), lanes)
            grad = dfirst_ref[here, :] * grads_ref[4:5, :]
            grad = grad - mask * (first_ref[here, :] * grads_ref[2:3, :] + grads_ref[3:4, :])
            low_ref[here, :] = grad.astype(bf16)

    def multiply(image):
        here = of_image(image)
        out_ref[here, :] = contract_last(low_ref[here, :], w_ref[...])

    def finish(image):
        for row in range(SIDE):
            here = of_row(image, row)
            for at in range(0, width, part):
                cut = slice(at, at + part)
                out_ref[here, cut] += slope_ref[here, cut].astype(f32) * terms_ref[4:5, cut]

    stages(start, multiply, finish)

    @at_end
    def _():
        done_ref[...] = jnp.zeros(done_ref.shape, f32)


def total_of(ref):
    total = ref[0].astype(f32)
    for j in range(1, ref.shape[0]):
        total = total + ref[j].astype(f32)
    return total.astype(bf16)


def total_kernel(part_ref, tile_ref, sum_ref, send_ref):
    sum_ref[...] = total_of(part_ref)
    send(send_ref, tile_ref)


def total_last_kernel(one_ref, part_ref, _, sum_ref):
    cut = one_ref.shape[0]
    sum_ref[:cut, :] = one_ref[...]
    sum_ref[cut:, :] = total_of(part_ref)


def shards_kernel(
    marks, place, *refs
):
    groups = len(refs) - 7
    out_ref, up_ref, down_ref, bias_ref, in_ref, mid_ref, all_ref = refs[groups:]
    for k in range(groups):
        all_ref[place[0] ^ k] = refs[k][...].astype(f32)

    def rows_from(start, count):
        return jnp.concatenate([all_ref[k, start : start + count, :] for k in range(groups)], axis=0)

    at = 0
    out_ref[...] = rows_from(at, marks[0])
    at += marks[0]
    up_ref[...] = rows_from(at, marks[1])
    at += marks[1]
    down_ref[...] = rows_from(at, marks[2])
    at += marks[2]
    bias_ref[...] = all_ref[0, at : at + 1, : bias_ref.shape[1]]
    at = marks[3]
    in_ref[...] = jnp.transpose(rows_from(at, marks[4]))
    at += marks[4]
    for tap in range(RADIX * TAPS):
        mid_ref[tap] = rows_from(at + tap * 8, 8)


def tiles(lanes, block=0):
    return pl.BlockSpec((STEP * 256, lanes), lambda i: (i, block))


def held(*shape):
    return pl.BlockSpec(shape, lambda i: (0,) * len(shape))


def token():
    return pl.BlockSpec(memory_space=pl.ANY)


def scalars():
    return pl.BlockSpec(memory_space=pltpu.SMEM)


def shaped(shape, dtype=f32):
    return jax.ShapeDtypeStruct(shape, dtype)


def call(kernel, steps, ins, outs, scratch=(), cost=5, limit=None, name=None):
    if limit is None:
        limit = 56 if steps > 1 else 24
    return pl.pallas_call(
        kernel,
        grid=(steps,),
        in_specs=ins,
        out_specs=[spec for spec, _ in outs],
        out_shape=[shape for _, shape in outs],
        scratch_shapes=[pltpu.VMEM(shape, dtype) for shape, dtype in scratch],
        compiler_params=pltpu.CompilerParams(
            dimension_semantics=("arbitrary",), vmem_limit_bytes=limit * 1024 * 1024
        ),
        cost_estimate=pl.CostEstimate(
            flops=int(cost * 1e9), bytes_accessed=int(cost * 3e6), transcendentals=0
        ),
        name=name,
    )


def whole_out(shape, dtype=f32):
    return held(*shape), shaped(shape, dtype)


def rows8(*vectors):
    stacked = jnp.stack(vectors, axis=0)
    return jnp.pad(stacked, ((0, 8 - len(vectors)), (0, 0)))


def local(
    features,
    half_sides,
    cotangent,
    conv_in,
    conv_mid,
    attn_down,
    attn_up,
    attn_bias,
    conv_out,
    gain_in,
    shift_in,
    gain_mid,
    shift_mid,
    gain_attn,
    shift_attn,
    gain_out,
    shift_out,
):
    images, pixels, width = features.shape
    rows = images * pixels
    steps = images // STEP
    pieces = lax.axis_size("fsdp")
    groups = lax.axis_size("dp")
    devices = pieces * groups
    images_all = images * devices
    bottleneck = conv_in.shape[1]
    att = attn_down.shape[1]
    mid = RADIX * bottleneck
    columns = TAPS * conv_mid.shape[2]
    odd = lax.rem(lax.axis_index("dp"), 2).reshape(1)

    down_rows, up_rows = attn_down.shape[0], attn_up.shape[1]
    own_columns = conv_mid.shape[3]
    small = [gain_in, shift_in, gain_mid, shift_mid, gain_attn, shift_attn, gain_out, shift_out, attn_bias]
    lengths = [item.shape[0] for item in small]
    aligned = (
        own_columns % 16 == 0
        and width == 128 * pieces
        and bottleneck == 8 * devices
        and groups == 4
        and pieces == len(ORDER)
    )
    mid_cut = conv_mid.transpose(0, 1, 3, 2)
    if aligned:
        place = lax.axis_index("fsdp").reshape(1)
        at = TAPS * own_columns
        cut = (at + 128 + down_rows + up_rows + 16, 128)
        in_send, most = call(
            prepare_kernel,
            1,
            [
                scalars(),
                held(*conv_in.shape),
                held(RADIX, at, 128),
                held(*attn_down.shape),
                held(up_rows, att),
                held(*conv_out.shape),
            ]
            + [held(1, length) for length in lengths],
            [
                whole_out((pieces, conv_in.shape[0], 128), bf16),
                whole_out(cut, bf16),
            ],
            [((16, 128), f32)],
            2,
            56,
            name="last_prepare",
        )(
            odd,
            conv_in,
            mid_cut.reshape(RADIX, at, 128),
            attn_down,
            attn_up.T,
            conv_out,
            *[item.reshape(1, -1) for item in small],
        )
        in_mine = swap_all(in_send, "fsdp").reshape(width, bottleneck // 2)
        in_other = neighbour(in_mine)

        most = most[None]
        most = jnp.concatenate([most, partner(most, 4)], axis=0)
        most = jnp.concatenate([most, partner(most, 2)], axis=0)
        shards = [most, partner(most, 1)]
        shards += [neighbour(item) for item in shards]
    else:
        in_send = jnp.broadcast_to(half_of(conv_in, 1)[None], (pieces, conv_in.shape[0], 128))
        vectors = jnp.stack([jnp.pad(item, (0, 128 - item.shape[0])) for item in small])
        most = jnp.concatenate([mid_cut.reshape(-1, 128), attn_down, attn_up.T, vectors], axis=0)
        most = lax.all_gather(most, "fsdp")
        at = RADIX * TAPS * own_columns
        in_mine = swap_all(in_send, "fsdp").reshape(width, bottleneck // 2)
        in_other = neighbour(in_mine)
        whole_down = most[:, at : at + down_rows].reshape(bottleneck, att)
        whole_up = most[:, at + down_rows : at + down_rows + up_rows].reshape(mid, att)

    x = features.reshape(rows, width)
    cot = cotangent.reshape(rows, width)

    def tiled(lanes, dtype=f32):
        return tiles(lanes), shaped((rows, lanes), dtype)

    def sending(count, dtype=f32):
        return whole_out((devices, count, 128), dtype)

    def received(count):
        return held(devices, count, 128)

    first, whole_in, out = call(
        first_kernel,
        steps,
        [scalars(), scalars(), tiles(width), held(width, bottleneck // 2), held(width, bottleneck // 2)],
        [tiled(bottleneck), whole_out((width, bottleneck), bf16), sending(8)],
        [((2, 8, bottleneck), f32), ((8, 128), f32)],
        8,
        name="first",
    )(half_sides, odd, x, in_mine, in_other)
    got = swap_all(out, AXES)
    cross, x_sum, power_x = call(
        cross_kernel,
        steps,
        [scalars(), tiles(width), tiles(bottleneck)],
        [
            whole_out((bottleneck, width)),
            whole_out((8, width)),
            whole_out((8, 128)),
        ],
        [((8, width), f32)],
        10,
        name="cross",
    )(half_sides, x, first)

    ins = [scalars(), tiles(bottleneck), received(8), token()]
    args = (half_sides, first, got, power_x)
    outs = [
        tiled(bottleneck, bf16),
        tiled(mid),
        whole_out((8, bottleneck)),
        whole_out((8, 128)),
        sending(8),
    ]
    scratch = [
        ((STEP, 256 + 2 * SIDE, RADIX * columns), bf16),
        ((2, 8, mid), f32),
        ((8, 128), f32),
    ]
    if aligned:
        ins += [scalars(), scalars()] + [held(*item.shape) for item in shards]
        args += (place, odd) + tuple(shards)
        outs += [whole_out((bottleneck, RADIX * columns), bf16)]
        outs += [whole_out((bottleneck, att), bf16), whole_out((mid, att), bf16)]
        outs += [whole_out((8, lanes)) for lanes in (mid, att, width, mid)]
        scratch += [((8, bottleneck), f32)]
    else:
        whole_mid = most[:, :at].reshape(pieces, RADIX * TAPS, own_columns, 128)
        whole_mid = whole_mid.transpose(0, 2, 1, 3).reshape(bottleneck, RADIX * columns)
        at += down_rows + up_rows
        found = [
            most[:, at + k, :length].reshape(-1).astype(f32) for k, length in enumerate(lengths)
        ]
        p_in, p_mid, p_attn, p_out = [rows8(found[2 * k], found[2 * k + 1]) for k in range(4)]
        p_bias = rows8(found[8])
        ins += [held(bottleneck, RADIX * columns), held(8, bottleneck)]
        args += (whole_mid, p_in)
    act_low, second, terms_in, count, out, *rest = call(
        functools.partial(second_kernel, lengths if aligned else None),
        steps,
        ins,
        outs,
        scratch,
        15,
        name="second",
    )(*args)
    if aligned:
        whole_mid, whole_down, whole_up, p_mid, p_attn, p_out, p_bias = rest
    got = swap_all(out, AXES)

    pooled, squeeze, terms_mid, out = call(
        pool_kernel,
        steps,
        [
            scalars(),
            tiles(mid),
            received(8),
            held(8, mid),
            held(8, 128),
            held(bottleneck, att),
            held(8, 128),
        ],
        [
            whole_out((images, bottleneck), bf16),
            whole_out((images, att)),
            whole_out((8, mid)),
            sending(8),
        ],
        [((images, bottleneck), f32), ((8, 128), f32)],
        7,
        name="pool",
    )(half_sides, second, got, p_mid, count, whole_down, power_x)
    got = swap_all(out, AXES)

    if aligned:
        whole_w_out, whole_out_t = call(
            functools.partial(out_weights_kernel, TAPS * own_columns),
            1,
            [scalars(), scalars(), token()] + [held(*item.shape) for item in shards],
            [whole_out((bottleneck, width), bf16), whole_out((width, bottleneck), bf16)],
            (),
            1,
            name="last_weights",
        )(place, odd, pooled, *shards)
    else:
        whole_w_out = lax.all_gather(conv_out, "fsdp", axis=1, tiled=True)
        whole_out_t = whole_w_out.T
    wide_rows = 2 * width // 128
    mixed, weights, excite, gate, gram_out, colsum, power_mix, out = call(
        functools.partial(mix_kernel, images_all),
        steps,
        [
            scalars(),
            tiles(mid),
            held(8, mid),
            held(images, att),
            received(8),
            held(8, att),
            held(mid, att),
            held(8, mid),
            held(bottleneck, width),
        ],
        [
            tiled(bottleneck, bf16),
            whole_out((images, mid)),
            whole_out((images, att), bf16),
            whole_out((8, att)),
            whole_out((bottleneck, width)),
            whole_out((8, bottleneck)),
            whole_out((8, 128)),
            sending(wide_rows),
        ],
        [((bottleneck, bottleneck), f32), ((2, 8, bottleneck), f32), ((wide_rows, 128), f32)],
        11,
        name="mix",
    )(half_sides, second, terms_mid, squeeze, got, p_attn, whole_up, p_bias, whole_w_out)
    got = swap_all(out, AXES)

    block, slope, back, grad_out, terms_out, power_out, out = call(
        out_kernel,
        steps,
        [
            scalars(),
            tiles(bottleneck),
            tiles(width),
            tiles(width),
            received(wide_rows),
            held(8, width),
            held(8, 128),
            held(bottleneck, width),
            held(width, bottleneck),
        ],
        [
            tiled(width, bf16),
            tiled(width, bf16),
            tiled(bottleneck),
            whole_out((bottleneck, width)),
            whole_out((8, width)),
            whole_out((8, 128)),
            sending(wide_rows, bf16),
        ],
        [
            ((STEP * 256, width), f32),
            ((8, width), f32),
            ((8, 128), f32),
            ((wide_rows, 128), f32),
            ((8, width), f32),
        ],
        25,
        name="output",
    )(half_sides, mixed, x, cot, got, p_out, count, whole_w_out, whole_out_t)
    got = swap_all(out, AXES)

    dmixed, sums, dup, dbias, dq, grads_out, out = call(
        gate_kernel,
        steps,
        [
            scalars(),
            tiles(mid),
            held(8, mid),
            tiles(bottleneck),
            tiles(bottleneck),
            received(wide_rows),
            held(8, width),
            held(8, width),
            held(8, 128),
            held(bottleneck, width),
            held(width, bottleneck),
            held(images, mid),
            held(images, att),
            held(images, att),
            held(8, att),
            held(mid, att),
            held(8, 128),
            held(8, 128),
        ],
        [
            tiled(bottleneck),
            whole_out((5, images, mid)),
            whole_out((mid, att)),
            whole_out((8, mid)),
            whole_out((images, att)),
            whole_out((8, width)),
            sending(8),
        ],
        [
            ((bottleneck, bottleneck), bf16),
            ((8, bottleneck), f32),
            ((wide_rows, 128), f32),
        ],
        13,
        name="gate",
    )(
        half_sides,
        second,
        terms_mid,
        back,
        mixed,
        got,
        terms_out,
        p_out,
        count,
        whole_w_out,
        whole_out_t,
        weights,
        excite,
        squeeze,
        gate,
        whole_up,
        power_out,
        power_mix,
    )
    got = swap_all(out, AXES)
    grad_conv_out = grad_out - colsum[0][:, None] * grads_out[3] - gram_out * grads_out[2]

    ddown, dpool, grads_attn, out = call(
        functools.partial(squeeze_kernel, images_all, width),
        1,
        [
            scalars(),
            held(images, att),
            held(images, att),
            held(8, att),
            received(8),
            held(images, bottleneck),
            held(bottleneck, att),
            held(images, mid),
            held(5, images, mid),
            held(8, mid),
            held(8, 128),
            held(8, width),
        ],
        [
            whole_out((bottleneck, att)),
            whole_out((images, bottleneck)),
            whole_out((8, att)),
            sending(8),
        ],
        [((8, 128), f32), ((images, bottleneck), f32)],
        1,
        name="squeeze",
    )(
        half_sides,
        dq,
        squeeze,
        gate,
        got,
        pooled,
        whole_down,
        weights,
        sums,
        p_mid,
        count,
        terms_out,
    )
    got = swap_all(out, AXES)

    out_cut = grad_conv_out.astype(bf16).reshape(bottleneck, pieces, -1).transpose(1, 0, 2)
    out_cut = out_cut.reshape(devices, -1, 128)
    bias_rows = jnp.pad(dbias[0].reshape(pieces, 1, up_rows), ((0, 0), (0, 0), (0, att - up_rows)))
    gates = jnp.concatenate(
        [
            dup.reshape(devices, -1, att),
            ddown.reshape(devices, -1, att),
            jnp.repeat(bias_rows, groups, axis=0),
        ],
        axis=1,
    ).astype(bf16)
    marks = [out_cut.shape[1], up_rows // groups, down_rows // groups]
    gates = jnp.concatenate([out_cut, gates], axis=1)
    gates = jnp.pad(gates, ((0, 0), (0, -gates.shape[1] % 16), (0, 0)))

    gates = to_owners(gates)
    dsecond, dfirst, in_grad, grads_mid, stat = call(
        conv_back_kernel,
        steps,
        [
            scalars(),
            tiles(mid),
            held(8, mid),
            received(8),
            held(8, mid),
            held(8, 128),
            tiles(bottleneck),
            held(images, mid),
            held(images, bottleneck),
            tiles(bottleneck),
            held(8, bottleneck),
            held(bottleneck, RADIX * columns),
            tiles(width),
        ],
        [
            tiled(mid, bf16),
            tiled(bottleneck),
            whole_out((bottleneck, width)),
            whole_out((8, mid)),
            whole_out((8, 128)),
        ],
        [
            ((STEP, 256 + 2 * SIDE, RADIX * columns), f32),
            ((2, 8, bottleneck), f32),
            ((8, 128), f32),
        ],
        20,
        name="conv_back",
    )(
        half_sides,
        second,
        terms_mid,
        got,
        p_mid,
        count,
        dmixed,
        weights,
        dpool,
        first,
        terms_in,
        whole_mid,
        x,
    )
    gates, out = call(
        total_kernel,
        1,
        [held(*gates.shape), held(8, 128)],
        [whole_out(gates.shape[1:], bf16), sending(8)],
        (),
        2,
        name="last_gates",
    )(gates, stat)
    got = swap_all(out, AXES)

    outs = []
    scratch = [((STEP, 256 + 2 * SIDE, RADIX * columns), bf16)]
    mid_rows = bottleneck // devices * RADIX * TAPS
    if aligned:
        outs += [whole_out((devices // 2, mid_rows, 128), bf16)] * 2
        scratch = [((bottleneck, RADIX * columns), f32)] + scratch
    else:
        outs += [whole_out((bottleneck, RADIX * columns))]
    conv_parts = call(
        functools.partial(conv_grad_kernel, aligned),
        steps,
        [scalars(), tiles(bottleneck), tiles(mid), token()],
        outs,
        scratch,
        15,
        name="conv_grad",
    )(odd, act_low, dsecond, gates)
    outs = [whole_out((8, bottleneck))]
    scratch = [((8, 128), f32)]
    in_rows = bottleneck // groups * (width // pieces) // 128
    if aligned:
        outs += [whole_out((devices // 2, in_rows, 128), bf16)] * 2
        scratch = [((bottleneck, width), f32)] + scratch
    grads_in, *in_parts = call(
        functools.partial(late_kernel, aligned),
        1,
        [
            scalars(),
            received(8),
            held(8, bottleneck),
            held(8, 128),
            held(bottleneck, width),
            held(bottleneck, width),
            held(8, width),
        ],
        outs,
        scratch,
        2,
        name="last_terms",
    )(odd, got, terms_in, count, in_grad, cross, x_sum)
    grad_features, done = call(
        last_kernel,
        steps,
        [
            scalars(),
            tiles(bottleneck),
            tiles(bottleneck),
            held(8, bottleneck),
            held(width, bottleneck),
            tiles(width),
            held(8, width),
        ],
        [tiled(width), whole_out((8, 128))],
        [((STEP * 256, bottleneck), bf16)],
        15,
        name="last",
    )(half_sides, dfirst, first, grads_in, whole_in, slope, terms_out)

    if aligned:
        mid_got, in_got = neighbour(conv_parts[1]), neighbour(in_parts[1])
        (late,) = call(
            merge_kernel,
            1,
            [held(*mid_got.shape)] * 2 + [held(*in_got.shape)] * 2,
            [whole_out((devices // 2, in_rows + mid_rows, 128), bf16)],
            (),
            2,
            name="last_merge",
        )(conv_parts[0], mid_got, in_parts[0], in_got)
    else:
        grad_conv_in = (
            in_grad * grads_in[4][:, None]
            - cross * grads_in[2][:, None]
            - column_total(x_sum) * grads_in[3][:, None]
        )
        in_cut = grad_conv_in.astype(bf16).reshape(bottleneck, pieces, -1).transpose(1, 0, 2)
        mid_cut = conv_parts[0].astype(bf16).reshape(devices, -1, RADIX * TAPS, 128)
        mid_cut = mid_cut.transpose(0, 2, 1, 3).reshape(devices, -1, 128)
        late = jnp.concatenate([in_cut.reshape(devices, -1, 128), mid_cut], axis=1)
        late = jnp.pad(late, ((0, 0), (0, -late.shape[1] % 16), (0, 0)))
        late = on_own_side(late)
    late = across_sides(late)
    (summed,) = call(
        total_last_kernel,
        1,
        [held(*gates.shape), held(*late.shape), token()],
        [whole_out((gates.shape[0] + late.shape[1], 128), bf16)],
        (),
        2,
        name="last_total",
    )(gates, late, done)
    marks += [gates.shape[0], in_rows]
    own_width = width // pieces
    if aligned:
        members = [summed] + [
            lax.ppermute(summed, "dp", [(i, i ^ k) for i in range(groups)])
            for k in range(1, groups)
        ]
        shard_out, shard_up, shard_down, shard_bias, shard_in, shard_mid = call(
            functools.partial(shards_kernel, marks),
            1,
            [scalars()] + [held(*summed.shape)] * groups,
            [
                whole_out((bottleneck, own_width)),
                whole_out((up_rows, att)),
                whole_out((down_rows, att)),
                whole_out((1, up_rows)),
                whole_out((own_width, bottleneck)),
                whole_out((RADIX * TAPS, own_columns, 128)),
            ],
            [((groups,) + summed.shape, f32)],
            2,
            name="last_shards",
        )(lax.axis_index("dp").reshape(1), *members)
        shard_bias = shard_bias.reshape(-1)
        shard_up = shard_up.T
        shard_mid = shard_mid.reshape(RADIX, TAPS, own_columns, 128).transpose(0, 1, 3, 2)
    else:
        summed = swap_all(jnp.broadcast_to(summed[None], (groups,) + summed.shape), "dp")
        summed = summed.astype(f32)
        shard_out = summed[:, : marks[0]].reshape(bottleneck, -1)
        at = marks[0]
        shard_up = summed[:, at : at + marks[1]].reshape(up_rows, att).T
        at += marks[1]
        shard_down = summed[:, at : at + marks[2]].reshape(down_rows, att)
        at += marks[2]
        shard_bias = summed[0, at, :up_rows]
        at = marks[3]
        shard_in = summed[:, at : at + in_rows].reshape(bottleneck, -1).T
        at += in_rows
        shard_mid = summed[:, at : at + mid_rows].reshape(groups, RADIX, TAPS, -1, 128)
        shard_mid = shard_mid.transpose(1, 2, 4, 0, 3).reshape(RADIX, TAPS, 128, own_columns)

    def own_part(row):
        length = row.shape[0] // pieces
        return lax.dynamic_slice_in_dim(row, lax.axis_index("fsdp") * length, length, 0)

    return (
        block.reshape(images, pixels, width),
        grad_features.reshape(images, pixels, width),
        grads_attn[2, :4],
        shard_in,
        shard_mid,
        shard_down,
        shard_up,
        shard_bias,
        shard_out,
        own_part(grads_in[1]),
        own_part(grads_in[0]),
        own_part(grads_mid[1]),
        own_part(grads_mid[0]),
        own_part(grads_attn[1]),
        own_part(grads_attn[0]),
        own_part(grads_out[1]),
        own_part(grads_out[0]),
    )


def solution(mesh):
    return jax.shard_map(
        local,
        mesh=mesh,
        in_specs=(
            P(("fsdp", "dp"), None, None),
            P(("fsdp", "dp")),
            P(("fsdp", "dp"), None, None),
            P("fsdp", None),
            P(None, None, None, "fsdp"),
            P("fsdp", None),
            P(None, "fsdp"),
            P("fsdp"),
            P(None, "fsdp"),
            P("fsdp"),
            P("fsdp"),
            P("fsdp"),
            P("fsdp"),
            P("fsdp"),
            P("fsdp"),
            P("fsdp"),
            P("fsdp"),
        ),
        out_specs=(
            P(("fsdp", "dp"), None, None),
            P(("fsdp", "dp"), None, None),
            P(),
            P("fsdp", None),
            P(None, None, None, "fsdp"),
            P("fsdp", None),
            P(None, "fsdp"),
            P("fsdp"),
            P(None, "fsdp"),
            P("fsdp"),
            P("fsdp"),
            P("fsdp"),
            P("fsdp"),
            P("fsdp"),
            P("fsdp"),
            P("fsdp"),
            P("fsdp"),
        ),
        check_vma=False,
    )
```

```python
import functools

import jax
import jax.numpy as jnp
from jax import lax
from jax.experimental import pallas as pl
from jax.experimental.pallas import tpu as pltpu
from jax.sharding import PartitionSpec as P

RADIX = 2
SIDE = 16
TAPS = 9
STEP = 4

epsilon = 1e-05
AXES = ("fsdp", "dp")
f32 = jnp.float32
bf16 = jnp.bfloat16
HIGH = lax.Precision.HIGHEST


def swap_all(values, axes):
    return lax.all_to_all(values, axes, 0, 0)


def gather_all(shard):
    pieces = lax.axis_size("fsdp")
    return swap_all(jnp.broadcast_to(shard[None], (pieces,) + shard.shape), "fsdp")


def neighbour(values):
    return lax.ppermute(values, "dp", [(i, i ^ 1) for i in range(lax.axis_size("dp"))])


ORDER = (0, 4, 2, 6, 1, 5, 3, 7)


def partner(values, k):
    pieces = lax.axis_size("fsdp")
    return lax.ppermute(values, "fsdp", [(i, i ^ k) for i in range(pieces)])


def on_own_side(parts):
    odd = lax.rem(lax.axis_index("dp"), 2)
    parts = parts.reshape((parts.shape[0] // 2, 2) + parts.shape[1:])
    mine = lax.dynamic_index_in_dim(parts, odd, 1, False)
    other = lax.dynamic_index_in_dim(parts, 1 - odd, 1, False)
    return (mine.astype(f32) + neighbour(other).astype(f32)).astype(bf16)


def across_sides(parts):
    count = parts.shape[0]
    sides = [[2 * i + side for i in range(count)] for side in range(2)]
    return lax.all_to_all(parts, AXES, 0, 0, axis_index_groups=sides)


def to_owners(parts):
    return across_sides(on_own_side(parts))


def half_of(shard, axis):
    odd = lax.rem(lax.axis_index("dp"), 2)
    return lax.dynamic_slice_in_dim(shard, odd * (shard.shape[axis] // 2), shard.shape[axis] // 2, axis)


def sigmoid(values):
    return 0.5 * jnp.tanh(0.5 * values) + 0.5


def fold(values):
    return values[:8] + values[8:]


def wide(mask, lanes):
    return jnp.concatenate([mask] * (lanes // mask.shape[1]), axis=1)


def half_silu(half, mask):
    return half * ((1.0 + jnp.tanh(half)) * mask)


def twice_slope(half):
    turned = jnp.tanh(half)
    return (1.0 + turned) * (1.0 + half * (1.0 - turned))


def places():
    return lax.broadcasted_iota(jnp.int32, (SIDE, 128), 0)


def row_mask(place, row, limit):
    return jnp.where((place < limit) & (row < limit), 1.0, 0.0).astype(f32)


def chunk(image, row):
    return pl.ds(pl.multiple_of(image * 256 + row * SIDE, SIDE), SIDE)


def of_image(image):
    return slice(image * 256, image * 256 + 256)


def of_row(image, row):
    return slice(image * 256 + row * SIDE, image * 256 + row * SIDE + SIDE)


def stages(*parts):
    for stage in range(STEP + len(parts) - 1):
        for late, part in reversed(list(enumerate(parts))):
            if 0 <= stage - late < STEP:
                part(stage - late)


def rows_of(carry, body, unroll=8):
    return lax.fori_loop(0, SIDE, body, carry, unroll=unroll)


def contract_lead(left, right):
    return lax.dot_general(left, right, (((0,), (0,)), ((), ())), preferred_element_type=f32)


def contract_last(left, right):
    return lax.dot_general(left, right, (((1,), (1,)), ((), ())), preferred_element_type=f32)


def three_parts(values):
    high = values.astype(bf16)
    rest = values - high.astype(f32)
    middle = rest.astype(bf16)
    low = (rest - middle.astype(f32)).astype(bf16)
    return jnp.concatenate([high, middle, low], axis=0)


def exact_dot(values, right):
    rows = values.shape[0]
    parts = jnp.dot(three_parts(values), right, preferred_element_type=f32)
    return parts[:rows] + (parts[rows : 2 * rows] + parts[2 * rows :])


def zeros_at_start(*refs):
    @pl.when(pl.program_id(0) == 0)
    def _():
        for ref in refs:
            ref[...] = jnp.zeros(ref.shape, ref.dtype)


def last_step():
    return pl.program_id(0) == pl.num_programs(0) - 1


def column_total(values):
    return jnp.sum(values, axis=0, keepdims=True)


def take(recv_ref, tile_ref):
    tile_ref[...] = lax.fori_loop(
        1,
        recv_ref.shape[0],
        lambda j, total: total + recv_ref[j].astype(f32),
        recv_ref[0].astype(f32),
        unroll=True if recv_ref.shape[0] <= 32 else 1,
    )


def row_at(tile_ref, start, lanes):
    return jnp.concatenate(
        [tile_ref[start + q : start + q + 1, :] for q in range(lanes // 128)], axis=1
    )


def put(tile_ref, start, row):
    for q in range(row.shape[1] // 128):
        tile_ref[start + q : start + q + 1, :] = row[:, q * 128 : (q + 1) * 128]


def send(send_ref, tile_ref):
    tile = tile_ref[...].astype(send_ref.dtype)

    def body(j, carry):
        send_ref[j] = tile
        return carry

    lax.fori_loop(0, send_ref.shape[0], body, 0, unroll=True if send_ref.shape[0] <= 32 else 1)


def norm_rows(sums, squares, counted, gain, shift):
    center = sums / counted
    spread = squares / counted - center * center
    inv = lax.rsqrt(spread + epsilon)
    scale = gain * inv
    return center, spread, inv, scale, shift - center * scale


def fill_half(whole_ref, mine_ref, other_ref, odd_ref):
    half = whole_ref.shape[1] // 2

    @pl.when(odd_ref[0] == 0)
    def _():
        whole_ref[:, :half] = mine_ref[...]
        whole_ref[:, half:] = other_ref[...]

    @pl.when(odd_ref[0] != 0)
    def _():
        whole_ref[:, :half] = other_ref[...]
        whole_ref[:, half:] = mine_ref[...]


def at_start(body):
    pl.when(pl.program_id(0) == 0)(body)


def at_end(body):
    pl.when(pl.program_id(0) == pl.num_programs(0) - 1)(body)


def lane_parts(values):
    total = values[:, :128]
    for at in range(128, values.shape[1], 128):
        total = total + values[:, at : at + 128]
    return total


def lane_sum(row):
    return jnp.broadcast_to(jnp.sum(row, axis=1, keepdims=True), (1, 128))


def prepare_kernel(odd, mid_ref, down_ref, up_ref, out_ref, *refs):
    *vector_refs, most_send, rows_ref = refs
    rows_ref[...] = jnp.zeros(rows_ref.shape, f32)
    for k, ref in enumerate(vector_refs):
        rows_ref[k : k + 1, : ref.shape[1]] = ref[...].astype(f32)
    at = mid_ref.shape[1] + 128
    for ref in (down_ref, up_ref):
        most_send[at : at + ref.shape[0], :] = ref[...]
        at += ref.shape[0]
    most_send[at : at + 16, :] = rows_ref[...].astype(bf16)
    for side in range(2):

        @pl.when(odd[0] == side)
        def _():
            at = mid_ref.shape[1]
            most_send[:at, :] = mid_ref[side]
            most_send[at : at + 128, :] = jnp.transpose(out_ref[side * 128 : side * 128 + 128, :])


def first_kernel(
    sides, odd, x_ref, mine_ref, other_ref, first_ref, w_ref, send_ref, acc_ref, tile_ref
):
    step = pl.program_id(0)
    zeros_at_start(acc_ref)
    at_start(lambda: fill_half(w_ref, mine_ref, other_ref, odd))
    place = places()
    lanes = first_ref.shape[1]
    sums = [acc_ref[0], acc_ref[1]]

    def multiply(image):
        first_ref[of_image(image), :] = jnp.dot(
            x_ref[of_image(image), :], w_ref[...], preferred_element_type=f32
        )

    def finish(image):
        limit = 2 * sides[step * STEP + image]
        for row in range(SIDE):
            here = of_row(image, row)
            values = first_ref[here, :] * wide(row_mask(place, row, limit), lanes)
            first_ref[here, :] = values
            sums[0] = sums[0] + fold(values)
            sums[1] = sums[1] + fold(values * values)

    stages(multiply, finish)
    acc_ref[0], acc_ref[1] = sums

    @at_end
    def _():
        count = jnp.int32(0)
        for image in range(sides.shape[0]):
            count = count + 4 * sides[image] * sides[image]
        tile_ref[...] = jnp.zeros(tile_ref.shape, f32)
        put(tile_ref, 0, column_total(acc_ref[0]))
        put(tile_ref, lanes // 128, column_total(acc_ref[1]))
        put(tile_ref, 2 * lanes // 128, jnp.full((1, 128), count, jnp.int32).astype(f32))
        send(send_ref, tile_ref)


def cross_kernel(
    sides, x_ref, first_ref, cross_ref, ones_ref, power_ref, square_ref
):
    step = pl.program_id(0)
    zeros_at_start(cross_ref, square_ref, ones_ref)
    place = places()
    lanes = x_ref.shape[1]
    sums = [square_ref[...], ones_ref[...]]

    def multiply(image):
        here = of_image(image)
        cross_ref[...] += contract_lead(first_ref[here, :].astype(bf16), x_ref[here, :])

    def add_up(image):
        limit = 2 * sides[step * STEP + image]
        for row in range(SIDE):
            values = x_ref[of_row(image, row), :].astype(f32) * wide(
                row_mask(place, row, limit), lanes
            )
            sums[0] = sums[0] + fold(values * values)
            sums[1] = sums[1] + fold(values)

    stages(multiply, add_up)
    square_ref[...], ones_ref[...] = sums

    @at_end
    def _():
        power_ref[...] = lane_parts(square_ref[...])


def write_patches(patch_ref, image, row, low, place):
    values = low.astype(f32)
    lanes = values.shape[1]
    inner = wide(place, lanes)
    left = jnp.where(inner == 0, 0.0, pltpu.roll(values, 1, 0)).astype(bf16)
    right = jnp.where(inner == SIDE - 1, 0.0, pltpu.roll(values, SIDE - 1, 0)).astype(bf16)
    for tap in range(TAPS):
        up, side = tap // 3, tap % 3
        source = (left, low, right)[side]
        here = (row + 2 - up) * SIDE
        if isinstance(row, int):
            here = slice(here, here + SIDE)
        else:
            here = pl.ds(pl.multiple_of(here, SIDE), SIDE)
        for group in range(lanes // 128):
            at = (group * TAPS + tap) * 128
            patch_ref[image, here, at : at + 128] = source[:, group * 128 : (group + 1) * 128]


def second_kernel(lengths, sides, first_ref, recv_ref, _, *refs):
    if lengths:
        member, odd, *refs = refs
        shard_refs, refs = refs[:4], refs[4:]
        act_ref, second_ref, terms_ref, count_ref, send_ref, w_ref, down_ref, up_ref, *refs = refs
        *param_refs, patch_ref, acc_ref, tile_ref, param_ref = refs
    else:
        w_ref, param_ref, act_ref, second_ref, terms_ref, count_ref, send_ref, *refs = refs
        patch_ref, acc_ref, tile_ref = refs
    step = pl.program_id(0)
    zeros_at_start(acc_ref, patch_ref)
    place = places()
    lanes = first_ref.shape[1]
    columns = TAPS * lanes // RADIX

    @at_start
    def _():
        if lengths:
            own = w_ref.shape[0] // len(ORDER)
            downs, ups = down_ref.shape[0] // len(ORDER), up_ref.shape[0] // len(ORDER)
            wholes = [jnp.zeros((16, length * len(ORDER)), f32) for length in lengths]
            lane = lax.broadcasted_iota(jnp.int32, (16, 128), 1)
            for index, k in enumerate(ORDER):
                piece = member[0] ^ k
                ref = shard_refs[index // 4]
                index = index % 4
                at = TAPS * own + 128
                down_ref[pl.ds(pl.multiple_of(piece * downs, downs), downs), :] = ref[
                    index, at : at + downs, :
                ]
                at += downs
                up_ref[pl.ds(pl.multiple_of(piece * ups, ups), ups), :] = ref[
                    index, at : at + ups, :
                ]
                at += ups
                rows = ref[index, at : at + 16, :].astype(f32)
                for length in sorted(set(lengths)):
                    part = jnp.where(lane < length, rows, 0.0)
                    spare = (length * len(ORDER) - 128) // 128
                    part = jnp.concatenate([part] + [jnp.zeros((16, 128), f32)] * spare, axis=1)
                    part = pltpu.roll(part, piece * length, 1)
                    wholes = [
                        whole + part if whole.shape == part.shape else whole for whole in wholes
                    ]
            for side in range(2):

                @pl.when(odd[0] == side)
                def _():
                    for index, k in enumerate(ORDER):
                        here = pl.ds(pl.multiple_of((member[0] ^ k) * own, own), own)
                        for refs, group in ((shard_refs[:2], side), (shard_refs[2:], 1 - side)):
                            for tap in range(TAPS):
                                at = (group * TAPS + tap) * 128
                                w_ref[here, at : at + 128] = refs[index // 4][
                                    index % 4, tap * own : (tap + 1) * own, :
                                ]

            for k, whole in enumerate(wholes):
                ref = ([param_ref] + param_refs)[k // 2]
                ref[k % 2 : k % 2 + 1, :] = whole[k : k + 1, :]
        take(recv_ref, tile_ref)
        count = tile_ref[2 * lanes // 128 : 2 * lanes // 128 + 1, :]
        count_ref[...] = jnp.broadcast_to(count, count_ref.shape)
        center, _, inv, scale, offset = norm_rows(
            row_at(tile_ref, 0, lanes),
            row_at(tile_ref, lanes // 128, lanes),
            wide(count, lanes),
            param_ref[0:1, :],
            param_ref[1:2, :],
        )
        terms_ref[0:1, :] = scale
        terms_ref[1:2, :] = offset
        terms_ref[2:3, :] = inv
        terms_ref[3:4, :] = -center * inv
        terms_ref[4:5, :] = center
        terms_ref[5:6, :] = 0.5 * scale
        terms_ref[6:7, :] = 0.5 * offset

    def start_image(image):
        limit = 2 * sides[step * STEP + image]
        for row in range(SIDE):
            here = slice(image * 256 + row * SIDE, image * 256 + row * SIDE + SIDE)
            act = half_silu(
                first_ref[here, :] * terms_ref[5:6, :] + terms_ref[6:7, :],
                wide(row_mask(place, row, limit), lanes),
            )
            low = act.astype(bf16)
            act_ref[here, :] = low
            write_patches(patch_ref, image, row, low, place)

    def multiply_image(image):
        for group in range(RADIX):
            second_ref[image * 256 : image * 256 + 256, group * lanes : (group + 1) * lanes] = (
                contract_last(
                    patch_ref[image, SIDE : SIDE + 256, group * columns : (group + 1) * columns],
                    w_ref[:, group * columns : (group + 1) * columns],
                )
            )

    def sum_image(image, carry):
        limit = 2 * sides[step * STEP + image]
        total, square = carry
        for row in range(SIDE):
            values = second_ref[image * 256 + row * SIDE : image * 256 + row * SIDE + SIDE, :]
            values = values * wide(row_mask(place, row, limit), values.shape[1])
            total, square = total + fold(values), square + fold(values * values)
        return total, square

    carry = (acc_ref[0], acc_ref[1])
    for stage in range(STEP + 2):
        if 0 <= stage - 1 < STEP:
            multiply_image(stage - 1)
        if stage < STEP:
            start_image(stage)
        if stage >= 2:
            carry = sum_image(stage - 2, carry)
    acc_ref[0], acc_ref[1] = carry

    @at_end
    def _():
        tile_ref[...] = jnp.zeros(tile_ref.shape, f32)
        put(tile_ref, 0, column_total(acc_ref[0]))
        put(tile_ref, RADIX * lanes // 128, column_total(acc_ref[1]))
        send(send_ref, tile_ref)


def pool_kernel(
    sides,
    second_ref,
    recv_ref,
    param_ref,
    count_ref,
    down_ref,
    power_ref,
    pooled_ref,
    squeeze_ref,
    terms_ref,
    send_ref,
    pool_ref,
    tile_ref,
):
    step = pl.program_id(0)
    place = places()
    lanes = second_ref.shape[1]

    @at_start
    def _():
        take(recv_ref, tile_ref)
        _, _, _, scale, offset = norm_rows(
            row_at(tile_ref, 0, lanes),
            row_at(tile_ref, lanes // 128, lanes),
            wide(count_ref[0:1, :], lanes),
            param_ref[0:1, :],
            param_ref[1:2, :],
        )
        terms_ref[0:1, :] = scale
        terms_ref[1:2, :] = offset
        terms_ref[2:3, :] = 0.5 * scale
        terms_ref[3:4, :] = 0.5 * offset

    for image in range(STEP):
        limit = 2 * sides[step * STEP + image]

        total = jnp.zeros((8, lanes), f32)
        for row in range(SIDE):
            act = half_silu(
                second_ref[of_row(image, row), :] * terms_ref[2:3, :] + terms_ref[3:4, :],
                wide(row_mask(place, row, limit), lanes),
            )
            total = total + fold(act)
        total = column_total(total)
        both = total[:, : lanes // 2] + total[:, lanes // 2 :]
        area = jnp.full(both.shape, limit * limit, jnp.int32).astype(f32)
        pool_ref[pl.ds(step * STEP + image, 1), :] = both / area

    @at_end
    def _():
        low = pool_ref[...].astype(bf16)
        pooled_ref[...] = low
        squeeze = jnp.dot(low, down_ref[...], preferred_element_type=f32)
        squeeze_ref[...] = squeeze
        tile_ref[...] = jnp.zeros(tile_ref.shape, f32)
        tile_ref[0:1, :] = column_total(squeeze)
        tile_ref[1:2, :] = column_total(squeeze * squeeze)
        tile_ref[2:3, :] = column_total(power_ref[...])
        send(send_ref, tile_ref)


def out_weights_kernel(start, place, odd, _, *refs):
    *shard_refs, w_ref, wt_ref = refs
    for side in range(2):

        @pl.when(odd[0] == side)
        def _():
            for index, k in enumerate(ORDER):
                here = pl.ds(pl.multiple_of((place[0] ^ k) * 128, 128), 128)
                for refs, half in ((shard_refs[:2], side), (shard_refs[2:], 1 - side)):
                    wt_ref[here, half * 128 : half * 128 + 128] = refs[index // 4][
                        index % 4, start : start + 128, :
                    ]

    w_ref[...] = jnp.transpose(wt_ref[...])


def mix_kernel(
    images_all,
    sides,
    second_ref,
    ab_ref,
    squeeze_ref,
    recv_ref,
    param_ref,
    up_ref,
    bias_ref,
    out_ref,
    mixed_ref,
    weights_ref,
    excite_ref,
    gate_ref,
    gw_ref,
    colsum_ref,
    power_ref,
    send_ref,
    gram_ref,
    acc_ref,
    tile_ref,
):
    step = pl.program_id(0)
    zeros_at_start(acc_ref, gram_ref)
    place = places()
    lanes = second_ref.shape[1]
    half = lanes // 2

    @at_start
    def _():
        tile_ref[0:8, :] = recv_ref[0]
        for j in range(1, recv_ref.shape[0]):
            tile_ref[0:8, :] += recv_ref[j]
        center, _, inv, scale, offset = norm_rows(
            tile_ref[0:1, :],
            tile_ref[1:2, :],
            jnp.float32(images_all),
            param_ref[0:1, :],
            param_ref[1:2, :],
        )
        gate_ref[0:1, :] = scale
        gate_ref[1:2, :] = offset
        gate_ref[2:3, :] = inv
        gate_ref[3:4, :] = -center * inv
        gate_ref[4:5, :] = tile_ref[2:3, :]
        pre = squeeze_ref[...] * scale + offset
        excite = (pre * sigmoid(pre)).astype(bf16)
        excite_ref[...] = excite
        logits = contract_last(excite, up_ref[...]) + bias_ref[0:1, :]
        one, two = logits[:, :half], logits[:, half:]
        top = jnp.maximum(one, two)
        one, two = jnp.exp(one - top), jnp.exp(two - top)
        weights_ref[:, :half] = one / (one + two)
        weights_ref[:, half:] = two / (one + two)

    sums = [acc_ref[0], acc_ref[1]]

    def mix(image):
        limit = 2 * sides[step * STEP + image]
        weights = weights_ref[pl.ds(step * STEP + image, 1), :]
        for row in range(SIDE):
            here = of_row(image, row)
            act = half_silu(
                second_ref[here, :] * ab_ref[2:3, :] + ab_ref[3:4, :],
                wide(row_mask(place, row, limit), lanes),
            )
            act = act * weights
            mixed = act[:, :half] + act[:, half:]
            low = mixed.astype(bf16)
            mixed_ref[here, :] = low
            sums[0] = sums[0] + fold(low.astype(f32))
            sums[1] = sums[1] + fold(mixed * mixed)

    def square(image):
        values = mixed_ref[of_image(image), :]
        gram_ref[...] += contract_lead(values, values)

    stages(mix, square)
    acc_ref[0], acc_ref[1] = sums

    @at_end
    def _():
        whole = out_ref[...].astype(f32)
        total = column_total(acc_ref[0])
        colsum_ref[...] = jnp.broadcast_to(total, colsum_ref.shape)
        power_ref[...] = lane_parts(acc_ref[1])
        both = jnp.concatenate([gram_ref[...], jnp.broadcast_to(total, (16, half))], axis=0)
        both = exact_dot(both, out_ref[...])
        gw = both[:half]
        gw_ref[...] = gw
        sums = both[half:]
        put(tile_ref, 0, sums[0:1, :])
        put(tile_ref, whole.shape[1] // 128, column_total(gw * whole))
        send(send_ref, tile_ref)


def out_kernel(
    sides,
    mixed_ref,
    x_ref,
    cot_ref,
    recv_ref,
    param_ref,
    count_ref,
    w_ref,
    wt_ref,
    block_ref,
    slope_ref,
    back_ref,
    grad_ref,
    terms_ref,
    power_ref,
    send_ref,
    third_ref,
    acc_ref,
    square_ref,
    tile_ref,
    half_ref,
):
    step = pl.program_id(0)
    zeros_at_start(acc_ref, square_ref, grad_ref)
    place = places()
    lanes = x_ref.shape[1]
    part = 512 if lanes % 512 == 0 else lanes

    @at_start
    def _():
        take(recv_ref, tile_ref)
        count = count_ref[0:1, :]
        gain, shift = param_ref[0:1, :], param_ref[1:2, :]
        center, spread, inv, scale, offset = norm_rows(
            row_at(tile_ref, 0, lanes),
            row_at(tile_ref, lanes // 128, lanes),
            wide(count, lanes),
            gain,
            shift,
        )
        branch = gain * gain * spread * inv * inv + shift * shift
        terms_ref[0:1, :] = scale
        terms_ref[1:2, :] = offset
        terms_ref[2:3, :] = center
        terms_ref[3:4, :] = inv
        terms_ref[4:5, :] = 1.0 / scale
        terms_ref[5:6, :] = wide(lane_sum(branch), lanes)
        half_ref[0:1, :] = 0.5 * scale
        half_ref[1:2, :] = 0.5 * offset

    squares = [square_ref[...]]
    sums = {at: acc_ref[:, at : at + part] for at in range(0, lanes, part)}

    def expand(image):
        third_ref[of_image(image), :] = jnp.dot(
            mixed_ref[of_image(image), :], w_ref[...], preferred_element_type=f32
        )

    def finish(image):
        limit = 2 * sides[step * STEP + image]
        for row in range(SIDE):
            here = of_row(image, row)
            mask = wide(row_mask(place, row, limit), part)
            for at in range(0, lanes, part):
                cut = slice(at, at + part)
                half = (
                    (x_ref[here, cut] * bf16(0.5)).astype(f32)
                    + third_ref[here, cut] * half_ref[0:1, cut]
                    + half_ref[1:2, cut]
                )
                turned = jnp.tanh(half)
                gate = (1.0 + turned) * mask
                output = half * gate
                block_ref[here, cut] = output.astype(bf16)
                slope = gate + output * (1.0 - turned)
                grad = cot_ref[here, cut].astype(f32) * (slope * half_ref[0:1, cut])
                slope_ref[here, cut] = grad.astype(bf16)
                sums[at] = sums[at] + fold(grad)
                squares[0] = squares[0] + lane_parts(fold(output * output))

    def contract(image):
        here = of_image(image)
        back_ref[here, :] = jnp.dot(slope_ref[here, :], wt_ref[...], preferred_element_type=f32)
        grad_ref[...] += contract_lead(mixed_ref[here, :], slope_ref[here, :])

    stages(expand, finish, contract)
    square_ref[...] = squares[0]
    for at, total in sums.items():
        acc_ref[:, at : at + part] = total

    @at_end
    def _():
        power_ref[...] = square_ref[...]
        total = column_total(acc_ref[...])
        put(tile_ref, 0, total)
        turned = column_total(grad_ref[...] * w_ref[...].astype(f32))
        put(tile_ref, lanes // 128, turned - terms_ref[2:3, :] * total)
        send(send_ref, tile_ref)


def mid_terms(second_ref, ab_ref, here, mask):
    half = second_ref[here, :] * ab_ref[2:3, :] + ab_ref[3:4, :]
    turned = jnp.tanh(half)
    gate = (1.0 + turned) * mask
    act = half * gate
    return half, act, gate + act * (1.0 - turned)


def gate_kernel(
    sides,
    second_ref,
    ab_ref,
    back_ref,
    mixed_ref,
    recv_ref,
    terms_ref,
    param_ref,
    count_ref,
    w_ref,
    wt_ref,
    weights_ref,
    excite_ref,
    squeeze_ref,
    gate_ref,
    up_ref,
    power_out_ref,
    power_mix_ref,
    dmixed_ref,
    sums_ref,
    dup_ref,
    dbias_ref,
    dq_ref,
    grads_ref,
    send_ref,
    turn_ref,
    row_ref,
    tile_ref,
):
    step = pl.program_id(0)
    place = places()
    lanes = second_ref.shape[1]
    half = lanes // 2
    width = w_ref.shape[1]

    @at_start
    def _():
        take(recv_ref, tile_ref)
        count = wide(count_ref[0:1, :], width)
        total = row_at(tile_ref, 0, width)
        scale, center, inv = terms_ref[0:1, :], terms_ref[2:3, :], terms_ref[3:4, :]
        gain_grad = row_at(tile_ref, width // 128, width) / param_ref[0:1, :]
        slant = scale * inv * gain_grad / count
        level = total / count - center * slant
        grads_ref[0:1, :] = total * terms_ref[4:5, :]
        grads_ref[1:2, :] = gain_grad
        grads_ref[2:3, :] = slant
        grads_ref[3:4, :] = level
        whole = w_ref[...].astype(f32)
        turn_ref[...] = jnp.dot(
            (whole * slant).astype(bf16), wt_ref[...], preferred_element_type=f32
        ).astype(bf16)
        row_ref[...] = exact_dot(jnp.broadcast_to(level, (16, width)), wt_ref[...])[:8]

    def turn(image):
        here = of_image(image)
        dmixed_ref[here, :] = back_ref[here, :] - jnp.dot(
            mixed_ref[here, :], turn_ref[...], preferred_element_type=f32
        )

    def add_up(image):
        limit = 2 * sides[step * STEP + image]
        totals = [jnp.zeros((8, lanes), f32) for _ in range(5)]
        for row in range(SIDE):
            here = of_row(image, row)
            mask = row_mask(place, row, limit)
            dmixed = (dmixed_ref[here, :] - row_ref[0:1, :]) * wide(mask, half)
            dmixed_ref[here, :] = dmixed
            both = jnp.concatenate([dmixed, dmixed], axis=1)
            pre, act, slope = mid_terms(second_ref, ab_ref, here, wide(mask, lanes))
            along = slope * both
            terms = (act * both, along, along * pre, slope, slope * pre)
            totals = [old + fold(new) for old, new in zip(totals, terms)]
        for index in range(5):
            part = column_total(totals[index]) * (0.5 if index in (1, 3) else 1.0)
            sums_ref[index, pl.ds(step * STEP + image, 1), :] = part

    stages(turn, add_up)

    @at_end
    def _():
        weights = weights_ref[...]
        grads = sums_ref[0]
        mean = weights * grads
        mean = mean[:, :half] + mean[:, half:]
        dlogits = weights * (grads - jnp.concatenate([mean, mean], axis=1))
        dbias_ref[...] = jnp.broadcast_to(column_total(dlogits), dbias_ref.shape)
        low = dlogits.astype(bf16)
        dup_ref[...] = contract_lead(low, excite_ref[...])
        dexcite = jnp.dot(low, up_ref[...], preferred_element_type=f32)
        squeeze = squeeze_ref[...]
        pre = squeeze * gate_ref[0:1, :] + gate_ref[1:2, :]
        normed = squeeze * gate_ref[2:3, :] + gate_ref[3:4, :]
        plain = sigmoid(pre)
        dq = dexcite * (plain * (1.0 + pre * (1.0 - plain)))
        dq_ref[...] = dq
        tile_ref[0:1, :] = column_total(dq)
        tile_ref[1:2, :] = column_total(dq * normed)
        tile_ref[2:3, :] = column_total(power_out_ref[...])
        tile_ref[3:4, :] = column_total(power_mix_ref[...])
        tile_ref[4:8, :] = jnp.zeros((4, 128), f32)
        tile = tile_ref[0:8, :]
        for j in range(send_ref.shape[0]):
            send_ref[j] = tile


def squeeze_kernel(
    images_all,
    width,
    sides,
    dq_ref,
    squeeze_ref,
    gate_ref,
    recv_ref,
    pooled_ref,
    down_ref,
    weights_ref,
    sums_ref,
    param_ref,
    count_ref,
    terms_ref,
    ddown_ref,
    dpool_ref,
    grads_ref,
    send_ref,
    tile_ref,
    area_ref,
):
    take(recv_ref, tile_ref)
    shift, gain = tile_ref[0:1, :], tile_ref[1:2, :]
    grads_ref[0:1, :] = shift
    grads_ref[1:2, :] = gain
    bottleneck = pooled_ref.shape[1]
    count = count_ref[0:1, :]
    powers = (
        lane_sum(gate_ref[4:5, :]) / (count * width),
        lane_sum(tile_ref[3:4, :]) / (count * bottleneck),
        terms_ref[5:6, :128] / width,
        lane_sum(tile_ref[2:3, :]) / (count * width),
    )
    place = lax.broadcasted_iota(jnp.int32, (1, 128), 1)
    norms = powers[3]
    for index in range(3):
        norms = jnp.where(place == index, powers[index], norms)
    grads_ref[2:3, :] = jnp.sqrt(norms)
    normed = squeeze_ref[...] * gate_ref[2:3, :] + gate_ref[3:4, :]
    dsqueeze = gate_ref[0:1, :] * (
        dq_ref[...] - (shift + normed * gain) / jnp.float32(images_all)
    )
    low = dsqueeze.astype(bf16)
    ddown_ref[...] = contract_lead(pooled_ref[...], low)
    for image in range(area_ref.shape[0]):
        area = 4 * sides[image] * sides[image]
        area_ref[image : image + 1, :] = jnp.full((1, bottleneck), area, jnp.int32).astype(f32)
    dpool = contract_last(low, down_ref[...]) / area_ref[...]
    dpool_ref[...] = dpool
    both = jnp.concatenate([dpool, dpool], axis=1)
    weights = weights_ref[...]
    total = column_total(weights * sums_ref[1] + both * sums_ref[3])
    product = column_total(weights * sums_ref[2] + both * sums_ref[4])
    lanes = weights.shape[1]
    put(tile_ref, 0, total)
    put(tile_ref, lanes // 128, (product - param_ref[1:2, :] * total) / param_ref[0:1, :])
    send(send_ref, tile_ref)


def conv_back_kernel(
    sides,
    second_ref,
    ab_ref,
    recv_ref,
    param_ref,
    count_ref,
    dmixed_ref,
    weights_ref,
    dpool_ref,
    first_ref,
    ab_in_ref,
    w_ref,
    x_ref,
    dsecond_ref,
    dfirst_ref,
    in_ref,
    grads_ref,
    stat_ref,
    column_ref,
    acc_ref,
    tile_ref,
):
    step = pl.program_id(0)
    zeros_at_start(acc_ref, column_ref, in_ref)
    place = places()
    lanes = second_ref.shape[1]
    half = lanes // 2
    quarter = half // RADIX
    columns = TAPS * quarter

    @at_start
    def _():
        take(recv_ref, tile_ref)
        total = row_at(tile_ref, 0, lanes)
        product = row_at(tile_ref, lanes // 128, lanes)
        count = wide(count_ref[0:1, :], lanes)
        slant = ab_ref[0:1, :] * product / (count * param_ref[0:1, :])
        grads_ref[0:1, :] = total
        grads_ref[1:2, :] = product
        grads_ref[2:3, :] = slant
        grads_ref[3:4, :] = ab_ref[0:1, :] * total / count - param_ref[1:2, :] * slant

    def start(image):
        limit = 2 * sides[step * STEP + image]
        weights = weights_ref[pl.ds(step * STEP + image, 1), :] * ab_ref[2:3, :]
        dpool = dpool_ref[pl.ds(step * STEP + image, 1), :]
        dpool = jnp.concatenate([dpool, dpool], axis=1) * ab_ref[2:3, :]
        slant, level = 2.0 * grads_ref[2:3, :], grads_ref[3:4, :]
        for row in range(SIDE):
            here = of_row(image, row)
            mask = wide(row_mask(place, row, limit), lanes)
            dmixed = dmixed_ref[here, :]
            both = jnp.concatenate([dmixed, dmixed], axis=1)
            pre = second_ref[here, :] * ab_ref[2:3, :] + ab_ref[3:4, :]
            grad = twice_slope(pre) * (weights * both + dpool)
            grad = mask * (grad - (pre * slant + level))
            dsecond_ref[here, :] = grad.astype(bf16)

    def multiply(image):
        for group in range(RADIX):
            column_ref[image, SIDE : SIDE + 256, group * columns : (group + 1) * columns] = jnp.dot(
                dsecond_ref[of_image(image), group * half : (group + 1) * half],
                w_ref[:, group * columns : (group + 1) * columns],
                preferred_element_type=f32,
            )

    sums = [acc_ref[0], acc_ref[1]]
    inner = wide(place, quarter)

    def finish(image):
        limit = 2 * sides[step * STEP + image]
        for row in range(SIDE):
            here = of_row(image, row)
            mask = row_mask(place, row, limit)
            parts = []
            for group in range(RADIX):
                summed = []
                for side in range(3):
                    pieces = []
                    for up in range(3):
                        at = group * columns + (up * 3 + side) * quarter
                        start_row = (row + 2 - up) * SIDE
                        pieces.append(
                            column_ref[image, start_row : start_row + SIDE, at : at + quarter]
                        )
                    summed.append(pieces[0] + pieces[1] + pieces[2])
                low = jnp.where(inner == SIDE - 1, 0.0, pltpu.roll(summed[0], SIDE - 1, 0))
                high = jnp.where(inner == 0, 0.0, pltpu.roll(summed[2], 1, 0))
                parts.append(summed[1] + low + high)
            dact = jnp.concatenate(parts, axis=1)
            first = first_ref[here, :]
            pre = first * ab_in_ref[5:6, :] + ab_in_ref[6:7, :]
            normed = first * ab_in_ref[2:3, :] + ab_in_ref[3:4, :]
            grad = dact * (twice_slope(pre) * wide(0.5 * mask, half))
            dfirst_ref[here, :] = grad
            sums[0] = sums[0] + fold(grad)
            sums[1] = sums[1] + fold(grad * normed)

    def cross(image):
        here = of_image(image)
        in_ref[...] += contract_lead(dfirst_ref[here, :].astype(bf16), x_ref[here, :])

    stages(start, multiply, finish, cross)
    acc_ref[0], acc_ref[1] = sums

    @at_end
    def _():
        stat_ref[...] = jnp.zeros(stat_ref.shape, f32)
        put(stat_ref, 0, column_total(acc_ref[0]))
        put(stat_ref, half // 128, column_total(acc_ref[1]))


def conv_grad_kernel(aligned, odd, act_ref, dsecond_ref, _, *refs):
    if aligned:
        mine_ref, other_ref, conv_ref, patch_ref = refs
    else:
        conv_ref, patch_ref = refs
    zeros_at_start(conv_ref, patch_ref)
    place = places()
    lanes = act_ref.shape[1]
    columns = TAPS * lanes // RADIX
    def start(image):
        for row in range(SIDE):
            write_patches(patch_ref, image, row, act_ref[of_row(image, row), :], place)

    def multiply(image):
        here = of_image(image)
        for group in range(RADIX):
            conv_ref[:, group * columns : (group + 1) * columns] += contract_lead(
                dsecond_ref[here, group * lanes : (group + 1) * lanes],
                patch_ref[image, SIDE : SIDE + 256, group * columns : (group + 1) * columns],
            )

    stages(start, multiply)

    if aligned:

        @at_end
        def _():
            for piece in range(mine_ref.shape[0]):
                for ref, side in ((mine_ref, odd[0]), (other_ref, 1 - odd[0])):
                    here = pl.ds(pl.multiple_of((2 * piece + side) * 8, 8), 8)
                    for pair in range(RADIX * TAPS // 2):
                        two = [
                            conv_ref[here, (2 * pair + k) * 128 : (2 * pair + k + 1) * 128]
                            for k in range(2)
                        ]
                        ref[piece, pair * 16 : pair * 16 + 16, :] = jnp.concatenate(
                            two, axis=0
                        ).astype(bf16)


def late_kernel(
    aligned, odd, recv_ref, terms_ref, count_ref, in_ref, cross_ref, ones_ref, grads_ref, *refs
):
    tile_ref = refs[-1]
    take(recv_ref, tile_ref)
    lanes = terms_ref.shape[1]
    total = row_at(tile_ref, 0, lanes)
    product = row_at(tile_ref, lanes // 128, lanes)
    count = wide(count_ref[0:1, :], lanes)
    slant = terms_ref[0:1, :] * terms_ref[2:3, :] * product / count
    level = terms_ref[0:1, :] * total / count - terms_ref[4:5, :] * slant
    grads_ref[0:1, :] = total
    grads_ref[1:2, :] = product
    grads_ref[2:3, :] = slant
    grads_ref[3:4, :] = level
    grads_ref[4:5, :] = terms_ref[0:1, :]
    grads_ref[5:8, :] = jnp.zeros((3, lanes), f32)
    if not aligned:
        return
    mine_ref, other_ref, full_ref, _ = refs
    columns = jnp.transpose(grads_ref[...])
    ones = column_total(ones_ref[...])
    full_ref[...] = (
        in_ref[...] * columns[:, 4:5]
        - cross_ref[...] * columns[:, 2:3]
        - ones * columns[:, 3:4]
    )
    rows = mine_ref.shape[1]
    groups = lanes // rows
    for piece in range(mine_ref.shape[0]):
        owner, pair = 2 * piece // groups, piece % (groups // 2)
        for ref, side in ((mine_ref, odd[0]), (other_ref, 1 - odd[0])):
            here = pl.ds(pl.multiple_of((2 * pair + side) * rows, rows), rows)
            ref[piece] = full_ref[here, owner * 128 : (owner + 1) * 128].astype(bf16)


def merge_kernel(mid_ref, mid_got_ref, in_ref, in_got_ref, out_ref):
    cut = in_ref.shape[1]
    for piece in range(out_ref.shape[0]):
        out_ref[piece, :cut, :] = (
            in_ref[piece].astype(f32) + in_got_ref[piece].astype(f32)
        ).astype(bf16)
        out_ref[piece, cut:, :] = (
            mid_ref[piece].astype(f32) + mid_got_ref[piece].astype(f32)
        ).astype(bf16)


def last_kernel(
    sides, dfirst_ref, first_ref, grads_ref, w_ref, slope_ref, terms_ref, out_ref, done_ref, low_ref
):
    step = pl.program_id(0)
    place = places()
    lanes = first_ref.shape[1]
    width = out_ref.shape[1]
    part = 512 if width % 512 == 0 else width
    def start(image):
        limit = 2 * sides[step * STEP + image]
        for row in range(SIDE):
            here = of_row(image, row)
            mask = wide(row_mask(place, row, limit), lanes)
            grad = dfirst_ref[here, :] * grads_ref[4:5, :]
            grad = grad - mask * (first_ref[here, :] * grads_ref[2:3, :] + grads_ref[3:4, :])
            low_ref[here, :] = grad.astype(bf16)

    def multiply(image):
        here = of_image(image)
        out_ref[here, :] = contract_last(low_ref[here, :], w_ref[...])

    def finish(image):
        for row in range(SIDE):
            here = of_row(image, row)
            for at in range(0, width, part):
                cut = slice(at, at + part)
                out_ref[here, cut] += slope_ref[here, cut].astype(f32) * terms_ref[4:5, cut]

    stages(start, multiply, finish)

    @at_end
    def _():
        done_ref[...] = jnp.zeros(done_ref.shape, f32)


def total_of(ref):
    total = ref[0].astype(f32)
    for j in range(1, ref.shape[0]):
        total = total + ref[j].astype(f32)
    return total.astype(bf16)


def total_kernel(part_ref, tile_ref, sum_ref, send_ref):
    sum_ref[...] = total_of(part_ref)
    send(send_ref, tile_ref)


def total_last_kernel(one_ref, part_ref, _, sum_ref):
    cut = one_ref.shape[0]
    sum_ref[:cut, :] = one_ref[...]
    sum_ref[cut:, :] = total_of(part_ref)


def shards_kernel(
    marks, place, *refs
):
    groups = len(refs) - 7
    out_ref, up_ref, down_ref, bias_ref, in_ref, mid_ref, all_ref = refs[groups:]
    for k in range(groups):
        all_ref[place[0] ^ k] = refs[k][...].astype(f32)

    def rows_from(start, count):
        return jnp.concatenate([all_ref[k, start : start + count, :] for k in range(groups)], axis=0)

    at = 0
    out_ref[...] = rows_from(at, marks[0])
    at += marks[0]
    up_ref[...] = rows_from(at, marks[1])
    at += marks[1]
    down_ref[...] = rows_from(at, marks[2])
    at += marks[2]
    bias_ref[...] = all_ref[0, at : at + 1, : bias_ref.shape[1]]
    at = marks[3]
    in_ref[...] = jnp.transpose(rows_from(at, marks[4]))
    at += marks[4]
    for tap in range(RADIX * TAPS):
        mid_ref[tap] = rows_from(at + tap * 8, 8)


def tiles(lanes, block=0):
    return pl.BlockSpec((STEP * 256, lanes), lambda i: (i, block))


def held(*shape):
    return pl.BlockSpec(shape, lambda i: (0,) * len(shape))


def token():
    return pl.BlockSpec(memory_space=pl.ANY)


def scalars():
    return pl.BlockSpec(memory_space=pltpu.SMEM)


def shaped(shape, dtype=f32):
    return jax.ShapeDtypeStruct(shape, dtype)


def call(kernel, steps, ins, outs, scratch=(), cost=5, limit=None, name=None):
    if limit is None:
        limit = 56 if steps > 1 else 24
    return pl.pallas_call(
        kernel,
        grid=(steps,),
        in_specs=ins,
        out_specs=[spec for spec, _ in outs],
        out_shape=[shape for _, shape in outs],
        scratch_shapes=[pltpu.VMEM(shape, dtype) for shape, dtype in scratch],
        compiler_params=pltpu.CompilerParams(
            dimension_semantics=("arbitrary",), vmem_limit_bytes=limit * 1024 * 1024
        ),
        cost_estimate=pl.CostEstimate(
            flops=int(cost * 1e9), bytes_accessed=int(cost * 3e6), transcendentals=0
        ),
        name=name,
    )


def whole_out(shape, dtype=f32):
    return held(*shape), shaped(shape, dtype)


def rows8(*vectors):
    stacked = jnp.stack(vectors, axis=0)
    return jnp.pad(stacked, ((0, 8 - len(vectors)), (0, 0)))


def local(
    features,
    half_sides,
    cotangent,
    conv_in,
    conv_mid,
    attn_down,
    attn_up,
    attn_bias,
    conv_out,
    gain_in,
    shift_in,
    gain_mid,
    shift_mid,
    gain_attn,
    shift_attn,
    gain_out,
    shift_out,
):
    images, pixels, width = features.shape
    rows = images * pixels
    steps = images // STEP
    pieces = lax.axis_size("fsdp")
    groups = lax.axis_size("dp")
    devices = pieces * groups
    images_all = images * devices
    bottleneck = conv_in.shape[1]
    att = attn_down.shape[1]
    mid = RADIX * bottleneck
    columns = TAPS * conv_mid.shape[2]
    odd = lax.rem(lax.axis_index("dp"), 2).reshape(1)

    down_rows, up_rows = attn_down.shape[0], attn_up.shape[1]
    own_columns = conv_mid.shape[3]
    small = [gain_in, shift_in, gain_mid, shift_mid, gain_attn, shift_attn, gain_out, shift_out, attn_bias]
    lengths = [item.shape[0] for item in small]
    aligned = (
        own_columns % 16 == 0
        and width == 128 * pieces
        and bottleneck == 8 * devices
        and groups == 4
        and pieces == len(ORDER)
    )
    mid_cut = conv_mid.transpose(0, 1, 3, 2)
    if aligned:
        place = lax.axis_index("fsdp").reshape(1)
        at = TAPS * own_columns
        cut = (at + 128 + down_rows + up_rows + 16, 128)
        (most,) = call(
            prepare_kernel,
            1,
            [
                scalars(),
                held(RADIX, at, 128),
                held(*attn_down.shape),
                held(up_rows, att),
                held(*conv_out.shape),
            ]
            + [held(1, length) for length in lengths],
            [
                whole_out(cut, bf16),
            ],
            [((16, 128), f32)],
            2,
            56,
            name="last_prepare",
        )(
            odd,
            mid_cut.reshape(RADIX, at, 128),
            attn_down,
            attn_up.T,
            conv_out,
            *[item.reshape(1, -1) for item in small],
        )
        most = most[None]
        got = partner(most, 4)
        half, _ = lax.optimization_barrier((half_of(conv_in, 1), got))
        in_mine = gather_all(half).reshape(width, bottleneck // 2)
        in_other = neighbour(in_mine)
        most = jnp.concatenate([most, got], axis=0)
        most = jnp.concatenate([most, partner(most, 2)], axis=0)
        shards = [most, partner(most, 1)]
        shards += [neighbour(item) for item in shards]
    else:
        in_send = jnp.broadcast_to(half_of(conv_in, 1)[None], (pieces, conv_in.shape[0], 128))
        vectors = jnp.stack([jnp.pad(item, (0, 128 - item.shape[0])) for item in small])
        most = jnp.concatenate([mid_cut.reshape(-1, 128), attn_down, attn_up.T, vectors], axis=0)
        most = lax.all_gather(most, "fsdp")
        at = RADIX * TAPS * own_columns
        in_mine = swap_all(in_send, "fsdp").reshape(width, bottleneck // 2)
        in_other = neighbour(in_mine)
        whole_down = most[:, at : at + down_rows].reshape(bottleneck, att)
        whole_up = most[:, at + down_rows : at + down_rows + up_rows].reshape(mid, att)

    x = features.reshape(rows, width)
    cot = cotangent.reshape(rows, width)

    def tiled(lanes, dtype=f32):
        return tiles(lanes), shaped((rows, lanes), dtype)

    def sending(count, dtype=f32):
        return whole_out((devices, count, 128), dtype)

    def received(count):
        return held(devices, count, 128)

    first, whole_in, out = call(
        first_kernel,
        steps,
        [scalars(), scalars(), tiles(width), held(width, bottleneck // 2), held(width, bottleneck // 2)],
        [tiled(bottleneck), whole_out((width, bottleneck), bf16), sending(8)],
        [((2, 8, bottleneck), f32), ((8, 128), f32)],
        8,
        name="first",
    )(half_sides, odd, x, in_mine, in_other)
    got = swap_all(out, AXES)
    cross, x_sum, power_x = call(
        cross_kernel,
        steps,
        [scalars(), tiles(width), tiles(bottleneck)],
        [
            whole_out((bottleneck, width)),
            whole_out((8, width)),
            whole_out((8, 128)),
        ],
        [((8, width), f32)],
        10,
        name="cross",
    )(half_sides, x, first)

    ins = [scalars(), tiles(bottleneck), received(8), token()]
    args = (half_sides, first, got, power_x)
    outs = [
        tiled(bottleneck, bf16),
        tiled(mid),
        whole_out((8, bottleneck)),
        whole_out((8, 128)),
        sending(8),
    ]
    scratch = [
        ((STEP, 256 + 2 * SIDE, RADIX * columns), bf16),
        ((2, 8, mid), f32),
        ((8, 128), f32),
    ]
    if aligned:
        ins += [scalars(), scalars()] + [held(*item.shape) for item in shards]
        args += (place, odd) + tuple(shards)
        outs += [whole_out((bottleneck, RADIX * columns), bf16)]
        outs += [whole_out((bottleneck, att), bf16), whole_out((mid, att), bf16)]
        outs += [whole_out((8, lanes)) for lanes in (mid, att, width, mid)]
        scratch += [((8, bottleneck), f32)]
    else:
        whole_mid = most[:, :at].reshape(pieces, RADIX * TAPS, own_columns, 128)
        whole_mid = whole_mid.transpose(0, 2, 1, 3).reshape(bottleneck, RADIX * columns)
        at += down_rows + up_rows
        found = [
            most[:, at + k, :length].reshape(-1).astype(f32) for k, length in enumerate(lengths)
        ]
        p_in, p_mid, p_attn, p_out = [rows8(found[2 * k], found[2 * k + 1]) for k in range(4)]
        p_bias = rows8(found[8])
        ins += [held(bottleneck, RADIX * columns), held(8, bottleneck)]
        args += (whole_mid, p_in)
    act_low, second, terms_in, count, out, *rest = call(
        functools.partial(second_kernel, lengths if aligned else None),
        steps,
        ins,
        outs,
        scratch,
        15,
        name="second",
    )(*args)
    if aligned:
        whole_mid, whole_down, whole_up, p_mid, p_attn, p_out, p_bias = rest
    got = swap_all(out, AXES)

    pooled, squeeze, terms_mid, out = call(
        pool_kernel,
        steps,
        [
            scalars(),
            tiles(mid),
            received(8),
            held(8, mid),
            held(8, 128),
            held(bottleneck, att),
            held(8, 128),
        ],
        [
            whole_out((images, bottleneck), bf16),
            whole_out((images, att)),
            whole_out((8, mid)),
            sending(8),
        ],
        [((images, bottleneck), f32), ((8, 128), f32)],
        7,
        name="pool",
    )(half_sides, second, got, p_mid, count, whole_down, power_x)
    got = swap_all(out, AXES)

    if aligned:
        whole_w_out, whole_out_t = call(
            functools.partial(out_weights_kernel, TAPS * own_columns),
            1,
            [scalars(), scalars(), token()] + [held(*item.shape) for item in shards],
            [whole_out((bottleneck, width), bf16), whole_out((width, bottleneck), bf16)],
            (),
            1,
            name="last_weights",
        )(place, odd, pooled, *shards)
    else:
        whole_w_out = lax.all_gather(conv_out, "fsdp", axis=1, tiled=True)
        whole_out_t = whole_w_out.T
    wide_rows = 2 * width // 128
    mixed, weights, excite, gate, gram_out, colsum, power_mix, out = call(
        functools.partial(mix_kernel, images_all),
        steps,
        [
            scalars(),
            tiles(mid),
            held(8, mid),
            held(images, att),
            received(8),
            held(8, att),
            held(mid, att),
            held(8, mid),
            held(bottleneck, width),
        ],
        [
            tiled(bottleneck, bf16),
            whole_out((images, mid)),
            whole_out((images, att), bf16),
            whole_out((8, att)),
            whole_out((bottleneck, width)),
            whole_out((8, bottleneck)),
            whole_out((8, 128)),
            sending(wide_rows),
        ],
        [((bottleneck, bottleneck), f32), ((2, 8, bottleneck), f32), ((wide_rows, 128), f32)],
        11,
        name="mix",
    )(half_sides, second, terms_mid, squeeze, got, p_attn, whole_up, p_bias, whole_w_out)
    got = swap_all(out, AXES)

    block, slope, back, grad_out, terms_out, power_out, out = call(
        out_kernel,
        steps,
        [
            scalars(),
            tiles(bottleneck),
            tiles(width),
            tiles(width),
            received(wide_rows),
            held(8, width),
            held(8, 128),
            held(bottleneck, width),
            held(width, bottleneck),
        ],
        [
            tiled(width, bf16),
            tiled(width, bf16),
            tiled(bottleneck),
            whole_out((bottleneck, width)),
            whole_out((8, width)),
            whole_out((8, 128)),
            sending(wide_rows, bf16),
        ],
        [
            ((STEP * 256, width), f32),
            ((8, width), f32),
            ((8, 128), f32),
            ((wide_rows, 128), f32),
            ((8, width), f32),
        ],
        25,
        name="output",
    )(half_sides, mixed, x, cot, got, p_out, count, whole_w_out, whole_out_t)
    got = swap_all(out, AXES)

    dmixed, sums, dup, dbias, dq, grads_out, out = call(
        gate_kernel,
        steps,
        [
            scalars(),
            tiles(mid),
            held(8, mid),
            tiles(bottleneck),
            tiles(bottleneck),
            received(wide_rows),
            held(8, width),
            held(8, width),
            held(8, 128),
            held(bottleneck, width),
            held(width, bottleneck),
            held(images, mid),
            held(images, att),
            held(images, att),
            held(8, att),
            held(mid, att),
            held(8, 128),
            held(8, 128),
        ],
        [
            tiled(bottleneck),
            whole_out((5, images, mid)),
            whole_out((mid, att)),
            whole_out((8, mid)),
            whole_out((images, att)),
            whole_out((8, width)),
            sending(8),
        ],
        [
            ((bottleneck, bottleneck), bf16),
            ((8, bottleneck), f32),
            ((wide_rows, 128), f32),
        ],
        13,
        name="gate",
    )(
        half_sides,
        second,
        terms_mid,
        back,
        mixed,
        got,
        terms_out,
        p_out,
        count,
        whole_w_out,
        whole_out_t,
        weights,
        excite,
        squeeze,
        gate,
        whole_up,
        power_out,
        power_mix,
    )
    got = swap_all(out, AXES)
    grad_conv_out = grad_out - colsum[0][:, None] * grads_out[3] - gram_out * grads_out[2]

    ddown, dpool, grads_attn, out = call(
        functools.partial(squeeze_kernel, images_all, width),
        1,
        [
            scalars(),
            held(images, att),
            held(images, att),
            held(8, att),
            received(8),
            held(images, bottleneck),
            held(bottleneck, att),
            held(images, mid),
            held(5, images, mid),
            held(8, mid),
            held(8, 128),
            held(8, width),
        ],
        [
            whole_out((bottleneck, att)),
            whole_out((images, bottleneck)),
            whole_out((8, att)),
            sending(8),
        ],
        [((8, 128), f32), ((images, bottleneck), f32)],
        1,
        name="squeeze",
    )(
        half_sides,
        dq,
        squeeze,
        gate,
        got,
        pooled,
        whole_down,
        weights,
        sums,
        p_mid,
        count,
        terms_out,
    )
    got = swap_all(out, AXES)

    out_cut = grad_conv_out.astype(bf16).reshape(bottleneck, pieces, -1).transpose(1, 0, 2)
    out_cut = out_cut.reshape(devices, -1, 128)
    bias_rows = jnp.pad(dbias[0].reshape(pieces, 1, up_rows), ((0, 0), (0, 0), (0, att - up_rows)))
    gates = jnp.concatenate(
        [
            dup.reshape(devices, -1, att),
            ddown.reshape(devices, -1, att),
            jnp.repeat(bias_rows, groups, axis=0),
        ],
        axis=1,
    ).astype(bf16)
    marks = [out_cut.shape[1], up_rows // groups, down_rows // groups]
    gates = jnp.concatenate([out_cut, gates], axis=1)
    gates = jnp.pad(gates, ((0, 0), (0, -gates.shape[1] % 16), (0, 0)))

    gates = to_owners(gates)
    dsecond, dfirst, in_grad, grads_mid, stat = call(
        conv_back_kernel,
        steps,
        [
            scalars(),
            tiles(mid),
            held(8, mid),
            received(8),
            held(8, mid),
            held(8, 128),
            tiles(bottleneck),
            held(images, mid),
            held(images, bottleneck),
            tiles(bottleneck),
            held(8, bottleneck),
            held(bottleneck, RADIX * columns),
            tiles(width),
        ],
        [
            tiled(mid, bf16),
            tiled(bottleneck),
            whole_out((bottleneck, width)),
            whole_out((8, mid)),
            whole_out((8, 128)),
        ],
        [
            ((STEP, 256 + 2 * SIDE, RADIX * columns), f32),
            ((2, 8, bottleneck), f32),
            ((8, 128), f32),
        ],
        20,
        name="conv_back",
    )(
        half_sides,
        second,
        terms_mid,
        got,
        p_mid,
        count,
        dmixed,
        weights,
        dpool,
        first,
        terms_in,
        whole_mid,
        x,
    )
    gates, out = call(
        total_kernel,
        1,
        [held(*gates.shape), held(8, 128)],
        [whole_out(gates.shape[1:], bf16), sending(8)],
        (),
        2,
        name="last_gates",
    )(gates, stat)
    got = swap_all(out, AXES)

    outs = []
    scratch = [((STEP, 256 + 2 * SIDE, RADIX * columns), bf16)]
    mid_rows = bottleneck // devices * RADIX * TAPS
    if aligned:
        outs += [whole_out((devices // 2, mid_rows, 128), bf16)] * 2
        scratch = [((bottleneck, RADIX * columns), f32)] + scratch
    else:
        outs += [whole_out((bottleneck, RADIX * columns))]
    conv_parts = call(
        functools.partial(conv_grad_kernel, aligned),
        steps,
        [scalars(), tiles(bottleneck), tiles(mid), token()],
        outs,
        scratch,
        15,
        name="conv_grad",
    )(odd, act_low, dsecond, gates)
    outs = [whole_out((8, bottleneck))]
    scratch = [((8, 128), f32)]
    in_rows = bottleneck // groups * (width // pieces) // 128
    if aligned:
        outs += [whole_out((devices // 2, in_rows, 128), bf16)] * 2
        scratch = [((bottleneck, width), f32)] + scratch
    grads_in, *in_parts = call(
        functools.partial(late_kernel, aligned),
        1,
        [
            scalars(),
            received(8),
            held(8, bottleneck),
            held(8, 128),
            held(bottleneck, width),
            held(bottleneck, width),
            held(8, width),
        ],
        outs,
        scratch,
        2,
        name="last_terms",
    )(odd, got, terms_in, count, in_grad, cross, x_sum)
    grad_features, done = call(
        last_kernel,
        steps,
        [
            scalars(),
            tiles(bottleneck),
            tiles(bottleneck),
            held(8, bottleneck),
            held(width, bottleneck),
            tiles(width),
            held(8, width),
        ],
        [tiled(width), whole_out((8, 128))],
        [((STEP * 256, bottleneck), bf16)],
        15,
        name="last",
    )(half_sides, dfirst, first, grads_in, whole_in, slope, terms_out)

    if aligned:
        mid_got, in_got = neighbour(conv_parts[1]), neighbour(in_parts[1])
        (late,) = call(
            merge_kernel,
            1,
            [held(*mid_got.shape)] * 2 + [held(*in_got.shape)] * 2,
            [whole_out((devices // 2, in_rows + mid_rows, 128), bf16)],
            (),
            2,
            name="last_merge",
        )(conv_parts[0], mid_got, in_parts[0], in_got)
    else:
        grad_conv_in = (
            in_grad * grads_in[4][:, None]
            - cross * grads_in[2][:, None]
            - column_total(x_sum) * grads_in[3][:, None]
        )
        in_cut = grad_conv_in.astype(bf16).reshape(bottleneck, pieces, -1).transpose(1, 0, 2)
        mid_cut = conv_parts[0].astype(bf16).reshape(devices, -1, RADIX * TAPS, 128)
        mid_cut = mid_cut.transpose(0, 2, 1, 3).reshape(devices, -1, 128)
        late = jnp.concatenate([in_cut.reshape(devices, -1, 128), mid_cut], axis=1)
        late = jnp.pad(late, ((0, 0), (0, -late.shape[1] % 16), (0, 0)))
        late = on_own_side(late)
    late = across_sides(late)
    (summed,) = call(
        total_last_kernel,
        1,
        [held(*gates.shape), held(*late.shape), token()],
        [whole_out((gates.shape[0] + late.shape[1], 128), bf16)],
        (),
        2,
        name="last_total",
    )(gates, late, done)
    marks += [gates.shape[0], in_rows]
    own_width = width // pieces
    if aligned:
        members = [summed] + [
            lax.ppermute(summed, "dp", [(i, i ^ k) for i in range(groups)])
            for k in range(1, groups)
        ]
        shard_out, shard_up, shard_down, shard_bias, shard_in, shard_mid = call(
            functools.partial(shards_kernel, marks),
            1,
            [scalars()] + [held(*summed.shape)] * groups,
            [
                whole_out((bottleneck, own_width)),
                whole_out((up_rows, att)),
                whole_out((down_rows, att)),
                whole_out((1, up_rows)),
                whole_out((own_width, bottleneck)),
                whole_out((RADIX * TAPS, own_columns, 128)),
            ],
            [((groups,) + summed.shape, f32)],
            2,
            name="last_shards",
        )(lax.axis_index("dp").reshape(1), *members)
        shard_bias = shard_bias.reshape(-1)
        shard_up = shard_up.T
        shard_mid = shard_mid.reshape(RADIX, TAPS, own_columns, 128).transpose(0, 1, 3, 2)
    else:
        summed = swap_all(jnp.broadcast_to(summed[None], (groups,) + summed.shape), "dp")
        summed = summed.astype(f32)
        shard_out = summed[:, : marks[0]].reshape(bottleneck, -1)
        at = marks[0]
        shard_up = summed[:, at : at + marks[1]].reshape(up_rows, att).T
        at += marks[1]
        shard_down = summed[:, at : at + marks[2]].reshape(down_rows, att)
        at += marks[2]
        shard_bias = summed[0, at, :up_rows]
        at = marks[3]
        shard_in = summed[:, at : at + in_rows].reshape(bottleneck, -1).T
        at += in_rows
        shard_mid = summed[:, at : at + mid_rows].reshape(groups, RADIX, TAPS, -1, 128)
        shard_mid = shard_mid.transpose(1, 2, 4, 0, 3).reshape(RADIX, TAPS, 128, own_columns)

    def own_part(row):
        length = row.shape[0] // pieces
        return lax.dynamic_slice_in_dim(row, lax.axis_index("fsdp") * length, length, 0)

    return (
        block.reshape(images, pixels, width),
        grad_features.reshape(images, pixels, width),
        grads_attn[2, :4],
        shard_in,
        shard_mid,
        shard_down,
        shard_up,
        shard_bias,
        shard_out,
        own_part(grads_in[1]),
        own_part(grads_in[0]),
        own_part(grads_mid[1]),
        own_part(grads_mid[0]),
        own_part(grads_attn[1]),
        own_part(grads_attn[0]),
        own_part(grads_out[1]),
        own_part(grads_out[0]),
    )


def solution(mesh):
    return jax.shard_map(
        local,
        mesh=mesh,
        in_specs=(
            P(("fsdp", "dp"), None, None),
            P(("fsdp", "dp")),
            P(("fsdp", "dp"), None, None),
            P("fsdp", None),
            P(None, None, None, "fsdp"),
            P("fsdp", None),
            P(None, "fsdp"),
            P("fsdp"),
            P(None, "fsdp"),
            P("fsdp"),
            P("fsdp"),
            P("fsdp"),
            P("fsdp"),
            P("fsdp"),
            P("fsdp"),
            P("fsdp"),
            P("fsdp"),
        ),
        out_specs=(
            P(("fsdp", "dp"), None, None),
            P(("fsdp", "dp"), None, None),
            P(),
            P("fsdp", None),
            P(None, None, None, "fsdp"),
            P("fsdp", None),
            P(None, "fsdp"),
            P("fsdp"),
            P(None, "fsdp"),
            P("fsdp"),
            P("fsdp"),
            P("fsdp"),
            P("fsdp"),
            P("fsdp"),
            P("fsdp"),
            P("fsdp"),
            P("fsdp"),
        ),
        check_vma=False,
    )
```

```python
import functools

import jax
import jax.numpy as jnp
from jax import lax
from jax.experimental import pallas as pl
from jax.experimental.pallas import tpu as pltpu
from jax.sharding import PartitionSpec as P

RADIX = 2
SIDE = 16
TAPS = 9
STEP = 4

epsilon = 1e-05
AXES = ("fsdp", "dp")
f32 = jnp.float32
bf16 = jnp.bfloat16
HIGH = lax.Precision.HIGHEST


def swap_all(values, axes):
    return lax.all_to_all(values, axes, 0, 0)


def gather_all(shard):
    pieces = lax.axis_size("fsdp")
    return swap_all(jnp.broadcast_to(shard[None], (pieces,) + shard.shape), "fsdp")


def neighbour(values):
    return lax.ppermute(values, "dp", [(i, i ^ 1) for i in range(lax.axis_size("dp"))])


ORDER = (0, 4, 2, 6, 1, 5, 3, 7)


def partner(values, k):
    pieces = lax.axis_size("fsdp")
    return lax.ppermute(values, "fsdp", [(i, i ^ k) for i in range(pieces)])


def on_own_side(parts):
    odd = lax.rem(lax.axis_index("dp"), 2)
    parts = parts.reshape((parts.shape[0] // 2, 2) + parts.shape[1:])
    mine = lax.dynamic_index_in_dim(parts, odd, 1, False)
    other = lax.dynamic_index_in_dim(parts, 1 - odd, 1, False)
    return (mine.astype(f32) + neighbour(other).astype(f32)).astype(bf16)


def across_sides(parts):
    count = parts.shape[0]
    sides = [[2 * i + side for i in range(count)] for side in range(2)]
    return lax.all_to_all(parts, AXES, 0, 0, axis_index_groups=sides)


def to_owners(parts):
    return across_sides(on_own_side(parts))


def half_of(shard, axis):
    odd = lax.rem(lax.axis_index("dp"), 2)
    return lax.dynamic_slice_in_dim(shard, odd * (shard.shape[axis] // 2), shard.shape[axis] // 2, axis)


def sigmoid(values):
    return 0.5 * jnp.tanh(0.5 * values) + 0.5


def fold(values):
    return values[:8] + values[8:]


def wide(mask, lanes):
    return jnp.concatenate([mask] * (lanes // mask.shape[1]), axis=1)


def half_silu(half, mask):
    return half * ((1.0 + jnp.tanh(half)) * mask)


def twice_slope(half):
    turned = jnp.tanh(half)
    return (1.0 + turned) * (1.0 + half * (1.0 - turned))


def places():
    return lax.broadcasted_iota(jnp.int32, (SIDE, 128), 0)


def row_mask(place, row, limit):
    return jnp.where((place < limit) & (row < limit), 1.0, 0.0).astype(f32)


def chunk(image, row):
    return pl.ds(pl.multiple_of(image * 256 + row * SIDE, SIDE), SIDE)


def of_image(image):
    return slice(image * 256, image * 256 + 256)


def of_row(image, row):
    return slice(image * 256 + row * SIDE, image * 256 + row * SIDE + SIDE)


def stages(*parts):
    for stage in range(STEP + len(parts) - 1):
        for late, part in reversed(list(enumerate(parts))):
            if 0 <= stage - late < STEP:
                part(stage - late)


def rows_of(carry, body, unroll=8):
    return lax.fori_loop(0, SIDE, body, carry, unroll=unroll)


def contract_lead(left, right):
    return lax.dot_general(left, right, (((0,), (0,)), ((), ())), preferred_element_type=f32)


def contract_last(left, right):
    return lax.dot_general(left, right, (((1,), (1,)), ((), ())), preferred_element_type=f32)


def three_parts(values):
    high = values.astype(bf16)
    rest = values - high.astype(f32)
    middle = rest.astype(bf16)
    low = (rest - middle.astype(f32)).astype(bf16)
    return jnp.concatenate([high, middle, low], axis=0)


def exact_dot(values, right):
    rows = values.shape[0]
    parts = jnp.dot(three_parts(values), right, preferred_element_type=f32)
    return parts[:rows] + (parts[rows : 2 * rows] + parts[2 * rows :])


def zeros_at_start(*refs):
    @pl.when(pl.program_id(0) == 0)
    def _():
        for ref in refs:
            ref[...] = jnp.zeros(ref.shape, ref.dtype)


def edge_zeros_at_start(ref, first, last):
    @pl.when(pl.program_id(0) == 0)
    def _():
        for row in (first, last):
            here = slice(row * SIDE, row * SIDE + SIDE)
            ref[:, here, :] = jnp.zeros((ref.shape[0], SIDE, ref.shape[2]), ref.dtype)


def last_step():
    return pl.program_id(0) == pl.num_programs(0) - 1


def column_total(values):
    return jnp.sum(values, axis=0, keepdims=True)


def take(recv_ref, tile_ref):
    tile_ref[...] = lax.fori_loop(
        1,
        recv_ref.shape[0],
        lambda j, total: total + recv_ref[j].astype(f32),
        recv_ref[0].astype(f32),
        unroll=True if recv_ref.shape[0] <= 32 else 1,
    )


def row_at(tile_ref, start, lanes):
    return jnp.concatenate(
        [tile_ref[start + q : start + q + 1, :] for q in range(lanes // 128)], axis=1
    )


def put(tile_ref, start, row):
    for q in range(row.shape[1] // 128):
        tile_ref[start + q : start + q + 1, :] = row[:, q * 128 : (q + 1) * 128]


def send(send_ref, tile_ref):
    tile = tile_ref[...].astype(send_ref.dtype)

    def body(j, carry):
        send_ref[j] = tile
        return carry

    lax.fori_loop(0, send_ref.shape[0], body, 0, unroll=True if send_ref.shape[0] <= 32 else 1)


def norm_rows(sums, squares, counted, gain, shift):
    center = sums / counted
    spread = squares / counted - center * center
    inv = lax.rsqrt(spread + epsilon)
    scale = gain * inv
    return center, spread, inv, scale, shift - center * scale


def fill_half(whole_ref, mine_ref, other_ref, odd_ref):
    half = whole_ref.shape[1] // 2

    @pl.when(odd_ref[0] == 0)
    def _():
        whole_ref[:, :half] = mine_ref[...]
        whole_ref[:, half:] = other_ref[...]

    @pl.when(odd_ref[0] != 0)
    def _():
        whole_ref[:, :half] = other_ref[...]
        whole_ref[:, half:] = mine_ref[...]


def at_start(body):
    pl.when(pl.program_id(0) == 0)(body)


def at_end(body):
    pl.when(pl.program_id(0) == pl.num_programs(0) - 1)(body)


def lane_parts(values):
    total = values[:, :128]
    for at in range(128, values.shape[1], 128):
        total = total + values[:, at : at + 128]
    return total


def lane_sum(row):
    return jnp.broadcast_to(jnp.sum(row, axis=1, keepdims=True), (1, 128))


def prepare_kernel(odd, mid_ref, down_ref, up_ref, out_ref, *refs):
    *vector_refs, most_send, rows_ref = refs
    rows_ref[...] = jnp.zeros(rows_ref.shape, f32)
    for k, ref in enumerate(vector_refs):
        rows_ref[k : k + 1, : ref.shape[1]] = ref[...].astype(f32)
    at = mid_ref.shape[1] + 128
    for ref in (down_ref, up_ref):
        most_send[at : at + ref.shape[0], :] = ref[...]
        at += ref.shape[0]
    most_send[at : at + 16, :] = rows_ref[...].astype(bf16)
    for side in range(2):

        @pl.when(odd[0] == side)
        def _():
            at = mid_ref.shape[1]
            most_send[:at, :] = mid_ref[side]
            most_send[at : at + 128, :] = jnp.transpose(out_ref[side * 128 : side * 128 + 128, :])


def first_kernel(
    sides, odd, x_ref, mine_ref, other_ref, first_ref, w_ref, send_ref, acc_ref, tile_ref
):
    step = pl.program_id(0)
    zeros_at_start(acc_ref)
    at_start(lambda: fill_half(w_ref, mine_ref, other_ref, odd))
    place = places()
    lanes = first_ref.shape[1]
    sums = [acc_ref[0], acc_ref[1]]

    def multiply(image):
        first_ref[of_image(image), :] = jnp.dot(
            x_ref[of_image(image), :], w_ref[...], preferred_element_type=f32
        )

    def finish(image):
        limit = 2 * sides[step * STEP + image]
        for row in range(SIDE):
            here = of_row(image, row)
            values = first_ref[here, :] * wide(row_mask(place, row, limit), lanes)
            first_ref[here, :] = values
            sums[0] = sums[0] + fold(values)
            sums[1] = sums[1] + fold(values * values)

    stages(multiply, finish)
    acc_ref[0], acc_ref[1] = sums

    @at_end
    def _():
        count = jnp.int32(0)
        for image in range(sides.shape[0]):
            count = count + 4 * sides[image] * sides[image]
        tile_ref[...] = jnp.zeros(tile_ref.shape, f32)
        put(tile_ref, 0, column_total(acc_ref[0]))
        put(tile_ref, lanes // 128, column_total(acc_ref[1]))
        put(tile_ref, 2 * lanes // 128, jnp.full((1, 128), count, jnp.int32).astype(f32))
        send(send_ref, tile_ref)


def cross_kernel(
    sides, x_ref, first_ref, cross_ref, ones_ref, power_ref, square_ref
):
    step = pl.program_id(0)
    zeros_at_start(cross_ref, square_ref, ones_ref)
    place = places()
    lanes = x_ref.shape[1]
    sums = [square_ref[...], ones_ref[...]]

    def multiply(image):
        here = of_image(image)
        cross_ref[...] += contract_lead(first_ref[here, :].astype(bf16), x_ref[here, :])

    def add_up(image):
        limit = 2 * sides[step * STEP + image]
        for row in range(SIDE):
            values = x_ref[of_row(image, row), :].astype(f32) * wide(
                row_mask(place, row, limit), lanes
            )
            sums[0] = sums[0] + fold(values * values)
            sums[1] = sums[1] + fold(values)

    stages(multiply, add_up)
    square_ref[...], ones_ref[...] = sums

    @at_end
    def _():
        power_ref[...] = lane_parts(square_ref[...])


def write_patches(patch_ref, image, row, low, place):
    values = low.astype(f32)
    lanes = values.shape[1]
    inner = wide(place, lanes)
    left = jnp.where(inner == 0, 0.0, pltpu.roll(values, 1, 0)).astype(bf16)
    right = jnp.where(inner == SIDE - 1, 0.0, pltpu.roll(values, SIDE - 1, 0)).astype(bf16)
    for tap in range(TAPS):
        up, side = tap // 3, tap % 3
        source = (left, low, right)[side]
        here = (row + 2 - up) * SIDE
        if isinstance(row, int):
            here = slice(here, here + SIDE)
        else:
            here = pl.ds(pl.multiple_of(here, SIDE), SIDE)
        for group in range(lanes // 128):
            at = (group * TAPS + tap) * 128
            patch_ref[image, here, at : at + 128] = source[:, group * 128 : (group + 1) * 128]


def second_kernel(lengths, sides, first_ref, recv_ref, _, *refs):
    if lengths:
        member, odd, *refs = refs
        shard_refs, refs = refs[:4], refs[4:]
        act_ref, second_ref, terms_ref, count_ref, send_ref, w_ref, down_ref, up_ref, *refs = refs
        *param_refs, patch_ref, acc_ref, tile_ref, param_ref = refs
    else:
        w_ref, param_ref, act_ref, second_ref, terms_ref, count_ref, send_ref, *refs = refs
        patch_ref, acc_ref, tile_ref = refs
    step = pl.program_id(0)
    zeros_at_start(acc_ref)
    edge_zeros_at_start(patch_ref, 1, SIDE)
    place = places()
    lanes = first_ref.shape[1]
    columns = TAPS * lanes // RADIX

    @at_start
    def _():
        if lengths:
            own = w_ref.shape[0] // len(ORDER)
            downs, ups = down_ref.shape[0] // len(ORDER), up_ref.shape[0] // len(ORDER)
            wholes = [jnp.zeros((16, length * len(ORDER)), f32) for length in lengths]
            lane = lax.broadcasted_iota(jnp.int32, (16, 128), 1)
            for index, k in enumerate(ORDER):
                piece = member[0] ^ k
                ref = shard_refs[index // 4]
                index = index % 4
                at = TAPS * own + 128
                down_ref[pl.ds(pl.multiple_of(piece * downs, downs), downs), :] = ref[
                    index, at : at + downs, :
                ]
                at += downs
                up_ref[pl.ds(pl.multiple_of(piece * ups, ups), ups), :] = ref[
                    index, at : at + ups, :
                ]
                at += ups
                rows = ref[index, at : at + 16, :].astype(f32)
                for length in sorted(set(lengths)):
                    part = jnp.where(lane < length, rows, 0.0)
                    spare = (length * len(ORDER) - 128) // 128
                    part = jnp.concatenate([part] + [jnp.zeros((16, 128), f32)] * spare, axis=1)
                    part = pltpu.roll(part, piece * length, 1)
                    wholes = [
                        whole + part if whole.shape == part.shape else whole for whole in wholes
                    ]
            for side in range(2):

                @pl.when(odd[0] == side)
                def _():
                    for index, k in enumerate(ORDER):
                        here = pl.ds(pl.multiple_of((member[0] ^ k) * own, own), own)
                        for refs, group in ((shard_refs[:2], side), (shard_refs[2:], 1 - side)):
                            for tap in range(TAPS):
                                at = (group * TAPS + tap) * 128
                                w_ref[here, at : at + 128] = refs[index // 4][
                                    index % 4, tap * own : (tap + 1) * own, :
                                ]

            for k, whole in enumerate(wholes):
                ref = ([param_ref] + param_refs)[k // 2]
                ref[k % 2 : k % 2 + 1, :] = whole[k : k + 1, :]
        take(recv_ref, tile_ref)
        count = tile_ref[2 * lanes // 128 : 2 * lanes // 128 + 1, :]
        count_ref[...] = jnp.broadcast_to(count, count_ref.shape)
        center, _, inv, scale, offset = norm_rows(
            row_at(tile_ref, 0, lanes),
            row_at(tile_ref, lanes // 128, lanes),
            wide(count, lanes),
            param_ref[0:1, :],
            param_ref[1:2, :],
        )
        terms_ref[0:1, :] = scale
        terms_ref[1:2, :] = offset
        terms_ref[2:3, :] = inv
        terms_ref[3:4, :] = -center * inv
        terms_ref[4:5, :] = center
        terms_ref[5:6, :] = 0.5 * scale
        terms_ref[6:7, :] = 0.5 * offset

    def start_image(image):
        limit = 2 * sides[step * STEP + image]
        for row in range(SIDE):
            here = slice(image * 256 + row * SIDE, image * 256 + row * SIDE + SIDE)
            act = half_silu(
                first_ref[here, :] * terms_ref[5:6, :] + terms_ref[6:7, :],
                wide(row_mask(place, row, limit), lanes),
            )
            low = act.astype(bf16)
            act_ref[here, :] = low
            write_patches(patch_ref, image, row, low, place)

    def multiply_image(image):
        for group in range(RADIX):
            second_ref[image * 256 : image * 256 + 256, group * lanes : (group + 1) * lanes] = (
                contract_last(
                    patch_ref[image, SIDE : SIDE + 256, group * columns : (group + 1) * columns],
                    w_ref[:, group * columns : (group + 1) * columns],
                )
            )

    def sum_image(image, carry):
        limit = 2 * sides[step * STEP + image]
        total, square = carry
        for row in range(SIDE):
            values = second_ref[image * 256 + row * SIDE : image * 256 + row * SIDE + SIDE, :]
            values = values * wide(row_mask(place, row, limit), values.shape[1])
            total, square = total + fold(values), square + fold(values * values)
        return total, square

    carry = (acc_ref[0], acc_ref[1])
    for stage in range(STEP + 2):
        if 0 <= stage - 1 < STEP:
            multiply_image(stage - 1)
        if stage < STEP:
            start_image(stage)
        if stage >= 2:
            carry = sum_image(stage - 2, carry)
    acc_ref[0], acc_ref[1] = carry

    @at_end
    def _():
        tile_ref[...] = jnp.zeros(tile_ref.shape, f32)
        put(tile_ref, 0, column_total(acc_ref[0]))
        put(tile_ref, RADIX * lanes // 128, column_total(acc_ref[1]))
        send(send_ref, tile_ref)


def pool_kernel(
    sides,
    second_ref,
    recv_ref,
    param_ref,
    count_ref,
    down_ref,
    power_ref,
    pooled_ref,
    squeeze_ref,
    terms_ref,
    send_ref,
    pool_ref,
    tile_ref,
):
    step = pl.program_id(0)
    place = places()
    lanes = second_ref.shape[1]

    @at_start
    def _():
        take(recv_ref, tile_ref)
        _, _, _, scale, offset = norm_rows(
            row_at(tile_ref, 0, lanes),
            row_at(tile_ref, lanes // 128, lanes),
            wide(count_ref[0:1, :], lanes),
            param_ref[0:1, :],
            param_ref[1:2, :],
        )
        terms_ref[0:1, :] = scale
        terms_ref[1:2, :] = offset
        terms_ref[2:3, :] = 0.5 * scale
        terms_ref[3:4, :] = 0.5 * offset

    for image in range(STEP):
        limit = 2 * sides[step * STEP + image]

        total = jnp.zeros((8, lanes), f32)
        for row in range(SIDE):
            act = half_silu(
                second_ref[of_row(image, row), :] * terms_ref[2:3, :] + terms_ref[3:4, :],
                wide(row_mask(place, row, limit), lanes),
            )
            total = total + fold(act)
        total = column_total(total)
        both = total[:, : lanes // 2] + total[:, lanes // 2 :]
        area = jnp.full(both.shape, limit * limit, jnp.int32).astype(f32)
        pool_ref[pl.ds(step * STEP + image, 1), :] = both / area

    @at_end
    def _():
        low = pool_ref[...].astype(bf16)
        pooled_ref[...] = low
        squeeze = jnp.dot(low, down_ref[...], preferred_element_type=f32)
        squeeze_ref[...] = squeeze
        tile_ref[...] = jnp.zeros(tile_ref.shape, f32)
        tile_ref[0:1, :] = column_total(squeeze)
        tile_ref[1:2, :] = column_total(squeeze * squeeze)
        tile_ref[2:3, :] = column_total(power_ref[...])
        send(send_ref, tile_ref)


def out_weights_kernel(start, place, odd, _, *refs):
    *shard_refs, w_ref, wt_ref = refs
    for side in range(2):

        @pl.when(odd[0] == side)
        def _():
            for index, k in enumerate(ORDER):
                here = pl.ds(pl.multiple_of((place[0] ^ k) * 128, 128), 128)
                for refs, half in ((shard_refs[:2], side), (shard_refs[2:], 1 - side)):
                    wt_ref[here, half * 128 : half * 128 + 128] = refs[index // 4][
                        index % 4, start : start + 128, :
                    ]

    w_ref[...] = jnp.transpose(wt_ref[...])


def mix_kernel(
    images_all,
    sides,
    second_ref,
    ab_ref,
    squeeze_ref,
    recv_ref,
    param_ref,
    up_ref,
    bias_ref,
    out_ref,
    mixed_ref,
    weights_ref,
    excite_ref,
    gate_ref,
    gw_ref,
    colsum_ref,
    power_ref,
    send_ref,
    gram_ref,
    acc_ref,
    tile_ref,
):
    step = pl.program_id(0)
    zeros_at_start(acc_ref, gram_ref)
    place = places()
    lanes = second_ref.shape[1]
    half = lanes // 2

    @at_start
    def _():
        tile_ref[0:8, :] = recv_ref[0]
        for j in range(1, recv_ref.shape[0]):
            tile_ref[0:8, :] += recv_ref[j]
        center, _, inv, scale, offset = norm_rows(
            tile_ref[0:1, :],
            tile_ref[1:2, :],
            jnp.float32(images_all),
            param_ref[0:1, :],
            param_ref[1:2, :],
        )
        gate_ref[0:1, :] = scale
        gate_ref[1:2, :] = offset
        gate_ref[2:3, :] = inv
        gate_ref[3:4, :] = -center * inv
        gate_ref[4:5, :] = tile_ref[2:3, :]
        pre = squeeze_ref[...] * scale + offset
        excite = (pre * sigmoid(pre)).astype(bf16)
        excite_ref[...] = excite
        logits = contract_last(excite, up_ref[...]) + bias_ref[0:1, :]
        one, two = logits[:, :half], logits[:, half:]
        top = jnp.maximum(one, two)
        one, two = jnp.exp(one - top), jnp.exp(two - top)
        weights_ref[:, :half] = one / (one + two)
        weights_ref[:, half:] = two / (one + two)

    sums = [acc_ref[0], acc_ref[1]]

    def mix(image):
        limit = 2 * sides[step * STEP + image]
        weights = weights_ref[pl.ds(step * STEP + image, 1), :]
        for row in range(SIDE):
            here = of_row(image, row)
            act = half_silu(
                second_ref[here, :] * ab_ref[2:3, :] + ab_ref[3:4, :],
                wide(row_mask(place, row, limit), lanes),
            )
            act = act * weights
            mixed = act[:, :half] + act[:, half:]
            low = mixed.astype(bf16)
            mixed_ref[here, :] = low
            sums[0] = sums[0] + fold(low.astype(f32))
            sums[1] = sums[1] + fold(mixed * mixed)

    def square(image):
        values = mixed_ref[of_image(image), :]
        gram_ref[...] += contract_lead(values, values)

    stages(mix, square)
    acc_ref[0], acc_ref[1] = sums

    @at_end
    def _():
        whole = out_ref[...].astype(f32)
        total = column_total(acc_ref[0])
        colsum_ref[...] = jnp.broadcast_to(total, colsum_ref.shape)
        power_ref[...] = lane_parts(acc_ref[1])
        both = jnp.concatenate([gram_ref[...], jnp.broadcast_to(total, (16, half))], axis=0)
        both = exact_dot(both, out_ref[...])
        gw = both[:half]
        gw_ref[...] = gw
        sums = both[half:]
        count = jnp.int32(0)
        for image in range(sides.shape[0]):
            count = count + 4 * sides[image] * sides[image]
        count = jnp.full((1, 128), count, jnp.int32).astype(f32)
        sums = sums[0:1, :]
        wide_count = wide(count, sums.shape[1])
        put(tile_ref, 0, column_total(gw * whole) - sums * sums / wide_count)
        at = sums.shape[1] // 128
        parts = three_parts(jnp.broadcast_to(total, (16, half))).astype(f32)
        for index in range(3):
            put(tile_ref, at + index * half // 128, parts[16 * index : 16 * index + 1, :])
        high = count.astype(bf16).astype(f32)
        tile_ref[at + 6 : at + 7, :] = high
        tile_ref[at + 7 : at + 8, :] = count - high
        send(send_ref, tile_ref)


def out_kernel(
    sides,
    mixed_ref,
    x_ref,
    cot_ref,
    recv_ref,
    param_ref,
    count_ref,
    w_ref,
    wt_ref,
    block_ref,
    slope_ref,
    back_ref,
    grad_ref,
    terms_ref,
    power_ref,
    send_ref,
    third_ref,
    acc_ref,
    square_ref,
    tile_ref,
    half_ref,
    flat_ref,
):
    step = pl.program_id(0)
    zeros_at_start(acc_ref, square_ref, grad_ref)
    place = places()
    lanes = x_ref.shape[1]
    part = 256 if lanes % 256 == 0 else lanes

    @at_start
    def _():
        devices, rows = recv_ref.shape[:2]
        for device in range(devices):
            flat_ref[device * rows : (device + 1) * rows, :] = recv_ref[device].astype(f32)
        take(recv_ref, tile_ref)

        def of_all(row):
            return flat_ref[pl.ds(row, devices, stride=rows), :]

        at = lanes // 128
        parts = [
            jnp.concatenate([of_all(at + 2 * index), of_all(at + 2 * index + 1)], axis=1)
            for index in range(3)
        ]
        parts = jnp.concatenate(parts, axis=0).astype(bf16)
        parts = jnp.dot(parts, w_ref[...], preferred_element_type=f32)
        sums = parts[:devices] + (parts[devices : 2 * devices] + parts[2 * devices :])
        counts = wide(of_all(at + 6) + of_all(at + 7), lanes)
        squares = column_total(sums * sums / counts) + row_at(tile_ref, 0, lanes)
        count = count_ref[0:1, :]
        gain, shift = param_ref[0:1, :], param_ref[1:2, :]
        center, spread, inv, scale, offset = norm_rows(
            column_total(sums), squares, wide(count, lanes), gain, shift
        )
        branch = gain * gain * spread * inv * inv + shift * shift
        terms_ref[0:1, :] = scale
        terms_ref[1:2, :] = offset
        terms_ref[2:3, :] = center
        terms_ref[3:4, :] = inv
        terms_ref[4:5, :] = 1.0 / scale
        terms_ref[5:6, :] = wide(lane_sum(branch), lanes)
        half_ref[0:1, :] = 0.5 * scale
        half_ref[1:2, :] = 0.5 * offset

    squares = [square_ref[...]]
    sums = {at: acc_ref[:, at : at + part] for at in range(0, lanes, part)}

    def expand(image):
        third_ref[of_image(image), :] = jnp.dot(
            mixed_ref[of_image(image), :], w_ref[...], preferred_element_type=f32
        )

    def finish(image):
        limit = 2 * sides[step * STEP + image]
        for row in range(SIDE):
            here = of_row(image, row)
            mask = wide(row_mask(place, row, limit), part)
            for at in range(0, lanes, part):
                cut = slice(at, at + part)
                half = (
                    (x_ref[here, cut] * bf16(0.5)).astype(f32)
                    + third_ref[here, cut] * half_ref[0:1, cut]
                    + half_ref[1:2, cut]
                )
                turned = jnp.tanh(half)
                gate = (1.0 + turned) * mask
                output = half * gate
                block_ref[here, cut] = output.astype(bf16)
                slope = gate + output * (1.0 - turned)
                grad = cot_ref[here, cut].astype(f32) * (slope * half_ref[0:1, cut])
                slope_ref[here, cut] = grad.astype(bf16)
                sums[at] = sums[at] + fold(grad)
                squares[0] = squares[0] + lane_parts(fold(output * output))

    def contract(image):
        here = of_image(image)
        back_ref[here, :] = jnp.dot(slope_ref[here, :], wt_ref[...], preferred_element_type=f32)
        grad_ref[...] += contract_lead(mixed_ref[here, :], slope_ref[here, :])

    stages(expand, finish, contract)
    square_ref[...] = squares[0]
    for at, total in sums.items():
        acc_ref[:, at : at + part] = total

    @at_end
    def _():
        power_ref[...] = square_ref[...]
        total = column_total(acc_ref[...])
        put(tile_ref, 0, total)
        turned = column_total(grad_ref[...] * w_ref[...].astype(f32))
        put(tile_ref, lanes // 128, turned - terms_ref[2:3, :] * total)
        send(send_ref, tile_ref)


def mid_terms(second_ref, ab_ref, here, mask):
    half = second_ref[here, :] * ab_ref[2:3, :] + ab_ref[3:4, :]
    turned = jnp.tanh(half)
    gate = (1.0 + turned) * mask
    act = half * gate
    return half, act, gate + act * (1.0 - turned)


def gate_kernel(
    sides,
    second_ref,
    ab_ref,
    back_ref,
    mixed_ref,
    recv_ref,
    terms_ref,
    param_ref,
    count_ref,
    w_ref,
    wt_ref,
    weights_ref,
    excite_ref,
    squeeze_ref,
    gate_ref,
    up_ref,
    power_out_ref,
    power_mix_ref,
    dmixed_ref,
    sums_ref,
    dup_ref,
    dbias_ref,
    dq_ref,
    grads_ref,
    send_ref,
    turn_ref,
    row_ref,
    tile_ref,
):
    step = pl.program_id(0)
    place = places()
    lanes = second_ref.shape[1]
    half = lanes // 2
    width = w_ref.shape[1]

    @at_start
    def _():
        take(recv_ref, tile_ref)
        count = wide(count_ref[0:1, :], width)
        total = row_at(tile_ref, 0, width)
        scale, center, inv = terms_ref[0:1, :], terms_ref[2:3, :], terms_ref[3:4, :]
        gain_grad = row_at(tile_ref, width // 128, width) / param_ref[0:1, :]
        slant = scale * inv * gain_grad / count
        level = total / count - center * slant
        grads_ref[0:1, :] = total * terms_ref[4:5, :]
        grads_ref[1:2, :] = gain_grad
        grads_ref[2:3, :] = slant
        grads_ref[3:4, :] = level
        whole = w_ref[...].astype(f32)
        turn_ref[...] = jnp.dot(
            (whole * slant).astype(bf16), wt_ref[...], preferred_element_type=f32
        ).astype(bf16)
        row_ref[...] = exact_dot(jnp.broadcast_to(level, (16, width)), wt_ref[...])[:8]

    def turn(image):
        here = of_image(image)
        dmixed_ref[here, :] = back_ref[here, :] - jnp.dot(
            mixed_ref[here, :], turn_ref[...], preferred_element_type=f32
        )

    def add_up(image):
        limit = 2 * sides[step * STEP + image]
        totals = [jnp.zeros((8, lanes), f32) for _ in range(5)]
        for row in range(SIDE):
            here = of_row(image, row)
            mask = row_mask(place, row, limit)
            dmixed = (dmixed_ref[here, :] - row_ref[0:1, :]) * wide(mask, half)
            dmixed_ref[here, :] = dmixed
            both = jnp.concatenate([dmixed, dmixed], axis=1)
            pre, act, slope = mid_terms(second_ref, ab_ref, here, wide(mask, lanes))
            along = slope * both
            terms = (act * both, along, along * pre, slope, slope * pre)
            totals = [old + fold(new) for old, new in zip(totals, terms)]
        for index in range(5):
            part = column_total(totals[index]) * (0.5 if index in (1, 3) else 1.0)
            sums_ref[index, pl.ds(step * STEP + image, 1), :] = part

    stages(turn, add_up)

    @at_end
    def _():
        weights = weights_ref[...]
        grads = sums_ref[0]
        mean = weights * grads
        mean = mean[:, :half] + mean[:, half:]
        dlogits = weights * (grads - jnp.concatenate([mean, mean], axis=1))
        dbias_ref[...] = jnp.broadcast_to(column_total(dlogits), dbias_ref.shape)
        low = dlogits.astype(bf16)
        dup_ref[...] = contract_lead(low, excite_ref[...])
        dexcite = jnp.dot(low, up_ref[...], preferred_element_type=f32)
        squeeze = squeeze_ref[...]
        pre = squeeze * gate_ref[0:1, :] + gate_ref[1:2, :]
        normed = squeeze * gate_ref[2:3, :] + gate_ref[3:4, :]
        plain = sigmoid(pre)
        dq = dexcite * (plain * (1.0 + pre * (1.0 - plain)))
        dq_ref[...] = dq
        tile_ref[0:1, :] = column_total(dq)
        tile_ref[1:2, :] = column_total(dq * normed)
        tile_ref[2:3, :] = column_total(power_out_ref[...])
        tile_ref[3:4, :] = column_total(power_mix_ref[...])
        tile_ref[4:8, :] = jnp.zeros((4, 128), f32)
        tile = tile_ref[0:8, :]
        for j in range(send_ref.shape[0]):
            send_ref[j] = tile


def squeeze_kernel(
    images_all,
    width,
    sides,
    dq_ref,
    squeeze_ref,
    gate_ref,
    recv_ref,
    pooled_ref,
    down_ref,
    weights_ref,
    sums_ref,
    param_ref,
    count_ref,
    terms_ref,
    ddown_ref,
    dpool_ref,
    grads_ref,
    send_ref,
    tile_ref,
    area_ref,
):
    take(recv_ref, tile_ref)
    shift, gain = tile_ref[0:1, :], tile_ref[1:2, :]
    grads_ref[0:1, :] = shift
    grads_ref[1:2, :] = gain
    bottleneck = pooled_ref.shape[1]
    count = count_ref[0:1, :]
    powers = (
        lane_sum(gate_ref[4:5, :]) / (count * width),
        lane_sum(tile_ref[3:4, :]) / (count * bottleneck),
        terms_ref[5:6, :128] / width,
        lane_sum(tile_ref[2:3, :]) / (count * width),
    )
    place = lax.broadcasted_iota(jnp.int32, (1, 128), 1)
    norms = powers[3]
    for index in range(3):
        norms = jnp.where(place == index, powers[index], norms)
    grads_ref[2:3, :] = jnp.sqrt(norms)
    normed = squeeze_ref[...] * gate_ref[2:3, :] + gate_ref[3:4, :]
    dsqueeze = gate_ref[0:1, :] * (
        dq_ref[...] - (shift + normed * gain) / jnp.float32(images_all)
    )
    low = dsqueeze.astype(bf16)
    ddown_ref[...] = contract_lead(pooled_ref[...], low)
    for image in range(area_ref.shape[0]):
        area = 4 * sides[image] * sides[image]
        area_ref[image : image + 1, :] = jnp.full((1, bottleneck), area, jnp.int32).astype(f32)
    dpool = contract_last(low, down_ref[...]) / area_ref[...]
    dpool_ref[...] = dpool
    both = jnp.concatenate([dpool, dpool], axis=1)
    weights = weights_ref[...]
    total = column_total(weights * sums_ref[1] + both * sums_ref[3])
    product = column_total(weights * sums_ref[2] + both * sums_ref[4])
    lanes = weights.shape[1]
    put(tile_ref, 0, total)
    put(tile_ref, lanes // 128, (product - param_ref[1:2, :] * total) / param_ref[0:1, :])
    send(send_ref, tile_ref)


def conv_back_kernel(
    sides,
    second_ref,
    ab_ref,
    recv_ref,
    param_ref,
    count_ref,
    dmixed_ref,
    weights_ref,
    dpool_ref,
    first_ref,
    ab_in_ref,
    w_ref,
    x_ref,
    dsecond_ref,
    dfirst_ref,
    in_ref,
    grads_ref,
    stat_ref,
    column_ref,
    acc_ref,
    tile_ref,
):
    step = pl.program_id(0)
    zeros_at_start(acc_ref, in_ref)
    edge_zeros_at_start(column_ref, 0, SIDE + 1)
    place = places()
    lanes = second_ref.shape[1]
    half = lanes // 2
    quarter = half // RADIX
    columns = TAPS * quarter

    @at_start
    def _():
        take(recv_ref, tile_ref)
        total = row_at(tile_ref, 0, lanes)
        product = row_at(tile_ref, lanes // 128, lanes)
        count = wide(count_ref[0:1, :], lanes)
        slant = ab_ref[0:1, :] * product / (count * param_ref[0:1, :])
        grads_ref[0:1, :] = total
        grads_ref[1:2, :] = product
        grads_ref[2:3, :] = slant
        grads_ref[3:4, :] = ab_ref[0:1, :] * total / count - param_ref[1:2, :] * slant

    def start(image):
        limit = 2 * sides[step * STEP + image]
        weights = weights_ref[pl.ds(step * STEP + image, 1), :] * ab_ref[2:3, :]
        dpool = dpool_ref[pl.ds(step * STEP + image, 1), :]
        dpool = jnp.concatenate([dpool, dpool], axis=1) * ab_ref[2:3, :]
        slant, level = 2.0 * grads_ref[2:3, :], grads_ref[3:4, :]
        for row in range(SIDE):
            here = of_row(image, row)
            mask = wide(row_mask(place, row, limit), lanes)
            dmixed = dmixed_ref[here, :]
            both = jnp.concatenate([dmixed, dmixed], axis=1)
            pre = second_ref[here, :] * ab_ref[2:3, :] + ab_ref[3:4, :]
            grad = twice_slope(pre) * (weights * both + dpool)
            grad = mask * (grad - (pre * slant + level))
            dsecond_ref[here, :] = grad.astype(bf16)

    def multiply(image):
        for group in range(RADIX):
            column_ref[image, SIDE : SIDE + 256, group * columns : (group + 1) * columns] = jnp.dot(
                dsecond_ref[of_image(image), group * half : (group + 1) * half],
                w_ref[:, group * columns : (group + 1) * columns],
                preferred_element_type=f32,
            )

    sums = [acc_ref[0], acc_ref[1]]
    inner = wide(place, quarter)

    def finish(image):
        limit = 2 * sides[step * STEP + image]
        for row in range(SIDE):
            here = of_row(image, row)
            mask = row_mask(place, row, limit)
            parts = []
            for group in range(RADIX):
                summed = []
                for side in range(3):
                    pieces = []
                    for up in range(3):
                        at = group * columns + (up * 3 + side) * quarter
                        start_row = (row + 2 - up) * SIDE
                        pieces.append(
                            column_ref[image, start_row : start_row + SIDE, at : at + quarter]
                        )
                    summed.append(pieces[0] + pieces[1] + pieces[2])
                low = jnp.where(inner == SIDE - 1, 0.0, pltpu.roll(summed[0], SIDE - 1, 0))
                high = jnp.where(inner == 0, 0.0, pltpu.roll(summed[2], 1, 0))
                parts.append(summed[1] + low + high)
            dact = jnp.concatenate(parts, axis=1)
            first = first_ref[here, :]
            pre = first * ab_in_ref[5:6, :] + ab_in_ref[6:7, :]
            normed = first * ab_in_ref[2:3, :] + ab_in_ref[3:4, :]
            grad = dact * (twice_slope(pre) * wide(0.5 * mask, half))
            dfirst_ref[here, :] = grad
            sums[0] = sums[0] + fold(grad)
            sums[1] = sums[1] + fold(grad * normed)

    def cross(image):
        here = of_image(image)
        in_ref[...] += contract_lead(dfirst_ref[here, :].astype(bf16), x_ref[here, :])

    stages(start, multiply, finish, cross)
    acc_ref[0], acc_ref[1] = sums

    @at_end
    def _():
        stat_ref[...] = jnp.zeros(stat_ref.shape, f32)
        put(stat_ref, 0, column_total(acc_ref[0]))
        put(stat_ref, half // 128, column_total(acc_ref[1]))


def conv_grad_kernel(aligned, odd, act_ref, dsecond_ref, _, *refs):
    if aligned:
        mine_ref, other_ref, conv_ref, patch_ref = refs
    else:
        conv_ref, patch_ref = refs
    zeros_at_start(conv_ref)
    edge_zeros_at_start(patch_ref, 1, SIDE)
    place = places()
    lanes = act_ref.shape[1]
    columns = TAPS * lanes // RADIX
    def start(image):
        for row in range(SIDE):
            write_patches(patch_ref, image, row, act_ref[of_row(image, row), :], place)

    def multiply(image):
        here = of_image(image)
        for group in range(RADIX):
            conv_ref[:, group * columns : (group + 1) * columns] += contract_lead(
                dsecond_ref[here, group * lanes : (group + 1) * lanes],
                patch_ref[image, SIDE : SIDE + 256, group * columns : (group + 1) * columns],
            )

    stages(start, multiply)

    if aligned:

        @at_end
        def _():
            for piece in range(mine_ref.shape[0]):
                for ref, side in ((mine_ref, odd[0]), (other_ref, 1 - odd[0])):
                    here = pl.ds(pl.multiple_of((2 * piece + side) * 8, 8), 8)
                    for pair in range(RADIX * TAPS // 2):
                        two = [
                            conv_ref[here, (2 * pair + k) * 128 : (2 * pair + k + 1) * 128]
                            for k in range(2)
                        ]
                        ref[piece, pair * 16 : pair * 16 + 16, :] = jnp.concatenate(
                            two, axis=0
                        ).astype(bf16)


def late_kernel(
    aligned, odd, recv_ref, terms_ref, count_ref, in_ref, cross_ref, ones_ref, grads_ref, *refs
):
    tile_ref = refs[-1]
    take(recv_ref, tile_ref)
    lanes = terms_ref.shape[1]
    total = row_at(tile_ref, 0, lanes)
    product = row_at(tile_ref, lanes // 128, lanes)
    count = wide(count_ref[0:1, :], lanes)
    slant = terms_ref[0:1, :] * terms_ref[2:3, :] * product / count
    level = terms_ref[0:1, :] * total / count - terms_ref[4:5, :] * slant
    grads_ref[0:1, :] = total
    grads_ref[1:2, :] = product
    grads_ref[2:3, :] = slant
    grads_ref[3:4, :] = level
    grads_ref[4:5, :] = terms_ref[0:1, :]
    grads_ref[5:8, :] = jnp.zeros((3, lanes), f32)
    if not aligned:
        return
    mine_ref, other_ref, full_ref, _ = refs
    columns = jnp.transpose(grads_ref[...])
    ones = column_total(ones_ref[...])
    full_ref[...] = (
        in_ref[...] * columns[:, 4:5]
        - cross_ref[...] * columns[:, 2:3]
        - ones * columns[:, 3:4]
    )
    rows = mine_ref.shape[1]
    groups = lanes // rows
    for piece in range(mine_ref.shape[0]):
        owner, pair = 2 * piece // groups, piece % (groups // 2)
        for ref, side in ((mine_ref, odd[0]), (other_ref, 1 - odd[0])):
            here = pl.ds(pl.multiple_of((2 * pair + side) * rows, rows), rows)
            ref[piece] = full_ref[here, owner * 128 : (owner + 1) * 128].astype(bf16)


def merge_kernel(mid_ref, mid_got_ref, in_ref, in_got_ref, out_ref):
    cut = in_ref.shape[1]
    for piece in range(out_ref.shape[0]):
        out_ref[piece, :cut, :] = (
            in_ref[piece].astype(f32) + in_got_ref[piece].astype(f32)
        ).astype(bf16)
        out_ref[piece, cut:, :] = (
            mid_ref[piece].astype(f32) + mid_got_ref[piece].astype(f32)
        ).astype(bf16)


def last_kernel(
    sides, dfirst_ref, first_ref, grads_ref, w_ref, slope_ref, terms_ref, out_ref, done_ref, low_ref
):
    step = pl.program_id(0)
    place = places()
    lanes = first_ref.shape[1]
    width = out_ref.shape[1]
    part = 512 if width % 512 == 0 else width
    def start(image):
        limit = 2 * sides[step * STEP + image]
        for row in range(SIDE):
            here = of_row(image, row)
            mask = wide(row_mask(place, row, limit), lanes)
            grad = dfirst_ref[here, :] * grads_ref[4:5, :]
            grad = grad - mask * (first_ref[here, :] * grads_ref[2:3, :] + grads_ref[3:4, :])
            low_ref[here, :] = grad.astype(bf16)

    def multiply(image):
        here = of_image(image)
        out_ref[here, :] = contract_last(low_ref[here, :], w_ref[...])

    def finish(image):
        for row in range(SIDE):
            here = of_row(image, row)
            for at in range(0, width, part):
                cut = slice(at, at + part)
                out_ref[here, cut] += slope_ref[here, cut].astype(f32) * terms_ref[4:5, cut]

    stages(start, multiply, finish)

    @at_end
    def _():
        done_ref[...] = jnp.zeros(done_ref.shape, f32)


def total_of(ref):
    total = ref[0].astype(f32)
    for j in range(1, ref.shape[0]):
        total = total + ref[j].astype(f32)
    return total.astype(bf16)


def total_kernel(part_ref, tile_ref, sum_ref, send_ref):
    sum_ref[...] = total_of(part_ref)
    send(send_ref, tile_ref)


def total_last_kernel(one_ref, part_ref, _, sum_ref):
    cut = one_ref.shape[0]
    sum_ref[:cut, :] = one_ref[...]
    sum_ref[cut:, :] = total_of(part_ref)


def shards_kernel(
    marks, place, *refs
):
    groups = len(refs) - 7
    out_ref, up_ref, down_ref, bias_ref, in_ref, mid_ref, all_ref = refs[groups:]
    for k in range(groups):
        all_ref[place[0] ^ k] = refs[k][...].astype(f32)

    def rows_from(start, count):
        return jnp.concatenate([all_ref[k, start : start + count, :] for k in range(groups)], axis=0)

    at = 0
    out_ref[...] = rows_from(at, marks[0])
    at += marks[0]
    up_ref[...] = rows_from(at, marks[1])
    at += marks[1]
    down_ref[...] = rows_from(at, marks[2])
    at += marks[2]
    bias_ref[...] = all_ref[0, at : at + 1, : bias_ref.shape[1]]
    at = marks[3]
    in_ref[...] = jnp.transpose(rows_from(at, marks[4]))
    at += marks[4]
    for tap in range(RADIX * TAPS):
        mid_ref[tap] = rows_from(at + tap * 8, 8)


def tiles(lanes, block=0):
    return pl.BlockSpec((STEP * 256, lanes), lambda i: (i, block))


def held(*shape):
    return pl.BlockSpec(shape, lambda i: (0,) * len(shape))


def token():
    return pl.BlockSpec(memory_space=pl.ANY)


def scalars():
    return pl.BlockSpec(memory_space=pltpu.SMEM)


def shaped(shape, dtype=f32):
    return jax.ShapeDtypeStruct(shape, dtype)


def call(kernel, steps, ins, outs, scratch=(), cost=5, limit=None, name=None):
    if limit is None:
        limit = 56 if steps > 1 else 24
    return pl.pallas_call(
        kernel,
        grid=(steps,),
        in_specs=ins,
        out_specs=[spec for spec, _ in outs],
        out_shape=[shape for _, shape in outs],
        scratch_shapes=[pltpu.VMEM(shape, dtype) for shape, dtype in scratch],
        compiler_params=pltpu.CompilerParams(
            dimension_semantics=("arbitrary",), vmem_limit_bytes=limit * 1024 * 1024
        ),
        cost_estimate=pl.CostEstimate(
            flops=int(cost * 1e9), bytes_accessed=int(cost * 3e6), transcendentals=0
        ),
        name=name,
    )


def whole_out(shape, dtype=f32):
    return held(*shape), shaped(shape, dtype)


def rows8(*vectors):
    stacked = jnp.stack(vectors, axis=0)
    return jnp.pad(stacked, ((0, 8 - len(vectors)), (0, 0)))


def local(
    features,
    half_sides,
    cotangent,
    conv_in,
    conv_mid,
    attn_down,
    attn_up,
    attn_bias,
    conv_out,
    gain_in,
    shift_in,
    gain_mid,
    shift_mid,
    gain_attn,
    shift_attn,
    gain_out,
    shift_out,
):
    images, pixels, width = features.shape
    rows = images * pixels
    steps = images // STEP
    pieces = lax.axis_size("fsdp")
    groups = lax.axis_size("dp")
    devices = pieces * groups
    images_all = images * devices
    bottleneck = conv_in.shape[1]
    att = attn_down.shape[1]
    mid = RADIX * bottleneck
    columns = TAPS * conv_mid.shape[2]
    odd = lax.rem(lax.axis_index("dp"), 2).reshape(1)

    down_rows, up_rows = attn_down.shape[0], attn_up.shape[1]
    own_columns = conv_mid.shape[3]
    small = [gain_in, shift_in, gain_mid, shift_mid, gain_attn, shift_attn, gain_out, shift_out, attn_bias]
    lengths = [item.shape[0] for item in small]
    aligned = (
        own_columns % 16 == 0
        and width == 128 * pieces
        and bottleneck == 8 * devices
        and groups == 4
        and pieces == len(ORDER)
    )
    mid_cut = conv_mid.transpose(0, 1, 3, 2)
    if aligned:
        place = lax.axis_index("fsdp").reshape(1)
        at = TAPS * own_columns
        cut = (at + 128 + down_rows + up_rows + 16, 128)
        (most,) = call(
            prepare_kernel,
            1,
            [
                scalars(),
                held(RADIX, at, 128),
                held(*attn_down.shape),
                held(up_rows, att),
                held(*conv_out.shape),
            ]
            + [held(1, length) for length in lengths],
            [
                whole_out(cut, bf16),
            ],
            [((16, 128), f32)],
            2,
            56,
            name="last_prepare",
        )(
            odd,
            mid_cut.reshape(RADIX, at, 128),
            attn_down,
            attn_up.T,
            conv_out,
            *[item.reshape(1, -1) for item in small],
        )
        most = most[None]
        got = partner(most, 4)
        half, _ = lax.optimization_barrier((half_of(conv_in, 1), got))
        in_mine = gather_all(half).reshape(width, bottleneck // 2)
        in_other = neighbour(in_mine)
        most = jnp.concatenate([most, got], axis=0)
        most = jnp.concatenate([most, partner(most, 2)], axis=0)
        shards = [most, partner(most, 1)]
        shards += [neighbour(item) for item in shards]
    else:
        in_send = jnp.broadcast_to(half_of(conv_in, 1)[None], (pieces, conv_in.shape[0], 128))
        vectors = jnp.stack([jnp.pad(item, (0, 128 - item.shape[0])) for item in small])
        most = jnp.concatenate([mid_cut.reshape(-1, 128), attn_down, attn_up.T, vectors], axis=0)
        most = lax.all_gather(most, "fsdp")
        at = RADIX * TAPS * own_columns
        in_mine = swap_all(in_send, "fsdp").reshape(width, bottleneck // 2)
        in_other = neighbour(in_mine)
        whole_down = most[:, at : at + down_rows].reshape(bottleneck, att)
        whole_up = most[:, at + down_rows : at + down_rows + up_rows].reshape(mid, att)

    x = features.reshape(rows, width)
    cot = cotangent.reshape(rows, width)

    def tiled(lanes, dtype=f32):
        return tiles(lanes), shaped((rows, lanes), dtype)

    def sending(count, dtype=f32):
        return whole_out((devices, count, 128), dtype)

    def received(count):
        return held(devices, count, 128)

    first, whole_in, out = call(
        first_kernel,
        steps,
        [scalars(), scalars(), tiles(width), held(width, bottleneck // 2), held(width, bottleneck // 2)],
        [tiled(bottleneck), whole_out((width, bottleneck), bf16), sending(8)],
        [((2, 8, bottleneck), f32), ((8, 128), f32)],
        8,
        name="first",
    )(half_sides, odd, x, in_mine, in_other)
    got = swap_all(out, AXES)
    cross, x_sum, power_x = call(
        cross_kernel,
        steps,
        [scalars(), tiles(width), tiles(bottleneck)],
        [
            whole_out((bottleneck, width)),
            whole_out((8, width)),
            whole_out((8, 128)),
        ],
        [((8, width), f32)],
        10,
        name="cross",
    )(half_sides, x, first)

    ins = [scalars(), tiles(bottleneck), received(8), token()]
    args = (half_sides, first, got, power_x)
    outs = [
        tiled(bottleneck, bf16),
        tiled(mid),
        whole_out((8, bottleneck)),
        whole_out((8, 128)),
        sending(8),
    ]
    scratch = [
        ((STEP, 256 + 2 * SIDE, RADIX * columns), bf16),
        ((2, 8, mid), f32),
        ((8, 128), f32),
    ]
    if aligned:
        ins += [scalars(), scalars()] + [held(*item.shape) for item in shards]
        args += (place, odd) + tuple(shards)
        outs += [whole_out((bottleneck, RADIX * columns), bf16)]
        outs += [whole_out((bottleneck, att), bf16), whole_out((mid, att), bf16)]
        outs += [whole_out((8, lanes)) for lanes in (mid, att, width, mid)]
        scratch += [((8, bottleneck), f32)]
    else:
        whole_mid = most[:, :at].reshape(pieces, RADIX * TAPS, own_columns, 128)
        whole_mid = whole_mid.transpose(0, 2, 1, 3).reshape(bottleneck, RADIX * columns)
        at += down_rows + up_rows
        found = [
            most[:, at + k, :length].reshape(-1).astype(f32) for k, length in enumerate(lengths)
        ]
        p_in, p_mid, p_attn, p_out = [rows8(found[2 * k], found[2 * k + 1]) for k in range(4)]
        p_bias = rows8(found[8])
        ins += [held(bottleneck, RADIX * columns), held(8, bottleneck)]
        args += (whole_mid, p_in)
    act_low, second, terms_in, count, out, *rest = call(
        functools.partial(second_kernel, lengths if aligned else None),
        steps,
        ins,
        outs,
        scratch,
        15,
        name="second",
    )(*args)
    if aligned:
        whole_mid, whole_down, whole_up, p_mid, p_attn, p_out, p_bias = rest
    got = swap_all(out, AXES)

    pooled, squeeze, terms_mid, out = call(
        pool_kernel,
        steps,
        [
            scalars(),
            tiles(mid),
            received(8),
            held(8, mid),
            held(8, 128),
            held(bottleneck, att),
            held(8, 128),
        ],
        [
            whole_out((images, bottleneck), bf16),
            whole_out((images, att)),
            whole_out((8, mid)),
            sending(8),
        ],
        [((images, bottleneck), f32), ((8, 128), f32)],
        7,
        name="pool",
    )(half_sides, second, got, p_mid, count, whole_down, power_x)
    got = swap_all(out, AXES)

    if aligned:
        whole_w_out, whole_out_t = call(
            functools.partial(out_weights_kernel, TAPS * own_columns),
            1,
            [scalars(), scalars(), token()] + [held(*item.shape) for item in shards],
            [whole_out((bottleneck, width), bf16), whole_out((width, bottleneck), bf16)],
            (),
            1,
            name="last_weights",
        )(place, odd, pooled, *shards)
    else:
        whole_w_out = lax.all_gather(conv_out, "fsdp", axis=1, tiled=True)
        whole_out_t = whole_w_out.T
    wide_rows = 2 * width // 128
    mixed, weights, excite, gate, gram_out, colsum, power_mix, out = call(
        functools.partial(mix_kernel, images_all),
        steps,
        [
            scalars(),
            tiles(mid),
            held(8, mid),
            held(images, att),
            received(8),
            held(8, att),
            held(mid, att),
            held(8, mid),
            held(bottleneck, width),
        ],
        [
            tiled(bottleneck, bf16),
            whole_out((images, mid)),
            whole_out((images, att), bf16),
            whole_out((8, att)),
            whole_out((bottleneck, width)),
            whole_out((8, bottleneck)),
            whole_out((8, 128)),
            sending(wide_rows, bf16),
        ],
        [((bottleneck, bottleneck), f32), ((2, 8, bottleneck), f32), ((wide_rows, 128), f32)],
        11,
        name="mix",
    )(half_sides, second, terms_mid, squeeze, got, p_attn, whole_up, p_bias, whole_w_out)
    got = swap_all(out, AXES)

    block, slope, back, grad_out, terms_out, power_out, out = call(
        out_kernel,
        steps,
        [
            scalars(),
            tiles(bottleneck),
            tiles(width),
            tiles(width),
            received(wide_rows),
            held(8, width),
            held(8, 128),
            held(bottleneck, width),
            held(width, bottleneck),
        ],
        [
            tiled(width, bf16),
            tiled(width, bf16),
            tiled(bottleneck),
            whole_out((bottleneck, width)),
            whole_out((8, width)),
            whole_out((8, 128)),
            sending(wide_rows, bf16),
        ],
        [
            ((STEP * 256, width), f32),
            ((8, width), f32),
            ((8, 128), f32),
            ((wide_rows, 128), f32),
            ((8, width), f32),
            ((devices * wide_rows, 128), f32),
        ],
        25,
        name="output",
    )(half_sides, mixed, x, cot, got, p_out, count, whole_w_out, whole_out_t)
    got = swap_all(out, AXES)

    dmixed, sums, dup, dbias, dq, grads_out, out = call(
        gate_kernel,
        steps,
        [
            scalars(),
            tiles(mid),
            held(8, mid),
            tiles(bottleneck),
            tiles(bottleneck),
            received(wide_rows),
            held(8, width),
            held(8, width),
            held(8, 128),
            held(bottleneck, width),
            held(width, bottleneck),
            held(images, mid),
            held(images, att),
            held(images, att),
            held(8, att),
            held(mid, att),
            held(8, 128),
            held(8, 128),
        ],
        [
            tiled(bottleneck),
            whole_out((5, images, mid)),
            whole_out((mid, att)),
            whole_out((8, mid)),
            whole_out((images, att)),
            whole_out((8, width)),
            sending(8),
        ],
        [
            ((bottleneck, bottleneck), bf16),
            ((8, bottleneck), f32),
            ((wide_rows, 128), f32),
        ],
        13,
        name="gate",
    )(
        half_sides,
        second,
        terms_mid,
        back,
        mixed,
        got,
        terms_out,
        p_out,
        count,
        whole_w_out,
        whole_out_t,
        weights,
        excite,
        squeeze,
        gate,
        whole_up,
        power_out,
        power_mix,
    )
    got = swap_all(out, AXES)
    grad_conv_out = grad_out - colsum[0][:, None] * grads_out[3] - gram_out * grads_out[2]

    ddown, dpool, grads_attn, out = call(
        functools.partial(squeeze_kernel, images_all, width),
        1,
        [
            scalars(),
            held(images, att),
            held(images, att),
            held(8, att),
            received(8),
            held(images, bottleneck),
            held(bottleneck, att),
            held(images, mid),
            held(5, images, mid),
            held(8, mid),
            held(8, 128),
            held(8, width),
        ],
        [
            whole_out((bottleneck, att)),
            whole_out((images, bottleneck)),
            whole_out((8, att)),
            sending(8),
        ],
        [((8, 128), f32), ((images, bottleneck), f32)],
        1,
        name="squeeze",
    )(
        half_sides,
        dq,
        squeeze,
        gate,
        got,
        pooled,
        whole_down,
        weights,
        sums,
        p_mid,
        count,
        terms_out,
    )
    got = swap_all(out, AXES)

    out_cut = grad_conv_out.astype(bf16).reshape(bottleneck, pieces, -1).transpose(1, 0, 2)
    out_cut = out_cut.reshape(devices, -1, 128)
    bias_rows = jnp.pad(dbias[0].reshape(pieces, 1, up_rows), ((0, 0), (0, 0), (0, att - up_rows)))
    gates = jnp.concatenate(
        [
            dup.reshape(devices, -1, att),
            ddown.reshape(devices, -1, att),
            jnp.repeat(bias_rows, groups, axis=0),
        ],
        axis=1,
    ).astype(bf16)
    marks = [out_cut.shape[1], up_rows // groups, down_rows // groups]
    gates = jnp.concatenate([out_cut, gates], axis=1)
    gates = jnp.pad(gates, ((0, 0), (0, -gates.shape[1] % 16), (0, 0)))

    gates = to_owners(gates)
    dsecond, dfirst, in_grad, grads_mid, stat = call(
        conv_back_kernel,
        steps,
        [
            scalars(),
            tiles(mid),
            held(8, mid),
            received(8),
            held(8, mid),
            held(8, 128),
            tiles(bottleneck),
            held(images, mid),
            held(images, bottleneck),
            tiles(bottleneck),
            held(8, bottleneck),
            held(bottleneck, RADIX * columns),
            tiles(width),
        ],
        [
            tiled(mid, bf16),
            tiled(bottleneck),
            whole_out((bottleneck, width)),
            whole_out((8, mid)),
            whole_out((8, 128)),
        ],
        [
            ((STEP, 256 + 2 * SIDE, RADIX * columns), f32),
            ((2, 8, bottleneck), f32),
            ((8, 128), f32),
        ],
        20,
        name="conv_back",
    )(
        half_sides,
        second,
        terms_mid,
        got,
        p_mid,
        count,
        dmixed,
        weights,
        dpool,
        first,
        terms_in,
        whole_mid,
        x,
    )
    gates, out = call(
        total_kernel,
        1,
        [held(*gates.shape), held(8, 128)],
        [whole_out(gates.shape[1:], bf16), sending(8)],
        (),
        2,
        name="last_gates",
    )(gates, stat)
    got = swap_all(out, AXES)

    outs = []
    scratch = [((STEP, 256 + 2 * SIDE, RADIX * columns), bf16)]
    mid_rows = bottleneck // devices * RADIX * TAPS
    if aligned:
        outs += [whole_out((devices // 2, mid_rows, 128), bf16)] * 2
        scratch = [((bottleneck, RADIX * columns), f32)] + scratch
    else:
        outs += [whole_out((bottleneck, RADIX * columns))]
    conv_parts = call(
        functools.partial(conv_grad_kernel, aligned),
        steps,
        [scalars(), tiles(bottleneck), tiles(mid), token()],
        outs,
        scratch,
        15,
        name="conv_grad",
    )(odd, act_low, dsecond, gates)
    outs = [whole_out((8, bottleneck))]
    scratch = [((8, 128), f32)]
    in_rows = bottleneck // groups * (width // pieces) // 128
    if aligned:
        outs += [whole_out((devices // 2, in_rows, 128), bf16)] * 2
        scratch = [((bottleneck, width), f32)] + scratch
    grads_in, *in_parts = call(
        functools.partial(late_kernel, aligned),
        1,
        [
            scalars(),
            received(8),
            held(8, bottleneck),
            held(8, 128),
            held(bottleneck, width),
            held(bottleneck, width),
            held(8, width),
        ],
        outs,
        scratch,
        2,
        name="last_terms",
    )(odd, got, terms_in, count, in_grad, cross, x_sum)
    grad_features, done = call(
        last_kernel,
        steps,
        [
            scalars(),
            tiles(bottleneck),
            tiles(bottleneck),
            held(8, bottleneck),
            held(width, bottleneck),
            tiles(width),
            held(8, width),
        ],
        [tiled(width), whole_out((8, 128))],
        [((STEP * 256, bottleneck), bf16)],
        15,
        name="last",
    )(half_sides, dfirst, first, grads_in, whole_in, slope, terms_out)

    if aligned:
        mid_got, in_got = neighbour(conv_parts[1]), neighbour(in_parts[1])
        (late,) = call(
            merge_kernel,
            1,
            [held(*mid_got.shape)] * 2 + [held(*in_got.shape)] * 2,
            [whole_out((devices // 2, in_rows + mid_rows, 128), bf16)],
            (),
            2,
            name="last_merge",
        )(conv_parts[0], mid_got, in_parts[0], in_got)
    else:
        grad_conv_in = (
            in_grad * grads_in[4][:, None]
            - cross * grads_in[2][:, None]
            - column_total(x_sum) * grads_in[3][:, None]
        )
        in_cut = grad_conv_in.astype(bf16).reshape(bottleneck, pieces, -1).transpose(1, 0, 2)
        mid_cut = conv_parts[0].astype(bf16).reshape(devices, -1, RADIX * TAPS, 128)
        mid_cut = mid_cut.transpose(0, 2, 1, 3).reshape(devices, -1, 128)
        late = jnp.concatenate([in_cut.reshape(devices, -1, 128), mid_cut], axis=1)
        late = jnp.pad(late, ((0, 0), (0, -late.shape[1] % 16), (0, 0)))
        late = on_own_side(late)
    late = across_sides(late)
    (summed,) = call(
        total_last_kernel,
        1,
        [held(*gates.shape), held(*late.shape), token()],
        [whole_out((gates.shape[0] + late.shape[1], 128), bf16)],
        (),
        2,
        name="last_total",
    )(gates, late, done)
    marks += [gates.shape[0], in_rows]
    own_width = width // pieces
    if aligned:
        members = [summed] + [
            lax.ppermute(summed, "dp", [(i, i ^ k) for i in range(groups)])
            for k in range(1, groups)
        ]
        shard_out, shard_up, shard_down, shard_bias, shard_in, shard_mid = call(
            functools.partial(shards_kernel, marks),
            1,
            [scalars()] + [held(*summed.shape)] * groups,
            [
                whole_out((bottleneck, own_width)),
                whole_out((up_rows, att)),
                whole_out((down_rows, att)),
                whole_out((1, up_rows)),
                whole_out((own_width, bottleneck)),
                whole_out((RADIX * TAPS, own_columns, 128)),
            ],
            [((groups,) + summed.shape, f32)],
            2,
            name="last_shards",
        )(lax.axis_index("dp").reshape(1), *members)
        shard_bias = shard_bias.reshape(-1)
        shard_up = shard_up.T
        shard_mid = shard_mid.reshape(RADIX, TAPS, own_columns, 128).transpose(0, 1, 3, 2)
    else:
        summed = swap_all(jnp.broadcast_to(summed[None], (groups,) + summed.shape), "dp")
        summed = summed.astype(f32)
        shard_out = summed[:, : marks[0]].reshape(bottleneck, -1)
        at = marks[0]
        shard_up = summed[:, at : at + marks[1]].reshape(up_rows, att).T
        at += marks[1]
        shard_down = summed[:, at : at + marks[2]].reshape(down_rows, att)
        at += marks[2]
        shard_bias = summed[0, at, :up_rows]
        at = marks[3]
        shard_in = summed[:, at : at + in_rows].reshape(bottleneck, -1).T
        at += in_rows
        shard_mid = summed[:, at : at + mid_rows].reshape(groups, RADIX, TAPS, -1, 128)
        shard_mid = shard_mid.transpose(1, 2, 4, 0, 3).reshape(RADIX, TAPS, 128, own_columns)

    def own_part(row):
        length = row.shape[0] // pieces
        return lax.dynamic_slice_in_dim(row, lax.axis_index("fsdp") * length, length, 0)

    return (
        block.reshape(images, pixels, width),
        grad_features.reshape(images, pixels, width),
        grads_attn[2, :4],
        shard_in,
        shard_mid,
        shard_down,
        shard_up,
        shard_bias,
        shard_out,
        own_part(grads_in[1]),
        own_part(grads_in[0]),
        own_part(grads_mid[1]),
        own_part(grads_mid[0]),
        own_part(grads_attn[1]),
        own_part(grads_attn[0]),
        own_part(grads_out[1]),
        own_part(grads_out[0]),
    )


def solution(mesh):
    return jax.shard_map(
        local,
        mesh=mesh,
        in_specs=(
            P(("fsdp", "dp"), None, None),
            P(("fsdp", "dp")),
            P(("fsdp", "dp"), None, None),
            P("fsdp", None),
            P(None, None, None, "fsdp"),
            P("fsdp", None),
            P(None, "fsdp"),
            P("fsdp"),
            P(None, "fsdp"),
            P("fsdp"),
            P("fsdp"),
            P("fsdp"),
            P("fsdp"),
            P("fsdp"),
            P("fsdp"),
            P("fsdp"),
            P("fsdp"),
        ),
        out_specs=(
            P(("fsdp", "dp"), None, None),
            P(("fsdp", "dp"), None, None),
            P(),
            P("fsdp", None),
            P(None, None, None, "fsdp"),
            P("fsdp", None),
            P(None, "fsdp"),
            P("fsdp"),
            P(None, "fsdp"),
            P("fsdp"),
            P("fsdp"),
            P("fsdp"),
            P("fsdp"),
            P("fsdp"),
            P("fsdp"),
            P("fsdp"),
            P("fsdp"),
        ),
        check_vma=False,
    )
```
